32 devices in a mesh: groups: 2 (over x), example: 8 (over z, y), cls: 2 (over core).
Axes of the slice: x: 2, y: 2, z: 4, core: 2. Of those that a mesh axis runs over, the one named last changes fastest.
Arguments:
- features: bfloat16 [2048, 4096], P(('groups', 'example'), 'cls'), parts along dimension 0
- weights: float32 [8192, 8192], P(('groups', 'cls'), 'example'), parts along dimension 0
- labels: int32 [2048], P(('groups', 'example')), parts along dimension 0, may hold values from 0 to 8191
- counts: int32 [16], P(('groups', 'example')), parts along dimension 0, may hold values from 16 to 128, as said below
- active: int32 [2], P('groups'), parts along dimension 0, may hold values from 4096 to 8192
Outputs:
- moved: float32 [8192, 8192], P(('groups', 'cls'), 'example'), parts along dimension 0
- losses: float32 [2048], P(('groups', 'example')), parts along dimension 0
The draws below stay inside these ranges and needn't reach their ends.
There are 2 independent parts, one for each index of `groups`. The reference program is written for one: setup_inputs(seed, part) draws one part's arguments, and reference() takes and returns one part's arrays. A program takes and returns all parts, laid end to end along the dimension named above; each array names one. Nothing has to cross between parts.
Inputs may be any that keep to these rules, and one draw needn't show every extreme that they name: `counts`: each block has at least 16 valid slots; some block is full in every draw.
All inputs are finite; a program needn't handle non-finite values.
Results may differ from the reference program's by a relative error of at most 0.006.
Values may be sent and summed in bfloat16 or wider, within the bound.
No kernel may reach another device: no remote copies, remote signals or barrier semaphores. Data moves between devices by JAX's collectives and lax.ppermute only.
A program may use at most 128 MiB of HBM per device.

```python
import math
import jax
import jax.numpy as jnp
import numpy as np

FEATURES = 4096
CLASSES = 8192
EX_DEV = 128
ITERS = 2
EXAMPLES = 1024


def draw_features(key, part):
    feature_pos = jnp.arange(FEATURES).astype(jnp.float32) / FEATURES
    rough = jnp.exp(jax.random.uniform(jax.random.fold_in(key, 1), (FEATURES,), jnp.float32, jnp.log(0.7), jnp.log(1.4)))
    col_scale = 0.4 * jnp.power(10.0, feature_pos) * rough
    row_scale = jnp.exp(jax.random.uniform(jax.random.fold_in(key, 2), (EXAMPLES, 1), jnp.float32, jnp.log(0.6), jnp.log(1.6)))
    base = jax.random.truncated_normal(jax.random.fold_in(key, 3), -4.0, 4.0, (EXAMPLES, FEATURES), jnp.float32)
    values = base * row_scale * col_scale
    return values.astype(jnp.bfloat16)


def draw_weights(key, part):
    class_scale = jnp.exp(jax.random.uniform(jax.random.fold_in(key, 21), (1, CLASSES), jnp.float32, jnp.log(0.5), jnp.log(5.0)))
    base = jax.random.truncated_normal(jax.random.fold_in(key, 22), -4.0, 4.0, (FEATURES, CLASSES), jnp.float32)
    values = base * class_scale / jnp.sqrt(float(FEATURES))
    return values


def draw_counts(key, part):
    blocks = EXAMPLES // EX_DEV
    lowest = max(EX_DEV // 8, 1)
    first_draw = jax.random.randint(jax.random.fold_in(key, 31), (blocks,), lowest, EX_DEV + 1)
    second_draw = jax.random.randint(jax.random.fold_in(key, 32), (blocks,), lowest, EX_DEV + 1)
    full_block = jax.random.randint(jax.random.fold_in(key, 33), (), 0, blocks)
    values = jnp.minimum(first_draw, second_draw)
    return jnp.where(jnp.arange(blocks) == full_block, EX_DEV, values).astype(jnp.int32)


def plant(drawn, rng, low, top_value):
    longest = drawn.shape.index(max(drawn.shape))
    spots = []
    for shift in (0, 1):
        where = [jax.random.randint(jax.random.fold_in(rng, axis), (), 0, length) for axis, length in enumerate(drawn.shape)]
        where[longest] = (where[longest] + shift) % drawn.shape[longest]
        spots.append(tuple(where))
    return drawn.at[spots[0]].set(low).at[spots[1]].set(top_value)


def cumulative_ranks(amount, skew):
    weights = [(1 << 20) // math.isqrt(rank ** skew) + 1 for rank in range(1, amount + 1)]
    spread = 1 + sum(weights) // (1 << 30)
    return np.cumsum(np.array([max(1, weight // spread) for weight in weights]))


def skewed_ids(own_key, dims, amount, slope):
    grid = cumulative_ranks(amount, slope)
    lot = jax.random.randint(jax.random.fold_in(own_key, 1), dims, 0, int(grid[amount - 1]))
    grade = jnp.searchsorted(jnp.asarray(grid, jnp.int32), lot, side="right")
    return jax.random.permutation(jax.random.fold_in(own_key, 2), amount)[grade].astype(jnp.int32)


def setup_inputs(seed: int = 0, part: int = 0) -> dict:
    arg_keys = jax.random.split(jax.random.key(seed), 6)
    part_keys = jax.random.split(jax.random.fold_in(arg_keys[5], part), 6)
    features = draw_features(jax.random.fold_in(jax.random.fold_in(arg_keys[5], part), 71), part)
    weights = draw_weights(jax.random.fold_in(jax.random.fold_in(arg_keys[5], part), 71), part)
    labels = plant(skewed_ids(part_keys[2], (EXAMPLES,), CLASSES, 2), jax.random.fold_in(part_keys[2], 3), 0, CLASSES - 1).astype(jnp.int32)
    counts = draw_counts(jax.random.fold_in(jax.random.fold_in(arg_keys[5], part), 71), part)
    active = jax.random.randint(part_keys[4], (1,), CLASSES // 2, CLASSES + 1).astype(jnp.int32)
    return {"features": features, "weights": weights, "labels": labels, "counts": counts, "active": active}


NEGATIVE = -1e30
LEARNING_RATE = 2e-5
DAMPING_SHARE = 0.1
EPSILON = 1e-6


def reference(features, weights, labels, counts, active):
    row_index = jnp.arange(EXAMPLES)
    is_valid = ((row_index % EX_DEV) < counts[row_index // EX_DEV]).astype(jnp.float32)
    valid_total = jnp.sum(counts).astype(jnp.float32)
    active_count = active[0]
    target = (labels % active_count).astype(jnp.int32)
    class_index = jnp.arange(CLASSES)
    is_active = class_index < active_count
    is_label = class_index[None, :] == target[:, None]
    squares = (features.astype(jnp.float32) * features.astype(jnp.float32)).astype(jnp.bfloat16)
    current = weights
    moved = jnp.zeros_like(weights)
    denominator = None
    losses = None
    for iteration in range(ITERS):
        current_low = current.astype(jnp.bfloat16)
        logits = jnp.dot(features, current_low, preferred_element_type=jnp.float32)
        masked = jnp.where(is_active[None, :], logits, NEGATIVE)
        row_peak = jnp.max(masked, axis=1)
        exponent = jnp.exp(masked - row_peak[:, None])
        row_total = jnp.sum(exponent, axis=1)
        label_logit = jnp.sum(jnp.where(is_label, logits, 0.0), axis=1)
        probability = exponent / row_total[:, None]
        residual = (is_valid[:, None] * (probability - is_label.astype(jnp.float32)) / valid_total).astype(jnp.bfloat16)
        gradient = jnp.dot(features.T, residual, preferred_element_type=jnp.float32)
        if iteration == 0:
            fisher_weight = (is_valid[:, None] * probability * (1.0 - probability) / valid_total).astype(jnp.bfloat16)
            fisher = jnp.dot(squares.T, fisher_weight, preferred_element_type=jnp.float32)
            damping = DAMPING_SHARE * jnp.sum(fisher) / (FEATURES * CLASSES) + EPSILON
            denominator = fisher + damping
        change = gradient / denominator
        current = current - LEARNING_RATE * change
        moved = moved - change
        losses = is_valid * (row_peak + jnp.log(row_total) - label_logit)
    return moved, losses
```

```python
import functools

import jax
import jax.numpy as jnp
from jax import lax
from jax.experimental import pallas as pl
from jax.experimental.pallas import tpu as pltpu
from jax.sharding import PartitionSpec as P

ITERS = 2
NEGATIVE = -1e30
LEARNING_RATE = 2e-05
DAMPING_SHARE = 0.1
EPSILON = 1e-06

F32 = jnp.float32
BF16 = jnp.bfloat16
VMEM = pl.BlockSpec(memory_space=pltpu.VMEM)
SMEM = pl.BlockSpec(memory_space=pltpu.SMEM)
STEP = 64
LANES = 128


def params(mib=24):
    return pltpu.CompilerParams(vmem_limit_bytes=mib << 20)


def swap(x, axis, n, offset):
    return lax.ppermute(x, axis, [(i, i ^ offset) for i in range(n)])


def gather_blocks(x, n):
    if n != 8:
        return [x] + [swap(x, "example", n, j) for j in range(1, n)]
    z_size, y_size = 4, 2

    def along_z(value, pairs):
        full = [(a * y_size + y, b * y_size + y) for a, b in pairs for y in range(y_size)]
        return lax.ppermute(value, "example", full)

    z = lax.axis_index("example") // y_size
    middle = (z == 1) | (z == 2)
    near = along_z(x, [(0, 1), (1, 0), (2, 3), (3, 2)])
    inner = along_z(x, [(1, 2), (2, 1)])
    y_own = swap(x, "example", n, 1)
    ends = along_z(inner, [(1, 0), (2, 3)])
    cross = along_z(near, [(1, 2), (2, 1)])
    y_near = swap(near, "example", n, 1)
    far = along_z(cross, [(1, 0), (2, 3)])
    second = jnp.where(middle, cross, ends)
    y_second = swap(second, "example", n, 1)
    third = jnp.where(middle, inner, far)
    y_third = swap(third, "example", n, 1)
    return [x, y_own, near, y_near, second, y_second, third, y_third]


def logits_kernel(count, *refs):
    blocks, w_ref = refs[:count], refs[count]
    out_ref, turned_ref = refs[count + 1 :]
    rows = blocks[0].shape[0]
    columns = 256
    for k in range(count):
        turned_ref[:, k * rows : (k + 1) * rows] = blocks[k][...].T
    for start in range(0, w_ref.shape[1], columns):
        for k in range(count):
            out_ref[k * rows : (k + 1) * rows, start : start + columns] = jnp.dot(
                blocks[k][...], w_ref[:, start : start + columns], preferred_element_type=F32
            )


def partial_logits(blocks, w_low):
    rows = sum(b.shape[0] for b in blocks)
    return pl.pallas_call(
        functools.partial(logits_kernel, len(blocks)),
        out_shape=(
            jax.ShapeDtypeStruct((rows, w_low.shape[1]), F32),
            jax.ShapeDtypeStruct((w_low.shape[0], rows), BF16),
        ),
        in_specs=[VMEM] * (len(blocks) + 1),
        out_specs=(VMEM, VMEM),
        compiler_params=params(),
        name="partial_logits",
    )(*blocks, w_low)


def lane_pack(columns, rows):
    lane = lax.broadcasted_iota(jnp.int32, (rows, LANES), 1)
    packed = jnp.zeros((rows, LANES), F32)
    for k, column in enumerate(columns):
        packed = jnp.where(lane == k, column, packed)
    return packed


def first_stats_kernel(previous, own_ref, other_ref, scalar_ref, *refs):
    earlier = refs[:previous]
    e_ref, stats_ref, pack_ref = refs[previous:]
    rows, classes = own_ref.shape
    active, class_start = scalar_ref[0], scalar_ref[1]

    def step(i, _):
        at = pl.ds(pl.multiple_of(i * STEP, STEP), STEP)
        logits = own_ref[at, :] + other_ref[at, :]
        index = class_start + lax.broadcasted_iota(jnp.int32, (1, classes), 1)
        live = index < active
        peak = jnp.max(jnp.where(live, logits, NEGATIVE), axis=1, keepdims=True)
        e = jnp.where(live, jnp.exp(logits - peak), 0.0)
        e_ref[at, :] = e
        total = jnp.sum(e, axis=1, keepdims=True)
        square = jnp.sum(e * e, axis=1, keepdims=True)
        pack_ref[at, :] = lane_pack((peak, total, square), STEP)
        return 0

    lax.fori_loop(0, rows // STEP, step, 0)
    done = 0
    for ref in earlier:
        stats_ref[:, done : done + ref.shape[1]] = ref[...]
        done += ref.shape[1]
    stats_ref[:, done:] = pack_ref[...].T[0:8, :]


def first_stats(own, other, scalars, earlier):
    rows = own.shape[0]
    total = rows + sum(s.shape[1] for s in earlier)
    return pl.pallas_call(
        functools.partial(first_stats_kernel, len(earlier)),
        out_shape=(
            jax.ShapeDtypeStruct(own.shape, F32),
            jax.ShapeDtypeStruct((8, total), F32),
        ),
        in_specs=[VMEM, VMEM, SMEM] + [VMEM] * len(earlier),
        out_specs=(VMEM, VMEM),
        scratch_shapes=[pltpu.VMEM((rows, LANES), F32)],
        compiler_params=params(),
        name="first_stats",
    )(own, other, scalars, *earlier)


def combine(stats_refs, rows):
    n = len(stats_refs)

    def row(d, k):
        ref = stats_refs[d]
        parts = [ref[k : k + 1, (j ^ d) * rows : (j ^ d) * rows + rows] for j in range(n)]
        return jnp.concatenate(parts, axis=1)

    peaks = [row(d, 0) for d in range(n)]
    peak = functools.reduce(jnp.maximum, peaks)
    scales = [jnp.exp(p - peak) for p in peaks]
    total = sum(row(d, 1) * scales[d] for d in range(n))
    return row, peak, scales, total


def to_columns(lines):
    width = lines[0].shape[1]
    stacked = jnp.concatenate(list(lines) + [jnp.zeros((LANES - len(lines), width), F32)], axis=0)
    return stacked.T


def first_weights_kernel(n, groups, entries, *refs):
    stats = refs[:n]
    side_ref, scalar_ref = refs[n], refs[n + 1]
    e_refs = refs[n + 2 : n + 2 + groups]
    residual_ref, fisher_ref, damping_ref, column_ref = refs[n + 2 + groups :]
    rows = side_ref.shape[2]
    classes = residual_ref.shape[1]
    class_start = scalar_ref[1]
    row, peak, scales, total = combine(stats, rows)
    square = sum(row(d, 2) * (scales[d] * scales[d]) for d in range(n))
    target = jnp.concatenate([side_ref[j, 0:1, :] for j in range(n)], axis=1)
    norm = jnp.concatenate([side_ref[j, 1:2, :] for j in range(n)], axis=1)
    valid = (target >= 0.0).astype(F32)
    valid_total = jnp.sum(valid, axis=1, keepdims=True)
    share = valid / valid_total
    inverse = 1.0 / total
    spread = share * (1.0 - square * inverse * inverse)
    fisher_sum = jnp.sum(norm * spread, axis=1, keepdims=True)
    damping_ref[...] = jnp.broadcast_to(
        DAMPING_SHARE * fisher_sum / entries + EPSILON, damping_ref.shape
    )
    column_ref[...] = to_columns((scales[0] * inverse, share, target))
    done = 0
    for e_ref in e_refs:
        def step(i, _, e_ref=e_ref, done=done):
            start = pl.multiple_of(i * STEP, STEP)
            at = pl.ds(pl.multiple_of(done + start, STEP), STEP)
            column = column_ref[at, :]
            probability = e_ref[pl.ds(start, STEP), :] * column[:, 0:1]
            index = class_start + lax.broadcasted_iota(jnp.int32, (1, classes), 1)
            hit = index == column[:, 2:3].astype(jnp.int32)
            part = column[:, 1:2]
            residual_ref[at, :] = (part * (probability - hit.astype(F32))).astype(BF16)
            fisher_ref[at, :] = (part * probability * (1.0 - probability)).astype(BF16)
            return 0

        lax.fori_loop(0, e_ref.shape[0] // STEP, step, 0)
        done += e_ref.shape[0]


def first_weights(stats, side, scalars, e_parts, entries):
    n = len(stats)
    all_rows = sum(e.shape[0] for e in e_parts)
    classes = e_parts[0].shape[1]
    weight = pltpu.VMEM((all_rows, classes), BF16)
    return pl.pallas_call(
        functools.partial(first_weights_kernel, n, len(e_parts), float(entries)),
        out_shape=(weight, weight, jax.ShapeDtypeStruct((1, LANES), F32)),
        in_specs=[VMEM] * (n + 1) + [SMEM] + [VMEM] * len(e_parts),
        out_specs=(VMEM, VMEM, VMEM),
        scratch_shapes=[pltpu.VMEM((all_rows, LANES), F32)],
        compiler_params=params(),
        name="first_weights",
    )(*stats, side, scalars, *e_parts)


def update_kernel(start, turned_ref, plain_ref, w_ref, residual_ref, fisher_ref, damping_ref,
                  moved_ref, inverse_ref, logits_ref, low_ref):
    features = turned_ref.shape[0]
    columns = moved_ref.shape[1]
    tile = 512
    damping = damping_ref[0:1, 0:1]
    own = slice(start, start + columns)

    def step(i, _):
        at = pl.ds(pl.multiple_of(i * tile, tile), tile)
        turned = turned_ref[at, :]
        gradient = jnp.dot(turned, residual_ref[:, own], preferred_element_type=F32)
        fisher = jnp.dot(turned * turned, fisher_ref[:, own], preferred_element_type=F32)
        inverse = 1.0 / (fisher + damping)
        change = gradient * inverse
        inverse_ref[at, :] = inverse
        moved_ref[at, :] = -change
        low_ref[at, :] = (w_ref[at, own] - LEARNING_RATE * change).astype(BF16)
        return 0

    lax.fori_loop(0, features // tile, step, 0)

    def logit_step(i, _):
        at = pl.ds(pl.multiple_of(i * tile, tile), tile)
        logits_ref[at, :] = jnp.dot(plain_ref[at, :], low_ref[...], preferred_element_type=F32)
        return 0

    lax.fori_loop(0, plain_ref.shape[0] // tile, logit_step, 0)


def update(turned, plain, weights, residual, fisher_weight, damping, start, columns):
    features, rows = turned.shape
    return pl.pallas_call(
        functools.partial(update_kernel, start),
        out_shape=(
            pltpu.VMEM((features, columns), F32),
            pltpu.VMEM((features, columns), F32),
            jax.ShapeDtypeStruct((rows, columns), F32),
        ),
        in_specs=[VMEM] * 6,
        out_specs=(VMEM, VMEM, VMEM),
        scratch_shapes=[pltpu.VMEM((features, columns), BF16)],
        compiler_params=params(),
        name="update",
    )(turned, plain, weights, residual, fisher_weight, damping)


def last_stats_kernel(chunks, *refs):
    own, other = refs[:chunks], refs[chunks : 2 * chunks]
    side_ref, scalar_ref = refs[2 * chunks : 2 * chunks + 2]
    e_ref, stats_ref, pack_ref, column_ref = refs[2 * chunks + 2 :]
    all_rows, classes = e_ref.shape
    active, class_start = scalar_ref[0], scalar_ref[1]
    n = side_ref.shape[0]
    column_ref[...] = to_columns(
        (jnp.concatenate([side_ref[j, 0:1, :] for j in range(n)], axis=1),)
    )

    def step(i, _):
        at = pl.ds(pl.multiple_of(i * STEP, STEP), STEP)
        logits = jnp.concatenate(
            [a[at, :] + b[at, :] for a, b in zip(own, other)], axis=1
        )
        index = class_start + lax.broadcasted_iota(jnp.int32, (1, classes), 1)
        live = index < active
        hit = index == column_ref[at, 0:1].astype(jnp.int32)
        label = jnp.sum(jnp.where(hit, logits, 0.0), axis=1, keepdims=True)
        peak = jnp.max(jnp.where(live, logits, NEGATIVE), axis=1, keepdims=True)
        e = jnp.where(live, jnp.exp(logits - peak), 0.0)
        e_ref[at, :] = e
        total = jnp.sum(e, axis=1, keepdims=True)
        pack_ref[at, :] = lane_pack((peak, total, label), STEP)
        return 0

    lax.fori_loop(0, all_rows // STEP, step, 0)
    stats_ref[...] = pack_ref[...].T[0:8, :]


def last_stats(own, other, side, scalars):
    all_rows = own[0].shape[0]
    classes = sum(c.shape[1] for c in own)
    return pl.pallas_call(
        functools.partial(last_stats_kernel, len(own)),
        out_shape=(
            pltpu.VMEM((all_rows, classes), F32),
            jax.ShapeDtypeStruct((8, all_rows), F32),
        ),
        in_specs=[VMEM] * (2 * len(own) + 1) + [SMEM],
        out_specs=(VMEM, VMEM),
        scratch_shapes=[pltpu.VMEM((all_rows, LANES), F32)] * 2,
        compiler_params=params(),
        name="last_stats",
    )(*own, *other, side, scalars)


def finish_kernel(n, chunks, *refs):
    stats = refs[:n]
    side_ref, scalar_ref, e_ref, turned_ref = refs[n : n + 4]
    moved_refs = refs[n + 4 : n + 4 + chunks]
    inverse_refs = refs[n + 4 + chunks : n + 4 + 2 * chunks]
    out_ref, loss_ref, residual_ref, column_ref = refs[n + 4 + 2 * chunks :]
    rows = side_ref.shape[2]
    all_rows, classes = e_ref.shape
    tile = out_ref.shape[0]
    program = pl.program_id(0)

    @pl.when(program == 0)
    def _():
        class_start = scalar_ref[1]
        row, peak, scales, total = combine(stats, rows)
        label = sum(row(d, 2) for d in range(n))
        target = jnp.concatenate([side_ref[j, 0:1, :] for j in range(n)], axis=1)
        valid = (target >= 0.0).astype(F32)
        share = valid / jnp.sum(valid, axis=1, keepdims=True)
        losses = valid * (peak + jnp.log(total) - label)
        loss_ref[...] = losses[:, 0:rows]
        column_ref[...] = to_columns((scales[0] / total, share, target))

        def step(i, _):
            at = pl.ds(pl.multiple_of(i * STEP, STEP), STEP)
            column = column_ref[at, :]
            probability = e_ref[at, :] * column[:, 0:1]
            index = class_start + lax.broadcasted_iota(jnp.int32, (1, classes), 1)
            hit = index == column[:, 2:3].astype(jnp.int32)
            residual_ref[at, :] = (column[:, 1:2] * (probability - hit.astype(F32))).astype(BF16)
            return 0

        lax.fori_loop(0, all_rows // STEP, step, 0)

    at = pl.ds(pl.multiple_of(program * tile, tile), tile)
    turned = turned_ref[at, :]
    done = 0
    for moved_ref, inverse_ref in zip(moved_refs, inverse_refs):
        own = slice(done, done + moved_ref.shape[1])
        gradient = jnp.dot(turned, residual_ref[:, own], preferred_element_type=F32)
        out_ref[:, own] = moved_ref[at, :] - gradient * inverse_ref[at, :]
        done += moved_ref.shape[1]


def finish(stats, side, scalars, e, turned, moved, inverse):
    n = len(stats)
    features, all_rows = turned.shape
    classes = e.shape[1]
    rows = side.shape[2]
    tile = 256
    return pl.pallas_call(
        functools.partial(finish_kernel, n, len(moved)),
        out_shape=(
            jax.ShapeDtypeStruct((features, classes), F32),
            jax.ShapeDtypeStruct((1, rows), F32),
        ),
        grid=(features // tile,),
        in_specs=[VMEM] * (n + 1) + [SMEM] + [VMEM] * (2 + 2 * len(moved)),
        out_specs=(
            pl.BlockSpec((tile, classes), lambda i: (i, 0)),
            pl.BlockSpec((1, rows), lambda i: (0, 0)),
        ),
        scratch_shapes=[pltpu.VMEM((all_rows, classes), BF16), pltpu.VMEM((all_rows, LANES), F32)],
        compiler_params=params(),
        name="finish",
    )(*stats, side, scalars, e, turned, *moved, *inverse)


def body(n, n_cls, features, weights, labels, counts, active):
    rows = features.shape[0]
    feature_count, classes = weights.shape
    entries = feature_count * n_cls * classes * n
    class_start = lax.axis_index("example") * classes
    scalars = jnp.stack([active[0], class_start]).astype(jnp.int32)

    slots = gather_blocks(features, n)
    w_low = weights.astype(BF16)

    target = jnp.where(jnp.arange(rows) < counts[0], labels % active[0], -1)
    low_squares = (features * features).astype(F32)
    norm = jnp.sum(low_squares, axis=1)
    norm = norm + swap(norm, "cls", n_cls, 1)
    side = jnp.stack([target.astype(F32), norm])[None]
    offset = 1
    while offset < n:
        side = jnp.concatenate([side, swap(side, "example", n, offset)], axis=0)
        offset *= 2

    bounds = [0] + list(range(1, n, 2)) + [n]
    groups = [slots[a:b] for a, b in zip(bounds[:-1], bounds[1:])]
    turned_parts, e_parts, own_stats = [], [], None
    for group in groups:
        logits, turned = partial_logits(group, w_low)
        turned_parts.append(turned)
        other = swap(logits, "cls", n_cls, 1)
        earlier = [] if own_stats is None else [own_stats]
        e, own_stats = first_stats(logits, other, scalars, earlier)
        e_parts.append(e)
    plain = jnp.concatenate(slots, axis=0)
    turned = jnp.concatenate(turned_parts, axis=1)

    stats = [own_stats] + [swap(own_stats, "example", n, d) for d in range(1, n)]
    residual, fisher_weight, damping = first_weights(stats, side, scalars, e_parts, entries)
    columns = 256
    moved, inverse, own, other = [], [], [], []
    for start in range(0, classes, columns):
        a, b, c = update(
            turned, plain, weights, residual, fisher_weight, damping, start, columns
        )
        moved.append(a)
        inverse.append(b)
        own.append(c)
        other.append(swap(c, "cls", n_cls, 1))
    e, own_stats = last_stats(own, other, side, scalars)
    stats = [own_stats] + [swap(own_stats, "example", n, d) for d in range(1, n)]
    out, losses = finish(stats, side, scalars, e, turned, moved, inverse)
    return out, losses.reshape(rows)


def solution(mesh):
    return jax.shard_map(
        functools.partial(body, mesh.shape["example"], mesh.shape["cls"]),
        mesh=mesh,
        in_specs=(
            P(("groups", "example"), "cls"),
            P(("groups", "cls"), "example"),
            P(("groups", "example")),
            P(("groups", "example")),
            P("groups"),
        ),
        out_specs=(P(("groups", "cls"), "example"), P(("groups", "example"))),
        check_vma=False,
    )
```

```python
import functools

import jax
import jax.numpy as jnp
from jax import lax
from jax.experimental import pallas as pl
from jax.experimental.pallas import tpu as pltpu
from jax.sharding import PartitionSpec as P

ITERS = 2
NEGATIVE = -1e30
LEARNING_RATE = 2e-05
DAMPING_SHARE = 0.1
EPSILON = 1e-06

F32 = jnp.float32
BF16 = jnp.bfloat16
VMEM = pl.BlockSpec(memory_space=pltpu.VMEM)
SMEM = pl.BlockSpec(memory_space=pltpu.SMEM)
STEP = 64
ANY = pl.BlockSpec(memory_space=pl.ANY)
LANES = 128


def params(mib=10):
    return pltpu.CompilerParams(vmem_limit_bytes=mib << 20)


def cost(flops=0, nbytes=0):
    return pl.CostEstimate(flops=int(flops), bytes_accessed=int(nbytes), transcendentals=0)


def swap(x, axis, n, offset):
    return lax.ppermute(x, axis, [(i, i ^ offset) for i in range(n)])


def gather_blocks(x, n):
    if n != 8:
        return [x] + [swap(x, "example", n, j) for j in range(1, n)]
    z_size, y_size = 4, 2

    def along_z(value, pairs):
        full = [(a * y_size + y, b * y_size + y) for a, b in pairs for y in range(y_size)]
        return lax.ppermute(value, "example", full)

    z = lax.axis_index("example") // y_size
    middle = (z == 1) | (z == 2)
    near = along_z(x, [(0, 1), (1, 0), (2, 3), (3, 2)])
    inner = along_z(x, [(1, 2), (2, 1)])
    y_own = swap(x, "example", n, 1)
    ends = along_z(inner, [(1, 0), (2, 3)])
    cross = along_z(near, [(1, 2), (2, 1)])
    y_near = swap(near, "example", n, 1)
    far = along_z(cross, [(1, 0), (2, 3)])
    second = jnp.where(middle, cross, ends)
    y_second = swap(second, "example", n, 1)
    third = jnp.where(middle, inner, far)
    y_third = swap(third, "example", n, 1)
    return [x, y_own, near, y_near, second, y_second, third, y_third]


def logits_kernel(count, start, refs_in, *refs):
    blocks, w_ref = refs[:count], refs[count]
    out_ref, plain_ref, turned_ref = refs[refs_in:]
    rows = blocks[0].shape[0]
    columns = 256
    for k in range(count):
        at = slice(start + k * rows, start + (k + 1) * rows)
        plain_ref[at, :] = blocks[k][...]
        turned_ref[:, at] = blocks[k][...].T
    for first in range(0, w_ref.shape[1], columns):
        for k in range(count):
            out_ref[k * rows : (k + 1) * rows, first : first + columns] = jnp.dot(
                blocks[k][...], w_ref[:, first : first + columns], preferred_element_type=F32
            )


def arriving_logits(blocks, w_low, start, all_rows, buffers, token):
    rows = sum(b.shape[0] for b in blocks)
    features, classes = w_low.shape
    extra = list(buffers) + ([] if token is None else [token])
    count = len(blocks)
    return pl.pallas_call(
        functools.partial(logits_kernel, count, start, count + 1 + len(extra)),
        out_shape=(
            jax.ShapeDtypeStruct((rows, classes), F32),
            pltpu.VMEM((all_rows, features), BF16),
            pltpu.VMEM((features, all_rows), BF16),
        ),
        in_specs=[VMEM] * (count + 1) + [VMEM] * len(extra),
        out_specs=(VMEM, VMEM, VMEM),
        input_output_aliases={count + 1: 1, count + 2: 2} if buffers else {},
        compiler_params=params(),
        cost_estimate=cost(2 * rows * features * classes),
        name="arriving_logits",
    )(*blocks, w_low, *extra)


def lane_pack(columns, rows):
    lane = lax.broadcasted_iota(jnp.int32, (rows, LANES), 1)
    packed = jnp.zeros((rows, LANES), F32)
    for k, column in enumerate(columns):
        packed = jnp.where(lane == k, column, packed)
    return packed


def put_stats(stats_ref, place, packed):
    lines = packed.T
    line = jnp.concatenate([lines[k : k + 1, :] for k in range(3)], axis=1)
    here = lax.broadcasted_iota(jnp.int32, stats_ref.shape, 0) == place
    stats_ref[...] = jnp.where(here, line, stats_ref[...])


def first_stats_kernel(slot, last, refs_in, own_ref, other_ref, scalar_ref, *refs):
    outs = refs[refs_in:]
    e_ref, stats_ref, pack_ref = outs[0], outs[1], outs[-1]
    rows, classes = own_ref.shape
    active, class_start, place = scalar_ref[0], scalar_ref[1], scalar_ref[2]
    index = class_start + lax.broadcasted_iota(jnp.int32, (1, classes), 1)
    live = index < active
    base = slot * LANES

    def step(i, _):
        start = pl.multiple_of(i * STEP, STEP)
        at = pl.ds(start, STEP)
        logits = own_ref[at, :] + other_ref[at, :]
        peak = jnp.max(jnp.where(live, logits, NEGATIVE), axis=1, keepdims=True)
        e = jnp.where(live, jnp.exp(logits - peak), 0.0)
        e_ref[pl.ds(pl.multiple_of(base + start, STEP), STEP), :] = e
        total = jnp.sum(e, axis=1, keepdims=True)
        square = jnp.sum(e * e, axis=1, keepdims=True)
        pack_ref[at, :] = lane_pack((peak, total, square), STEP)
        return 0

    lax.fori_loop(0, rows // STEP, step, 0)
    for k in range(rows // LANES):
        put_stats(stats_ref, place ^ (slot + k), pack_ref[k * LANES : (k + 1) * LANES, :])
    if last:
        outs[2][...] = jnp.broadcast_to(stats_ref[...][None], outs[2].shape)


def first_stats(own, other, scalars, slot, n, buffers):
    rows, classes = own.shape
    last = slot + rows // LANES == n
    shapes = [pltpu.VMEM((n * LANES, classes), F32), pltpu.VMEM((n, 3 * LANES), F32)]
    if last:
        shapes.append(jax.ShapeDtypeStruct((n, n, 3 * LANES), F32))
    return pl.pallas_call(
        functools.partial(first_stats_kernel, slot, last, len(buffers)),
        out_shape=tuple(shapes),
        in_specs=[VMEM, VMEM, SMEM] + [VMEM] * len(buffers),
        out_specs=(VMEM,) * len(shapes),
        input_output_aliases={3: 0, 4: 1} if buffers else {},
        scratch_shapes=[pltpu.VMEM((rows, LANES), F32)],
        compiler_params=params(),
        cost_estimate=cost(0, 24 * rows * classes),
        name="first_stats",
    )(own, other, scalars, *buffers)


def combine(own_ref, all_ref):
    n = all_ref.shape[0]
    part = lambda d, k: all_ref[d, :, k * LANES : (k + 1) * LANES]
    peaks = [part(d, 0) for d in range(n)]
    peak = functools.reduce(jnp.maximum, peaks)
    scales = [jnp.exp(p - peak) for p in peaks]
    total = sum(part(d, 1) * scales[d] for d in range(n))
    own_scale = jnp.exp(own_ref[:, 0:LANES] - peak)
    return part, peak, scales, total, own_scale


def to_slots(value, line_ref, place):
    n = value.shape[0]
    line_ref[...] = value
    return jnp.concatenate([line_ref[pl.ds(place ^ j, 1), :] for j in range(n)], axis=0)


def to_columns(lines):
    stacked = jnp.concatenate(lines, axis=0)
    rest = jnp.zeros((LANES - stacked.shape[0], LANES), F32)
    return jnp.concatenate([stacked, rest], axis=0).T


def first_weights_kernel(entries, own_ref, all_ref, side_ref, scalar_ref, e_ref,
                         residual_ref, fisher_ref, damping_ref, column_ref, line_ref):
    n = all_ref.shape[0]
    classes = residual_ref.shape[1]
    class_start, place = scalar_ref[1], scalar_ref[2]
    part, peak, scales, total, own_scale = combine(own_ref, all_ref)
    square = sum(part(d, 2) * (scales[d] * scales[d]) for d in range(n))
    inverse = 1.0 / total
    spread = to_slots(1.0 - square * inverse * inverse, line_ref, place)
    factor = to_slots(own_scale * inverse, line_ref, place)
    target, norm = side_ref[0:n, :], side_ref[n : 2 * n, :]
    valid = (target >= 0.0).astype(F32)
    share = valid / jnp.sum(valid)
    fisher_sum = jnp.sum(norm * share * spread)
    damping_ref[...] = jnp.full(
        damping_ref.shape, DAMPING_SHARE * fisher_sum / entries + EPSILON, F32
    )
    column_ref[...] = to_columns([factor, share, target])
    index = class_start + lax.broadcasted_iota(jnp.int32, (1, classes), 1)
    for j in range(n):
        def step(i, _, j=j):
            start = pl.multiple_of(i * STEP, STEP)
            at = pl.ds(pl.multiple_of(j * LANES + start, STEP), STEP)
            column = column_ref[pl.ds(start, STEP), :]
            probability = e_ref[at, :] * column[:, j : j + 1]
            hit = index == column[:, 2 * n + j : 2 * n + j + 1].astype(jnp.int32)
            part = column[:, n + j : n + j + 1]
            residual_ref[at, :] = (part * (probability - hit.astype(F32))).astype(BF16)
            fisher_ref[at, :] = (part * probability * (1.0 - probability)).astype(BF16)
            return 0

        lax.fori_loop(0, LANES // STEP, step, 0)


def first_weights(own, every, side, scalars, e, entries):
    n = own.shape[0]
    return pl.pallas_call(
        functools.partial(first_weights_kernel, float(entries)),
        out_shape=(
            pltpu.VMEM(e.shape, BF16),
            pltpu.VMEM(e.shape, BF16),
            pltpu.VMEM((8, LANES), F32),
        ),
        in_specs=[VMEM] * 3 + [SMEM, VMEM],
        out_specs=(VMEM, VMEM, VMEM),
        scratch_shapes=[pltpu.VMEM((LANES, LANES), F32), pltpu.VMEM((n, LANES), F32)],
        compiler_params=params(),
        cost_estimate=cost(0, 8 * e.size),
        name="first_weights",
    )(own, every, side, scalars, e)


def update_kernel(start, turned_ref, w_ref, residual_ref, fisher_ref, damping_ref,
                  moved_ref, inverse_ref, low_ref):
    features = turned_ref.shape[0]
    columns = moved_ref.shape[1]
    tile = 512
    damping = damping_ref[0:1, 0:1]
    own = slice(start, start + columns)
    for first in range(0, features, tile):
        at = slice(first, first + tile)
        turned = turned_ref[at, :]
        gradient = jnp.dot(turned, residual_ref[:, own], preferred_element_type=F32)
        fisher = jnp.dot(turned * turned, fisher_ref[:, own], preferred_element_type=F32)
        inverse = 1.0 / (fisher + damping)
        change = gradient * inverse
        inverse_ref[at, :] = inverse
        moved_ref[at, :] = -change
        low_ref[at, :] = (w_ref[at, own] - LEARNING_RATE * change).astype(BF16)


def update(turned, weights, residual, fisher_weight, damping, start, columns):
    features, rows = turned.shape
    return pl.pallas_call(
        functools.partial(update_kernel, start),
        out_shape=(
            pltpu.VMEM((features, columns), F32),
            pltpu.VMEM((features, columns), F32),
            pltpu.VMEM((features, columns), BF16),
        ),
        in_specs=[VMEM] * 5,
        out_specs=(VMEM, VMEM, VMEM),
        compiler_params=params(),
        cost_estimate=cost(4 * rows * features * columns),
        name="update",
    )(turned, weights, residual, fisher_weight, damping)


def next_logits_kernel(start, plain_ref, low_ref, out_ref):
    tile = min(512, out_ref.shape[0])
    for first in range(0, out_ref.shape[0], tile):
        out_ref[first : first + tile, :] = jnp.dot(
            plain_ref[start + first : start + first + tile, :],
            low_ref[...],
            preferred_element_type=F32,
        )


def next_logits(plain, low, start, rows):
    features, columns = low.shape
    return pl.pallas_call(
        functools.partial(next_logits_kernel, start),
        out_shape=jax.ShapeDtypeStruct((rows, columns), F32),
        in_specs=[VMEM, VMEM],
        out_specs=VMEM,
        compiler_params=params(),
        cost_estimate=cost(2 * rows * features * columns),
        name="next_logits",
    )(plain, low)


def last_stats_kernel(slot, last, pieces, offsets, refs_in, *refs):
    own, other = refs[:pieces], refs[pieces : 2 * pieces]
    side_ref, scalar_ref = refs[2 * pieces : 2 * pieces + 2]
    outs = refs[2 * pieces + 2 + refs_in :]
    e_ref, stats_ref, pack_ref, column_ref = outs[0], outs[1], outs[-2], outs[-1]
    rows, classes = pack_ref.shape[0], e_ref.shape[1]
    active, class_start, place = scalar_ref[0], scalar_ref[1], scalar_ref[2]
    n = stats_ref.shape[0]
    column_ref[...] = to_columns([side_ref[0:n, :]])
    index = class_start + lax.broadcasted_iota(jnp.int32, (1, classes), 1)
    live = index < active
    for k in range(rows // LANES):
        def step(i, _, k=k):
            start = pl.multiple_of(i * STEP, STEP)

            def rows_of(base):
                return pl.ds(pl.multiple_of(base + k * LANES + start, STEP), STEP)

            logits = jnp.concatenate(
                [a[rows_of(o), :] + b[rows_of(o), :] for a, b, o in zip(own, other, offsets)],
                axis=1,
            )
            column = column_ref[pl.ds(start, STEP), slot + k : slot + k + 1]
            hit = index == column.astype(jnp.int32)
            label = jnp.sum(jnp.where(hit, logits, 0.0), axis=1, keepdims=True)
            peak = jnp.max(jnp.where(live, logits, NEGATIVE), axis=1, keepdims=True)
            e = jnp.where(live, jnp.exp(logits - peak), 0.0)
            e_ref[rows_of(slot * LANES), :] = e
            total = jnp.sum(e, axis=1, keepdims=True)
            pack_ref[rows_of(0), :] = lane_pack((peak, total, label), STEP)
            return 0

        lax.fori_loop(0, LANES // STEP, step, 0)
    for k in range(rows // LANES):
        put_stats(stats_ref, place ^ (slot + k), pack_ref[k * LANES : (k + 1) * LANES, :])
    if last:
        outs[2][...] = jnp.broadcast_to(stats_ref[...][None], outs[2].shape)


def last_stats(own, other, offsets, side, scalars, slot, rows, n, buffers):
    classes = sum(c.shape[1] for c in own)
    last = slot + rows // LANES == n
    shapes = [pltpu.VMEM((n * LANES, classes), F32), pltpu.VMEM((n, 3 * LANES), F32)]
    if last:
        shapes.append(jax.ShapeDtypeStruct((n, n, 3 * LANES), F32))
    first = 2 * len(own) + 2
    return pl.pallas_call(
        functools.partial(last_stats_kernel, slot, last, len(own), tuple(offsets), len(buffers)),
        out_shape=tuple(shapes),
        in_specs=[VMEM] * (2 * len(own) + 1) + [SMEM] + [VMEM] * len(buffers),
        out_specs=(VMEM,) * len(shapes),
        input_output_aliases={first: 0, first + 1: 1} if buffers else {},
        scratch_shapes=[pltpu.VMEM((rows, LANES), F32), pltpu.VMEM((LANES, LANES), F32)],
        compiler_params=params(),
        cost_estimate=cost(0, 24 * rows * classes),
        name="last_stats",
    )(*own, *other, side, scalars, *buffers)


def finish_kernel(chunks, own_ref, all_ref, side_ref, scalar_ref, e_ref, turned_ref, *refs):
    moved_refs, inverse_refs = refs[:chunks], refs[chunks : 2 * chunks]
    out_ref, loss_ref, residual_ref, column_ref, line_ref = refs[2 * chunks :]
    n = all_ref.shape[0]
    classes = e_ref.shape[1]
    tile = out_ref.shape[0]
    program = pl.program_id(0)

    @pl.when(program == 0)
    def _():
        class_start, place = scalar_ref[1], scalar_ref[2]
        part, peak, scales, total, own_scale = combine(own_ref, all_ref)
        label = sum(part(d, 2) for d in range(n))
        target = side_ref[0:n, :]
        valid = (target >= 0.0).astype(F32)
        share = valid / jnp.sum(valid)
        losses = to_slots(peak + jnp.log(total) - label, line_ref, place)
        loss_ref[...] = (valid * losses)[0:1, :]
        factor = to_slots(own_scale / total, line_ref, place)
        column_ref[...] = to_columns([factor, share, target])
        index = class_start + lax.broadcasted_iota(jnp.int32, (1, classes), 1)
        for j in range(n):
            def step(i, _, j=j):
                start = pl.multiple_of(i * STEP, STEP)
                at = pl.ds(pl.multiple_of(j * LANES + start, STEP), STEP)
                column = column_ref[pl.ds(start, STEP), :]
                probability = e_ref[at, :] * column[:, j : j + 1]
                hit = index == column[:, 2 * n + j : 2 * n + j + 1].astype(jnp.int32)
                part = column[:, n + j : n + j + 1]
                residual_ref[at, :] = (part * (probability - hit.astype(F32))).astype(BF16)
                return 0

            lax.fori_loop(0, LANES // STEP, step, 0)

    at = pl.ds(pl.multiple_of(program * tile, tile), tile)
    turned = turned_ref[at, :]
    done = 0
    for moved_ref, inverse_ref in zip(moved_refs, inverse_refs):
        own = slice(done, done + moved_ref.shape[1])
        gradient = jnp.dot(turned, residual_ref[:, own], preferred_element_type=F32)
        out_ref[:, own] = moved_ref[at, :] - gradient * inverse_ref[at, :]
        done += moved_ref.shape[1]


def finish(own, every, side, scalars, e, turned, moved, inverse):
    n = own.shape[0]
    features, all_rows = turned.shape
    classes = e.shape[1]
    tile = 256
    return pl.pallas_call(
        functools.partial(finish_kernel, len(moved)),
        out_shape=(
            jax.ShapeDtypeStruct((features, classes), F32),
            jax.ShapeDtypeStruct((1, LANES), F32),
        ),
        grid=(features // tile,),
        in_specs=[VMEM] * 3 + [SMEM] + [VMEM] * (2 + 2 * len(moved)),
        out_specs=(
            pl.BlockSpec((tile, classes), lambda i: (i, 0)),
            pl.BlockSpec((1, LANES), lambda i: (0, 0)),
        ),
        scratch_shapes=[
            pltpu.VMEM((all_rows, classes), BF16),
            pltpu.VMEM((LANES, LANES), F32),
            pltpu.VMEM((n, LANES), F32),
        ],
        compiler_params=params(12),
        cost_estimate=cost(2 * all_rows * features * classes),
        name="finish",
    )(own, every, side, scalars, e, turned, *moved, *inverse)


def exchange(copies):
    return lax.all_to_all(copies, "example", 0, 0)


def body(n, n_cls, features, weights, labels, counts, active):
    rows = features.shape[0]
    all_rows = rows * n
    feature_count, classes = weights.shape
    entries = feature_count * n_cls * classes * n
    place = lax.axis_index("example")
    scalars = jnp.stack([active[0], place * classes, place]).astype(jnp.int32)

    slots = gather_blocks(features, n)
    w_low = weights.astype(BF16)

    target = jnp.where(jnp.arange(rows) < counts[0], labels % active[0], -1)
    low_squares = (features * features).astype(F32)
    norm = jnp.sum(low_squares, axis=1)
    norm = norm + swap(norm, "cls", n_cls, 1)
    side = jnp.stack([target.astype(F32), norm])[:, None, :]
    offset = 1
    while offset < n:
        side = jnp.concatenate([side, swap(side, "example", n, offset)], axis=1)
        offset *= 2
    side = side.reshape(2 * n, rows)

    bounds = [0] + list(range(1, n, 2)) + [n]
    buffers, kept, token = (), (), None
    for first, end in zip(bounds[:-1], bounds[1:]):
        logits, *buffers = arriving_logits(
            slots[first:end], w_low, first * rows, all_rows, buffers, token
        )
        other = swap(logits, "cls", n_cls, 1)
        e, own_stats, *copies = first_stats(logits, other, scalars, first, n, kept)
        kept, token = (e, own_stats), own_stats
    plain, turned = buffers
    every = exchange(copies[0])
    residual, fisher_weight, damping = first_weights(own_stats, every, side, scalars, e, entries)

    columns = min(512, classes)
    moved, inverse, own, other, offsets = [], [], [], [], []
    half = all_rows // 2
    for start in range(0, classes, columns):
        a, b, low = update(turned, weights, residual, fisher_weight, damping, start, columns)
        moved.append(a)
        inverse.append(b)
        if start + columns < classes:
            own.append(next_logits(plain, low, 0, all_rows))
            other.append(swap(own[-1], "cls", n_cls, 1))
    kept = ()
    late = [next_logits(plain, low, first, half) for first in (0, half)]
    late_other = [swap(c, "cls", n_cls, 1) for c in late]
    for first, c, d in zip((0, half), late, late_other):
        offsets = [first] * len(own) + [0]
        e, own_stats, *copies = last_stats(
            own + [c], other + [d], offsets, side, scalars, first // rows, half, n, kept
        )
        kept = (e, own_stats)
    every = exchange(copies[0])
    out, losses = finish(own_stats, every, side, scalars, e, turned, moved, inverse)
    return out, losses.reshape(rows)


def solution(mesh):
    return jax.shard_map(
        functools.partial(body, mesh.shape["example"], mesh.shape["cls"]),
        mesh=mesh,
        in_specs=(
            P(("groups", "example"), "cls"),
            P(("groups", "cls"), "example"),
            P(("groups", "example")),
            P(("groups", "example")),
            P("groups"),
        ),
        out_specs=(P(("groups", "cls"), "example"), P(("groups", "example"))),
        check_vma=False,
    )
```

```python
import functools

import jax
import jax.numpy as jnp
from jax import lax
from jax.experimental import pallas as pl
from jax.experimental.pallas import tpu as pltpu
from jax.sharding import PartitionSpec as P

ITERS = 2
NEGATIVE = -1e30
LEARNING_RATE = 2e-05
DAMPING_SHARE = 0.1
EPSILON = 1e-06

F32 = jnp.float32
BF16 = jnp.bfloat16
VMEM = pl.BlockSpec(memory_space=pltpu.VMEM)
SMEM = pl.BlockSpec(memory_space=pltpu.SMEM)
STEP = 64
ANY = pl.BlockSpec(memory_space=pl.ANY)
LANES = 128


def params(mib=10):
    return pltpu.CompilerParams(vmem_limit_bytes=mib << 20)


def cost(flops=0, nbytes=0):
    return pl.CostEstimate(flops=int(flops), bytes_accessed=int(nbytes), transcendentals=0)


def swap(x, axis, n, offset):
    return lax.ppermute(x, axis, [(i, i ^ offset) for i in range(n)])


def gather_blocks(x, n):
    if n != 8:
        return [x] + [swap(x, "example", n, j) for j in range(1, n)]
    z_size, y_size = 4, 2

    def along_z(value, pairs):
        full = [(a * y_size + y, b * y_size + y) for a, b in pairs for y in range(y_size)]
        return lax.ppermute(value, "example", full)

    z = lax.axis_index("example") // y_size
    middle = (z == 1) | (z == 2)
    near = along_z(x, [(0, 1), (1, 0), (2, 3), (3, 2)])
    inner = along_z(x, [(1, 2), (2, 1)])
    y_own = swap(x, "example", n, 1)
    ends = along_z(inner, [(1, 0), (2, 3)])
    cross = along_z(near, [(1, 2), (2, 1)])
    y_near = swap(near, "example", n, 1)
    far = along_z(cross, [(1, 0), (2, 3)])
    second = jnp.where(middle, cross, ends)
    y_second = swap(second, "example", n, 1)
    third = jnp.where(middle, inner, far)
    y_third = swap(third, "example", n, 1)
    return [x, y_own, near, y_near, second, y_second, third, y_third]


def arriving_kernel(count, *refs):
    blocks, w_ref, out_ref = refs[:count], refs[count], refs[-1]
    rows = blocks[0].shape[0]
    columns = 256
    for first in range(0, w_ref.shape[1], columns):
        for k in range(count):
            out_ref[k * rows : (k + 1) * rows, first : first + columns] = jnp.dot(
                blocks[k][...], w_ref[:, first : first + columns], preferred_element_type=F32
            )


def arriving_logits(blocks, w_low, tokens):
    rows = sum(b.shape[0] for b in blocks)
    return pl.pallas_call(
        functools.partial(arriving_kernel, len(blocks)),
        out_shape=jax.ShapeDtypeStruct((rows, w_low.shape[1]), F32),
        in_specs=[VMEM] * (len(blocks) + 1) + [ANY] * len(tokens),
        out_specs=VMEM,
        compiler_params=params(),
        name="arriving_logits",
    )(*blocks, w_low, *tokens)


def turn_kernel(*refs):
    blocks, out_ref = refs[:-1], refs[-1]
    rows = blocks[0].shape[0]
    for k, block in enumerate(blocks):
        out_ref[:, k * rows : (k + 1) * rows] = block[...].T


def turn(blocks):
    rows = sum(b.shape[0] for b in blocks)
    return pl.pallas_call(
        turn_kernel,
        out_shape=pltpu.VMEM((blocks[0].shape[1], rows), BF16),
        in_specs=[VMEM] * len(blocks),
        out_specs=VMEM,
        compiler_params=params(),
        name="turn",
    )(*blocks)


def lane_pack(columns, rows):
    lane = lax.broadcasted_iota(jnp.int32, (rows, LANES), 1)
    packed = jnp.zeros((rows, LANES), F32)
    for k, column in enumerate(columns):
        packed = jnp.where(lane == k, column, packed)
    return packed


def put_stats(packed, place, shape):
    lines = packed.T
    line = jnp.concatenate([lines[k : k + 1, :] for k in range(3)], axis=1)
    here = lax.broadcasted_iota(jnp.int32, shape, 0) == place
    return jnp.where(here, line, 0.0)


def first_stats_kernel(slot, earlier, last, own_ref, other_ref, scalar_ref, *refs):
    side_ref = refs[0] if last else None
    older = refs[int(last) : int(last) + earlier]
    e_ref, stats_ref = refs[int(last) + earlier : int(last) + earlier + 2]
    pack_ref = refs[-1]
    rows, classes = own_ref.shape
    active, class_start, place = scalar_ref[0], scalar_ref[1], scalar_ref[2]
    index = class_start + lax.broadcasted_iota(jnp.int32, (1, classes), 1)
    live = index < active

    def step(i, _):
        at = pl.ds(pl.multiple_of(i * STEP, STEP), STEP)
        logits = jnp.where(live, own_ref[at, :] + other_ref[at, :], NEGATIVE)
        peak = jnp.max(logits, axis=1, keepdims=True)
        e = jnp.exp(logits - peak)
        e_ref[at, :] = e
        total = jnp.sum(e, axis=1, keepdims=True)
        square = jnp.sum(e * e, axis=1, keepdims=True)
        pack_ref[at, :] = lane_pack((peak, total, square), STEP)
        return 0

    lax.fori_loop(0, rows // STEP, step, 0)
    shape = stats_ref.shape
    stats = older[0][...] if earlier else jnp.zeros(shape, F32)
    for k in range(rows // LANES):
        stats += put_stats(pack_ref[k * LANES : (k + 1) * LANES, :], place ^ (slot + k), shape)
    stats_ref[...] = stats
    if last:
        copies_ref = refs[int(last) + earlier + 2]
        lines = [jnp.broadcast_to(side_ref[k : k + 1, :], (shape[0], LANES)) for k in range(2)]
        full = jnp.concatenate([stats] + lines, axis=1)
        copies_ref[...] = jnp.broadcast_to(full[None], copies_ref.shape)


def first_stats(own, other, scalars, slot, n, earlier, side):
    rows, classes = own.shape
    last = side is not None
    shapes = [jax.ShapeDtypeStruct(own.shape, F32), jax.ShapeDtypeStruct((n, 3 * LANES), F32)]
    if last:
        shapes.append(jax.ShapeDtypeStruct((n, n, 5 * LANES), F32))
    extra = ([side] if last else []) + list(earlier)
    return pl.pallas_call(
        functools.partial(first_stats_kernel, slot, len(earlier), last),
        out_shape=tuple(shapes),
        in_specs=[VMEM, VMEM, SMEM] + [VMEM] * len(extra),
        out_specs=(VMEM,) * len(shapes),
        scratch_shapes=[pltpu.VMEM((rows, LANES), F32)],
        compiler_params=params(),
        name="first_stats",
    )(own, other, scalars, *extra)


def combine(own_ref, all_ref):
    n = all_ref.shape[0]
    part = lambda d, k: all_ref[d, :, k * LANES : (k + 1) * LANES]
    peaks = [part(d, 0) for d in range(n)]
    peak = functools.reduce(jnp.maximum, peaks)
    scales = [jnp.exp(p - peak) for p in peaks]
    total = sum(part(d, 1) * scales[d] for d in range(n))
    own_scale = jnp.exp(own_ref[:, 0:LANES] - peak)
    return part, peak, scales, total, own_scale


def to_slots(value, line_ref, place):
    n = value.shape[0]
    line_ref[...] = value
    return jnp.concatenate([line_ref[pl.ds(place ^ j, 1), :] for j in range(n)], axis=0)


def to_columns(lines):
    stacked = jnp.concatenate(lines, axis=0)
    rest = jnp.zeros((LANES - stacked.shape[0], LANES), F32)
    return jnp.concatenate([stacked, rest], axis=0).T


def first_weights_kernel(entries, parts, own_ref, all_ref, scalar_ref, *refs):
    e_refs = refs[:parts]
    residual_ref, fisher_ref, damping_ref, target_ref, column_ref, line_ref = refs[parts:]
    n = all_ref.shape[0]
    classes = residual_ref.shape[1]
    class_start, place = scalar_ref[1], scalar_ref[2]
    part, peak, scales, total, own_scale = combine(own_ref, all_ref)
    square = sum(part(d, 2) * (scales[d] * scales[d]) for d in range(n))
    inverse = 1.0 / total
    spread = 1.0 - square * inverse * inverse
    target = jnp.concatenate([all_ref[d, 0:1, 3 * LANES : 4 * LANES] for d in range(n)], axis=0)
    norm = jnp.concatenate([all_ref[d, 0:1, 4 * LANES : 5 * LANES] for d in range(n)], axis=0)
    valid = (target >= 0.0).astype(F32)
    share = valid / jnp.sum(valid)
    fisher_sum = jnp.sum(norm * share * spread)
    damping_ref[...] = jnp.full(
        damping_ref.shape, DAMPING_SHARE * fisher_sum / entries + EPSILON, F32
    )
    factor = to_slots(own_scale * inverse, line_ref, place)
    share = to_slots(share, line_ref, place)
    target = to_slots(target, line_ref, place)
    target_ref[...] = target
    column_ref[...] = to_columns([factor, share, target])
    index = class_start + lax.broadcasted_iota(jnp.int32, (1, classes), 1)
    done = 0
    for e_ref in e_refs:
        for k in range(e_ref.shape[0] // LANES):
            j = done + k

            def step(i, _, j=j, k=k, e_ref=e_ref):
                start = pl.multiple_of(i * STEP, STEP)
                at = pl.ds(pl.multiple_of(j * LANES + start, STEP), STEP)
                column = column_ref[pl.ds(start, STEP), :]
                e = e_ref[pl.ds(pl.multiple_of(k * LANES + start, STEP), STEP), :]
                probability = e * column[:, j : j + 1]
                hit = index == column[:, 2 * n + j : 2 * n + j + 1].astype(jnp.int32)
                part = column[:, n + j : n + j + 1]
                residual_ref[at, :] = (part * (probability - hit.astype(F32))).astype(BF16)
                fisher_ref[at, :] = (part * probability * (1.0 - probability)).astype(BF16)
                return 0

            lax.fori_loop(0, LANES // STEP, step, 0)
        done += e_ref.shape[0] // LANES


def first_weights(own, every, scalars, e_parts, entries):
    n = own.shape[0]
    classes = e_parts[0].shape[1]
    weight = pltpu.VMEM((n * LANES, classes), BF16)
    return pl.pallas_call(
        functools.partial(first_weights_kernel, float(entries), len(e_parts)),
        out_shape=(
            weight,
            weight,
            jax.ShapeDtypeStruct((8, LANES), F32),
            jax.ShapeDtypeStruct((n, LANES), F32),
        ),
        in_specs=[VMEM] * 2 + [SMEM] + [VMEM] * len(e_parts),
        out_specs=(VMEM,) * 4,
        scratch_shapes=[pltpu.VMEM((LANES, LANES), F32), pltpu.VMEM((n, LANES), F32)],
        compiler_params=params(),
        cost_estimate=cost(0, 8 * n * LANES * classes),
        name="first_weights",
    )(own, every, scalars, *e_parts)


def row_product(parts, at, right_ref, own, square=False):
    done, total = 0, None
    for ref in parts:
        rows = ref.shape[1]
        left = ref[at, :]
        left = left * left if square else left
        term = jnp.dot(left, right_ref[done : done + rows, own], preferred_element_type=F32)
        total = term if total is None else total + term
        done += rows
    return total


def update_kernel(start, tile, parts, *refs):
    turned = refs[:parts]
    w_ref, residual_ref, fisher_ref, damping_ref = refs[parts : parts + 4]
    moved_ref, inverse_ref, low_ref, held_ref, sems = refs[parts + 4 :]
    features, columns = moved_ref.shape
    damping = damping_ref[0:1, 0:1]
    own = slice(start, start + columns)
    copies = []
    for k in range(features // tile):
        copies.append(
            pltpu.make_async_copy(
                w_ref.at[k * tile : (k + 1) * tile, own], held_ref.at[k], sems.at[k]
            )
        )
        copies[-1].start()
    for k in range(features // tile):
        at = slice(k * tile, (k + 1) * tile)
        gradient = row_product(turned, at, residual_ref, own)
        fisher = row_product(turned, at, fisher_ref, own, square=True)
        inverse = 1.0 / (fisher + damping)
        change = gradient * inverse
        inverse_ref[at, :] = inverse
        moved_ref[at, :] = -change
        copies[k].wait()
        low_ref[at, :] = (held_ref[k] - LEARNING_RATE * change).astype(BF16)


def update(turned, weights, residual, fisher_weight, damping, start, columns):
    features, rows = turned[0].shape[0], residual.shape[0]
    tile = 512
    return pl.pallas_call(
        functools.partial(update_kernel, start, tile, len(turned)),
        out_shape=(
            pltpu.VMEM((features, columns), F32),
            pltpu.VMEM((features, columns), F32),
            pltpu.VMEM((features, columns), BF16),
        ),
        in_specs=[VMEM] * len(turned) + [ANY] + [VMEM] * 3,
        out_specs=(VMEM, VMEM, VMEM),
        scratch_shapes=[
            pltpu.VMEM((features // tile, tile, columns), F32),
            pltpu.SemaphoreType.DMA((features // tile,)),
        ],
        compiler_params=params(14),
        cost_estimate=cost(4 * rows * features * columns),
        name="update",
    )(*turned, weights, residual, fisher_weight, damping)


def next_logits_kernel(*refs):
    blocks, low_ref, out_ref = refs[:-2], refs[-2], refs[-1]
    rows = blocks[0].shape[0]
    for k, block in enumerate(blocks):
        out_ref[k * rows : (k + 1) * rows, :] = jnp.dot(
            block[...], low_ref[...], preferred_element_type=F32
        )


def next_logits(blocks, low):
    features, columns = low.shape
    rows = sum(b.shape[0] for b in blocks)
    return pl.pallas_call(
        next_logits_kernel,
        out_shape=jax.ShapeDtypeStruct((rows, columns), F32),
        in_specs=[VMEM] * (len(blocks) + 1),
        out_specs=VMEM,
        compiler_params=params(),
        cost_estimate=cost(2 * rows * features * columns),
        name="next_logits",
    )(*blocks, low)


def last_stats_kernel(slot, last, pieces, offsets, earlier, *refs):
    own, other = refs[:pieces], refs[pieces : 2 * pieces]
    target_ref, scalar_ref = refs[2 * pieces : 2 * pieces + 2]
    older = refs[2 * pieces + 2 : 2 * pieces + 2 + earlier]
    outs = refs[2 * pieces + 2 + earlier :]
    e_ref, stats_ref, pack_ref, column_ref = outs[0], outs[1], outs[-2], outs[-1]
    rows, classes = e_ref.shape
    active, class_start, place = scalar_ref[0], scalar_ref[1], scalar_ref[2]
    n = stats_ref.shape[0]
    column_ref[...] = to_columns([target_ref[...]])
    index = class_start + lax.broadcasted_iota(jnp.int32, (1, classes), 1)
    live = index < active
    for k in range(rows // LANES):
        def step(i, _, k=k):
            start = pl.multiple_of(i * STEP, STEP)

            def rows_of(base):
                return pl.ds(pl.multiple_of(base + k * LANES + start, STEP), STEP)

            logits = jnp.concatenate(
                [a[rows_of(o), :] + b[rows_of(o), :] for a, b, o in zip(own, other, offsets)],
                axis=1,
            )
            column = column_ref[pl.ds(start, STEP), slot + k : slot + k + 1]
            hit = index == column.astype(jnp.int32)
            label = jnp.sum(jnp.where(hit, logits, 0.0), axis=1, keepdims=True)
            logits = jnp.where(live, logits, NEGATIVE)
            peak = jnp.max(logits, axis=1, keepdims=True)
            e = jnp.exp(logits - peak)
            e_ref[rows_of(0), :] = e
            total = jnp.sum(e, axis=1, keepdims=True)
            pack_ref[rows_of(0), :] = lane_pack((peak, total, label), STEP)
            return 0

        lax.fori_loop(0, LANES // STEP, step, 0)
    shape = stats_ref.shape
    stats = older[0][...] if earlier else jnp.zeros(shape, F32)
    for k in range(rows // LANES):
        stats += put_stats(pack_ref[k * LANES : (k + 1) * LANES, :], place ^ (slot + k), shape)
    stats_ref[...] = stats
    if last:
        outs[2][...] = jnp.broadcast_to(stats[None], outs[2].shape)


def last_stats(own, other, offsets, target, scalars, slot, rows, n, earlier):
    classes = sum(c.shape[1] for c in own)
    last = slot + rows // LANES == n
    shapes = [
        jax.ShapeDtypeStruct((rows, classes), F32),
        jax.ShapeDtypeStruct((n, 3 * LANES), F32),
    ]
    if last:
        shapes.append(jax.ShapeDtypeStruct((n, n, 3 * LANES), F32))
    return pl.pallas_call(
        functools.partial(
            last_stats_kernel, slot, last, len(own), tuple(offsets), len(earlier)
        ),
        out_shape=tuple(shapes),
        in_specs=[VMEM] * (2 * len(own) + 1) + [SMEM] + [VMEM] * len(earlier),
        out_specs=(VMEM,) * len(shapes),
        scratch_shapes=[pltpu.VMEM((rows, LANES), F32), pltpu.VMEM((LANES, LANES), F32)],
        compiler_params=params(),
        cost_estimate=cost(0, 24 * rows * classes),
        name="last_stats",
    )(*own, *other, target, scalars, *earlier)


def finish_kernel(chunks, parts, e_parts, tile, own_ref, all_ref, target_ref, scalar_ref, *refs):
    e_refs = refs[:e_parts]
    turned = refs[e_parts : e_parts + parts]
    refs = refs[e_parts + parts :]
    moved_refs, inverse_refs = refs[:chunks], refs[chunks : 2 * chunks]
    out_ref, loss_ref, residual_ref, column_ref, line_ref, held_ref, sems = refs[2 * chunks :]
    n = all_ref.shape[0]
    classes = residual_ref.shape[1]
    class_start, place = scalar_ref[1], scalar_ref[2]
    part, peak, scales, total, own_scale = combine(own_ref, all_ref)
    label = sum(part(d, 2) for d in range(n))
    target = target_ref[...]
    valid = (target >= 0.0).astype(F32)
    share = valid / jnp.sum(valid)
    losses = to_slots(peak + jnp.log(total) - label, line_ref, place)
    loss_ref[...] = (valid * losses)[0:1, :]
    factor = to_slots(own_scale / total, line_ref, place)
    column_ref[...] = to_columns([factor, share, target])
    index = class_start + lax.broadcasted_iota(jnp.int32, (1, classes), 1)
    done = 0
    for e_ref in e_refs:
        for k in range(e_ref.shape[0] // LANES):
            j = done + k

            def step(i, _, j=j, k=k, e_ref=e_ref):
                start = pl.multiple_of(i * STEP, STEP)
                at = pl.ds(pl.multiple_of(j * LANES + start, STEP), STEP)
                column = column_ref[pl.ds(start, STEP), :]
                e = e_ref[pl.ds(pl.multiple_of(k * LANES + start, STEP), STEP), :]
                probability = e * column[:, j : j + 1]
                hit = index == column[:, 2 * n + j : 2 * n + j + 1].astype(jnp.int32)
                part = column[:, n + j : n + j + 1]
                residual_ref[at, :] = (part * (probability - hit.astype(F32))).astype(BF16)
                return 0

            lax.fori_loop(0, LANES // STEP, step, 0)
        done += e_ref.shape[0] // LANES

    copies = []
    for k in range(out_ref.shape[0] // tile):
        at = slice(k * tile, (k + 1) * tile)
        done = 0
        for moved_ref, inverse_ref in zip(moved_refs, inverse_refs):
            own = slice(done, done + moved_ref.shape[1])
            gradient = row_product(turned, at, residual_ref, own)
            held_ref[k, :, own] = moved_ref[at, :] - gradient * inverse_ref[at, :]
            done += moved_ref.shape[1]
        copies.append(pltpu.make_async_copy(held_ref.at[k], out_ref.at[at, :], sems.at[k]))
        copies[-1].start()
    for copy in copies:
        copy.wait()


def finish(own, every, target, scalars, e_parts, turned, moved, inverse):
    n = own.shape[0]
    features = turned[0].shape[0]
    classes = e_parts[0].shape[1]
    all_rows = n * LANES
    tile = 512
    return pl.pallas_call(
        functools.partial(finish_kernel, len(moved), len(turned), len(e_parts), tile),
        out_shape=(
            jax.ShapeDtypeStruct((features, classes), F32),
            jax.ShapeDtypeStruct((1, LANES), F32),
        ),
        in_specs=[VMEM] * 3 + [SMEM] + [VMEM] * (len(e_parts) + len(turned) + 2 * len(moved)),
        out_specs=(ANY, VMEM),
        scratch_shapes=[
            pltpu.VMEM((all_rows, classes), BF16),
            pltpu.VMEM((LANES, LANES), F32),
            pltpu.VMEM((n, LANES), F32),
            pltpu.VMEM((features // tile, tile, classes), F32),
            pltpu.SemaphoreType.DMA((features // tile,)),
        ],
        compiler_params=params(16),
        cost_estimate=cost(2 * all_rows * features * classes),
        name="finish",
    )(own, every, target, scalars, *e_parts, *turned, *moved, *inverse)


def exchange(copies):
    return lax.all_to_all(copies, "example", 0, 0)


def body(n, n_cls, features, weights, labels, counts, active):
    rows = features.shape[0]
    all_rows = rows * n
    feature_count, classes = weights.shape
    entries = feature_count * n_cls * classes * n
    place = lax.axis_index("example")
    scalars = jnp.stack([active[0], place * classes, place]).astype(jnp.int32)

    slots = gather_blocks(features, n)
    w_low = weights.astype(BF16)

    target = jnp.where(jnp.arange(rows) < counts[0], labels % active[0], -1)
    norm = jnp.sum((features * features).astype(F32), axis=1)
    norm = norm + swap(norm, "cls", n_cls, 1)
    side = jnp.stack([target.astype(F32), norm])

    turned, e_parts, earlier, tokens = [], [], (), ()
    for first in range(0, n, 2):
        pair = slots[first : first + 2]
        groups = [(first, pair)] if first + 2 < n else [(first, pair[:1]), (first + 1, pair[1:])]
        for slot, blocks in groups:
            logits = arriving_logits(blocks, w_low, tokens)
            other = swap(logits, "cls", n_cls, 1)
            last = slot + len(blocks) == n
            e, own_stats, *copies = first_stats(
                logits, other, scalars, slot, n, earlier, side if last else None
            )
            e_parts.append(e)
            earlier = (own_stats,)
            tokens = (own_stats,) + tuple(turned[-1:])
        turned.append(turn(pair))
    every = exchange(copies[0])
    residual, fisher_weight, damping, target = first_weights(
        own_stats, every, scalars, e_parts, entries
    )

    columns = min(512, classes)
    moved, inverse, own, other = [], [], [], []
    for start in range(0, classes, columns):
        a, b, low = update(turned, weights, residual, fisher_weight, damping, start, columns)
        moved.append(a)
        inverse.append(b)
        if start + columns < classes:
            own.append(next_logits(slots, low))
            other.append(swap(own[-1], "cls", n_cls, 1))
    half = n // 2
    late = [next_logits(slots[first : first + half], low) for first in (0, half)]
    late_other = [swap(c, "cls", n_cls, 1) for c in late]
    e_parts, earlier = [], ()
    for first, c, d in zip((0, half), late, late_other):
        offsets = [first * rows] * len(own) + [0]
        e, own_stats, *copies = last_stats(
            own + [c], other + [d], offsets, target, scalars, first, half * rows, n, earlier
        )
        e_parts.append(e)
        earlier = (own_stats,)
    every = exchange(copies[0])
    out, losses = finish(
        own_stats, every, target, scalars, e_parts, turned, moved, inverse
    )
    return out, losses.reshape(rows)


def solution(mesh):
    return jax.shard_map(
        functools.partial(body, mesh.shape["example"], mesh.shape["cls"]),
        mesh=mesh,
        in_specs=(
            P(("groups", "example"), "cls"),
            P(("groups", "cls"), "example"),
            P(("groups", "example")),
            P(("groups", "example")),
            P("groups"),
        ),
        out_specs=(P(("groups", "cls"), "example"), P(("groups", "example"))),
        check_vma=False,
    )
```

```python
import functools

import jax
import jax.numpy as jnp
from jax import lax
from jax.experimental import pallas as pl
from jax.experimental.pallas import tpu as pltpu
from jax.sharding import PartitionSpec as P

ITERS = 2
NEGATIVE = -1e30
LEARNING_RATE = 2e-05
DAMPING_SHARE = 0.1
EPSILON = 1e-06

F32 = jnp.float32
BF16 = jnp.bfloat16
VMEM = pl.BlockSpec(memory_space=pltpu.VMEM)
SMEM = pl.BlockSpec(memory_space=pltpu.SMEM)
HBM = pl.BlockSpec(memory_space=pltpu.HBM)
ANY = pl.BlockSpec(memory_space=pl.ANY)
STEP = 64
LANES = 128


def params(mib=10):
    return pltpu.CompilerParams(vmem_limit_bytes=mib << 20)


def cost(flops=0, nbytes=0):
    return pl.CostEstimate(flops=int(flops), bytes_accessed=int(nbytes), transcendentals=0)


def swap(x, axis, n, offset):
    return lax.ppermute(x, axis, [(i, i ^ offset) for i in range(n)])


def pick_kernel(y_size, first_ref, second_ref, out_ref):
    z = lax.axis_index("example") // y_size
    middle = (z == 1) | (z == 2)

    @pl.when(middle)
    def _():
        out_ref[...] = first_ref[...]

    @pl.when(jnp.logical_not(middle))
    def _():
        out_ref[...] = second_ref[...]


def pick(y_size, first, second):
    return pl.pallas_call(
        functools.partial(pick_kernel, y_size),
        out_shape=pltpu.VMEM(first.shape, first.dtype),
        in_specs=[VMEM, VMEM],
        out_specs=VMEM,
        compiler_params=params(),
        cost_estimate=cost(1, 1),
        name="pick",
    )(first, second)


def gather_blocks(x, n):
    if n != 8:
        return [x] + [swap(x, "example", n, j) for j in range(1, n)], [()] * (n // 2)
    z_size, y_size = 4, 2

    def along_z(value, pairs):
        full = [(a * y_size + y, b * y_size + y) for a, b in pairs for y in range(y_size)]
        return lax.ppermute(value, "example", full)

    near = along_z(x, [(0, 1), (1, 0), (2, 3), (3, 2)])
    y_own = swap(x, "example", n, 1)
    inner = along_z(x, [(1, 2), (2, 1)])
    y_near = swap(near, "example", n, 1)
    cross = along_z(near, [(1, 2), (2, 1)])
    ends = along_z(inner, [(1, 0), (2, 3)])
    second = pick(y_size, cross, ends)
    y_second = swap(second, "example", n, 1)
    far = along_z(cross, [(1, 0), (2, 3)])
    third = pick(y_size, inner, far)
    y_third = swap(third, "example", n, 1)
    slots = [x, y_own, near, y_near, second, y_second, third, y_third]
    return slots, [(near, inner), (second,), (third,), ()]


def prepare_kernel(tile, w_ref, x_ref, labels_ref, counts_ref, active_ref,
                   low_ref, target_ref, norm_ref, held_ref, sems):
    count = w_ref.shape[0] // tile
    copies = [
        pltpu.make_async_copy(
            w_ref.at[k * tile : (k + 1) * tile, :], held_ref.at[k % 4], sems.at[k % 4]
        )
        for k in range(count)
    ]
    for copy in copies[:4]:
        copy.start()
    rows = x_ref.shape[0]
    slot = lax.broadcasted_iota(jnp.int32, (1, rows), 1)
    target = jnp.where(slot < counts_ref[0], labels_ref[...] % active_ref[0], -1)
    target_ref[...] = target.astype(F32)
    squares = (x_ref[...] * x_ref[...]).astype(F32)
    norm = jnp.sum(squares, axis=1, keepdims=True)
    norm_ref[...] = jnp.broadcast_to(norm, (rows, LANES)).T[0:1, :]
    for k in range(count):
        copies[k].wait()
        low_ref[k * tile : (k + 1) * tile, :] = held_ref[k % 4].astype(BF16)
        if k + 4 < count:
            copies[k + 4].start()


def prepare(weights, features, labels, counts, active):
    rows = features.shape[0]
    feature_count, classes = weights.shape
    tile = 256
    line = jax.ShapeDtypeStruct((1, rows), F32)
    return pl.pallas_call(
        functools.partial(prepare_kernel, tile),
        out_shape=(pltpu.VMEM((feature_count, classes), BF16), line, line),
        in_specs=[HBM, VMEM, VMEM, SMEM, SMEM],
        out_specs=(VMEM,) * 3,
        scratch_shapes=[pltpu.VMEM((4, tile, classes), F32), pltpu.SemaphoreType.DMA((4,))],
        compiler_params=params(),
        cost_estimate=cost(1, 1),
        name="prepare",
    )(weights, features, labels.reshape(1, rows), counts, active)


def arriving_kernel(count, *refs):
    blocks, w_ref, out_ref = refs[:count], refs[count], refs[-1]
    rows = blocks[0].shape[0]
    columns = 256
    for first in range(0, w_ref.shape[1], columns):
        for k in range(count):
            out_ref[k * rows : (k + 1) * rows, first : first + columns] = jnp.dot(
                blocks[k][...], w_ref[:, first : first + columns], preferred_element_type=F32
            )


def arriving_logits(blocks, w_low, tokens):
    rows = sum(b.shape[0] for b in blocks)
    return pl.pallas_call(
        functools.partial(arriving_kernel, len(blocks)),
        out_shape=jax.ShapeDtypeStruct((rows, w_low.shape[1]), F32),
        in_specs=[VMEM] * (len(blocks) + 1) + [ANY] * len(tokens),
        out_specs=VMEM,
        compiler_params=params(),
        cost_estimate=cost(1, 1),
        name="arriving_logits",
    )(*blocks, w_low, *tokens)


def turn_kernel(*refs):
    blocks, out_ref = refs[:-1], refs[-1]
    rows = blocks[0].shape[0]
    for k, block in enumerate(blocks):
        out_ref[:, k * rows : (k + 1) * rows] = block[...].T


def turn(blocks):
    rows = sum(b.shape[0] for b in blocks)
    return pl.pallas_call(
        turn_kernel,
        out_shape=pltpu.VMEM((blocks[0].shape[1], rows), BF16),
        in_specs=[VMEM] * len(blocks),
        out_specs=VMEM,
        compiler_params=params(),
        cost_estimate=cost(1, 1),
        name="turn",
    )(*blocks)


def lane_pack(columns, rows):
    lane = lax.broadcasted_iota(jnp.int32, (rows, LANES), 1)
    packed = jnp.zeros((rows, LANES), F32)
    for k, column in enumerate(columns):
        packed = jnp.where(lane == k, column, packed)
    return packed


def put_stats(packed, place, shape):
    lines = packed.T
    line = jnp.concatenate([lines[k : k + 1, :] for k in range(3)], axis=1)
    here = lax.broadcasted_iota(jnp.int32, shape, 0) == place
    return jnp.where(here, line, 0.0)


def first_stats_kernel(slot, earlier, last, tokens, own_ref, other_ref, active_ref, *refs):
    lines = refs[: 3 * last]
    older = refs[3 * last : 3 * last + earlier]
    outs = refs[3 * last + earlier + tokens :]
    e_ref, stats_ref = outs[0], outs[1]
    pack_ref = refs[-1]
    rows, classes = own_ref.shape
    active, place = active_ref[0], lax.axis_index("example")
    class_start = place * classes
    index = class_start + lax.broadcasted_iota(jnp.int32, (1, classes), 1)
    live = index < active

    def step(i, _):
        at = pl.ds(pl.multiple_of(i * STEP, STEP), STEP)
        logits = jnp.where(live, own_ref[at, :] + other_ref[at, :], NEGATIVE)
        peak = jnp.max(logits, axis=1, keepdims=True)
        e = jnp.exp(logits - peak)
        e_ref[at, :] = e
        total = jnp.sum(e, axis=1, keepdims=True)
        square = jnp.sum(e * e, axis=1, keepdims=True)
        pack_ref[at, :] = lane_pack((peak, total, square), STEP)
        return 0

    lax.fori_loop(0, rows // STEP, step, 0)
    shape = stats_ref.shape
    stats = older[0][...] if earlier else jnp.zeros(shape, F32)
    for k in range(rows // LANES):
        stats += put_stats(pack_ref[k * LANES : (k + 1) * LANES, :], place ^ (slot + k), shape)
    stats_ref[...] = stats
    if last:
        copies_ref = outs[2]
        target, norm = lines[0][...], lines[1][...] + lines[2][...]
        wide = [jnp.broadcast_to(line, (shape[0], LANES)) for line in (target, norm)]
        full = jnp.concatenate([stats] + wide, axis=1)
        copies_ref[...] = jnp.broadcast_to(full[None], copies_ref.shape)


def first_stats(own, other, active, slot, n, earlier, side, tokens):
    rows, classes = own.shape
    last = len(side) > 0
    shapes = [jax.ShapeDtypeStruct(own.shape, F32), jax.ShapeDtypeStruct((n, 3 * LANES), F32)]
    if last:
        shapes.append(jax.ShapeDtypeStruct((n, n, 5 * LANES), F32))
    extra = list(side) + list(earlier)
    return pl.pallas_call(
        functools.partial(first_stats_kernel, slot, len(earlier), last, len(tokens)),
        out_shape=tuple(shapes),
        in_specs=[VMEM, VMEM, SMEM] + [VMEM] * len(extra) + [ANY] * len(tokens),
        out_specs=(VMEM,) * len(shapes),
        scratch_shapes=[pltpu.VMEM((rows, LANES), F32)],
        compiler_params=params(),
        cost_estimate=cost(1, 1),
        name="first_stats",
    )(own, other, active, *extra, *tokens)


def combine(own_ref, all_ref):
    n = all_ref.shape[0]
    part = lambda d, k: all_ref[d, :, k * LANES : (k + 1) * LANES]
    peaks = [part(d, 0) for d in range(n)]
    peak = functools.reduce(jnp.maximum, peaks)
    scales = [jnp.exp(p - peak) for p in peaks]
    total = sum(part(d, 1) * scales[d] for d in range(n))
    own_scale = jnp.exp(own_ref[:, 0:LANES] - peak)
    return part, peak, scales, total, own_scale


def to_slots(value, line_ref, place):
    n = value.shape[0]
    line_ref[...] = value
    return jnp.concatenate([line_ref[pl.ds(place ^ j, 1), :] for j in range(n)], axis=0)


def to_columns(lines):
    stacked = jnp.concatenate(lines, axis=0)
    rest = jnp.zeros((LANES - stacked.shape[0], LANES), F32)
    return jnp.concatenate([stacked, rest], axis=0).T


def first_weights_kernel(entries, parts, blocks, turns, own_ref, all_ref, *refs):
    e_refs = refs[:parts]
    block_refs, turn_refs = refs[parts : parts + blocks], refs[parts + blocks :][:turns]
    refs = refs[parts + blocks + turns :]
    residual_ref, fisher_ref, damping_ref, target_ref, plain_ref, turned_ref = refs[:6]
    column_ref, line_ref, sems = refs[6:]
    copies = []
    for k, ref in enumerate(block_refs):
        at = slice(k * LANES, (k + 1) * LANES)
        copies.append(pltpu.make_async_copy(ref, plain_ref.at[at, :], sems.at[k]))
    for k, ref in enumerate(turn_refs):
        at = slice(k * ref.shape[1], (k + 1) * ref.shape[1])
        copies.append(pltpu.make_async_copy(ref, turned_ref.at[:, at], sems.at[blocks + k]))
    for copy in copies:
        copy.start()
    n = all_ref.shape[0]
    classes = residual_ref.shape[1]
    place = lax.axis_index("example")
    class_start = place * classes
    part, peak, scales, total, own_scale = combine(own_ref, all_ref)
    square = sum(part(d, 2) * (scales[d] * scales[d]) for d in range(n))
    inverse = 1.0 / total
    spread = 1.0 - square * inverse * inverse
    target = jnp.concatenate([all_ref[d, 0:1, 3 * LANES : 4 * LANES] for d in range(n)], axis=0)
    norm = jnp.concatenate([all_ref[d, 0:1, 4 * LANES : 5 * LANES] for d in range(n)], axis=0)
    valid = (target >= 0.0).astype(F32)
    share = valid / jnp.sum(valid)
    fisher_sum = jnp.sum(norm * share * spread)
    damping_ref[...] = jnp.full(
        damping_ref.shape, DAMPING_SHARE * fisher_sum / entries + EPSILON, F32
    )
    factor = to_slots(own_scale * inverse, line_ref, place)
    share = to_slots(share, line_ref, place)
    target = to_slots(target, line_ref, place)
    target_ref[...] = target
    column_ref[...] = to_columns([factor, share, target])
    index = class_start + lax.broadcasted_iota(jnp.int32, (1, classes), 1)
    done = 0
    for e_ref in e_refs:
        for k in range(e_ref.shape[0] // LANES):
            j = done + k

            def step(i, _, j=j, k=k, e_ref=e_ref):
                start = pl.multiple_of(i * STEP, STEP)
                at = pl.ds(pl.multiple_of(j * LANES + start, STEP), STEP)
                column = column_ref[pl.ds(start, STEP), :]
                e = e_ref[pl.ds(pl.multiple_of(k * LANES + start, STEP), STEP), :]
                probability = e * column[:, j : j + 1]
                hit = index == column[:, 2 * n + j : 2 * n + j + 1].astype(jnp.int32)
                part = column[:, n + j : n + j + 1]
                residual_ref[at, :] = (part * (probability - hit.astype(F32))).astype(BF16)
                fisher_ref[at, :] = (part * probability * (1.0 - probability)).astype(BF16)
                return 0

            lax.fori_loop(0, LANES // STEP, step, 0)
        done += e_ref.shape[0] // LANES
    for copy in copies:
        copy.wait()


def first_weights(own, every, e_parts, slots, turned, entries):
    n = own.shape[0]
    classes = e_parts[0].shape[1]
    weight = pltpu.VMEM((n * LANES, classes), BF16)
    return pl.pallas_call(
        functools.partial(
            first_weights_kernel, float(entries), len(e_parts), len(slots), len(turned)
        ),
        out_shape=(
            weight,
            weight,
            jax.ShapeDtypeStruct((8, LANES), F32),
            jax.ShapeDtypeStruct((n, LANES), F32),
            pltpu.VMEM((n * LANES, slots[0].shape[1]), BF16),
            pltpu.VMEM((slots[0].shape[1], n * LANES), BF16),
        ),
        in_specs=[VMEM] * (2 + len(e_parts) + len(slots) + len(turned)),
        out_specs=(VMEM,) * 6,
        scratch_shapes=[
            pltpu.VMEM((LANES, LANES), F32),
            pltpu.VMEM((n, LANES), F32),
            pltpu.SemaphoreType.DMA((len(slots) + len(turned),)),
        ],
        compiler_params=params(),
        cost_estimate=cost(0, 8 * n * LANES * classes),
        name="first_weights",
    )(own, every, *e_parts, *slots, *turned)


def update_kernel(start, tile, turned_ref, w_ref, residual_ref, fisher_ref, damping_ref,
                  moved_ref, inverse_ref, low_ref, held_ref, sems):
    features, columns = moved_ref.shape
    damping = damping_ref[0:1, 0:1]
    own = slice(start, start + columns)
    copies = []
    for k in range(features // tile):
        copies.append(
            pltpu.make_async_copy(
                w_ref.at[k * tile : (k + 1) * tile, own], held_ref.at[k], sems.at[k]
            )
        )
        copies[-1].start()
    for k in range(features // tile):
        at = slice(k * tile, (k + 1) * tile)
        turned = turned_ref[at, :]
        gradient = jnp.dot(turned, residual_ref[:, own], preferred_element_type=F32)
        fisher = jnp.dot(turned * turned, fisher_ref[:, own], preferred_element_type=F32)
        inverse = 1.0 / (fisher + damping)
        change = gradient * inverse
        inverse_ref[at, :] = inverse
        moved_ref[at, :] = -change
        copies[k].wait()
        low_ref[at, :] = (held_ref[k] - LEARNING_RATE * change).astype(BF16)


def update(turned, weights, residual, fisher_weight, damping, start, columns):
    features, rows = turned.shape
    tile = 512
    return pl.pallas_call(
        functools.partial(update_kernel, start, tile),
        out_shape=(
            pltpu.VMEM((features, columns), F32),
            pltpu.VMEM((features, columns), F32),
            pltpu.VMEM((features, columns), BF16),
        ),
        in_specs=[VMEM, HBM] + [VMEM] * 3,
        out_specs=(VMEM, VMEM, VMEM),
        scratch_shapes=[
            pltpu.VMEM((features // tile, tile, columns), F32),
            pltpu.SemaphoreType.DMA((features // tile,)),
        ],
        compiler_params=params(14),
        cost_estimate=cost(4 * rows * features * columns),
        name="update",
    )(turned, weights, residual, fisher_weight, damping)


def next_logits_kernel(start, tile, plain_ref, low_ref, out_ref):
    for first in range(0, out_ref.shape[0], tile):
        out_ref[first : first + tile, :] = jnp.dot(
            plain_ref[start + first : start + first + tile, :],
            low_ref[...],
            preferred_element_type=F32,
        )


def next_logits(plain, low, start, rows):
    features, columns = low.shape
    return pl.pallas_call(
        functools.partial(next_logits_kernel, start, min(512, rows)),
        out_shape=jax.ShapeDtypeStruct((rows, columns), F32),
        in_specs=[VMEM, VMEM],
        out_specs=VMEM,
        compiler_params=params(),
        cost_estimate=cost(2 * rows * features * columns),
        name="next_logits",
    )(plain, low)


def last_stats_kernel(slot, last, pieces, offsets, earlier, *refs):
    own, other = refs[:pieces], refs[pieces : 2 * pieces]
    target_ref, active_ref = refs[2 * pieces : 2 * pieces + 2]
    older = refs[2 * pieces + 2 : 2 * pieces + 2 + earlier]
    outs = refs[2 * pieces + 2 + earlier :]
    e_ref, stats_ref, pack_ref, column_ref = outs[0], outs[1], outs[-2], outs[-1]
    rows, classes = e_ref.shape
    active, place = active_ref[0], lax.axis_index("example")
    class_start = place * classes
    n = stats_ref.shape[0]
    column_ref[...] = to_columns([target_ref[...]])
    index = class_start + lax.broadcasted_iota(jnp.int32, (1, classes), 1)
    live = index < active
    for k in range(rows // LANES):
        def step(i, _, k=k):
            start = pl.multiple_of(i * STEP, STEP)

            def rows_of(base):
                return pl.ds(pl.multiple_of(base + k * LANES + start, STEP), STEP)

            logits = jnp.concatenate(
                [a[rows_of(o), :] + b[rows_of(o), :] for a, b, o in zip(own, other, offsets)],
                axis=1,
            )
            column = column_ref[pl.ds(start, STEP), slot + k : slot + k + 1]
            hit = index == column.astype(jnp.int32)
            label = jnp.sum(jnp.where(hit, logits, 0.0), axis=1, keepdims=True)
            logits = jnp.where(live, logits, NEGATIVE)
            peak = jnp.max(logits, axis=1, keepdims=True)
            e = jnp.exp(logits - peak)
            e_ref[rows_of(0), :] = e
            total = jnp.sum(e, axis=1, keepdims=True)
            pack_ref[rows_of(0), :] = lane_pack((peak, total, label), STEP)
            return 0

        lax.fori_loop(0, LANES // STEP, step, 0)
    shape = stats_ref.shape
    stats = older[0][...] if earlier else jnp.zeros(shape, F32)
    for k in range(rows // LANES):
        stats += put_stats(pack_ref[k * LANES : (k + 1) * LANES, :], place ^ (slot + k), shape)
    stats_ref[...] = stats
    if last:
        outs[2][...] = jnp.broadcast_to(stats[None], outs[2].shape)


def last_stats(own, other, offsets, target, active, slot, rows, n, earlier):
    classes = sum(c.shape[1] for c in own)
    last = slot + rows // LANES == n
    shapes = [
        jax.ShapeDtypeStruct((rows, classes), F32),
        jax.ShapeDtypeStruct((n, 3 * LANES), F32),
    ]
    if last:
        shapes.append(jax.ShapeDtypeStruct((n, n, 3 * LANES), F32))
    return pl.pallas_call(
        functools.partial(
            last_stats_kernel, slot, last, len(own), tuple(offsets), len(earlier)
        ),
        out_shape=tuple(shapes),
        in_specs=[VMEM] * (2 * len(own) + 1) + [SMEM] + [VMEM] * len(earlier),
        out_specs=(VMEM,) * len(shapes),
        scratch_shapes=[pltpu.VMEM((rows, LANES), F32), pltpu.VMEM((LANES, LANES), F32)],
        compiler_params=params(),
        cost_estimate=cost(0, 24 * rows * classes),
        name="last_stats",
    )(*own, *other, target, active, *earlier)


def finish_kernel(chunks, e_parts, tile, own_ref, all_ref, target_ref, turned_ref, *refs):
    e_refs = refs[:e_parts]
    refs = refs[e_parts:]
    moved_refs, inverse_refs = refs[:chunks], refs[chunks : 2 * chunks]
    out_ref, loss_ref, residual_ref, column_ref, line_ref, held_ref, sems = refs[2 * chunks :]
    n = all_ref.shape[0]
    classes = residual_ref.shape[1]
    place = lax.axis_index("example")
    class_start = place * classes
    part, peak, scales, total, own_scale = combine(own_ref, all_ref)
    label = sum(part(d, 2) for d in range(n))
    target = target_ref[...]
    valid = (target >= 0.0).astype(F32)
    share = valid / jnp.sum(valid)
    losses = to_slots(peak + jnp.log(total) - label, line_ref, place)
    loss_ref[...] = (valid * losses)[0:1, :]
    factor = to_slots(own_scale / total, line_ref, place)
    column_ref[...] = to_columns([factor, share, target])
    index = class_start + lax.broadcasted_iota(jnp.int32, (1, classes), 1)
    done = 0
    for e_ref in e_refs:
        for k in range(e_ref.shape[0] // LANES):
            j = done + k

            def step(i, _, j=j, k=k, e_ref=e_ref):
                start = pl.multiple_of(i * STEP, STEP)
                at = pl.ds(pl.multiple_of(j * LANES + start, STEP), STEP)
                column = column_ref[pl.ds(start, STEP), :]
                e = e_ref[pl.ds(pl.multiple_of(k * LANES + start, STEP), STEP), :]
                probability = e * column[:, j : j + 1]
                hit = index == column[:, 2 * n + j : 2 * n + j + 1].astype(jnp.int32)
                part = column[:, n + j : n + j + 1]
                residual_ref[at, :] = (part * (probability - hit.astype(F32))).astype(BF16)
                return 0

            lax.fori_loop(0, LANES // STEP, step, 0)
        done += e_ref.shape[0] // LANES

    copies = []
    for k in range(out_ref.shape[0] // tile):
        at = slice(k * tile, (k + 1) * tile)
        done = 0
        for moved_ref, inverse_ref in zip(moved_refs, inverse_refs):
            own = slice(done, done + moved_ref.shape[1])
            gradient = jnp.dot(
                turned_ref[at, :], residual_ref[:, own], preferred_element_type=F32
            )
            held_ref[k, :, own] = moved_ref[at, :] - gradient * inverse_ref[at, :]
            done += moved_ref.shape[1]
        copies.append(pltpu.make_async_copy(held_ref.at[k], out_ref.at[at, :], sems.at[k]))
        copies[-1].start()
    for copy in copies:
        copy.wait()


def finish(own, every, target, e_parts, turned, moved, inverse):
    n = own.shape[0]
    features, all_rows = turned.shape
    classes = e_parts[0].shape[1]
    tile = 512
    return pl.pallas_call(
        functools.partial(finish_kernel, len(moved), len(e_parts), tile),
        out_shape=(
            jax.ShapeDtypeStruct((features, classes), F32),
            jax.ShapeDtypeStruct((1, LANES), F32),
        ),
        in_specs=[VMEM] * (4 + len(e_parts) + 2 * len(moved)),
        out_specs=(ANY, VMEM),
        scratch_shapes=[
            pltpu.VMEM((all_rows, classes), BF16),
            pltpu.VMEM((LANES, LANES), F32),
            pltpu.VMEM((n, LANES), F32),
            pltpu.VMEM((features // tile, tile, classes), F32),
            pltpu.SemaphoreType.DMA((features // tile,)),
        ],
        compiler_params=params(16),
        cost_estimate=cost(2 * all_rows * features * classes),
        name="finish",
    )(own, every, target, turned, *e_parts, *moved, *inverse)


def exchange(copies):
    return lax.all_to_all(copies, "example", 0, 0)


def body(n, n_cls, features, weights, labels, counts, active):
    rows = features.shape[0]
    all_rows = rows * n
    feature_count, classes = weights.shape
    entries = feature_count * n_cls * classes * n
    weights = pltpu.with_memory_space_constraint(weights, pltpu.HBM)
    slots, waits = gather_blocks(features, n)
    w_low, target, norm = prepare(weights, features, labels, counts, active)
    side = (target, norm, swap(norm, "cls", n_cls, 1))

    groups = [(first, slots[first : first + 2]) for first in range(0, n - 2, 2)]
    groups += [(n - 2, slots[n - 2 : n - 1]), (n - 1, slots[n - 1 :])]
    count = len(groups)
    logits, turned, e_parts, stats = [], [], [], []

    def statistics(g, tokens):
        last = g == count - 1
        other = swap(logits[g], "cls", n_cls, 1)
        e, found, *copies = first_stats(
            logits[g], other, active, groups[g][0], n, tuple(stats[-1:]),
            side if last else (), tokens,
        )
        e_parts.append(e)
        stats.append(found)
        return copies

    for g in range(count):
        tokens = tuple(stats[-1:]) + tuple(turned[-1:]) + tuple(waits[g] if g < n // 2 else ())
        logits.append(arriving_logits(groups[g][1], w_low, tokens))
        if g < n // 2:
            turned.append(turn(slots[2 * g : 2 * g + 2]))
        if 1 <= g < count - 2:
            statistics(g - 1, (logits[g],))
    for g in range(max(count - 3, 0), count):
        copies = statistics(g, (logits[-1], turned[-1]))
    own_stats = stats[-1]
    every = exchange(copies[0])
    residual, fisher_weight, damping, target, plain, turned = first_weights(
        own_stats, every, e_parts, slots, turned, entries
    )

    columns = min(512, classes)
    moved, inverse, own, other = [], [], [], []
    for start in range(0, classes, columns):
        a, b, low = update(turned, weights, residual, fisher_weight, damping, start, columns)
        moved.append(a)
        inverse.append(b)
        if start + columns < classes:
            own.append(next_logits(plain, low, 0, all_rows))
            other.append(swap(own[-1], "cls", n_cls, 1))
    half = n // 2
    late = [next_logits(plain, low, first * rows, half * rows) for first in (0, half)]
    late_other = [swap(c, "cls", n_cls, 1) for c in late]
    e_parts, earlier = [], ()
    for first, c, d in zip((0, half), late, late_other):
        offsets = [first * rows] * len(own) + [0]
        e, own_stats, *copies = last_stats(
            own + [c], other + [d], offsets, target, active, first, half * rows, n, earlier
        )
        e_parts.append(e)
        earlier = (own_stats,)
    every = exchange(copies[0])
    out, losses = finish(own_stats, every, target, e_parts, turned, moved, inverse)
    return out, losses.reshape(rows)


def solution(mesh):
    return jax.shard_map(
        functools.partial(body, mesh.shape["example"], mesh.shape["cls"]),
        mesh=mesh,
        in_specs=(
            P(("groups", "example"), "cls"),
            P(("groups", "cls"), "example"),
            P(("groups", "example")),
            P(("groups", "example")),
            P("groups"),
        ),
        out_specs=(P(("groups", "cls"), "example"), P(("groups", "example"))),
        check_vma=False,
    )
```

```python
import functools

import jax
import jax.numpy as jnp
from jax import lax
from jax.experimental import pallas as pl
from jax.experimental.pallas import tpu as pltpu
from jax.sharding import PartitionSpec as P

ITERS = 2
NEGATIVE = -1e30
LEARNING_RATE = 2e-05
DAMPING_SHARE = 0.1
EPSILON = 1e-06

F32 = jnp.float32
BF16 = jnp.bfloat16
VMEM = pl.BlockSpec(memory_space=pltpu.VMEM)
SMEM = pl.BlockSpec(memory_space=pltpu.SMEM)
HBM = pl.BlockSpec(memory_space=pltpu.HBM)
ANY = pl.BlockSpec(memory_space=pl.ANY)
STEP = 64
LANES = 128


def params(mib=10):
    return pltpu.CompilerParams(vmem_limit_bytes=mib << 20)


def cost(flops=0, nbytes=0):
    return pl.CostEstimate(flops=int(flops), bytes_accessed=int(nbytes), transcendentals=0)


def swap(x, axis, n, offset):
    return lax.ppermute(x, axis, [(i, i ^ offset) for i in range(n)])


def pick_kernel(y_size, first_ref, second_ref, out_ref):
    z = lax.axis_index("example") // y_size
    middle = (z == 1) | (z == 2)

    @pl.when(middle)
    def _():
        out_ref[...] = first_ref[...]

    @pl.when(jnp.logical_not(middle))
    def _():
        out_ref[...] = second_ref[...]


def pick(y_size, first, second):
    return pl.pallas_call(
        functools.partial(pick_kernel, y_size),
        out_shape=pltpu.VMEM(first.shape, first.dtype),
        in_specs=[VMEM, VMEM],
        out_specs=VMEM,
        compiler_params=params(),
        cost_estimate=cost(1, 1),
        name="pick",
    )(first, second)


def gather_blocks(x, n):
    if n != 8:
        return [x] + [swap(x, "example", n, j) for j in range(1, n)], [()] * (n // 2)
    z_size, y_size = 4, 2

    def along_z(value, pairs):
        full = [(a * y_size + y, b * y_size + y) for a, b in pairs for y in range(y_size)]
        return lax.ppermute(value, "example", full)

    tie = lax.optimization_barrier
    y_own = swap(x, "example", n, 1)
    near = along_z(x, [(0, 1), (1, 0), (2, 3), (3, 2)])
    inner = along_z(x, [(1, 2), (2, 1)])
    near, y_own = tie((near, y_own))
    y_near = swap(near, "example", n, 1)
    cross = along_z(near, [(1, 2), (2, 1)])
    ends = along_z(inner, [(1, 0), (2, 3)])
    cross, y_near, ends = tie((cross, y_near, ends))
    second = pick(y_size, cross, ends)
    y_second = swap(second, "example", n, 1)
    far = along_z(cross, [(1, 0), (2, 3)])
    far, y_second = tie((far, y_second))
    third = pick(y_size, inner, far)
    y_third = swap(third, "example", n, 1)
    slots = [x, y_own, near, y_near, second, y_second, third, y_third]
    return slots, [(near, inner), (second,), (third,), ()]


def prepare_kernel(tile, w_ref, x_ref, labels_ref, counts_ref, active_ref,
                   low_ref, target_ref, norm_ref, held_ref, sems):
    count = w_ref.shape[0] // tile
    copies = [
        pltpu.make_async_copy(
            w_ref.at[k * tile : (k + 1) * tile, :], held_ref.at[k % 4], sems.at[k % 4]
        )
        for k in range(count)
    ]
    for copy in copies[:4]:
        copy.start()
    rows = x_ref.shape[0]
    slot = lax.broadcasted_iota(jnp.int32, (1, rows), 1)
    target = jnp.where(slot < counts_ref[0], labels_ref[...] % active_ref[0], -1)
    target_ref[...] = target.astype(F32)
    squares = (x_ref[...] * x_ref[...]).astype(F32)
    norm = jnp.sum(squares, axis=1, keepdims=True)
    norm_ref[...] = jnp.broadcast_to(norm, (rows, LANES)).T[0:1, :]
    for k in range(count):
        copies[k].wait()
        low_ref[k * tile : (k + 1) * tile, :] = held_ref[k % 4].astype(BF16)
        if k + 4 < count:
            copies[k + 4].start()


def prepare(weights, features, labels, counts, active):
    rows = features.shape[0]
    feature_count, classes = weights.shape
    tile = 256
    line = jax.ShapeDtypeStruct((1, rows), F32)
    return pl.pallas_call(
        functools.partial(prepare_kernel, tile),
        out_shape=(pltpu.VMEM((feature_count, classes), BF16), line, line),
        in_specs=[HBM, VMEM, VMEM, SMEM, SMEM],
        out_specs=(VMEM,) * 3,
        scratch_shapes=[pltpu.VMEM((4, tile, classes), F32), pltpu.SemaphoreType.DMA((4,))],
        compiler_params=params(),
        cost_estimate=cost(1, 1),
        name="prepare",
    )(weights, features, labels.reshape(1, rows), counts, active)


def arriving_kernel(count, *refs):
    blocks, w_ref, out_ref = refs[:count], refs[count], refs[-1]
    rows = blocks[0].shape[0]
    columns = 256
    for first in range(0, w_ref.shape[1], columns):
        for k in range(count):
            out_ref[k * rows : (k + 1) * rows, first : first + columns] = jnp.dot(
                blocks[k][...], w_ref[:, first : first + columns], preferred_element_type=F32
            )


def arriving_logits(blocks, w_low, tokens):
    rows = sum(b.shape[0] for b in blocks)
    return pl.pallas_call(
        functools.partial(arriving_kernel, len(blocks)),
        out_shape=jax.ShapeDtypeStruct((rows, w_low.shape[1]), F32),
        in_specs=[VMEM] * (len(blocks) + 1) + [ANY] * len(tokens),
        out_specs=VMEM,
        compiler_params=params(),
        cost_estimate=cost(1, 1),
        name="arriving_logits",
    )(*blocks, w_low, *tokens)


def turn_kernel(*refs):
    blocks, out_ref = refs[:-1], refs[-1]
    rows = blocks[0].shape[0]
    for k, block in enumerate(blocks):
        out_ref[:, k * rows : (k + 1) * rows] = block[...].T


def turn(blocks):
    rows = sum(b.shape[0] for b in blocks)
    return pl.pallas_call(
        turn_kernel,
        out_shape=pltpu.VMEM((blocks[0].shape[1], rows), BF16),
        in_specs=[VMEM] * len(blocks),
        out_specs=VMEM,
        compiler_params=params(),
        cost_estimate=cost(1, 1),
        name="turn",
    )(*blocks)


def lane_pack(columns, rows):
    lane = lax.broadcasted_iota(jnp.int32, (rows, LANES), 1)
    packed = jnp.zeros((rows, LANES), F32)
    for k, column in enumerate(columns):
        packed = jnp.where(lane == k, column, packed)
    return packed


def put_stats(packed, place, shape):
    lines = packed.T
    line = jnp.concatenate([lines[k : k + 1, :] for k in range(3)], axis=1)
    here = lax.broadcasted_iota(jnp.int32, shape, 0) == place
    return jnp.where(here, line, 0.0)


def first_stats_kernel(slot, earlier, last, tokens, own_ref, other_ref, active_ref, *refs):
    lines = refs[: 3 * last]
    older = refs[3 * last : 3 * last + earlier]
    outs = refs[3 * last + earlier + tokens :]
    e_ref, stats_ref = outs[0], outs[1]
    pack_ref = refs[-1]
    rows, classes = own_ref.shape
    active, place = active_ref[0], lax.axis_index("example")
    class_start = place * classes
    index = class_start + lax.broadcasted_iota(jnp.int32, (1, classes), 1)
    live = index < active

    def step(i, _):
        at = pl.ds(pl.multiple_of(i * STEP, STEP), STEP)
        logits = jnp.where(live, own_ref[at, :] + other_ref[at, :], NEGATIVE)
        peak = jnp.max(logits, axis=1, keepdims=True)
        e = jnp.exp(logits - peak)
        e_ref[at, :] = e
        total = jnp.sum(e, axis=1, keepdims=True)
        square = jnp.sum(e * e, axis=1, keepdims=True)
        pack_ref[at, :] = lane_pack((peak, total, square), STEP)
        return 0

    lax.fori_loop(0, rows // STEP, step, 0)
    shape = stats_ref.shape
    stats = older[0][...] if earlier else jnp.zeros(shape, F32)
    for k in range(rows // LANES):
        stats += put_stats(pack_ref[k * LANES : (k + 1) * LANES, :], place ^ (slot + k), shape)
    stats_ref[...] = stats
    if last:
        copies_ref = outs[2]
        target, norm = lines[0][...], lines[1][...] + lines[2][...]
        wide = [jnp.broadcast_to(line, (shape[0], LANES)) for line in (target, norm)]
        full = jnp.concatenate([stats] + wide, axis=1)
        copies_ref[...] = jnp.broadcast_to(full[None], copies_ref.shape)


def first_stats(own, other, active, slot, n, earlier, side, tokens):
    rows, classes = own.shape
    last = len(side) > 0
    shapes = [jax.ShapeDtypeStruct(own.shape, F32), jax.ShapeDtypeStruct((n, 3 * LANES), F32)]
    if last:
        shapes.append(jax.ShapeDtypeStruct((n, n, 5 * LANES), F32))
    extra = list(side) + list(earlier)
    return pl.pallas_call(
        functools.partial(first_stats_kernel, slot, len(earlier), last, len(tokens)),
        out_shape=tuple(shapes),
        in_specs=[VMEM, VMEM, SMEM] + [VMEM] * len(extra) + [ANY] * len(tokens),
        out_specs=(VMEM,) * len(shapes),
        scratch_shapes=[pltpu.VMEM((rows, LANES), F32)],
        compiler_params=params(),
        cost_estimate=cost(1, 1),
        name="first_stats",
    )(own, other, active, *extra, *tokens)


def combine(own_ref, all_ref):
    n = all_ref.shape[0]
    part = lambda d, k: all_ref[d, :, k * LANES : (k + 1) * LANES]
    peaks = [part(d, 0) for d in range(n)]
    peak = functools.reduce(jnp.maximum, peaks)
    scales = [jnp.exp(p - peak) for p in peaks]
    total = sum(part(d, 1) * scales[d] for d in range(n))
    own_scale = jnp.exp(own_ref[:, 0:LANES] - peak)
    return part, peak, scales, total, own_scale


def to_slots(value, line_ref, place):
    n = value.shape[0]
    line_ref[...] = value
    return jnp.concatenate([line_ref[pl.ds(place ^ j, 1), :] for j in range(n)], axis=0)


def to_columns(lines):
    stacked = jnp.concatenate(lines, axis=0)
    rest = jnp.zeros((LANES - stacked.shape[0], LANES), F32)
    return jnp.concatenate([stacked, rest], axis=0).T


def first_weights_kernel(entries, parts, blocks, turns, own_ref, all_ref, *refs):
    e_refs = refs[:parts]
    block_refs, turn_refs = refs[parts : parts + blocks], refs[parts + blocks :][:turns]
    refs = refs[parts + blocks + turns :]
    residual_ref, fisher_ref, damping_ref, target_ref, plain_ref, turned_ref = refs[:6]
    column_ref, line_ref, sems = refs[6:]
    copies = []
    for k, ref in enumerate(block_refs):
        at = slice(k * LANES, (k + 1) * LANES)
        copies.append(pltpu.make_async_copy(ref, plain_ref.at[at, :], sems.at[k]))
    for k, ref in enumerate(turn_refs):
        at = slice(k * ref.shape[1], (k + 1) * ref.shape[1])
        copies.append(pltpu.make_async_copy(ref, turned_ref.at[:, at], sems.at[blocks + k]))
    for copy in copies:
        copy.start()
    n = all_ref.shape[0]
    classes = residual_ref.shape[1]
    place = lax.axis_index("example")
    class_start = place * classes
    part, peak, scales, total, own_scale = combine(own_ref, all_ref)
    square = sum(part(d, 2) * (scales[d] * scales[d]) for d in range(n))
    inverse = 1.0 / total
    spread = 1.0 - square * inverse * inverse
    target = jnp.concatenate([all_ref[d, 0:1, 3 * LANES : 4 * LANES] for d in range(n)], axis=0)
    norm = jnp.concatenate([all_ref[d, 0:1, 4 * LANES : 5 * LANES] for d in range(n)], axis=0)
    valid = (target >= 0.0).astype(F32)
    share = valid / jnp.sum(valid)
    fisher_sum = jnp.sum(norm * share * spread)
    damping_ref[...] = jnp.full(
        damping_ref.shape, DAMPING_SHARE * fisher_sum / entries + EPSILON, F32
    )
    factor = to_slots(own_scale * inverse, line_ref, place)
    share = to_slots(share, line_ref, place)
    target = to_slots(target, line_ref, place)
    target_ref[...] = target
    column_ref[...] = to_columns([factor, share, target])
    index = class_start + lax.broadcasted_iota(jnp.int32, (1, classes), 1)
    done = 0
    for e_ref in e_refs:
        for k in range(e_ref.shape[0] // LANES):
            j = done + k

            def step(i, _, j=j, k=k, e_ref=e_ref):
                start = pl.multiple_of(i * STEP, STEP)
                at = pl.ds(pl.multiple_of(j * LANES + start, STEP), STEP)
                column = column_ref[pl.ds(start, STEP), :]
                e = e_ref[pl.ds(pl.multiple_of(k * LANES + start, STEP), STEP), :]
                probability = e * column[:, j : j + 1]
                hit = index == column[:, 2 * n + j : 2 * n + j + 1].astype(jnp.int32)
                part = column[:, n + j : n + j + 1]
                residual_ref[at, :] = (part * (probability - hit.astype(F32))).astype(BF16)
                fisher_ref[at, :] = (part * probability * (1.0 - probability)).astype(BF16)
                return 0

            lax.fori_loop(0, LANES // STEP, step, 0)
        done += e_ref.shape[0] // LANES
    for copy in copies:
        copy.wait()


def first_weights(own, every, e_parts, slots, turned, entries):
    n = own.shape[0]
    classes = e_parts[0].shape[1]
    weight = pltpu.VMEM((n * LANES, classes), BF16)
    return pl.pallas_call(
        functools.partial(
            first_weights_kernel, float(entries), len(e_parts), len(slots), len(turned)
        ),
        out_shape=(
            weight,
            weight,
            jax.ShapeDtypeStruct((8, LANES), F32),
            jax.ShapeDtypeStruct((n, LANES), F32),
            pltpu.VMEM((n * LANES, slots[0].shape[1]), BF16),
            pltpu.VMEM((slots[0].shape[1], n * LANES), BF16),
        ),
        in_specs=[VMEM] * (2 + len(e_parts) + len(slots) + len(turned)),
        out_specs=(VMEM,) * 6,
        scratch_shapes=[
            pltpu.VMEM((LANES, LANES), F32),
            pltpu.VMEM((n, LANES), F32),
            pltpu.SemaphoreType.DMA((len(slots) + len(turned),)),
        ],
        compiler_params=params(),
        cost_estimate=cost(0, 8 * n * LANES * classes),
        name="first_weights",
    )(own, every, *e_parts, *slots, *turned)


def update_kernel(start, tile, turned_ref, w_ref, residual_ref, fisher_ref, damping_ref,
                  moved_ref, inverse_ref, low_ref, held_ref, sems):
    features, columns = moved_ref.shape
    damping = damping_ref[0:1, 0:1]
    own = slice(start, start + columns)
    copies = []
    for k in range(features // tile):
        copies.append(
            pltpu.make_async_copy(
                w_ref.at[k * tile : (k + 1) * tile, own], held_ref.at[k], sems.at[k]
            )
        )
        copies[-1].start()
    for k in range(features // tile):
        at = slice(k * tile, (k + 1) * tile)
        turned = turned_ref[at, :]
        gradient = jnp.dot(turned, residual_ref[:, own], preferred_element_type=F32)
        fisher = jnp.dot(turned * turned, fisher_ref[:, own], preferred_element_type=F32)
        inverse = 1.0 / (fisher + damping)
        change = gradient * inverse
        inverse_ref[at, :] = inverse
        moved_ref[at, :] = -change
        copies[k].wait()
        low_ref[at, :] = (held_ref[k] - LEARNING_RATE * change).astype(BF16)


def update(turned, weights, residual, fisher_weight, damping, start, columns):
    features, rows = turned.shape
    tile = 512
    return pl.pallas_call(
        functools.partial(update_kernel, start, tile),
        out_shape=(
            pltpu.VMEM((features, columns), F32),
            pltpu.VMEM((features, columns), F32),
            pltpu.VMEM((features, columns), BF16),
        ),
        in_specs=[VMEM, HBM] + [VMEM] * 3,
        out_specs=(VMEM, VMEM, VMEM),
        scratch_shapes=[
            pltpu.VMEM((features // tile, tile, columns), F32),
            pltpu.SemaphoreType.DMA((features // tile,)),
        ],
        compiler_params=params(14),
        cost_estimate=cost(4 * rows * features * columns),
        name="update",
    )(turned, weights, residual, fisher_weight, damping)


def next_logits_kernel(start, tile, plain_ref, low_ref, out_ref):
    for first in range(0, out_ref.shape[0], tile):
        out_ref[first : first + tile, :] = jnp.dot(
            plain_ref[start + first : start + first + tile, :],
            low_ref[...],
            preferred_element_type=F32,
        )


def next_logits(plain, low, start, rows):
    features, columns = low.shape
    return pl.pallas_call(
        functools.partial(next_logits_kernel, start, min(512, rows)),
        out_shape=jax.ShapeDtypeStruct((rows, columns), F32),
        in_specs=[VMEM, VMEM],
        out_specs=VMEM,
        compiler_params=params(),
        cost_estimate=cost(2 * rows * features * columns),
        name="next_logits",
    )(plain, low)


def last_stats_kernel(slot, last, pieces, offsets, earlier, *refs):
    own, other = refs[:pieces], refs[pieces : 2 * pieces]
    target_ref, active_ref = refs[2 * pieces : 2 * pieces + 2]
    older = refs[2 * pieces + 2 : 2 * pieces + 2 + earlier]
    outs = refs[2 * pieces + 2 + earlier :]
    e_ref, stats_ref, pack_ref, column_ref = outs[0], outs[1], outs[-2], outs[-1]
    rows, classes = e_ref.shape
    active, place = active_ref[0], lax.axis_index("example")
    class_start = place * classes
    n = stats_ref.shape[0]
    column_ref[...] = to_columns([target_ref[...]])
    index = class_start + lax.broadcasted_iota(jnp.int32, (1, classes), 1)
    live = index < active
    for k in range(rows // LANES):
        def step(i, _, k=k):
            start = pl.multiple_of(i * STEP, STEP)

            def rows_of(base):
                return pl.ds(pl.multiple_of(base + k * LANES + start, STEP), STEP)

            logits = jnp.concatenate(
                [a[rows_of(o), :] + b[rows_of(o), :] for a, b, o in zip(own, other, offsets)],
                axis=1,
            )
            column = column_ref[pl.ds(start, STEP), slot + k : slot + k + 1]
            hit = index == column.astype(jnp.int32)
            label = jnp.sum(jnp.where(hit, logits, 0.0), axis=1, keepdims=True)
            logits = jnp.where(live, logits, NEGATIVE)
            peak = jnp.max(logits, axis=1, keepdims=True)
            e = jnp.exp(logits - peak)
            e_ref[rows_of(0), :] = e
            total = jnp.sum(e, axis=1, keepdims=True)
            pack_ref[rows_of(0), :] = lane_pack((peak, total, label), STEP)
            return 0

        lax.fori_loop(0, LANES // STEP, step, 0)
    shape = stats_ref.shape
    stats = older[0][...] if earlier else jnp.zeros(shape, F32)
    for k in range(rows // LANES):
        stats += put_stats(pack_ref[k * LANES : (k + 1) * LANES, :], place ^ (slot + k), shape)
    stats_ref[...] = stats
    if last:
        outs[2][...] = jnp.broadcast_to(stats[None], outs[2].shape)


def last_stats(own, other, offsets, target, active, slot, rows, n, earlier):
    classes = sum(c.shape[1] for c in own)
    last = slot + rows // LANES == n
    shapes = [
        jax.ShapeDtypeStruct((rows, classes), F32),
        jax.ShapeDtypeStruct((n, 3 * LANES), F32),
    ]
    if last:
        shapes.append(jax.ShapeDtypeStruct((n, n, 3 * LANES), F32))
    return pl.pallas_call(
        functools.partial(
            last_stats_kernel, slot, last, len(own), tuple(offsets), len(earlier)
        ),
        out_shape=tuple(shapes),
        in_specs=[VMEM] * (2 * len(own) + 1) + [SMEM] + [VMEM] * len(earlier),
        out_specs=(VMEM,) * len(shapes),
        scratch_shapes=[pltpu.VMEM((rows, LANES), F32), pltpu.VMEM((LANES, LANES), F32)],
        compiler_params=params(),
        cost_estimate=cost(0, 24 * rows * classes),
        name="last_stats",
    )(*own, *other, target, active, *earlier)


def finish_kernel(chunks, e_parts, tile, own_ref, all_ref, target_ref, turned_ref, *refs):
    e_refs = refs[:e_parts]
    refs = refs[e_parts:]
    moved_refs, inverse_refs = refs[:chunks], refs[chunks : 2 * chunks]
    out_ref, loss_ref, residual_ref, column_ref, line_ref, held_ref, sems = refs[2 * chunks :]
    n = all_ref.shape[0]
    classes = residual_ref.shape[1]
    place = lax.axis_index("example")
    class_start = place * classes
    part, peak, scales, total, own_scale = combine(own_ref, all_ref)
    label = sum(part(d, 2) for d in range(n))
    target = target_ref[...]
    valid = (target >= 0.0).astype(F32)
    share = valid / jnp.sum(valid)
    losses = to_slots(peak + jnp.log(total) - label, line_ref, place)
    loss_ref[...] = (valid * losses)[0:1, :]
    factor = to_slots(own_scale / total, line_ref, place)
    column_ref[...] = to_columns([factor, share, target])
    index = class_start + lax.broadcasted_iota(jnp.int32, (1, classes), 1)
    done = 0
    for e_ref in e_refs:
        for k in range(e_ref.shape[0] // LANES):
            j = done + k

            def step(i, _, j=j, k=k, e_ref=e_ref):
                start = pl.multiple_of(i * STEP, STEP)
                at = pl.ds(pl.multiple_of(j * LANES + start, STEP), STEP)
                column = column_ref[pl.ds(start, STEP), :]
                e = e_ref[pl.ds(pl.multiple_of(k * LANES + start, STEP), STEP), :]
                probability = e * column[:, j : j + 1]
                hit = index == column[:, 2 * n + j : 2 * n + j + 1].astype(jnp.int32)
                part = column[:, n + j : n + j + 1]
                residual_ref[at, :] = (part * (probability - hit.astype(F32))).astype(BF16)
                return 0

            lax.fori_loop(0, LANES // STEP, step, 0)
        done += e_ref.shape[0] // LANES

    copies = []
    for k in range(out_ref.shape[0] // tile):
        at = slice(k * tile, (k + 1) * tile)
        done = 0
        for moved_ref, inverse_ref in zip(moved_refs, inverse_refs):
            own = slice(done, done + moved_ref.shape[1])
            gradient = jnp.dot(
                turned_ref[at, :], residual_ref[:, own], preferred_element_type=F32
            )
            held_ref[k, :, own] = moved_ref[at, :] - gradient * inverse_ref[at, :]
            done += moved_ref.shape[1]
        copies.append(pltpu.make_async_copy(held_ref.at[k], out_ref.at[at, :], sems.at[k]))
        copies[-1].start()
    for copy in copies:
        copy.wait()


def finish(own, every, target, e_parts, turned, moved, inverse):
    n = own.shape[0]
    features, all_rows = turned.shape
    classes = e_parts[0].shape[1]
    tile = 512
    return pl.pallas_call(
        functools.partial(finish_kernel, len(moved), len(e_parts), tile),
        out_shape=(
            jax.ShapeDtypeStruct((features, classes), F32),
            jax.ShapeDtypeStruct((1, LANES), F32),
        ),
        in_specs=[VMEM] * (4 + len(e_parts) + 2 * len(moved)),
        out_specs=(ANY, VMEM),
        scratch_shapes=[
            pltpu.VMEM((all_rows, classes), BF16),
            pltpu.VMEM((LANES, LANES), F32),
            pltpu.VMEM((n, LANES), F32),
            pltpu.VMEM((features // tile, tile, classes), F32),
            pltpu.SemaphoreType.DMA((features // tile,)),
        ],
        compiler_params=params(16),
        cost_estimate=cost(2 * all_rows * features * classes),
        name="finish",
    )(own, every, target, turned, *e_parts, *moved, *inverse)


def exchange(copies):
    return lax.all_to_all(copies, "example", 0, 0)


def body(n, n_cls, features, weights, labels, counts, active):
    rows = features.shape[0]
    all_rows = rows * n
    feature_count, classes = weights.shape
    entries = feature_count * n_cls * classes * n
    weights = pltpu.with_memory_space_constraint(weights, pltpu.HBM)
    slots, waits = gather_blocks(features, n)
    w_low, target, norm = prepare(weights, features, labels, counts, active)
    side = (target, norm, swap(norm, "cls", n_cls, 1))

    groups = [(first, slots[first : first + 2]) for first in range(0, n - 2, 2)]
    groups += [(n - 2, slots[n - 2 : n - 1]), (n - 1, slots[n - 1 :])]
    count = len(groups)
    logits, turned, e_parts, stats = [], [], [], []

    def statistics(g, tokens):
        last = g == count - 1
        other = swap(logits[g], "cls", n_cls, 1)
        e, found, *copies = first_stats(
            logits[g], other, active, groups[g][0], n, tuple(stats[-1:]),
            side if last else (), tokens,
        )
        e_parts.append(e)
        stats.append(found)
        return copies

    behind = max(count - 3, 0)
    for g in range(count):
        if g == count - 1 and behind:
            *logits[behind:], slots[-1] = lax.optimization_barrier(
                (*logits[behind:], slots[-1])
            )
            groups[-1] = (n - 1, slots[n - 1 :])
        tokens = tuple(stats[-1:]) + tuple(turned[-1:]) + tuple(waits[g] if g < n // 2 else ())
        logits.append(arriving_logits(groups[g][1], w_low, tokens))
        if g < n // 2 - 1:
            turned.append(turn(slots[2 * g : 2 * g + 2]))
        if g == 0 and behind:
            logits[0], slots[3] = lax.optimization_barrier((logits[0], slots[3]))
            groups[1] = (2, slots[2:4])
        if g < behind:
            statistics(g, ())
    turned.append(turn(slots[n - 2 :]))
    for g in range(behind, count):
        copies = statistics(g, (logits[-1], turned[-1]))
    own_stats = stats[-1]
    every = exchange(copies[0])
    residual, fisher_weight, damping, target, plain, turned = first_weights(
        own_stats, every, e_parts, slots, turned, entries
    )

    columns = min(512, classes)
    moved, inverse, own, other = [], [], [], []
    for start in range(0, classes, columns):
        a, b, low = update(turned, weights, residual, fisher_weight, damping, start, columns)
        moved.append(a)
        inverse.append(b)
        if start + columns < classes:
            own.append(next_logits(plain, low, 0, all_rows))
            other.append(swap(own[-1], "cls", n_cls, 1))
    half = n // 2
    late = [next_logits(plain, low, first * rows, half * rows) for first in (0, half)]
    late_other = [swap(c, "cls", n_cls, 1) for c in late]
    e_parts, earlier = [], ()
    for first, c, d in zip((0, half), late, late_other):
        offsets = [first * rows] * len(own) + [0]
        e, own_stats, *copies = last_stats(
            own + [c], other + [d], offsets, target, active, first, half * rows, n, earlier
        )
        e_parts.append(e)
        earlier = (own_stats,)
    every = exchange(copies[0])
    out, losses = finish(own_stats, every, target, e_parts, turned, moved, inverse)
    return out, losses.reshape(rows)


def solution(mesh):
    return jax.shard_map(
        functools.partial(body, mesh.shape["example"], mesh.shape["cls"]),
        mesh=mesh,
        in_specs=(
            P(("groups", "example"), "cls"),
            P(("groups", "cls"), "example"),
            P(("groups", "example")),
            P(("groups", "example")),
            P("groups"),
        ),
        out_specs=(P(("groups", "cls"), "example"), P(("groups", "example"))),
        check_vma=False,
    )
```

```python
import functools

import jax
import jax.numpy as jnp
from jax import lax
from jax.experimental import pallas as pl
from jax.experimental.pallas import tpu as pltpu
from jax.sharding import PartitionSpec as P

ITERS = 2
NEGATIVE = -1e30
LEARNING_RATE = 2e-05
DAMPING_SHARE = 0.1
EPSILON = 1e-06

F32 = jnp.float32
BF16 = jnp.bfloat16
VMEM = pl.BlockSpec(memory_space=pltpu.VMEM)
SMEM = pl.BlockSpec(memory_space=pltpu.SMEM)
HBM = pl.BlockSpec(memory_space=pltpu.HBM)
ANY = pl.BlockSpec(memory_space=pl.ANY)
STEP = 64
LANES = 128


def params(mib=10):
    return pltpu.CompilerParams(vmem_limit_bytes=mib << 20)


def cost(flops=0, nbytes=0):
    return pl.CostEstimate(flops=int(flops), bytes_accessed=int(nbytes), transcendentals=0)


def swap(x, axis, n, offset):
    return lax.ppermute(x, axis, [(i, i ^ offset) for i in range(n)])


def gray(v):
    return v ^ (v >> 1)


def block_of(place, slot, n):
    if n != 8:
        return lax.rem(place + n - slot, n)
    z, y = place // 2, place % 2
    return gray((gray(z) + 4 - slot // 2) & 3) * 2 + (y ^ (slot % 2))


def gather_blocks(x, n):
    if n != 8:
        ring = [(i, (i + 1) % n) for i in range(n)]
        slots = [x]
        for _ in range(n - 1):
            slots.append(lax.ppermute(slots[-1], "example", ring))
        return slots, [()] * (n // 2)
    hops = ((0, 1), (1, 3), (3, 2), (2, 0))
    ring = [(a * 2 + y, b * 2 + y) for a, b in hops for y in range(2)]
    slots, held = [], x
    for step in range(4):
        across = swap(held, "example", n, 1)
        if step < 3:
            later = lax.ppermute(held, "example", ring)
            across, later = lax.optimization_barrier((across, later))
        slots += [held, across]
        held = later
    return slots, [(slots[2 * k + 2],) for k in range(3)] + [()]


def prepare_kernel(tile, w_ref, x_ref, labels_ref, counts_ref, active_ref,
                   low_ref, target_ref, norm_ref, held_ref, sems):
    count = w_ref.shape[0] // tile
    copies = [
        pltpu.make_async_copy(
            w_ref.at[k * tile : (k + 1) * tile, :], held_ref.at[k % 4], sems.at[k % 4]
        )
        for k in range(count)
    ]
    for copy in copies[:4]:
        copy.start()
    rows = x_ref.shape[0]
    slot = lax.broadcasted_iota(jnp.int32, (1, rows), 1)
    target = jnp.where(slot < counts_ref[0], labels_ref[...] % active_ref[0], -1)
    target_ref[...] = target.astype(F32)
    squares = (x_ref[...] * x_ref[...]).astype(F32)
    norm = jnp.sum(squares, axis=1, keepdims=True)
    norm_ref[...] = jnp.broadcast_to(norm, (rows, LANES)).T[0:1, :]
    for k in range(count):
        copies[k].wait()
        low_ref[k * tile : (k + 1) * tile, :] = held_ref[k % 4].astype(BF16)
        if k + 4 < count:
            copies[k + 4].start()


def prepare(weights, features, labels, counts, active):
    rows = features.shape[0]
    feature_count, classes = weights.shape
    tile = 256
    line = jax.ShapeDtypeStruct((1, rows), F32)
    return pl.pallas_call(
        functools.partial(prepare_kernel, tile),
        out_shape=(pltpu.VMEM((feature_count, classes), BF16), line, line),
        in_specs=[HBM, VMEM, VMEM, SMEM, SMEM],
        out_specs=(VMEM,) * 3,
        scratch_shapes=[pltpu.VMEM((4, tile, classes), F32), pltpu.SemaphoreType.DMA((4,))],
        compiler_params=params(),
        cost_estimate=cost(1, 1),
        name="prepare",
    )(weights, features, labels.reshape(1, rows), counts, active)


def arriving_kernel(count, pieces, *refs):
    blocks, w_ref, outs = refs[:count], refs[count], refs[-pieces:]
    rows = outs[0].shape[0]
    columns = 256
    for first in range(0, w_ref.shape[1], columns):
        own = slice(first, first + columns)
        done = 0
        for block in blocks:
            found = jnp.dot(block[...], w_ref[:, own], preferred_element_type=F32)
            for k in range(found.shape[0] // rows):
                outs[done][:, own] = found[k * rows : (k + 1) * rows, :]
                done += 1


def arriving_logits(blocks, w_low, tokens):
    pieces = sum(b.shape[0] for b in blocks) // STEP
    return pl.pallas_call(
        functools.partial(arriving_kernel, len(blocks), pieces),
        out_shape=(jax.ShapeDtypeStruct((STEP, w_low.shape[1]), F32),) * pieces,
        in_specs=[VMEM] * (len(blocks) + 1) + [ANY] * len(tokens),
        out_specs=(VMEM,) * pieces,
        compiler_params=params(),
        cost_estimate=cost(1, 1),
        name="arriving_logits",
    )(*blocks, w_low, *tokens)


def turn_kernel(*refs):
    blocks, out_ref = refs[:-1], refs[-1]
    rows = blocks[0].shape[0]
    for k, block in enumerate(blocks):
        out_ref[:, k * rows : (k + 1) * rows] = block[...].T


def turn(blocks):
    rows = sum(b.shape[0] for b in blocks)
    return pl.pallas_call(
        turn_kernel,
        out_shape=pltpu.VMEM((blocks[0].shape[1], rows), BF16),
        in_specs=[VMEM] * len(blocks),
        out_specs=VMEM,
        compiler_params=params(),
        cost_estimate=cost(1, 1),
        name="turn",
    )(*blocks)


def lane_pack(columns, rows):
    lane = lax.broadcasted_iota(jnp.int32, (rows, LANES), 1)
    packed = jnp.zeros((rows, LANES), F32)
    for k, column in enumerate(columns):
        packed = jnp.where(lane == k, column, packed)
    return packed


def put_stats(packed, place, shape):
    lines = packed.T
    line = jnp.concatenate([lines[k : k + 1, :] for k in range(3)], axis=1)
    here = lax.broadcasted_iota(jnp.int32, shape, 0) == place
    return jnp.where(here, line, 0.0)


def first_stats_kernel(slot, pieces, earlier, last, tokens, *refs):
    own, other = refs[:pieces], refs[pieces : 2 * pieces]
    active_ref, refs = refs[2 * pieces], refs[2 * pieces + 1 :]
    lines = refs[: 3 * last]
    older = refs[3 * last : 3 * last + earlier]
    outs = refs[3 * last + earlier + tokens :]
    e_ref, stats_ref, pack_ref = outs[0], outs[1], outs[-1]
    rows, classes = e_ref.shape
    active, place = active_ref[0], lax.axis_index("example")
    class_start = place * classes
    index = class_start + lax.broadcasted_iota(jnp.int32, (1, classes), 1)
    live = index < active
    for k in range(pieces):
        at = slice(k * STEP, (k + 1) * STEP)
        logits = jnp.where(live, own[k][...] + other[k][...], NEGATIVE)
        peak = jnp.max(logits, axis=1, keepdims=True)
        e = jnp.exp(logits - peak)
        e_ref[at, :] = e
        total = jnp.sum(e, axis=1, keepdims=True)
        square = jnp.sum(e * e, axis=1, keepdims=True)
        pack_ref[at, :] = lane_pack((peak, total, square), STEP)
    shape = stats_ref.shape
    n = shape[0]
    stats = older[0][...] if earlier else jnp.zeros(shape, F32)
    for k in range(rows // LANES):
        stats += put_stats(pack_ref[k * LANES : (k + 1) * LANES, :], block_of(place, slot + k, n), shape)
    stats_ref[...] = stats
    if last:
        copies_ref = outs[2]
        target, norm = lines[0][...], lines[1][...] + lines[2][...]
        wide = [jnp.broadcast_to(line, (shape[0], LANES)) for line in (target, norm)]
        full = jnp.concatenate([stats] + wide, axis=1)
        copies_ref[...] = jnp.broadcast_to(full[None], copies_ref.shape)


def first_stats(own, other, active, slot, n, earlier, side, tokens):
    pieces, classes = len(own), own[0].shape[1]
    rows = pieces * STEP
    last = len(side) > 0
    shapes = [jax.ShapeDtypeStruct((rows, classes), F32), jax.ShapeDtypeStruct((n, 3 * LANES), F32)]
    if last:
        shapes.append(jax.ShapeDtypeStruct((n, n, 5 * LANES), F32))
    extra = list(side) + list(earlier)
    return pl.pallas_call(
        functools.partial(
            first_stats_kernel, slot, pieces, len(earlier), last, len(tokens)
        ),
        out_shape=tuple(shapes),
        in_specs=[VMEM] * (2 * pieces) + [SMEM] + [VMEM] * len(extra) + [ANY] * len(tokens),
        out_specs=(VMEM,) * len(shapes),
        scratch_shapes=[pltpu.VMEM((rows, LANES), F32)],
        compiler_params=params(),
        cost_estimate=cost(1, 1),
        name="first_stats",
    )(*own, *other, active, *extra, *tokens)


def combine(own_ref, all_ref):
    n = all_ref.shape[0]
    part = lambda d, k: all_ref[d, :, k * LANES : (k + 1) * LANES]
    peaks = [part(d, 0) for d in range(n)]
    peak = functools.reduce(jnp.maximum, peaks)
    scales = [jnp.exp(p - peak) for p in peaks]
    total = sum(part(d, 1) * scales[d] for d in range(n))
    own_scale = jnp.exp(own_ref[:, 0:LANES] - peak)
    return part, peak, scales, total, own_scale


def to_slots(value, line_ref, place):
    n = value.shape[0]
    line_ref[...] = value
    return jnp.concatenate([line_ref[pl.ds(block_of(place, j, n), 1), :] for j in range(n)], axis=0)


def to_columns(lines):
    stacked = jnp.concatenate(lines, axis=0)
    rest = jnp.zeros((LANES - stacked.shape[0], LANES), F32)
    return jnp.concatenate([stacked, rest], axis=0).T


def first_weights_kernel(entries, parts, blocks, turns, own_ref, all_ref, *refs):
    e_refs = refs[:parts]
    block_refs, turn_refs = refs[parts : parts + blocks], refs[parts + blocks :][:turns]
    refs = refs[parts + blocks + turns :]
    residual_ref, fisher_ref, damping_ref, target_ref, plain_ref, turned_ref = refs[:6]
    column_ref, line_ref, sems = refs[6:]
    copies = []
    for k, ref in enumerate(block_refs):
        at = slice(k * LANES, (k + 1) * LANES)
        copies.append(pltpu.make_async_copy(ref, plain_ref.at[at, :], sems.at[k]))
    for k, ref in enumerate(turn_refs):
        at = slice(k * ref.shape[1], (k + 1) * ref.shape[1])
        copies.append(pltpu.make_async_copy(ref, turned_ref.at[:, at], sems.at[blocks + k]))
    for copy in copies:
        copy.start()
    n = all_ref.shape[0]
    classes = residual_ref.shape[1]
    place = lax.axis_index("example")
    class_start = place * classes
    part, peak, scales, total, own_scale = combine(own_ref, all_ref)
    square = sum(part(d, 2) * (scales[d] * scales[d]) for d in range(n))
    inverse = 1.0 / total
    spread = 1.0 - square * inverse * inverse
    target = jnp.concatenate([all_ref[d, 0:1, 3 * LANES : 4 * LANES] for d in range(n)], axis=0)
    norm = jnp.concatenate([all_ref[d, 0:1, 4 * LANES : 5 * LANES] for d in range(n)], axis=0)
    valid = (target >= 0.0).astype(F32)
    share = valid / jnp.sum(valid)
    fisher_sum = jnp.sum(norm * share * spread)
    damping_ref[...] = jnp.full(
        damping_ref.shape, DAMPING_SHARE * fisher_sum / entries + EPSILON, F32
    )
    factor = to_slots(own_scale * inverse, line_ref, place)
    share = to_slots(share, line_ref, place)
    target = to_slots(target, line_ref, place)
    target_ref[...] = target
    column_ref[...] = to_columns([factor, share, target])
    index = class_start + lax.broadcasted_iota(jnp.int32, (1, classes), 1)
    done = 0
    for e_ref in e_refs:
        for k in range(e_ref.shape[0] // LANES):
            j = done + k

            def step(i, _, j=j, k=k, e_ref=e_ref):
                start = pl.multiple_of(i * STEP, STEP)
                at = pl.ds(pl.multiple_of(j * LANES + start, STEP), STEP)
                column = column_ref[pl.ds(start, STEP), :]
                e = e_ref[pl.ds(pl.multiple_of(k * LANES + start, STEP), STEP), :]
                probability = e * column[:, j : j + 1]
                hit = index == column[:, 2 * n + j : 2 * n + j + 1].astype(jnp.int32)
                part = column[:, n + j : n + j + 1]
                residual_ref[at, :] = (part * (probability - hit.astype(F32))).astype(BF16)
                fisher_ref[at, :] = (part * probability * (1.0 - probability)).astype(BF16)
                return 0

            lax.fori_loop(0, LANES // STEP, step, 0)
        done += e_ref.shape[0] // LANES
    for copy in copies:
        copy.wait()


def first_weights(own, every, e_parts, slots, turned, entries):
    n = own.shape[0]
    classes = e_parts[0].shape[1]
    weight = pltpu.VMEM((n * LANES, classes), BF16)
    return pl.pallas_call(
        functools.partial(
            first_weights_kernel, float(entries), len(e_parts), len(slots), len(turned)
        ),
        out_shape=(
            weight,
            weight,
            jax.ShapeDtypeStruct((8, LANES), F32),
            jax.ShapeDtypeStruct((n, LANES), F32),
            pltpu.VMEM((n * LANES, slots[0].shape[1]), BF16),
            pltpu.VMEM((slots[0].shape[1], n * LANES), BF16),
        ),
        in_specs=[VMEM] * (2 + len(e_parts) + len(slots) + len(turned)),
        out_specs=(VMEM,) * 6,
        scratch_shapes=[
            pltpu.VMEM((LANES, LANES), F32),
            pltpu.VMEM((n, LANES), F32),
            pltpu.SemaphoreType.DMA((len(slots) + len(turned),)),
        ],
        compiler_params=params(),
        cost_estimate=cost(0, 8 * n * LANES * classes),
        name="first_weights",
    )(own, every, *e_parts, *slots, *turned)


def update_kernel(start, tile, turned_ref, w_ref, residual_ref, fisher_ref, damping_ref,
                  moved_ref, inverse_ref, low_ref, held_ref, sems):
    features, columns = moved_ref.shape
    damping = damping_ref[0:1, 0:1]
    own = slice(start, start + columns)
    copies = []
    for k in range(features // tile):
        copies.append(
            pltpu.make_async_copy(
                w_ref.at[k * tile : (k + 1) * tile, own], held_ref.at[k], sems.at[k]
            )
        )
        copies[-1].start()
    for k in range(features // tile):
        at = slice(k * tile, (k + 1) * tile)
        turned = turned_ref[at, :]
        gradient = jnp.dot(turned, residual_ref[:, own], preferred_element_type=F32)
        fisher = jnp.dot(turned * turned, fisher_ref[:, own], preferred_element_type=F32)
        inverse = 1.0 / (fisher + damping)
        change = gradient * inverse
        inverse_ref[at, :] = inverse
        moved_ref[at, :] = -change
        copies[k].wait()
        low_ref[at, :] = (held_ref[k] - LEARNING_RATE * change).astype(BF16)


def update(turned, weights, residual, fisher_weight, damping, start, columns):
    features, rows = turned.shape
    tile = 512
    return pl.pallas_call(
        functools.partial(update_kernel, start, tile),
        out_shape=(
            pltpu.VMEM((features, columns), F32),
            pltpu.VMEM((features, columns), F32),
            pltpu.VMEM((features, columns), BF16),
        ),
        in_specs=[VMEM, HBM] + [VMEM] * 3,
        out_specs=(VMEM, VMEM, VMEM),
        scratch_shapes=[
            pltpu.VMEM((features // tile, tile, columns), F32),
            pltpu.SemaphoreType.DMA((features // tile,)),
        ],
        compiler_params=params(14),
        cost_estimate=cost(4 * rows * features * columns),
        name="update",
    )(turned, weights, residual, fisher_weight, damping)


def next_logits_kernel(start, tile, plain_ref, low_ref, out_ref):
    for first in range(0, out_ref.shape[0], tile):
        out_ref[first : first + tile, :] = jnp.dot(
            plain_ref[start + first : start + first + tile, :],
            low_ref[...],
            preferred_element_type=F32,
        )


def next_logits(plain, low, start, rows):
    features, columns = low.shape
    return pl.pallas_call(
        functools.partial(next_logits_kernel, start, min(512, rows)),
        out_shape=jax.ShapeDtypeStruct((rows, columns), F32),
        in_specs=[VMEM, VMEM],
        out_specs=VMEM,
        compiler_params=params(),
        cost_estimate=cost(2 * rows * features * columns),
        name="next_logits",
    )(plain, low)


def last_stats_kernel(slot, last, pieces, offsets, earlier, *refs):
    own, other = refs[:pieces], refs[pieces : 2 * pieces]
    target_ref, active_ref = refs[2 * pieces : 2 * pieces + 2]
    older = refs[2 * pieces + 2 : 2 * pieces + 2 + earlier]
    outs = refs[2 * pieces + 2 + earlier :]
    e_ref, stats_ref, pack_ref, column_ref = outs[0], outs[1], outs[-2], outs[-1]
    rows, classes = e_ref.shape
    active, place = active_ref[0], lax.axis_index("example")
    class_start = place * classes
    n = stats_ref.shape[0]
    column_ref[...] = to_columns([target_ref[...]])
    index = class_start + lax.broadcasted_iota(jnp.int32, (1, classes), 1)
    live = index < active
    for k in range(rows // LANES):
        def step(i, _, k=k):
            start = pl.multiple_of(i * STEP, STEP)

            def rows_of(base):
                return pl.ds(pl.multiple_of(base + k * LANES + start, STEP), STEP)

            logits = jnp.concatenate(
                [a[rows_of(o), :] + b[rows_of(o), :] for a, b, o in zip(own, other, offsets)],
                axis=1,
            )
            column = column_ref[pl.ds(start, STEP), slot + k : slot + k + 1]
            hit = index == column.astype(jnp.int32)
            label = jnp.sum(jnp.where(hit, logits, 0.0), axis=1, keepdims=True)
            logits = jnp.where(live, logits, NEGATIVE)
            peak = jnp.max(logits, axis=1, keepdims=True)
            e = jnp.exp(logits - peak)
            e_ref[rows_of(0), :] = e
            total = jnp.sum(e, axis=1, keepdims=True)
            pack_ref[rows_of(0), :] = lane_pack((peak, total, label), STEP)
            return 0

        lax.fori_loop(0, LANES // STEP, step, 0)
    shape = stats_ref.shape
    n = shape[0]
    stats = older[0][...] if earlier else jnp.zeros(shape, F32)
    for k in range(rows // LANES):
        stats += put_stats(pack_ref[k * LANES : (k + 1) * LANES, :], block_of(place, slot + k, n), shape)
    stats_ref[...] = stats
    if last:
        outs[2][...] = jnp.broadcast_to(stats[None], outs[2].shape)


def last_stats(own, other, offsets, target, active, slot, rows, n, earlier):
    classes = sum(c.shape[1] for c in own)
    last = slot + rows // LANES == n
    shapes = [
        jax.ShapeDtypeStruct((rows, classes), F32),
        jax.ShapeDtypeStruct((n, 3 * LANES), F32),
    ]
    if last:
        shapes.append(jax.ShapeDtypeStruct((n, n, 3 * LANES), F32))
    return pl.pallas_call(
        functools.partial(
            last_stats_kernel, slot, last, len(own), tuple(offsets), len(earlier)
        ),
        out_shape=tuple(shapes),
        in_specs=[VMEM] * (2 * len(own) + 1) + [SMEM] + [VMEM] * len(earlier),
        out_specs=(VMEM,) * len(shapes),
        scratch_shapes=[pltpu.VMEM((rows, LANES), F32), pltpu.VMEM((LANES, LANES), F32)],
        compiler_params=params(),
        cost_estimate=cost(0, 24 * rows * classes),
        name="last_stats",
    )(*own, *other, target, active, *earlier)


def finish_kernel(chunks, e_parts, tile, own_ref, all_ref, target_ref, turned_ref, *refs):
    e_refs = refs[:e_parts]
    refs = refs[e_parts:]
    moved_refs, inverse_refs = refs[:chunks], refs[chunks : 2 * chunks]
    out_ref, loss_ref, residual_ref, column_ref, line_ref, held_ref, sems = refs[2 * chunks :]
    n = all_ref.shape[0]
    classes = residual_ref.shape[1]
    place = lax.axis_index("example")
    class_start = place * classes
    part, peak, scales, total, own_scale = combine(own_ref, all_ref)
    label = sum(part(d, 2) for d in range(n))
    target = target_ref[...]
    valid = (target >= 0.0).astype(F32)
    share = valid / jnp.sum(valid)
    losses = to_slots(peak + jnp.log(total) - label, line_ref, place)
    loss_ref[...] = (valid * losses)[0:1, :]
    factor = to_slots(own_scale / total, line_ref, place)
    column_ref[...] = to_columns([factor, share, target])
    index = class_start + lax.broadcasted_iota(jnp.int32, (1, classes), 1)
    done = 0
    for e_ref in e_refs:
        for k in range(e_ref.shape[0] // LANES):
            j = done + k

            def step(i, _, j=j, k=k, e_ref=e_ref):
                start = pl.multiple_of(i * STEP, STEP)
                at = pl.ds(pl.multiple_of(j * LANES + start, STEP), STEP)
                column = column_ref[pl.ds(start, STEP), :]
                e = e_ref[pl.ds(pl.multiple_of(k * LANES + start, STEP), STEP), :]
                probability = e * column[:, j : j + 1]
                hit = index == column[:, 2 * n + j : 2 * n + j + 1].astype(jnp.int32)
                part = column[:, n + j : n + j + 1]
                residual_ref[at, :] = (part * (probability - hit.astype(F32))).astype(BF16)
                return 0

            lax.fori_loop(0, LANES // STEP, step, 0)
        done += e_ref.shape[0] // LANES

    copies = []
    for k in range(out_ref.shape[0] // tile):
        at = slice(k * tile, (k + 1) * tile)
        done = 0
        for moved_ref, inverse_ref in zip(moved_refs, inverse_refs):
            own = slice(done, done + moved_ref.shape[1])
            gradient = jnp.dot(
                turned_ref[at, :], residual_ref[:, own], preferred_element_type=F32
            )
            held_ref[k, :, own] = moved_ref[at, :] - gradient * inverse_ref[at, :]
            done += moved_ref.shape[1]
        copies.append(pltpu.make_async_copy(held_ref.at[k], out_ref.at[at, :], sems.at[k]))
        copies[-1].start()
    for copy in copies:
        copy.wait()


def finish(own, every, target, e_parts, turned, moved, inverse):
    n = own.shape[0]
    features, all_rows = turned.shape
    classes = e_parts[0].shape[1]
    tile = 512
    return pl.pallas_call(
        functools.partial(finish_kernel, len(moved), len(e_parts), tile),
        out_shape=(
            jax.ShapeDtypeStruct((features, classes), F32),
            jax.ShapeDtypeStruct((1, LANES), F32),
        ),
        in_specs=[VMEM] * (4 + len(e_parts) + 2 * len(moved)),
        out_specs=(ANY, VMEM),
        scratch_shapes=[
            pltpu.VMEM((all_rows, classes), BF16),
            pltpu.VMEM((LANES, LANES), F32),
            pltpu.VMEM((n, LANES), F32),
            pltpu.VMEM((features // tile, tile, classes), F32),
            pltpu.SemaphoreType.DMA((features // tile,)),
        ],
        compiler_params=params(16),
        cost_estimate=cost(2 * all_rows * features * classes),
        name="finish",
    )(own, every, target, turned, *e_parts, *moved, *inverse)


def exchange(copies):
    return lax.all_to_all(copies, "example", 0, 0)


def body(n, n_cls, features, weights, labels, counts, active):
    rows = features.shape[0]
    all_rows = rows * n
    feature_count, classes = weights.shape
    entries = feature_count * n_cls * classes * n
    weights = pltpu.with_memory_space_constraint(weights, pltpu.HBM)
    slots, waits = gather_blocks(features, n)
    w_low, target, norm = prepare(weights, features, labels, counts, active)
    side = (target, norm, swap(norm, "cls", n_cls, 1))

    groups = [(first, slots[first : first + 2]) for first in range(0, n - 2, 2)]
    groups += [(n - 2, slots[n - 2 : n - 1]), (n - 1, slots[n - 1 :])]
    count = len(groups)
    logits, turned, e_parts, stats = [], [], [], []

    def statistics(g, tokens):
        last = g == count - 1
        other = [swap(piece, "cls", n_cls, 1) for piece in logits[g]]
        e, found, *copies = first_stats(
            logits[g], other, active, groups[g][0], n, tuple(stats[-1:]),
            side if last else (), tokens,
        )
        e_parts.append(e)
        stats.append(found)
        return copies

    behind = max(count - 3, 0)
    for g in range(count):
        if g == count - 1 and behind:
            logits[behind:], slots[-1] = lax.optimization_barrier((logits[behind:], slots[-1]))
            groups[-1] = (n - 1, slots[n - 1 :])
        tokens = tuple(stats[-1:]) + tuple(turned[-1:]) + tuple(waits[g] if g < n // 2 else ())
        logits.append(list(arriving_logits(groups[g][1], w_low, tokens)))
        if g < n // 2 - 1:
            turned.append(turn(slots[2 * g : 2 * g + 2]))
        if g == 0 and behind:
            logits[0], slots[3] = lax.optimization_barrier((logits[0], slots[3]))
            groups[1] = (2, slots[2:4])
        if g < behind:
            statistics(g, ())
    turned.append(turn(slots[n - 2 :]))
    for g in range(behind, count):
        copies = statistics(g, (logits[-1][0], turned[-1]))
    own_stats = stats[-1]
    every = exchange(copies[0])
    residual, fisher_weight, damping, target, plain, turned = first_weights(
        own_stats, every, e_parts, slots, turned, entries
    )

    columns = min(512, classes)
    moved, inverse, own, other = [], [], [], []
    for start in range(0, classes, columns):
        a, b, low = update(turned, weights, residual, fisher_weight, damping, start, columns)
        moved.append(a)
        inverse.append(b)
        if start + columns < classes:
            own.append(next_logits(plain, low, 0, all_rows))
            other.append(swap(own[-1], "cls", n_cls, 1))
    half = n // 2
    late = [next_logits(plain, low, first * rows, half * rows) for first in (0, half)]
    late_other = [swap(c, "cls", n_cls, 1) for c in late]
    e_parts, earlier = [], ()
    for first, c, d in zip((0, half), late, late_other):
        offsets = [first * rows] * len(own) + [0]
        e, own_stats, *copies = last_stats(
            own + [c], other + [d], offsets, target, active, first, half * rows, n, earlier
        )
        e_parts.append(e)
        earlier = (own_stats,)
    every = exchange(copies[0])
    out, losses = finish(own_stats, every, target, e_parts, turned, moved, inverse)
    return out, losses.reshape(rows)


def solution(mesh):
    return jax.shard_map(
        functools.partial(body, mesh.shape["example"], mesh.shape["cls"]),
        mesh=mesh,
        in_specs=(
            P(("groups", "example"), "cls"),
            P(("groups", "cls"), "example"),
            P(("groups", "example")),
            P(("groups", "example")),
            P("groups"),
        ),
        out_specs=(P(("groups", "cls"), "example"), P(("groups", "example"))),
        check_vma=False,
    )
```

```python
import functools

import jax
import jax.numpy as jnp
from jax import lax
from jax.experimental import pallas as pl
from jax.experimental.pallas import tpu as pltpu
from jax.sharding import PartitionSpec as P

ITERS = 2
NEGATIVE = -1e30
LEARNING_RATE = 2e-05
DAMPING_SHARE = 0.1
EPSILON = 1e-06

F32 = jnp.float32
BF16 = jnp.bfloat16
VMEM = pl.BlockSpec(memory_space=pltpu.VMEM)
SMEM = pl.BlockSpec(memory_space=pltpu.SMEM)
HBM = pl.BlockSpec(memory_space=pltpu.HBM)
ANY = pl.BlockSpec(memory_space=pl.ANY)
STEP = 64
LANES = 128


def params(mib=10):
    return pltpu.CompilerParams(vmem_limit_bytes=mib << 20)


def cost(flops=0, nbytes=0):
    return pl.CostEstimate(flops=int(flops), bytes_accessed=int(nbytes), transcendentals=0)


def swap(x, axis, n, offset):
    return lax.ppermute(x, axis, [(i, i ^ offset) for i in range(n)])


def gray(v):
    return v ^ (v >> 1)


def block_of(place, slot, n):
    if n != 8:
        return lax.rem(place + n - slot, n)
    z, y = place // 2, place % 2
    return gray((gray(z) + 4 - slot // 2) & 3) * 2 + (y ^ (slot % 2))


def halves_kernel(first_ref, second_ref, upper_ref, lower_ref):
    rows = upper_ref.shape[0]
    upper_ref[...] = first_ref[0:rows, :]
    lower_ref[...] = second_ref[rows : 2 * rows, :]


def halves(first, second):
    half = pltpu.VMEM((first.shape[0] // 2, first.shape[1]), first.dtype)
    return pl.pallas_call(
        halves_kernel,
        out_shape=(half, half),
        in_specs=[VMEM, VMEM],
        out_specs=(VMEM, VMEM),
        compiler_params=params(),
        cost_estimate=cost(1, 1),
        name="halves",
    )(first, second)


def gather_blocks(x, n, early):
    if n != 8:
        ring = [(i, (i + 1) % n) for i in range(n)]
        slots = [x]
        for _ in range(n - 1):
            slots.append(lax.ppermute(slots[-1], "example", ring))
        return [[slot] for slot in slots], [()] * (n // 2), early
    hops = ((0, 1), (1, 3), (3, 2), (2, 0))
    ring = [(a * 2 + y, b * 2 + y) for a, b in hops for y in range(2)]
    slots, held = [], x
    for step in range(3):
        across = swap(held, "example", n, 1)
        later = lax.ppermute(held, "example", ring)
        if step == 0:
            across, later, early = lax.optimization_barrier((across, later, early))
        else:
            across, later = lax.optimization_barrier((across, later))
        slots += [[held], [across]]
        held = later
    upper, lower = halves(held, across)
    last = [swap(upper, "example", n, 1), lax.ppermute(lower, "example", ring)]
    slots += [[held], last]
    return slots, [tuple(slots[2 * k + 2]) for k in range(3)] + [()], early


def prepare_kernel(tile, w_ref, x_ref, labels_ref, counts_ref, active_ref,
                   low_ref, target_ref, norm_ref, held_ref, block_ref, label_ref, sems):
    count, depth = w_ref.shape[0] // tile, held_ref.shape[0]
    first = [
        pltpu.make_async_copy(x_ref, block_ref, sems.at[depth]),
        pltpu.make_async_copy(labels_ref, label_ref, sems.at[depth + 1]),
    ]
    copies = [
        pltpu.make_async_copy(
            w_ref.at[k * tile : (k + 1) * tile, :], held_ref.at[k % depth], sems.at[k % depth]
        )
        for k in range(count)
    ]
    for copy in first + copies[:depth]:
        copy.start()
    for copy in first:
        copy.wait()
    rows = x_ref.shape[0]
    slot = lax.broadcasted_iota(jnp.int32, (1, rows), 1)
    target = jnp.where(slot < counts_ref[0], label_ref[...] % active_ref[0], -1)
    target_ref[...] = target.astype(F32)
    squares = (block_ref[...] * block_ref[...]).astype(F32)
    norm = jnp.sum(squares, axis=1, keepdims=True)
    norm_ref[...] = jnp.broadcast_to(norm, (rows, LANES)).T[0:1, :]
    for k in range(count):
        copies[k].wait()
        low_ref[k * tile : (k + 1) * tile, :] = held_ref[k % depth].astype(BF16)
        if k + depth < count:
            copies[k + depth].start()


def prepare(weights, features, labels, counts, active):
    rows = features.shape[0]
    feature_count, classes = weights.shape
    tile, depth = 256, 6
    line = jax.ShapeDtypeStruct((1, rows), F32)
    return pl.pallas_call(
        functools.partial(prepare_kernel, tile),
        out_shape=(pltpu.VMEM((feature_count, classes), BF16), line, line),
        in_specs=[HBM, HBM, HBM, SMEM, SMEM],
        out_specs=(VMEM,) * 3,
        scratch_shapes=[
            pltpu.VMEM((depth, tile, classes), F32),
            pltpu.VMEM(features.shape, BF16),
            pltpu.VMEM((1, rows), jnp.int32),
            pltpu.SemaphoreType.DMA((depth + 2,)),
        ],
        compiler_params=params(12),
        cost_estimate=cost(1, 1),
        name="prepare",
    )(
        weights,
        pltpu.with_memory_space_constraint(features, pltpu.HBM),
        pltpu.with_memory_space_constraint(labels.reshape(1, rows), pltpu.HBM),
        counts,
        active,
    )


def arriving_kernel(count, pieces, *refs):
    parts, w_ref = refs[:count], refs[count]
    plain_ref, outs = refs[-pieces - 1], refs[-pieces:]
    done = 0
    for part in parts:
        plain_ref[done : done + part.shape[0], :] = part[...]
        done += part.shape[0]
    columns = 256
    for first in range(0, w_ref.shape[1], columns):
        own = slice(first, first + columns)
        found = jnp.dot(plain_ref[...], w_ref[:, own], preferred_element_type=F32)
        for k, out in enumerate(outs):
            out[:, own] = found[k * STEP : (k + 1) * STEP, :]


def arriving_logits(parts, w_low, tokens):
    rows = sum(p.shape[0] for p in parts)
    pieces = rows // STEP
    plain, *logits = pl.pallas_call(
        functools.partial(arriving_kernel, len(parts), pieces),
        out_shape=(pltpu.VMEM((rows, w_low.shape[0]), BF16),)
        + (jax.ShapeDtypeStruct((STEP, w_low.shape[1]), F32),) * pieces,
        in_specs=[VMEM] * (len(parts) + 1) + [ANY] * len(tokens),
        out_specs=(VMEM,) * (pieces + 1),
        compiler_params=params(),
        cost_estimate=cost(1, 1),
        name="arriving_logits",
    )(*parts, w_low, *tokens)
    return plain, logits


def turn_kernel(*refs):
    blocks, out_ref = refs[:-1], refs[-1]
    done = 0
    for block in blocks:
        out_ref[:, done : done + block.shape[0]] = block[...].T
        done += block.shape[0]


def turn(blocks):
    rows = sum(b.shape[0] for b in blocks)
    return pl.pallas_call(
        turn_kernel,
        out_shape=pltpu.VMEM((blocks[0].shape[1], rows), BF16),
        in_specs=[VMEM] * len(blocks),
        out_specs=VMEM,
        compiler_params=params(),
        cost_estimate=cost(1, 1),
        name="turn",
    )(*blocks)


def lane_pack(columns, rows):
    lane = lax.broadcasted_iota(jnp.int32, (rows, LANES), 1)
    packed = jnp.zeros((rows, LANES), F32)
    for k, column in enumerate(columns):
        packed = jnp.where(lane == k, column, packed)
    return packed


def put_stats(packed, place, shape):
    lines = packed.T
    line = jnp.concatenate([lines[k : k + 1, :] for k in range(3)], axis=1)
    here = lax.broadcasted_iota(jnp.int32, shape, 0) == place
    return jnp.where(here, line, 0.0)


def first_stats_kernel(slot, pieces, earlier, last, tokens, *refs):
    own, other = refs[:pieces], refs[pieces : 2 * pieces]
    active_ref, refs = refs[2 * pieces], refs[2 * pieces + 1 :]
    lines = refs[: 3 * last]
    older = refs[3 * last : 3 * last + earlier]
    outs = refs[3 * last + earlier + tokens :]
    e_ref, stats_ref, pack_ref = outs[0], outs[1], outs[-1]
    rows, classes = e_ref.shape
    active, place = active_ref[0], lax.axis_index("example")
    class_start = place * classes
    index = class_start + lax.broadcasted_iota(jnp.int32, (1, classes), 1)
    live = index < active
    for k in range(pieces):
        at = slice(k * STEP, (k + 1) * STEP)
        logits = jnp.where(live, own[k][...] + other[k][...], NEGATIVE)
        peak = jnp.max(logits, axis=1, keepdims=True)
        e = jnp.exp(logits - peak)
        e_ref[at, :] = e
        total = jnp.sum(e, axis=1, keepdims=True)
        square = jnp.sum(e * e, axis=1, keepdims=True)
        pack_ref[at, :] = lane_pack((peak, total, square), STEP)
    shape = stats_ref.shape
    n = shape[0]
    stats = older[0][...] if earlier else jnp.zeros(shape, F32)
    for k in range(rows // LANES):
        stats += put_stats(pack_ref[k * LANES : (k + 1) * LANES, :], block_of(place, slot + k, n), shape)
    stats_ref[...] = stats
    if last:
        copies_ref = outs[2]
        target, norm = lines[0][...], lines[1][...] + lines[2][...]
        wide = [jnp.broadcast_to(line, (shape[0], LANES)) for line in (target, norm)]
        full = jnp.concatenate([stats] + wide, axis=1)
        copies_ref[...] = jnp.broadcast_to(full[None], copies_ref.shape)


def first_stats(own, other, active, slot, n, earlier, side, tokens):
    pieces, classes = len(own), own[0].shape[1]
    rows = pieces * STEP
    last = len(side) > 0
    shapes = [jax.ShapeDtypeStruct((rows, classes), F32), jax.ShapeDtypeStruct((n, 3 * LANES), F32)]
    if last:
        shapes.append(jax.ShapeDtypeStruct((n, n, 5 * LANES), F32))
    extra = list(side) + list(earlier)
    return pl.pallas_call(
        functools.partial(
            first_stats_kernel, slot, pieces, len(earlier), last, len(tokens)
        ),
        out_shape=tuple(shapes),
        in_specs=[VMEM] * (2 * pieces) + [SMEM] + [VMEM] * len(extra) + [ANY] * len(tokens),
        out_specs=(VMEM,) * len(shapes),
        scratch_shapes=[pltpu.VMEM((rows, LANES), F32)],
        compiler_params=params(),
        cost_estimate=cost(1, 1),
        name="first_stats",
    )(*own, *other, active, *extra, *tokens)


def combine(own_ref, all_ref):
    n = all_ref.shape[0]
    part = lambda d, k: all_ref[d, :, k * LANES : (k + 1) * LANES]
    peaks = [part(d, 0) for d in range(n)]
    peak = functools.reduce(jnp.maximum, peaks)
    scales = [jnp.exp(p - peak) for p in peaks]
    total = sum(part(d, 1) * scales[d] for d in range(n))
    own_scale = jnp.exp(own_ref[:, 0:LANES] - peak)
    return part, peak, scales, total, own_scale


def to_slots(value, line_ref, place):
    n = value.shape[0]
    line_ref[...] = value
    return jnp.concatenate([line_ref[pl.ds(block_of(place, j, n), 1), :] for j in range(n)], axis=0)


def to_columns(lines):
    stacked = jnp.concatenate(lines, axis=0)
    rest = jnp.zeros((LANES - stacked.shape[0], LANES), F32)
    return jnp.concatenate([stacked, rest], axis=0).T


def first_weights_kernel(entries, parts, blocks, turns, own_ref, all_ref, *refs):
    e_refs = refs[:parts]
    block_refs, turn_refs = refs[parts : parts + blocks], refs[parts + blocks :][:turns]
    refs = refs[parts + blocks + turns :]
    residual_ref, fisher_ref, damping_ref, target_ref, plain_ref, turned_ref = refs[:6]
    column_ref, line_ref, sems = refs[6:]
    copies = []
    done = 0
    for k, ref in enumerate(block_refs):
        at = slice(done, done + ref.shape[0])
        copies.append(pltpu.make_async_copy(ref, plain_ref.at[at, :], sems.at[k]))
        done += ref.shape[0]
    for k, ref in enumerate(turn_refs):
        at = slice(k * ref.shape[1], (k + 1) * ref.shape[1])
        copies.append(pltpu.make_async_copy(ref, turned_ref.at[:, at], sems.at[blocks + k]))
    for copy in copies:
        copy.start()
    n = all_ref.shape[0]
    classes = residual_ref.shape[1]
    place = lax.axis_index("example")
    class_start = place * classes
    part, peak, scales, total, own_scale = combine(own_ref, all_ref)
    square = sum(part(d, 2) * (scales[d] * scales[d]) for d in range(n))
    inverse = 1.0 / total
    spread = 1.0 - square * inverse * inverse
    target = jnp.concatenate([all_ref[d, 0:1, 3 * LANES : 4 * LANES] for d in range(n)], axis=0)
    norm = jnp.concatenate([all_ref[d, 0:1, 4 * LANES : 5 * LANES] for d in range(n)], axis=0)
    valid = (target >= 0.0).astype(F32)
    share = valid / jnp.sum(valid)
    fisher_sum = jnp.sum(norm * share * spread)
    damping_ref[...] = jnp.full(
        damping_ref.shape, DAMPING_SHARE * fisher_sum / entries + EPSILON, F32
    )
    factor = to_slots(own_scale * inverse, line_ref, place)
    share = to_slots(share, line_ref, place)
    target = to_slots(target, line_ref, place)
    target_ref[...] = target
    column_ref[...] = to_columns([factor, share, target])
    index = class_start + lax.broadcasted_iota(jnp.int32, (1, classes), 1)
    done = 0
    for e_ref in e_refs:
        for k in range(e_ref.shape[0] // LANES):
            j = done + k

            def step(i, _, j=j, k=k, e_ref=e_ref):
                start = i * STEP
                at = pl.ds(j * LANES + start, STEP)
                column = column_ref[pl.ds(start, STEP), :]
                e = e_ref[pl.ds(k * LANES + start, STEP), :]
                probability = e * column[:, j : j + 1]
                hit = index == column[:, 2 * n + j : 2 * n + j + 1].astype(jnp.int32)
                part = column[:, n + j : n + j + 1]
                residual_ref[at, :] = (part * (probability - hit.astype(F32))).astype(BF16)
                fisher_ref[at, :] = (part * probability * (1.0 - probability)).astype(BF16)
                return 0

            for i in range(LANES // STEP):
                step(i, 0)
        done += e_ref.shape[0] // LANES
    for copy in copies:
        copy.wait()


def first_weights(own, every, e_parts, slots, turned, entries):
    n = own.shape[0]
    classes = e_parts[0].shape[1]
    weight = pltpu.VMEM((n * LANES, classes), BF16)
    return pl.pallas_call(
        functools.partial(
            first_weights_kernel, float(entries), len(e_parts), len(slots), len(turned)
        ),
        out_shape=(
            weight,
            weight,
            jax.ShapeDtypeStruct((8, LANES), F32),
            jax.ShapeDtypeStruct((n, LANES), F32),
            pltpu.VMEM((n * LANES, slots[0].shape[1]), BF16),
            pltpu.VMEM((slots[0].shape[1], n * LANES), BF16),
        ),
        in_specs=[VMEM] * (2 + len(e_parts) + len(slots) + len(turned)),
        out_specs=(VMEM,) * 6,
        scratch_shapes=[
            pltpu.VMEM((LANES, LANES), F32),
            pltpu.VMEM((n, LANES), F32),
            pltpu.SemaphoreType.DMA((len(slots) + len(turned),)),
        ],
        compiler_params=params(),
        cost_estimate=cost(0, 8 * n * LANES * classes),
        name="first_weights",
    )(own, every, *e_parts, *slots, *turned)


def update_kernel(start, tile, turned_ref, w_ref, residual_ref, fisher_ref, damping_ref,
                  moved_ref, inverse_ref, low_ref, held_ref, sems):
    features, columns = moved_ref.shape
    damping = damping_ref[0:1, 0:1]
    own = slice(start, start + columns)
    copies = []
    for k in range(features // tile):
        copies.append(
            pltpu.make_async_copy(
                w_ref.at[k * tile : (k + 1) * tile, own], held_ref.at[k], sems.at[k]
            )
        )
        copies[-1].start()
    for k in range(features // tile):
        at = slice(k * tile, (k + 1) * tile)
        turned = turned_ref[at, :]
        gradient = jnp.dot(turned, residual_ref[:, own], preferred_element_type=F32)
        fisher = jnp.dot(turned * turned, fisher_ref[:, own], preferred_element_type=F32)
        inverse = 1.0 / (fisher + damping)
        change = gradient * inverse
        inverse_ref[at, :] = inverse
        moved_ref[at, :] = -change
        copies[k].wait()
        low_ref[at, :] = (held_ref[k] - LEARNING_RATE * change).astype(BF16)


def update(turned, weights, residual, fisher_weight, damping, start, columns):
    features, rows = turned.shape
    tile = 512
    return pl.pallas_call(
        functools.partial(update_kernel, start, tile),
        out_shape=(
            pltpu.VMEM((features, columns), F32),
            pltpu.VMEM((features, columns), F32),
            pltpu.VMEM((features, columns), BF16),
        ),
        in_specs=[VMEM, HBM] + [VMEM] * 3,
        out_specs=(VMEM, VMEM, VMEM),
        scratch_shapes=[
            pltpu.VMEM((features // tile, tile, columns), F32),
            pltpu.SemaphoreType.DMA((features // tile,)),
        ],
        compiler_params=params(14),
        cost_estimate=cost(4 * rows * features * columns),
        name="update",
    )(turned, weights, residual, fisher_weight, damping)


def next_logits_kernel(start, tile, plain_ref, low_ref, out_ref):
    for first in range(0, out_ref.shape[0], tile):
        out_ref[first : first + tile, :] = jnp.dot(
            plain_ref[start + first : start + first + tile, :],
            low_ref[...],
            preferred_element_type=F32,
        )


def next_logits(plain, low, start, rows):
    features, columns = low.shape
    return pl.pallas_call(
        functools.partial(next_logits_kernel, start, min(512, rows)),
        out_shape=jax.ShapeDtypeStruct((rows, columns), F32),
        in_specs=[VMEM, VMEM],
        out_specs=VMEM,
        compiler_params=params(),
        cost_estimate=cost(2 * rows * features * columns),
        name="next_logits",
    )(plain, low)


def last_stats_kernel(slot, last, pieces, offsets, earlier, *refs):
    own, other = refs[:pieces], refs[pieces : 2 * pieces]
    target_ref, active_ref = refs[2 * pieces : 2 * pieces + 2]
    older = refs[2 * pieces + 2 : 2 * pieces + 2 + earlier]
    outs = refs[2 * pieces + 2 + earlier :]
    e_ref, stats_ref, pack_ref, column_ref = outs[0], outs[1], outs[-2], outs[-1]
    rows, classes = e_ref.shape
    active, place = active_ref[0], lax.axis_index("example")
    class_start = place * classes
    n = stats_ref.shape[0]
    column_ref[...] = to_columns([target_ref[...]])
    index = class_start + lax.broadcasted_iota(jnp.int32, (1, classes), 1)
    live = index < active
    for k in range(rows // LANES):
        def step(i, _, k=k):
            start = i * STEP

            def rows_of(base):
                return pl.ds(base + k * LANES + start, STEP)

            logits = jnp.concatenate(
                [a[rows_of(o), :] + b[rows_of(o), :] for a, b, o in zip(own, other, offsets)],
                axis=1,
            )
            column = column_ref[pl.ds(start, STEP), slot + k : slot + k + 1]
            hit = index == column.astype(jnp.int32)
            label = jnp.sum(jnp.where(hit, logits, 0.0), axis=1, keepdims=True)
            logits = jnp.where(live, logits, NEGATIVE)
            peak = jnp.max(logits, axis=1, keepdims=True)
            e = jnp.exp(logits - peak)
            e_ref[rows_of(0), :] = e
            total = jnp.sum(e, axis=1, keepdims=True)
            pack_ref[rows_of(0), :] = lane_pack((peak, total, label), STEP)
            return 0

        for i in range(LANES // STEP):
            step(i, 0)
    shape = stats_ref.shape
    n = shape[0]
    stats = older[0][...] if earlier else jnp.zeros(shape, F32)
    for k in range(rows // LANES):
        stats += put_stats(pack_ref[k * LANES : (k + 1) * LANES, :], block_of(place, slot + k, n), shape)
    stats_ref[...] = stats
    if last:
        outs[2][...] = jnp.broadcast_to(stats[None], outs[2].shape)


def last_stats(own, other, offsets, target, active, slot, rows, n, earlier):
    classes = sum(c.shape[1] for c in own)
    last = slot + rows // LANES == n
    shapes = [
        jax.ShapeDtypeStruct((rows, classes), F32),
        jax.ShapeDtypeStruct((n, 3 * LANES), F32),
    ]
    if last:
        shapes.append(jax.ShapeDtypeStruct((n, n, 3 * LANES), F32))
    return pl.pallas_call(
        functools.partial(
            last_stats_kernel, slot, last, len(own), tuple(offsets), len(earlier)
        ),
        out_shape=tuple(shapes),
        in_specs=[VMEM] * (2 * len(own) + 1) + [SMEM] + [VMEM] * len(earlier),
        out_specs=(VMEM,) * len(shapes),
        scratch_shapes=[pltpu.VMEM((rows, LANES), F32), pltpu.VMEM((LANES, LANES), F32)],
        compiler_params=params(),
        cost_estimate=cost(0, 24 * rows * classes),
        name="last_stats",
    )(*own, *other, target, active, *earlier)


def finish_kernel(chunks, e_parts, tile, own_ref, all_ref, target_ref, turned_ref, *refs):
    e_refs = refs[:e_parts]
    refs = refs[e_parts:]
    moved_refs, inverse_refs = refs[:chunks], refs[chunks : 2 * chunks]
    out_ref, loss_ref, residual_ref, column_ref, line_ref, held_ref, sems = refs[2 * chunks :]
    n = all_ref.shape[0]
    classes = residual_ref.shape[1]
    place = lax.axis_index("example")
    class_start = place * classes
    part, peak, scales, total, own_scale = combine(own_ref, all_ref)
    label = sum(part(d, 2) for d in range(n))
    target = target_ref[...]
    valid = (target >= 0.0).astype(F32)
    share = valid / jnp.sum(valid)
    losses = to_slots(peak + jnp.log(total) - label, line_ref, place)
    loss_ref[...] = (valid * losses)[0:1, :]
    factor = to_slots(own_scale / total, line_ref, place)
    column_ref[...] = to_columns([factor, share, target])
    index = class_start + lax.broadcasted_iota(jnp.int32, (1, classes), 1)
    done = 0
    for e_ref in e_refs:
        for k in range(e_ref.shape[0] // LANES):
            j = done + k

            def step(i, _, j=j, k=k, e_ref=e_ref):
                start = i * STEP
                at = pl.ds(j * LANES + start, STEP)
                column = column_ref[pl.ds(start, STEP), :]
                e = e_ref[pl.ds(k * LANES + start, STEP), :]
                probability = e * column[:, j : j + 1]
                hit = index == column[:, 2 * n + j : 2 * n + j + 1].astype(jnp.int32)
                part = column[:, n + j : n + j + 1]
                residual_ref[at, :] = (part * (probability - hit.astype(F32))).astype(BF16)
                return 0

            for i in range(LANES // STEP):
                step(i, 0)
        done += e_ref.shape[0] // LANES

    copies = []
    for k in range(out_ref.shape[0] // tile):
        at = slice(k * tile, (k + 1) * tile)
        done = 0
        for moved_ref, inverse_ref in zip(moved_refs, inverse_refs):
            own = slice(done, done + moved_ref.shape[1])
            gradient = jnp.dot(
                turned_ref[at, :], residual_ref[:, own], preferred_element_type=F32
            )
            held_ref[k, :, own] = moved_ref[at, :] - gradient * inverse_ref[at, :]
            done += moved_ref.shape[1]
        copies.append(pltpu.make_async_copy(held_ref.at[k], out_ref.at[at, :], sems.at[k]))
        copies[-1].start()
    for copy in copies:
        copy.wait()


def finish(own, every, target, e_parts, turned, moved, inverse):
    n = own.shape[0]
    features, all_rows = turned.shape
    classes = e_parts[0].shape[1]
    tile = 512
    return pl.pallas_call(
        functools.partial(finish_kernel, len(moved), len(e_parts), tile),
        out_shape=(
            jax.ShapeDtypeStruct((features, classes), F32),
            jax.ShapeDtypeStruct((1, LANES), F32),
        ),
        in_specs=[VMEM] * (4 + len(e_parts) + 2 * len(moved)),
        out_specs=(ANY, VMEM),
        scratch_shapes=[
            pltpu.VMEM((all_rows, classes), BF16),
            pltpu.VMEM((LANES, LANES), F32),
            pltpu.VMEM((n, LANES), F32),
            pltpu.VMEM((features // tile, tile, classes), F32),
            pltpu.SemaphoreType.DMA((features // tile,)),
        ],
        compiler_params=params(16),
        cost_estimate=cost(2 * all_rows * features * classes),
        name="finish",
    )(own, every, target, turned, *e_parts, *moved, *inverse)


def exchange(copies):
    return lax.all_to_all(copies, "example", 0, 0)


def body(n, n_cls, features, weights, labels, counts, active):
    rows = features.shape[0]
    all_rows = rows * n
    feature_count, classes = weights.shape
    entries = feature_count * n_cls * classes * n
    weights = pltpu.with_memory_space_constraint(weights, pltpu.HBM)
    w_low, target, norm = prepare(weights, features, labels, counts, active)
    slots, waits, w_low = gather_blocks(features, n, w_low)
    side = (target, norm, swap(norm, "cls", n_cls, 1))

    groups = [[k, k + 1] for k in range(0, n - 2, 2)] + [[n - 2], [n - 1]]
    count = len(groups)
    behind = max(count - 3, 0)
    plain, logits, turned, e_parts, stats = [], [], [], [], []

    def statistics(g, tokens):
        last = g == count - 1
        other = [swap(piece, "cls", n_cls, 1) for piece in logits[g]]
        e, found, *copies = first_stats(
            logits[g], other, active, groups[g][0], n, tuple(stats[-1:]),
            side if last else (), tokens,
        )
        e_parts.append(e)
        stats.append(found)
        return copies

    for g in range(count):
        if g == count - 1 and behind:
            logits[behind:], slots[-1][-1] = lax.optimization_barrier(
                (logits[behind:], slots[-1][-1])
            )
        parts = [part for slot in groups[g] for part in slots[slot]]
        tokens = tuple(stats[-1:]) + tuple(turned[-1:]) + tuple(waits[g] if g < n // 2 else ())
        block, found = arriving_logits(parts, w_low, tokens)
        plain.append(block)
        logits.append(found)
        if g < n // 2 - 1:
            turned.append(turn([block]))
        if g < behind:
            logits[g], slots[2 * g + 3][-1] = lax.optimization_barrier(
                (logits[g], slots[2 * g + 3][-1])
            )
            statistics(g, ())
    turned.append(turn(plain[-2:]))
    for g in range(behind, count):
        copies = statistics(g, (logits[-1][0], turned[-1]))
    own_stats = stats[-1]
    every = exchange(copies[0])
    residual, fisher_weight, damping, target, plain, turned = first_weights(
        own_stats, every, e_parts, plain, turned, entries
    )

    columns = min(512, classes)
    moved, inverse, own, other = [], [], [], []
    for start in range(0, classes, columns):
        a, b, low = update(turned, weights, residual, fisher_weight, damping, start, columns)
        moved.append(a)
        inverse.append(b)
        if start + columns < classes:
            own.append(next_logits(plain, low, 0, all_rows))
            other.append(swap(own[-1], "cls", n_cls, 1))
    half = n // 2
    late = [next_logits(plain, low, first * rows, half * rows) for first in (0, half)]
    late_other = [swap(c, "cls", n_cls, 1) for c in late]
    e_parts, earlier = [], ()
    for first, c, d in zip((0, half), late, late_other):
        offsets = [first * rows] * len(own) + [0]
        e, own_stats, *copies = last_stats(
            own + [c], other + [d], offsets, target, active, first, half * rows, n, earlier
        )
        e_parts.append(e)
        earlier = (own_stats,)
    every = exchange(copies[0])
    out, losses = finish(own_stats, every, target, e_parts, turned, moved, inverse)
    return out, losses.reshape(rows)


def solution(mesh):
    return jax.shard_map(
        functools.partial(body, mesh.shape["example"], mesh.shape["cls"]),
        mesh=mesh,
        in_specs=(
            P(("groups", "example"), "cls"),
            P(("groups", "cls"), "example"),
            P(("groups", "example")),
            P(("groups", "example")),
            P("groups"),
        ),
        out_specs=(P(("groups", "cls"), "example"), P(("groups", "example"))),
        check_vma=False,
    )
```

```python
import functools

import jax
import jax.numpy as jnp
from jax import lax
from jax.experimental import pallas as pl
from jax.experimental.pallas import tpu as pltpu
from jax.sharding import PartitionSpec as P

ITERS = 2
NEGATIVE = -1e30
LEARNING_RATE = 2e-05
DAMPING_SHARE = 0.1
EPSILON = 1e-06

F32 = jnp.float32
BF16 = jnp.bfloat16
VMEM = pl.BlockSpec(memory_space=pltpu.VMEM)
SMEM = pl.BlockSpec(memory_space=pltpu.SMEM)
HBM = pl.BlockSpec(memory_space=pltpu.HBM)
ANY = pl.BlockSpec(memory_space=pl.ANY)
STEP = 64
LANES = 128


def params(mib=10):
    return pltpu.CompilerParams(vmem_limit_bytes=mib << 20)


def cost(flops=0, nbytes=0):
    return pl.CostEstimate(flops=int(flops), bytes_accessed=int(nbytes), transcendentals=0)


def swap(x, axis, n, offset):
    return lax.ppermute(x, axis, [(i, i ^ offset) for i in range(n)])


def gray(v):
    return v ^ (v >> 1)


def block_of(place, slot, n):
    if n != 8:
        return lax.rem(place + n - slot, n)
    z, y = place // 2, place % 2
    return gray((gray(z) + 4 - slot // 2) & 3) * 2 + (y ^ (slot % 2))


def halves_kernel(first_ref, second_ref, upper_ref, lower_ref):
    rows = upper_ref.shape[0]
    upper_ref[...] = first_ref[0:rows, :]
    lower_ref[...] = second_ref[rows : 2 * rows, :]


def halves(first, second):
    half = pltpu.VMEM((first.shape[0] // 2, first.shape[1]), first.dtype)
    return pl.pallas_call(
        halves_kernel,
        out_shape=(half, half),
        in_specs=[VMEM, VMEM],
        out_specs=(VMEM, VMEM),
        compiler_params=params(),
        cost_estimate=cost(1, 1),
        name="halves",
    )(first, second)


def gather_blocks(x, n, early):
    if n != 8:
        ring = [(i, (i + 1) % n) for i in range(n)]
        slots = [x]
        for _ in range(n - 1):
            slots.append(lax.ppermute(slots[-1], "example", ring))
        return [[slot] for slot in slots], [()] * (n // 2), early
    hops = ((0, 1), (1, 3), (3, 2), (2, 0))
    ring = [(a * 2 + y, b * 2 + y) for a, b in hops for y in range(2)]
    slots, held = [], x
    for step in range(3):
        across = swap(held, "example", n, 1)
        later = lax.ppermute(held, "example", ring)
        if step == 0:
            across, later, early = lax.optimization_barrier((across, later, early))
        else:
            across, later = lax.optimization_barrier((across, later))
        slots += [[held], [across]]
        held = later
    upper, lower = halves(held, across)
    last = [swap(upper, "example", n, 1), lax.ppermute(lower, "example", ring)]
    slots += [[held], last]
    return slots, [tuple(slots[2 * k + 2]) for k in range(3)] + [()], early


def prepare_kernel(tile, w_ref, x_ref, labels_ref, counts_ref, active_ref,
                   low_ref, target_ref, norm_ref, held_ref, block_ref, label_ref, sems):
    count, depth = w_ref.shape[0] // tile, held_ref.shape[0]
    first = [
        pltpu.make_async_copy(x_ref, block_ref, sems.at[depth]),
        pltpu.make_async_copy(labels_ref, label_ref, sems.at[depth + 1]),
    ]
    copies = [
        pltpu.make_async_copy(
            w_ref.at[k * tile : (k + 1) * tile, :], held_ref.at[k % depth], sems.at[k % depth]
        )
        for k in range(count)
    ]
    for copy in first + copies[:depth]:
        copy.start()
    for copy in first:
        copy.wait()
    rows = x_ref.shape[0]
    slot = lax.broadcasted_iota(jnp.int32, (1, rows), 1)
    target = jnp.where(slot < counts_ref[0], label_ref[...] % active_ref[0], -1)
    target_ref[...] = target.astype(F32)
    squares = (block_ref[...] * block_ref[...]).astype(F32)
    norm = jnp.sum(squares, axis=1, keepdims=True)
    norm_ref[...] = jnp.broadcast_to(norm, (rows, LANES)).T[0:1, :]
    for k in range(count):
        copies[k].wait()
        low_ref[k * tile : (k + 1) * tile, :] = held_ref[k % depth].astype(BF16)
        if k + depth < count:
            copies[k + depth].start()


def prepare(weights, features, labels, counts, active):
    rows = features.shape[0]
    feature_count, classes = weights.shape
    tile, depth = 256, 6
    line = jax.ShapeDtypeStruct((1, rows), F32)
    return pl.pallas_call(
        functools.partial(prepare_kernel, tile),
        out_shape=(pltpu.VMEM((feature_count, classes), BF16), line, line),
        in_specs=[HBM, HBM, HBM, SMEM, SMEM],
        out_specs=(VMEM,) * 3,
        scratch_shapes=[
            pltpu.VMEM((depth, tile, classes), F32),
            pltpu.VMEM(features.shape, BF16),
            pltpu.VMEM((1, rows), jnp.int32),
            pltpu.SemaphoreType.DMA((depth + 2,)),
        ],
        compiler_params=params(12),
        cost_estimate=cost(1, 1),
        name="prepare",
    )(
        weights,
        pltpu.with_memory_space_constraint(features, pltpu.HBM),
        pltpu.with_memory_space_constraint(labels.reshape(1, rows), pltpu.HBM),
        counts,
        active,
    )


def arriving_kernel(count, pieces, start, *refs):
    parts, w_ref = refs[:count], refs[count]
    plain_ref, outs = refs[-pieces - 1], refs[-pieces:]
    done = start
    for part in parts:
        plain_ref[done : done + part.shape[0], :] = part[...]
        done += part.shape[0]
    columns = 256
    for first in range(0, w_ref.shape[1], columns):
        own = slice(first, first + columns)
        found = jnp.dot(plain_ref[start:done, :], w_ref[:, own], preferred_element_type=F32)
        for k, out in enumerate(outs):
            out[:, own] = found[k * STEP : (k + 1) * STEP, :]


def arriving_logits(parts, w_low, plain, start, all_rows, tokens):
    rows = sum(p.shape[0] for p in parts)
    pieces, count = rows // STEP, len(parts)
    plain, *logits = pl.pallas_call(
        functools.partial(arriving_kernel, count, pieces, start),
        out_shape=(pltpu.VMEM((all_rows, w_low.shape[0]), BF16),)
        + (jax.ShapeDtypeStruct((STEP, w_low.shape[1]), F32),) * pieces,
        in_specs=[VMEM] * (count + 1 + len(plain)) + [ANY] * len(tokens),
        out_specs=(VMEM,) * (pieces + 1),
        input_output_aliases={count + 1: 0} if plain else {},
        compiler_params=params(),
        cost_estimate=cost(1, 1),
        name="arriving_logits",
    )(*parts, w_low, *plain, *tokens)
    return plain, logits


def turn_kernel(start, rows, plain_ref, *refs):
    turned_ref, squares_ref = refs[-2:]
    at = slice(start, start + rows)
    block = plain_ref[at, :].T
    turned_ref[:, at] = block
    squares_ref[:, at] = block * block


def turn(plain, start, rows, buffers):
    buffer = pltpu.VMEM(plain.shape[::-1], BF16)
    return pl.pallas_call(
        functools.partial(turn_kernel, start, rows),
        out_shape=(buffer, buffer),
        in_specs=[VMEM] * (1 + len(buffers)),
        out_specs=(VMEM, VMEM),
        input_output_aliases={1: 0, 2: 1} if buffers else {},
        compiler_params=params(),
        cost_estimate=cost(1, 1),
        name="turn",
    )(plain, *buffers)


def lane_pack(columns, rows):
    lane = lax.broadcasted_iota(jnp.int32, (rows, LANES), 1)
    packed = jnp.zeros((rows, LANES), F32)
    for k, column in enumerate(columns):
        packed = jnp.where(lane == k, column, packed)
    return packed


def put_stats(packed, place, shape):
    lines = packed.T
    line = jnp.concatenate([lines[k : k + 1, :] for k in range(3)], axis=1)
    here = lax.broadcasted_iota(jnp.int32, shape, 0) == place
    return jnp.where(here, line, 0.0)


def first_stats_kernel(slot, pieces, earlier, last, tokens, *refs):
    own, other = refs[:pieces], refs[pieces : 2 * pieces]
    active_ref, refs = refs[2 * pieces], refs[2 * pieces + 1 :]
    lines = refs[: 3 * last]
    older = refs[3 * last : 3 * last + earlier]
    outs = refs[3 * last + earlier + tokens :]
    e_ref, stats_ref, pack_ref = outs[0], outs[1], outs[-1]
    rows, classes = e_ref.shape
    active, place = active_ref[0], lax.axis_index("example")
    class_start = place * classes
    index = class_start + lax.broadcasted_iota(jnp.int32, (1, classes), 1)
    live = index < active
    for k in range(pieces):
        at = slice(k * STEP, (k + 1) * STEP)
        logits = jnp.where(live, own[k][...] + other[k][...], NEGATIVE)
        peak = jnp.max(logits, axis=1, keepdims=True)
        e = jnp.exp(logits - peak)
        e_ref[at, :] = e
        total = jnp.sum(e, axis=1, keepdims=True)
        square = jnp.sum(e * e, axis=1, keepdims=True)
        pack_ref[at, :] = lane_pack((peak, total, square), STEP)
    shape = stats_ref.shape
    n = shape[0]
    stats = older[0][...] if earlier else jnp.zeros(shape, F32)
    for k in range(rows // LANES):
        stats += put_stats(pack_ref[k * LANES : (k + 1) * LANES, :], block_of(place, slot + k, n), shape)
    stats_ref[...] = stats
    if last:
        copies_ref = outs[2]
        target, norm = lines[0][...], lines[1][...] + lines[2][...]
        wide = [jnp.broadcast_to(line, (shape[0], LANES)) for line in (target, norm)]
        full = jnp.concatenate([stats] + wide, axis=1)
        copies_ref[...] = jnp.broadcast_to(full[None], copies_ref.shape)


def first_stats(own, other, active, slot, n, earlier, side, tokens):
    pieces, classes = len(own), own[0].shape[1]
    rows = pieces * STEP
    last = len(side) > 0
    shapes = [jax.ShapeDtypeStruct((rows, classes), F32), jax.ShapeDtypeStruct((n, 3 * LANES), F32)]
    if last:
        shapes.append(jax.ShapeDtypeStruct((n, n, 5 * LANES), F32))
    extra = list(side) + list(earlier)
    return pl.pallas_call(
        functools.partial(
            first_stats_kernel, slot, pieces, len(earlier), last, len(tokens)
        ),
        out_shape=tuple(shapes),
        in_specs=[VMEM] * (2 * pieces) + [SMEM] + [VMEM] * len(extra) + [ANY] * len(tokens),
        out_specs=(VMEM,) * len(shapes),
        scratch_shapes=[pltpu.VMEM((rows, LANES), F32)],
        compiler_params=params(),
        cost_estimate=cost(1, 1),
        name="first_stats",
    )(*own, *other, active, *extra, *tokens)


def combine(own_ref, all_ref):
    n = all_ref.shape[0]
    part = lambda d, k: all_ref[d, :, k * LANES : (k + 1) * LANES]
    peaks = [part(d, 0) for d in range(n)]
    peak = functools.reduce(jnp.maximum, peaks)
    scales = [jnp.exp(p - peak) for p in peaks]
    total = sum(part(d, 1) * scales[d] for d in range(n))
    own_scale = jnp.exp(own_ref[:, 0:LANES] - peak)
    return part, peak, scales, total, own_scale


def to_slots(value, line_ref, place):
    n = value.shape[0]
    line_ref[...] = value
    return jnp.concatenate([line_ref[pl.ds(block_of(place, j, n), 1), :] for j in range(n)], axis=0)


def to_columns(lines):
    stacked = jnp.concatenate(lines, axis=0)
    rest = jnp.zeros((LANES - stacked.shape[0], LANES), F32)
    return jnp.concatenate([stacked, rest], axis=0).T


def first_weights_kernel(entries, parts, own_ref, all_ref, *refs):
    e_refs = refs[:parts]
    residual_ref, fisher_ref, damping_ref, target_ref, column_ref, line_ref = refs[parts:]
    n = all_ref.shape[0]
    classes = residual_ref.shape[1]
    place = lax.axis_index("example")
    class_start = place * classes
    part, peak, scales, total, own_scale = combine(own_ref, all_ref)
    square = sum(part(d, 2) * (scales[d] * scales[d]) for d in range(n))
    inverse = 1.0 / total
    spread = 1.0 - square * inverse * inverse
    target = jnp.concatenate([all_ref[d, 0:1, 3 * LANES : 4 * LANES] for d in range(n)], axis=0)
    norm = jnp.concatenate([all_ref[d, 0:1, 4 * LANES : 5 * LANES] for d in range(n)], axis=0)
    valid = (target >= 0.0).astype(F32)
    share = valid / jnp.sum(valid)
    fisher_sum = jnp.sum(norm * share * spread)
    damping_ref[...] = jnp.full(
        damping_ref.shape, DAMPING_SHARE * fisher_sum / entries + EPSILON, F32
    )
    factor = to_slots(own_scale * inverse, line_ref, place)
    share = to_slots(share, line_ref, place)
    target = to_slots(target, line_ref, place)
    target_ref[...] = target
    column_ref[...] = to_columns([factor, share, target])
    index = class_start + lax.broadcasted_iota(jnp.int32, (1, classes), 1)
    done = 0
    for e_ref in e_refs:
        for k in range(e_ref.shape[0] // LANES):
            j = done + k

            def step(i, _, j=j, k=k, e_ref=e_ref):
                start = i * STEP
                at = pl.ds(j * LANES + start, STEP)
                column = column_ref[pl.ds(start, STEP), :]
                e = e_ref[pl.ds(k * LANES + start, STEP), :]
                probability = e * column[:, j : j + 1]
                hit = index == column[:, 2 * n + j : 2 * n + j + 1].astype(jnp.int32)
                part = column[:, n + j : n + j + 1]
                residual_ref[at, :] = (part * (probability - hit.astype(F32))).astype(BF16)
                fisher_ref[at, :] = (part * probability * (1.0 - probability)).astype(BF16)
                return 0

            for i in range(LANES // STEP):
                step(i, 0)
        done += e_ref.shape[0] // LANES


def first_weights(own, every, e_parts, entries):
    n = own.shape[0]
    classes = e_parts[0].shape[1]
    weight = pltpu.VMEM((n * LANES, classes), BF16)
    return pl.pallas_call(
        functools.partial(first_weights_kernel, float(entries), len(e_parts)),
        out_shape=(
            weight,
            weight,
            jax.ShapeDtypeStruct((8, LANES), F32),
            jax.ShapeDtypeStruct((n, LANES), F32),
        ),
        in_specs=[VMEM] * (2 + len(e_parts)),
        out_specs=(VMEM,) * 4,
        scratch_shapes=[pltpu.VMEM((LANES, LANES), F32), pltpu.VMEM((n, LANES), F32)],
        compiler_params=params(),
        cost_estimate=cost(0, 8 * n * LANES * classes),
        name="first_weights",
    )(own, every, *e_parts)


def update_kernel(start, tile, turned_ref, squares_ref, w_ref, residual_ref, fisher_ref,
                  damping_ref, moved_ref, inverse_ref, low_ref, held_ref, sems):
    features, columns = moved_ref.shape
    damping = damping_ref[0:1, 0:1]
    own = slice(start, start + columns)
    count = features // tile
    copies = []
    for k in range(count):
        copies.append(
            pltpu.make_async_copy(
                w_ref.at[k * tile : (k + 1) * tile, own], held_ref.at[k], sems.at[k]
            )
        )
        copies[-1].start()

    def settle(k, gradient, fisher):
        at = slice(k * tile, (k + 1) * tile)
        inverse = 1.0 / (fisher + damping)
        change = gradient * inverse
        inverse_ref[at, :] = inverse
        moved_ref[at, :] = -change
        low_ref[at, :] = (held_ref[k] - LEARNING_RATE * change).astype(BF16)

    for copy in copies:
        copy.wait()
    before = None
    for k in range(count):
        at = slice(k * tile, (k + 1) * tile)
        fisher = jnp.dot(squares_ref[at, :], fisher_ref[:, own], preferred_element_type=F32)
        if before is not None:
            settle(*before)
        gradient = jnp.dot(turned_ref[at, :], residual_ref[:, own], preferred_element_type=F32)
        before = (k, gradient, fisher)
    settle(*before)


def update(turned, squares, weights, residual, fisher_weight, damping, start, columns):
    features, rows = turned.shape
    tile = 256
    return pl.pallas_call(
        functools.partial(update_kernel, start, tile),
        out_shape=(
            pltpu.VMEM((features, columns), F32),
            pltpu.VMEM((features, columns), F32),
            pltpu.VMEM((features, columns), BF16),
        ),
        in_specs=[VMEM, VMEM, HBM] + [VMEM] * 3,
        out_specs=(VMEM, VMEM, VMEM),
        scratch_shapes=[
            pltpu.VMEM((features // tile, tile, columns), F32),
            pltpu.SemaphoreType.DMA((features // tile,)),
        ],
        compiler_params=params(14),
        cost_estimate=cost(4 * rows * features * columns),
        name="update",
    )(turned, squares, weights, residual, fisher_weight, damping)


def next_logits_kernel(start, tile, plain_ref, low_ref, out_ref):
    for first in range(0, out_ref.shape[0], tile):
        out_ref[first : first + tile, :] = jnp.dot(
            plain_ref[start + first : start + first + tile, :],
            low_ref[...],
            preferred_element_type=F32,
        )


def next_logits(plain, low, start, rows):
    features, columns = low.shape
    return pl.pallas_call(
        functools.partial(next_logits_kernel, start, min(512, rows)),
        out_shape=jax.ShapeDtypeStruct((rows, columns), F32),
        in_specs=[VMEM, VMEM],
        out_specs=VMEM,
        compiler_params=params(),
        cost_estimate=cost(2 * rows * features * columns),
        name="next_logits",
    )(plain, low)


def last_stats_kernel(slot, last, pieces, offsets, earlier, *refs):
    own, other = refs[:pieces], refs[pieces : 2 * pieces]
    target_ref, active_ref = refs[2 * pieces : 2 * pieces + 2]
    older = refs[2 * pieces + 2 : 2 * pieces + 2 + earlier]
    outs = refs[2 * pieces + 2 + earlier :]
    e_ref, stats_ref, pack_ref, column_ref = outs[0], outs[1], outs[-2], outs[-1]
    rows, classes = e_ref.shape
    active, place = active_ref[0], lax.axis_index("example")
    class_start = place * classes
    n = stats_ref.shape[0]
    column_ref[...] = to_columns([target_ref[...]])
    index = class_start + lax.broadcasted_iota(jnp.int32, (1, classes), 1)
    live = index < active
    for k in range(rows // LANES):
        def step(i, _, k=k):
            start = i * STEP

            def rows_of(base):
                return pl.ds(base + k * LANES + start, STEP)

            logits = jnp.concatenate(
                [a[rows_of(o), :] + b[rows_of(o), :] for a, b, o in zip(own, other, offsets)],
                axis=1,
            )
            column = column_ref[pl.ds(start, STEP), slot + k : slot + k + 1]
            hit = index == column.astype(jnp.int32)
            label = jnp.sum(jnp.where(hit, logits, 0.0), axis=1, keepdims=True)
            logits = jnp.where(live, logits, NEGATIVE)
            peak = jnp.max(logits, axis=1, keepdims=True)
            e = jnp.exp(logits - peak)
            e_ref[rows_of(0), :] = e
            total = jnp.sum(e, axis=1, keepdims=True)
            pack_ref[rows_of(0), :] = lane_pack((peak, total, label), STEP)
            return 0

        for i in range(LANES // STEP):
            step(i, 0)
    shape = stats_ref.shape
    n = shape[0]
    stats = older[0][...] if earlier else jnp.zeros(shape, F32)
    for k in range(rows // LANES):
        stats += put_stats(pack_ref[k * LANES : (k + 1) * LANES, :], block_of(place, slot + k, n), shape)
    stats_ref[...] = stats
    if last:
        outs[2][...] = jnp.broadcast_to(stats[None], outs[2].shape)


def last_stats(own, other, offsets, target, active, slot, rows, n, earlier):
    classes = sum(c.shape[1] for c in own)
    last = slot + rows // LANES == n
    shapes = [
        jax.ShapeDtypeStruct((rows, classes), F32),
        jax.ShapeDtypeStruct((n, 3 * LANES), F32),
    ]
    if last:
        shapes.append(jax.ShapeDtypeStruct((n, n, 3 * LANES), F32))
    return pl.pallas_call(
        functools.partial(
            last_stats_kernel, slot, last, len(own), tuple(offsets), len(earlier)
        ),
        out_shape=tuple(shapes),
        in_specs=[VMEM] * (2 * len(own) + 1) + [SMEM] + [VMEM] * len(earlier),
        out_specs=(VMEM,) * len(shapes),
        scratch_shapes=[pltpu.VMEM((rows, LANES), F32), pltpu.VMEM((LANES, LANES), F32)],
        compiler_params=params(),
        cost_estimate=cost(0, 24 * rows * classes),
        name="last_stats",
    )(*own, *other, target, active, *earlier)


def finish_kernel(chunks, e_parts, tile, own_ref, all_ref, target_ref, turned_ref, *refs):
    e_refs = refs[:e_parts]
    refs = refs[e_parts:]
    moved_refs, inverse_refs = refs[:chunks], refs[chunks : 2 * chunks]
    out_ref, loss_ref, residual_ref, column_ref, line_ref, held_ref, sems = refs[2 * chunks :]
    n = all_ref.shape[0]
    classes = residual_ref.shape[1]
    place = lax.axis_index("example")
    class_start = place * classes
    part, peak, scales, total, own_scale = combine(own_ref, all_ref)
    label = sum(part(d, 2) for d in range(n))
    target = target_ref[...]
    valid = (target >= 0.0).astype(F32)
    share = valid / jnp.sum(valid)
    losses = to_slots(peak + jnp.log(total) - label, line_ref, place)
    loss_ref[...] = (valid * losses)[0:1, :]
    factor = to_slots(own_scale / total, line_ref, place)
    column_ref[...] = to_columns([factor, share, target])
    index = class_start + lax.broadcasted_iota(jnp.int32, (1, classes), 1)
    done = 0
    for e_ref in e_refs:
        for k in range(e_ref.shape[0] // LANES):
            j = done + k

            def step(i, _, j=j, k=k, e_ref=e_ref):
                start = i * STEP
                at = pl.ds(j * LANES + start, STEP)
                column = column_ref[pl.ds(start, STEP), :]
                e = e_ref[pl.ds(k * LANES + start, STEP), :]
                probability = e * column[:, j : j + 1]
                hit = index == column[:, 2 * n + j : 2 * n + j + 1].astype(jnp.int32)
                part = column[:, n + j : n + j + 1]
                residual_ref[at, :] = (part * (probability - hit.astype(F32))).astype(BF16)
                return 0

            for i in range(LANES // STEP):
                step(i, 0)
        done += e_ref.shape[0] // LANES

    copies = []
    for k in range(out_ref.shape[0] // tile):
        at = slice(k * tile, (k + 1) * tile)
        done = 0
        for moved_ref, inverse_ref in zip(moved_refs, inverse_refs):
            own = slice(done, done + moved_ref.shape[1])
            gradient = jnp.dot(
                turned_ref[at, :], residual_ref[:, own], preferred_element_type=F32
            )
            held_ref[k, :, own] = moved_ref[at, :] - gradient * inverse_ref[at, :]
            done += moved_ref.shape[1]
        copies.append(pltpu.make_async_copy(held_ref.at[k], out_ref.at[at, :], sems.at[k]))
        copies[-1].start()
    for copy in copies:
        copy.wait()


def finish(own, every, target, e_parts, turned, moved, inverse):
    n = own.shape[0]
    features, all_rows = turned.shape
    classes = e_parts[0].shape[1]
    tile = 512
    return pl.pallas_call(
        functools.partial(finish_kernel, len(moved), len(e_parts), tile),
        out_shape=(
            jax.ShapeDtypeStruct((features, classes), F32),
            jax.ShapeDtypeStruct((1, LANES), F32),
        ),
        in_specs=[VMEM] * (4 + len(e_parts) + 2 * len(moved)),
        out_specs=(ANY, VMEM),
        scratch_shapes=[
            pltpu.VMEM((all_rows, classes), BF16),
            pltpu.VMEM((LANES, LANES), F32),
            pltpu.VMEM((n, LANES), F32),
            pltpu.VMEM((features // tile, tile, classes), F32),
            pltpu.SemaphoreType.DMA((features // tile,)),
        ],
        compiler_params=params(16),
        cost_estimate=cost(2 * all_rows * features * classes),
        name="finish",
    )(own, every, target, turned, *e_parts, *moved, *inverse)


def exchange(copies):
    return lax.all_to_all(copies, "example", 0, 0)


def body(n, n_cls, features, weights, labels, counts, active):
    rows = features.shape[0]
    all_rows = rows * n
    feature_count, classes = weights.shape
    entries = feature_count * n_cls * classes * n
    weights = pltpu.with_memory_space_constraint(weights, pltpu.HBM)
    w_low, target, norm = prepare(weights, features, labels, counts, active)
    slots, waits, w_low = gather_blocks(features, n, w_low)
    side = (target, norm, swap(norm, "cls", n_cls, 1))

    groups = [[k, k + 1] for k in range(0, n - 2, 2)] + [[n - 2], [n - 1]]
    count = len(groups)
    behind = max(count - 3, 0)
    plain, buffers, logits, e_parts, stats = (), (), [], [], []

    def statistics(g, tokens):
        last = g == count - 1
        other = [swap(piece, "cls", n_cls, 1) for piece in logits[g]]
        e, found, *copies = first_stats(
            logits[g], other, active, groups[g][0], n, tuple(stats[-1:]),
            side if last else (), tokens,
        )
        e_parts.append(e)
        stats.append(found)
        return copies

    for g in range(count):
        if g == count - 1 and behind:
            logits[behind:], slots[-1] = lax.optimization_barrier((logits[behind:], slots[-1]))
        parts = [part for slot in groups[g] for part in slots[slot]]
        tokens = tuple(stats[-1:]) + tuple(buffers[:1]) + tuple(waits[g] if g < n // 2 else ())
        start = groups[g][0] * rows
        block, found = arriving_logits(parts, w_low, plain, start, all_rows, tokens)
        plain = (block,)
        logits.append(found)
        if g < n // 2 - 1:
            buffers = turn(block, start, 2 * rows, buffers)
        if g < behind:
            logits[g], slots[2 * g + 3][-1] = lax.optimization_barrier(
                (logits[g], slots[2 * g + 3][-1])
            )
            statistics(g, ())
    plain = plain[0]
    turned, squares = turn(plain, (n - 2) * rows, 2 * rows, buffers)
    for g in range(behind, count):
        copies = statistics(g, (logits[-1][0], turned))
    own_stats = stats[-1]
    every = exchange(copies[0])
    residual, fisher_weight, damping, target = first_weights(own_stats, every, e_parts, entries)

    columns = min(512, classes)
    moved, inverse, own, other = [], [], [], []
    for start in range(0, classes, columns):
        a, b, low = update(
            turned, squares, weights, residual, fisher_weight, damping, start, columns
        )
        moved.append(a)
        inverse.append(b)
        if start + columns < classes:
            own.append(next_logits(plain, low, 0, all_rows))
            other.append(swap(own[-1], "cls", n_cls, 1))
    half = n // 2
    late = [next_logits(plain, low, first * rows, half * rows) for first in (0, half)]
    late_other = [swap(c, "cls", n_cls, 1) for c in late]
    e_parts, earlier = [], ()
    for first, c, d in zip((0, half), late, late_other):
        offsets = [first * rows] * len(own) + [0]
        e, own_stats, *copies = last_stats(
            own + [c], other + [d], offsets, target, active, first, half * rows, n, earlier
        )
        e_parts.append(e)
        earlier = (own_stats,)
    every = exchange(copies[0])
    out, losses = finish(own_stats, every, target, e_parts, turned, moved, inverse)
    return out, losses.reshape(rows)


def solution(mesh):
    return jax.shard_map(
        functools.partial(body, mesh.shape["example"], mesh.shape["cls"]),
        mesh=mesh,
        in_specs=(
            P(("groups", "example"), "cls"),
            P(("groups", "cls"), "example"),
            P(("groups", "example")),
            P(("groups", "example")),
            P("groups"),
        ),
        out_specs=(P(("groups", "cls"), "example"), P(("groups", "example"))),
        check_vma=False,
    )
```

```python
import functools

import jax
import jax.numpy as jnp
from jax import lax
from jax.experimental import pallas as pl
from jax.experimental.pallas import tpu as pltpu
from jax.sharding import PartitionSpec as P

ITERS = 2
NEGATIVE = -1e30
LEARNING_RATE = 2e-05
DAMPING_SHARE = 0.1
EPSILON = 1e-06

F32 = jnp.float32
BF16 = jnp.bfloat16
VMEM = pl.BlockSpec(memory_space=pltpu.VMEM)
SMEM = pl.BlockSpec(memory_space=pltpu.SMEM)
HBM = pl.BlockSpec(memory_space=pltpu.HBM)
ANY = pl.BlockSpec(memory_space=pl.ANY)
STEP = 64
LANES = 128


def params(mib=10):
    return pltpu.CompilerParams(vmem_limit_bytes=mib << 20)


def cost(flops=0, nbytes=0):
    return pl.CostEstimate(flops=int(flops), bytes_accessed=int(nbytes), transcendentals=0)


def swap(x, axis, n, offset):
    return lax.ppermute(x, axis, [(i, i ^ offset) for i in range(n)])


def gray(v):
    return v ^ (v >> 1)


def block_of(place, slot, n):
    if n != 8:
        return lax.rem(place + n - slot, n)
    z, y = place // 2, place % 2
    return gray((gray(z) + 4 - slot // 2) & 3) * 2 + (y ^ (slot % 2))


def halves_kernel(first_ref, second_ref, upper_ref, lower_ref):
    rows = upper_ref.shape[0]
    upper_ref[...] = first_ref[0:rows, :]
    lower_ref[...] = second_ref[rows : 2 * rows, :]


def halves(first, second):
    half = pltpu.VMEM((first.shape[0] // 2, first.shape[1]), first.dtype)
    return pl.pallas_call(
        halves_kernel,
        out_shape=(half, half),
        in_specs=[VMEM, VMEM],
        out_specs=(VMEM, VMEM),
        compiler_params=params(),
        cost_estimate=cost(1, 1),
        name="halves",
    )(first, second)


def gather_blocks(x, n, early):
    if n != 8:
        ring = [(i, (i + 1) % n) for i in range(n)]
        slots = [x]
        for _ in range(n - 1):
            slots.append(lax.ppermute(slots[-1], "example", ring))
        return [[slot] for slot in slots], [()] * (n // 2), early, [slot for slot in slots[3::2]]
    hops = ((0, 1), (1, 3), (3, 2), (2, 0))
    ring = [(a * 2 + y, b * 2 + y) for a, b in hops for y in range(2)]
    slots, held = [], x
    for step in range(3):
        across = swap(held, "example", n, 1)
        later = lax.ppermute(held, "example", ring)
        if step == 0:
            across, later, early = lax.optimization_barrier((across, later, early))
        else:
            across, later = lax.optimization_barrier((across, later))
        slots += [[held], [across]]
        held = later
    upper, lower = halves(held, across)
    last = [swap(upper, "example", n, 1), lax.ppermute(lower, "example", ring)]
    slots += [[held], last]
    return slots, [tuple(slots[2 * k + 2]) for k in range(3)] + [()], early, [slots[3][0], upper]


def prepare_kernel(tile, chunks, w_ref, x_ref, labels_ref, counts_ref, active_ref, *refs):
    kept = refs[:chunks]
    low_ref, target_ref, norm_ref, block_ref, label_ref, sems = refs[chunks:]
    first = [
        pltpu.make_async_copy(x_ref, block_ref, sems.at[0]),
        pltpu.make_async_copy(labels_ref, label_ref, sems.at[1]),
    ]
    copies = []
    for k in range(w_ref.shape[0] // tile):
        at = slice(k * tile, (k + 1) * tile)
        for c, keep in enumerate(kept):
            own = slice(c * keep.shape[1], (c + 1) * keep.shape[1])
            copy = pltpu.make_async_copy(
                w_ref.at[at, own], keep.at[at, :], sems.at[2 + len(copies)]
            )
            copies.append((copy, keep, at, own))
    for copy in first + [c[0] for c in copies]:
        copy.start()
    for copy in first:
        copy.wait()
    rows = x_ref.shape[0]
    slot = lax.broadcasted_iota(jnp.int32, (1, rows), 1)
    target = jnp.where(slot < counts_ref[0], label_ref[...] % active_ref[0], -1)
    target_ref[...] = target.astype(F32)
    squares = (block_ref[...] * block_ref[...]).astype(F32)
    norm = jnp.sum(squares, axis=1, keepdims=True)
    norm_ref[...] = jnp.broadcast_to(norm, (rows, LANES)).T[0:1, :]
    for copy, keep, at, own in copies:
        copy.wait()
        low_ref[at, own] = keep[at, :].astype(BF16)


def prepare(weights, features, labels, counts, active, columns):
    rows = features.shape[0]
    feature_count, classes = weights.shape
    tile, chunks = 256, classes // columns
    line = jax.ShapeDtypeStruct((1, rows), F32)
    *kept, low, target, norm = pl.pallas_call(
        functools.partial(prepare_kernel, tile, chunks),
        out_shape=(pltpu.VMEM((feature_count, columns), F32),) * chunks
        + (pltpu.VMEM((feature_count, classes), BF16), line, line),
        in_specs=[HBM, HBM, HBM, SMEM, SMEM],
        out_specs=(VMEM,) * (chunks + 3),
        scratch_shapes=[
            pltpu.VMEM(features.shape, BF16),
            pltpu.VMEM((1, rows), jnp.int32),
            pltpu.SemaphoreType.DMA((2 + chunks * (feature_count // tile),)),
        ],
        compiler_params=params(),
        cost_estimate=cost(1, 1),
        name="prepare",
    )(
        weights,
        pltpu.with_memory_space_constraint(features, pltpu.HBM),
        pltpu.with_memory_space_constraint(labels.reshape(1, rows), pltpu.HBM),
        counts,
        active,
    )
    return kept, low, target, norm


def arriving_kernel(count, pieces, start, *refs):
    parts, w_ref = refs[:count], refs[count]
    plain_ref, outs = refs[-pieces - 1], refs[-pieces:]
    done = start
    for part in parts:
        plain_ref[done : done + part.shape[0], :] = part[...]
        done += part.shape[0]
    columns = 256
    for first in range(0, w_ref.shape[1], columns):
        own = slice(first, first + columns)
        found = jnp.dot(plain_ref[start:done, :], w_ref[:, own], preferred_element_type=F32)
        for k, out in enumerate(outs):
            out[:, own] = found[k * STEP : (k + 1) * STEP, :]


def arriving_logits(parts, w_low, plain, start, all_rows, tokens):
    rows = sum(p.shape[0] for p in parts)
    pieces, count = rows // STEP, len(parts)
    plain, *logits = pl.pallas_call(
        functools.partial(arriving_kernel, count, pieces, start),
        out_shape=(pltpu.VMEM((all_rows, w_low.shape[0]), BF16),)
        + (jax.ShapeDtypeStruct((STEP, w_low.shape[1]), F32),) * pieces,
        in_specs=[VMEM] * (count + 1 + len(plain)) + [ANY] * len(tokens),
        out_specs=(VMEM,) * (pieces + 1),
        input_output_aliases={count + 1: 0} if plain else {},
        compiler_params=params(),
        cost_estimate=cost(1, 1),
        name="arriving_logits",
    )(*parts, w_low, *plain, *tokens)
    return plain, logits


def turn_kernel(start, rows, plain_ref, *refs):
    turned_ref, squares_ref = refs[-2:]
    at = slice(start, start + rows)
    block = plain_ref[at, :].T
    turned_ref[:, at] = block
    squares_ref[:, at] = block * block


def turn(plain, start, rows, buffers):
    buffer = pltpu.VMEM(plain.shape[::-1], BF16)
    return pl.pallas_call(
        functools.partial(turn_kernel, start, rows),
        out_shape=(buffer, buffer),
        in_specs=[VMEM] * (1 + len(buffers)),
        out_specs=(VMEM, VMEM),
        input_output_aliases={1: 0, 2: 1} if buffers else {},
        compiler_params=params(),
        cost_estimate=cost(1, 1),
        name="turn",
    )(plain, *buffers)


def lane_pack(columns, rows):
    lane = lax.broadcasted_iota(jnp.int32, (rows, LANES), 1)
    packed = jnp.zeros((rows, LANES), F32)
    for k, column in enumerate(columns):
        packed = jnp.where(lane == k, column, packed)
    return packed


def put_stats(packed, place, shape):
    lines = packed.T
    line = jnp.concatenate([lines[k : k + 1, :] for k in range(3)], axis=1)
    here = lax.broadcasted_iota(jnp.int32, shape, 0) == place
    return jnp.where(here, line, 0.0)


def first_stats_kernel(slot, pieces, earlier, last, tokens, *refs):
    own, other = refs[:pieces], refs[pieces : 2 * pieces]
    active_ref, refs = refs[2 * pieces], refs[2 * pieces + 1 :]
    lines = refs[: 3 * last]
    older = refs[3 * last : 3 * last + earlier]
    outs = refs[3 * last + earlier + tokens :]
    e_ref, stats_ref, pack_ref = outs[0], outs[1], outs[-1]
    rows, classes = e_ref.shape
    active, place = active_ref[0], lax.axis_index("example")
    class_start = place * classes
    index = class_start + lax.broadcasted_iota(jnp.int32, (1, classes), 1)
    live = index < active
    for k in range(pieces):
        at = slice(k * STEP, (k + 1) * STEP)
        logits = jnp.where(live, own[k][...] + other[k][...], NEGATIVE)
        peak = jnp.max(logits, axis=1, keepdims=True)
        e = jnp.exp(logits - peak)
        e_ref[at, :] = e
        total = jnp.sum(e, axis=1, keepdims=True)
        square = jnp.sum(e * e, axis=1, keepdims=True)
        pack_ref[at, :] = lane_pack((peak, total, square), STEP)
    shape = stats_ref.shape
    n = shape[0]
    stats = older[0][...] if earlier else jnp.zeros(shape, F32)
    for k in range(rows // LANES):
        stats += put_stats(pack_ref[k * LANES : (k + 1) * LANES, :], block_of(place, slot + k, n), shape)
    stats_ref[...] = stats
    if last:
        copies_ref = outs[2]
        target, norm = lines[0][...], lines[1][...] + lines[2][...]
        wide = [jnp.broadcast_to(line, (shape[0], LANES)) for line in (target, norm)]
        full = jnp.concatenate([stats] + wide, axis=1)
        copies_ref[...] = jnp.broadcast_to(full[None], copies_ref.shape)


def first_stats(own, other, active, slot, n, earlier, side, tokens):
    pieces, classes = len(own), own[0].shape[1]
    rows = pieces * STEP
    last = len(side) > 0
    shapes = [jax.ShapeDtypeStruct((rows, classes), F32), jax.ShapeDtypeStruct((n, 3 * LANES), F32)]
    if last:
        shapes.append(jax.ShapeDtypeStruct((n, n, 5 * LANES), F32))
    extra = list(side) + list(earlier)
    return pl.pallas_call(
        functools.partial(
            first_stats_kernel, slot, pieces, len(earlier), last, len(tokens)
        ),
        out_shape=tuple(shapes),
        in_specs=[VMEM] * (2 * pieces) + [SMEM] + [VMEM] * len(extra) + [ANY] * len(tokens),
        out_specs=(VMEM,) * len(shapes),
        scratch_shapes=[pltpu.VMEM((rows, LANES), F32)],
        compiler_params=params(),
        cost_estimate=cost(1, 1),
        name="first_stats",
    )(*own, *other, active, *extra, *tokens)


def combine(own_ref, all_ref):
    n = all_ref.shape[0]
    part = lambda d, k: all_ref[d, :, k * LANES : (k + 1) * LANES]
    peaks = [part(d, 0) for d in range(n)]
    peak = functools.reduce(jnp.maximum, peaks)
    scales = [jnp.exp(p - peak) for p in peaks]
    total = sum(part(d, 1) * scales[d] for d in range(n))
    own_scale = jnp.exp(own_ref[:, 0:LANES] - peak)
    return part, peak, scales, total, own_scale


def to_slots(value, line_ref, place):
    n = value.shape[0]
    line_ref[...] = value
    return jnp.concatenate([line_ref[pl.ds(block_of(place, j, n), 1), :] for j in range(n)], axis=0)


def to_columns(lines):
    stacked = jnp.concatenate(lines, axis=0)
    rest = jnp.zeros((LANES - stacked.shape[0], LANES), F32)
    return jnp.concatenate([stacked, rest], axis=0).T


def first_weights_kernel(entries, parts, own_ref, all_ref, *refs):
    e_refs = refs[:parts]
    residual_ref, fisher_ref, damping_ref, target_ref, column_ref, line_ref = refs[parts:]
    n = all_ref.shape[0]
    classes = residual_ref.shape[1]
    place = lax.axis_index("example")
    class_start = place * classes
    part, peak, scales, total, own_scale = combine(own_ref, all_ref)
    square = sum(part(d, 2) * (scales[d] * scales[d]) for d in range(n))
    inverse = 1.0 / total
    spread = 1.0 - square * inverse * inverse
    target = jnp.concatenate([all_ref[d, 0:1, 3 * LANES : 4 * LANES] for d in range(n)], axis=0)
    norm = jnp.concatenate([all_ref[d, 0:1, 4 * LANES : 5 * LANES] for d in range(n)], axis=0)
    valid = (target >= 0.0).astype(F32)
    share = valid / jnp.sum(valid)
    fisher_sum = jnp.sum(norm * share * spread)
    damping_ref[...] = jnp.full(
        damping_ref.shape, DAMPING_SHARE * fisher_sum / entries + EPSILON, F32
    )
    factor = to_slots(own_scale * inverse, line_ref, place)
    share = to_slots(share, line_ref, place)
    target = to_slots(target, line_ref, place)
    target_ref[...] = target
    column_ref[...] = to_columns([factor, share, target])
    index = class_start + lax.broadcasted_iota(jnp.int32, (1, classes), 1)
    done = 0
    for e_ref in e_refs:
        for k in range(e_ref.shape[0] // LANES):
            j = done + k

            def step(i, _, j=j, k=k, e_ref=e_ref):
                start = i * STEP
                at = pl.ds(j * LANES + start, STEP)
                column = column_ref[pl.ds(start, STEP), :]
                e = e_ref[pl.ds(k * LANES + start, STEP), :]
                probability = e * column[:, j : j + 1]
                hit = index == column[:, 2 * n + j : 2 * n + j + 1].astype(jnp.int32)
                part = column[:, n + j : n + j + 1]
                residual_ref[at, :] = (part * (probability - hit.astype(F32))).astype(BF16)
                fisher_ref[at, :] = (part * probability * (1.0 - probability)).astype(BF16)
                return 0

            for i in range(LANES // STEP):
                step(i, 0)
        done += e_ref.shape[0] // LANES


def first_weights(own, every, e_parts, entries):
    n = own.shape[0]
    classes = e_parts[0].shape[1]
    weight = pltpu.VMEM((n * LANES, classes), BF16)
    return pl.pallas_call(
        functools.partial(first_weights_kernel, float(entries), len(e_parts)),
        out_shape=(
            weight,
            weight,
            jax.ShapeDtypeStruct((8, LANES), F32),
            jax.ShapeDtypeStruct((n, LANES), F32),
        ),
        in_specs=[VMEM] * (2 + len(e_parts)),
        out_specs=(VMEM,) * 4,
        scratch_shapes=[pltpu.VMEM((LANES, LANES), F32), pltpu.VMEM((n, LANES), F32)],
        compiler_params=params(),
        cost_estimate=cost(0, 8 * n * LANES * classes),
        name="first_weights",
    )(own, every, *e_parts)


def update_kernel(start, tile, turned_ref, squares_ref, w_ref, residual_ref, fisher_ref,
                  damping_ref, moved_ref, inverse_ref, low_ref):
    features, columns = moved_ref.shape
    damping = damping_ref[0:1, 0:1]
    own = slice(start, start + columns)
    for k in range(features // tile):
        at = slice(k * tile, (k + 1) * tile)
        fisher = jnp.dot(squares_ref[at, :], fisher_ref[:, own], preferred_element_type=F32)
        gradient = jnp.dot(turned_ref[at, :], residual_ref[:, own], preferred_element_type=F32)
        inverse = 1.0 / (fisher + damping)
        change = gradient * inverse
        inverse_ref[at, :] = inverse
        low_ref[at, :] = (w_ref[at, :] - LEARNING_RATE * change).astype(BF16)
        moved_ref[at, :] = -change


def update(turned, squares, weights, residual, fisher_weight, damping, start):
    features, rows = turned.shape
    columns = weights.shape[1]
    return pl.pallas_call(
        functools.partial(update_kernel, start, 512),
        out_shape=(
            pltpu.VMEM((features, columns), F32),
            pltpu.VMEM((features, columns), F32),
            pltpu.VMEM((features, columns), BF16),
        ),
        in_specs=[VMEM] * 6,
        out_specs=(VMEM, VMEM, VMEM),
        input_output_aliases={2: 0},
        compiler_params=params(),
        cost_estimate=cost(4 * rows * features * columns),
        name="update",
    )(turned, squares, weights, residual, fisher_weight, damping)


def next_logits_kernel(start, tile, plain_ref, low_ref, out_ref):
    for first in range(0, out_ref.shape[0], tile):
        out_ref[first : first + tile, :] = jnp.dot(
            plain_ref[start + first : start + first + tile, :],
            low_ref[...],
            preferred_element_type=F32,
        )


def next_logits(plain, low, start, rows):
    features, columns = low.shape
    return pl.pallas_call(
        functools.partial(next_logits_kernel, start, min(512, rows)),
        out_shape=jax.ShapeDtypeStruct((rows, columns), F32),
        in_specs=[VMEM, VMEM],
        out_specs=VMEM,
        compiler_params=params(),
        cost_estimate=cost(2 * rows * features * columns),
        name="next_logits",
    )(plain, low)


def last_stats_kernel(slot, last, pieces, offsets, earlier, *refs):
    own, other = refs[:pieces], refs[pieces : 2 * pieces]
    target_ref, active_ref = refs[2 * pieces : 2 * pieces + 2]
    older = refs[2 * pieces + 2 : 2 * pieces + 2 + earlier]
    outs = refs[2 * pieces + 2 + earlier :]
    e_ref, stats_ref, pack_ref, column_ref = outs[0], outs[1], outs[-2], outs[-1]
    rows, classes = e_ref.shape
    active, place = active_ref[0], lax.axis_index("example")
    class_start = place * classes
    n = stats_ref.shape[0]
    column_ref[...] = to_columns([target_ref[...]])
    index = class_start + lax.broadcasted_iota(jnp.int32, (1, classes), 1)
    live = index < active
    for k in range(rows // LANES):
        def step(i, _, k=k):
            start = i * STEP

            def rows_of(base):
                return pl.ds(base + k * LANES + start, STEP)

            logits = jnp.concatenate(
                [a[rows_of(o), :] + b[rows_of(o), :] for a, b, o in zip(own, other, offsets)],
                axis=1,
            )
            column = column_ref[pl.ds(start, STEP), slot + k : slot + k + 1]
            hit = index == column.astype(jnp.int32)
            label = jnp.sum(jnp.where(hit, logits, 0.0), axis=1, keepdims=True)
            logits = jnp.where(live, logits, NEGATIVE)
            peak = jnp.max(logits, axis=1, keepdims=True)
            e = jnp.exp(logits - peak)
            e_ref[rows_of(0), :] = e
            total = jnp.sum(e, axis=1, keepdims=True)
            pack_ref[rows_of(0), :] = lane_pack((peak, total, label), STEP)
            return 0

        for i in range(LANES // STEP):
            step(i, 0)
    shape = stats_ref.shape
    n = shape[0]
    stats = older[0][...] if earlier else jnp.zeros(shape, F32)
    for k in range(rows // LANES):
        stats += put_stats(pack_ref[k * LANES : (k + 1) * LANES, :], block_of(place, slot + k, n), shape)
    stats_ref[...] = stats
    if last:
        outs[2][...] = jnp.broadcast_to(stats[None], outs[2].shape)


def last_stats(own, other, offsets, target, active, slot, rows, n, earlier):
    classes = sum(c.shape[1] for c in own)
    last = slot + rows // LANES == n
    shapes = [
        jax.ShapeDtypeStruct((rows, classes), F32),
        jax.ShapeDtypeStruct((n, 3 * LANES), F32),
    ]
    if last:
        shapes.append(jax.ShapeDtypeStruct((n, n, 3 * LANES), F32))
    return pl.pallas_call(
        functools.partial(
            last_stats_kernel, slot, last, len(own), tuple(offsets), len(earlier)
        ),
        out_shape=tuple(shapes),
        in_specs=[VMEM] * (2 * len(own) + 1) + [SMEM] + [VMEM] * len(earlier),
        out_specs=(VMEM,) * len(shapes),
        scratch_shapes=[pltpu.VMEM((rows, LANES), F32), pltpu.VMEM((LANES, LANES), F32)],
        compiler_params=params(),
        cost_estimate=cost(0, 24 * rows * classes),
        name="last_stats",
    )(*own, *other, target, active, *earlier)


def finish_kernel(chunks, e_parts, tile, own_ref, all_ref, target_ref, turned_ref, *refs):
    e_refs = refs[:e_parts]
    refs = refs[e_parts:]
    moved_refs, inverse_refs = refs[:chunks], refs[chunks : 2 * chunks]
    out_ref, loss_ref, residual_ref, column_ref, line_ref, held_ref, sems = refs[2 * chunks :]
    n = all_ref.shape[0]
    classes = residual_ref.shape[1]
    place = lax.axis_index("example")
    class_start = place * classes
    part, peak, scales, total, own_scale = combine(own_ref, all_ref)
    label = sum(part(d, 2) for d in range(n))
    target = target_ref[...]
    valid = (target >= 0.0).astype(F32)
    share = valid / jnp.sum(valid)
    losses = to_slots(peak + jnp.log(total) - label, line_ref, place)
    loss_ref[...] = (valid * losses)[0:1, :]
    factor = to_slots(own_scale / total, line_ref, place)
    column_ref[...] = to_columns([factor, share, target])
    index = class_start + lax.broadcasted_iota(jnp.int32, (1, classes), 1)
    done = 0
    for e_ref in e_refs:
        for k in range(e_ref.shape[0] // LANES):
            j = done + k

            def step(i, _, j=j, k=k, e_ref=e_ref):
                start = i * STEP
                at = pl.ds(j * LANES + start, STEP)
                column = column_ref[pl.ds(start, STEP), :]
                e = e_ref[pl.ds(k * LANES + start, STEP), :]
                probability = e * column[:, j : j + 1]
                hit = index == column[:, 2 * n + j : 2 * n + j + 1].astype(jnp.int32)
                part = column[:, n + j : n + j + 1]
                residual_ref[at, :] = (part * (probability - hit.astype(F32))).astype(BF16)
                return 0

            for i in range(LANES // STEP):
                step(i, 0)
        done += e_ref.shape[0] // LANES

    copies = []
    for k in range(out_ref.shape[0] // tile):
        at = slice(k * tile, (k + 1) * tile)
        done = 0
        for moved_ref, inverse_ref in zip(moved_refs, inverse_refs):
            own = slice(done, done + moved_ref.shape[1])
            gradient = jnp.dot(
                turned_ref[at, :], residual_ref[:, own], preferred_element_type=F32
            )
            held_ref[k, :, own] = moved_ref[at, :] - gradient * inverse_ref[at, :]
            done += moved_ref.shape[1]
        copies.append(pltpu.make_async_copy(held_ref.at[k], out_ref.at[at, :], sems.at[k]))
        copies[-1].start()
    for copy in copies:
        copy.wait()


def finish(own, every, target, e_parts, turned, moved, inverse):
    n = own.shape[0]
    features, all_rows = turned.shape
    classes = e_parts[0].shape[1]
    tile = 512
    return pl.pallas_call(
        functools.partial(finish_kernel, len(moved), len(e_parts), tile),
        out_shape=(
            jax.ShapeDtypeStruct((features, classes), F32),
            jax.ShapeDtypeStruct((1, LANES), F32),
        ),
        in_specs=[VMEM] * (4 + len(e_parts) + 2 * len(moved)),
        out_specs=(ANY, VMEM),
        scratch_shapes=[
            pltpu.VMEM((all_rows, classes), BF16),
            pltpu.VMEM((LANES, LANES), F32),
            pltpu.VMEM((n, LANES), F32),
            pltpu.VMEM((features // tile, tile, classes), F32),
            pltpu.SemaphoreType.DMA((features // tile,)),
        ],
        compiler_params=params(16),
        cost_estimate=cost(2 * all_rows * features * classes),
        name="finish",
    )(own, every, target, turned, *e_parts, *moved, *inverse)


def exchange(copies):
    return lax.all_to_all(copies, "example", 0, 0)


def body(n, n_cls, features, weights, labels, counts, active):
    rows = features.shape[0]
    all_rows = rows * n
    feature_count, classes = weights.shape
    entries = feature_count * n_cls * classes * n
    weights = pltpu.with_memory_space_constraint(weights, pltpu.HBM)
    columns = min(512, classes)
    kept, w_low, target, norm = prepare(weights, features, labels, counts, active, columns)
    slots, waits, w_low, gates = gather_blocks(features, n, w_low)
    side = (target, norm, swap(norm, "cls", n_cls, 1))

    groups = [[k, k + 1] for k in range(0, n - 2, 2)] + [[n - 2], [n - 1]]
    count = len(groups)
    behind = max(count - 3, 0)
    plain, buffers, logits, e_parts, stats = (), (), [], [], []

    def statistics(g, tokens):
        last = g == count - 1
        other = [swap(piece, "cls", n_cls, 1) for piece in logits[g]]
        e, found, *copies = first_stats(
            logits[g], other, active, groups[g][0], n, tuple(stats[-1:]),
            side if last else (), tokens,
        )
        e_parts.append(e)
        stats.append(found)
        return copies

    for g in range(count):
        if g == count - 1 and behind:
            logits[behind:], slots[-1] = lax.optimization_barrier((logits[behind:], slots[-1]))
        parts = [part for slot in groups[g] for part in slots[slot]]
        tokens = tuple(stats[-1:]) + tuple(buffers[:1]) + tuple(waits[g] if g < n // 2 else ())
        start = groups[g][0] * rows
        block, found = arriving_logits(parts, w_low, plain, start, all_rows, tokens)
        plain = (block,)
        logits.append(found)
        if g < n // 2 - 1:
            buffers = turn(block, start, 2 * rows, buffers)
        if g < behind:
            logits[g], _ = lax.optimization_barrier((logits[g], gates[g]))
            statistics(g, ())
    plain = plain[0]
    turned, squares = turn(plain, (n - 2) * rows, 2 * rows, buffers)
    for g in range(behind, count):
        copies = statistics(g, (logits[-1][0], turned))
    own_stats = stats[-1]
    every = exchange(copies[0])
    residual, fisher_weight, damping, target = first_weights(own_stats, every, e_parts, entries)

    moved, inverse, own, other = [], [], [], []
    for start in range(0, classes, columns):
        a, b, low = update(
            turned, squares, kept[start // columns], residual, fisher_weight, damping, start
        )
        moved.append(a)
        inverse.append(b)
        if start + columns < classes:
            own.append(next_logits(plain, low, 0, all_rows))
            other.append(swap(own[-1], "cls", n_cls, 1))
    half = n // 2
    late = [next_logits(plain, low, first * rows, half * rows) for first in (0, half)]
    late_other = [swap(c, "cls", n_cls, 1) for c in late]
    e_parts, earlier = [], ()
    for first, c, d in zip((0, half), late, late_other):
        offsets = [first * rows] * len(own) + [0]
        e, own_stats, *copies = last_stats(
            own + [c], other + [d], offsets, target, active, first, half * rows, n, earlier
        )
        e_parts.append(e)
        earlier = (own_stats,)
    every = exchange(copies[0])
    out, losses = finish(own_stats, every, target, e_parts, turned, moved, inverse)
    return out, losses.reshape(rows)


def solution(mesh):
    return jax.shard_map(
        functools.partial(body, mesh.shape["example"], mesh.shape["cls"]),
        mesh=mesh,
        in_specs=(
            P(("groups", "example"), "cls"),
            P(("groups", "cls"), "example"),
            P(("groups", "example")),
            P(("groups", "example")),
            P("groups"),
        ),
        out_specs=(P(("groups", "cls"), "example"), P(("groups", "example"))),
        check_vma=False,
    )
```

```python
import functools

import jax
import jax.numpy as jnp
from jax import lax
from jax.experimental import pallas as pl
from jax.experimental.pallas import tpu as pltpu
from jax.sharding import PartitionSpec as P

ITERS = 2
NEGATIVE = -1e30
LEARNING_RATE = 2e-05
DAMPING_SHARE = 0.1
EPSILON = 1e-06

F32 = jnp.float32
BF16 = jnp.bfloat16
VMEM = pl.BlockSpec(memory_space=pltpu.VMEM)
SMEM = pl.BlockSpec(memory_space=pltpu.SMEM)
HBM = pl.BlockSpec(memory_space=pltpu.HBM)
ANY = pl.BlockSpec(memory_space=pl.ANY)
STEP = 64
LANES = 128


def params(mib=10):
    return pltpu.CompilerParams(vmem_limit_bytes=mib << 20)


def cost(flops=0, nbytes=0):
    return pl.CostEstimate(flops=int(flops), bytes_accessed=int(nbytes), transcendentals=0)


def swap(x, axis, n, offset):
    return lax.ppermute(x, axis, [(i, i ^ offset) for i in range(n)])


def gray(v):
    return v ^ (v >> 1)


def block_of(place, slot, n):
    if n != 8:
        return lax.rem(place + n - slot, n)
    z, y = place // 2, place % 2
    return gray((gray(z) + 4 - slot // 2) & 3) * 2 + (y ^ (slot % 2))


def half_kernel(start, *refs):
    block_ref, out_ref = refs[0], refs[-1]
    out_ref[...] = block_ref[start : start + out_ref.shape[0], :]


def half(block, upper, tokens):
    rows = block.shape[0] // 2
    return pl.pallas_call(
        functools.partial(half_kernel, 0 if upper else rows),
        out_shape=pltpu.VMEM((rows, block.shape[1]), block.dtype),
        in_specs=[VMEM] + [ANY] * len(tokens),
        out_specs=VMEM,
        compiler_params=params(),
        cost_estimate=cost(1, 1),
        name="half",
    )(block, *tokens)


def gather_blocks(x, n, early):
    if n != 8:
        ring = [(i, (i + 1) % n) for i in range(n)]
        slots = [x]
        for _ in range(n - 1):
            slots.append(lax.ppermute(slots[-1], "example", ring))
        return [[slot] for slot in slots], [()] * (n // 2), early, [slot for slot in slots[3::2]]
    hops = ((0, 1), (1, 3), (3, 2), (2, 0))
    ring = [(a * 2 + y, b * 2 + y) for a, b in hops for y in range(2)]
    tie = lax.optimization_barrier
    slots, held, ready = [], x, x
    for step in range(3):
        across = swap(ready, "example", n, 1)
        later = lax.ppermute(held, "example", ring)
        slots += [[held], [across]]
        if step == 0:
            later, early = tie((later, early))
        if step < 2:
            ready, _ = tie((later, across))
        held = later
    upper = half(held, True, ())
    lower = half(across, False, (upper,))
    last = [swap(upper, "example", n, 1), lax.ppermute(lower, "example", ring)]
    slots += [[held], last]
    return slots, [tuple(slots[2 * k + 2]) for k in range(3)] + [()], early, [slots[3][0], upper]


def prepare_kernel(tile, chunks, w_ref, x_ref, labels_ref, counts_ref, active_ref, *refs):
    kept = refs[:chunks]
    low_ref, target_ref, norm_ref, block_ref, label_ref, sems = refs[chunks:]
    first = [
        pltpu.make_async_copy(x_ref, block_ref, sems.at[0]),
        pltpu.make_async_copy(labels_ref, label_ref, sems.at[1]),
    ]
    copies = []
    for k in range(w_ref.shape[0] // tile):
        at = slice(k * tile, (k + 1) * tile)
        for c, keep in enumerate(kept):
            own = slice(c * keep.shape[1], (c + 1) * keep.shape[1])
            copy = pltpu.make_async_copy(
                w_ref.at[at, own], keep.at[at, :], sems.at[2 + len(copies)]
            )
            copies.append((copy, keep, at, own))
    for copy in first + [c[0] for c in copies]:
        copy.start()
    for copy in first:
        copy.wait()
    rows = x_ref.shape[0]
    slot = lax.broadcasted_iota(jnp.int32, (1, rows), 1)
    target = jnp.where(slot < counts_ref[0], label_ref[...] % active_ref[0], -1)
    target_ref[...] = target.astype(F32)
    squares = (block_ref[...] * block_ref[...]).astype(F32)
    norm = jnp.sum(squares, axis=1, keepdims=True)
    norm_ref[...] = jnp.broadcast_to(norm, (rows, LANES)).T[0:1, :]
    for copy, keep, at, own in copies:
        copy.wait()
        low_ref[at, own] = keep[at, :].astype(BF16)


def prepare(weights, features, labels, counts, active, columns):
    rows = features.shape[0]
    feature_count, classes = weights.shape
    tile, chunks = 256, classes // columns
    line = jax.ShapeDtypeStruct((1, rows), F32)
    *kept, low, target, norm = pl.pallas_call(
        functools.partial(prepare_kernel, tile, chunks),
        out_shape=(pltpu.VMEM((feature_count, columns), F32),) * chunks
        + (pltpu.VMEM((feature_count, classes), BF16), line, line),
        in_specs=[HBM, HBM, HBM, SMEM, SMEM],
        out_specs=(VMEM,) * (chunks + 3),
        scratch_shapes=[
            pltpu.VMEM(features.shape, BF16),
            pltpu.VMEM((1, rows), jnp.int32),
            pltpu.SemaphoreType.DMA((2 + chunks * (feature_count // tile),)),
        ],
        compiler_params=params(),
        cost_estimate=cost(1, 1),
        name="prepare",
    )(
        weights,
        pltpu.with_memory_space_constraint(features, pltpu.HBM),
        pltpu.with_memory_space_constraint(labels.reshape(1, rows), pltpu.HBM),
        counts,
        active,
    )
    return kept, low, target, norm


def arriving_kernel(count, pieces, start, *refs):
    parts, w_ref = refs[:count], refs[count]
    plain_ref, outs = refs[-pieces - 1], refs[-pieces:]
    done = start
    for part in parts:
        plain_ref[done : done + part.shape[0], :] = part[...]
        done += part.shape[0]
    columns = 256
    for first in range(0, w_ref.shape[1], columns):
        own = slice(first, first + columns)
        found = jnp.dot(plain_ref[start:done, :], w_ref[:, own], preferred_element_type=F32)
        for k, out in enumerate(outs):
            out[:, own] = found[k * out.shape[0] : (k + 1) * out.shape[0], :]


def arriving_logits(parts, w_low, plain, start, all_rows, piece, tokens):
    rows = sum(p.shape[0] for p in parts)
    pieces, count = rows // piece, len(parts)
    plain, *logits = pl.pallas_call(
        functools.partial(arriving_kernel, count, pieces, start),
        out_shape=(pltpu.VMEM((all_rows, w_low.shape[0]), BF16),)
        + (jax.ShapeDtypeStruct((piece, w_low.shape[1]), F32),) * pieces,
        in_specs=[VMEM] * (count + 1 + len(plain)) + [ANY] * len(tokens),
        out_specs=(VMEM,) * (pieces + 1),
        input_output_aliases={count + 1: 0} if plain else {},
        compiler_params=params(),
        cost_estimate=cost(1, 1),
        name="arriving_logits",
    )(*parts, w_low, *plain, *tokens)
    return plain, logits


def turn_kernel(start, rows, plain_ref, *refs):
    turned_ref, squares_ref = refs[-2:]
    at = slice(start, start + rows)
    block = plain_ref[at, :].T
    turned_ref[:, at] = block
    squares_ref[:, at] = block * block


def turn(plain, start, rows, buffers):
    buffer = pltpu.VMEM(plain.shape[::-1], BF16)
    return pl.pallas_call(
        functools.partial(turn_kernel, start, rows),
        out_shape=(buffer, buffer),
        in_specs=[VMEM] * (1 + len(buffers)),
        out_specs=(VMEM, VMEM),
        input_output_aliases={1: 0, 2: 1} if buffers else {},
        compiler_params=params(),
        cost_estimate=cost(1, 1),
        name="turn",
    )(plain, *buffers)


def lane_pack(columns, rows):
    lane = lax.broadcasted_iota(jnp.int32, (rows, LANES), 1)
    packed = jnp.zeros((rows, LANES), F32)
    for k, column in enumerate(columns):
        packed = jnp.where(lane == k, column, packed)
    return packed


def put_stats(packed, place, shape):
    lines = packed.T
    line = jnp.concatenate([lines[k : k + 1, :] for k in range(3)], axis=1)
    here = lax.broadcasted_iota(jnp.int32, shape, 0) == place
    return jnp.where(here, line, 0.0)


def first_stats_kernel(slot, pieces, earlier, last, tokens, *refs):
    own, other = refs[:pieces], refs[pieces : 2 * pieces]
    active_ref, refs = refs[2 * pieces], refs[2 * pieces + 1 :]
    lines = refs[: 3 * last]
    older = refs[3 * last : 3 * last + earlier]
    outs = refs[3 * last + earlier + tokens :]
    e_ref, stats_ref, pack_ref = outs[0], outs[1], outs[-1]
    rows, classes = e_ref.shape
    active, place = active_ref[0], lax.axis_index("example")
    class_start = place * classes
    index = class_start + lax.broadcasted_iota(jnp.int32, (1, classes), 1)
    live = index < active
    for k in range(rows // STEP):
        at = slice(k * STEP, (k + 1) * STEP)
        piece, first = k * STEP // own[0].shape[0], k * STEP % own[0].shape[0]
        here = slice(first, first + STEP)
        logits = jnp.where(live, own[piece][here, :] + other[piece][here, :], NEGATIVE)
        peak = jnp.max(logits, axis=1, keepdims=True)
        e = jnp.exp(logits - peak)
        e_ref[at, :] = e
        total = jnp.sum(e, axis=1, keepdims=True)
        square = jnp.sum(e * e, axis=1, keepdims=True)
        pack_ref[at, :] = lane_pack((peak, total, square), STEP)
    shape = stats_ref.shape
    n = shape[0]
    stats = older[0][...] if earlier else jnp.zeros(shape, F32)
    for k in range(rows // LANES):
        stats += put_stats(pack_ref[k * LANES : (k + 1) * LANES, :], block_of(place, slot + k, n), shape)
    stats_ref[...] = stats
    if last:
        copies_ref = outs[2]
        target, norm = lines[0][...], lines[1][...] + lines[2][...]
        wide = [jnp.broadcast_to(line, (shape[0], LANES)) for line in (target, norm)]
        full = jnp.concatenate([stats] + wide, axis=1)
        copies_ref[...] = jnp.broadcast_to(full[None], copies_ref.shape)


def first_stats(own, other, active, slot, n, earlier, side, tokens):
    pieces, classes = len(own), own[0].shape[1]
    rows = pieces * own[0].shape[0]
    last = len(side) > 0
    shapes = [jax.ShapeDtypeStruct((rows, classes), F32), jax.ShapeDtypeStruct((n, 3 * LANES), F32)]
    if last:
        shapes.append(jax.ShapeDtypeStruct((n, n, 5 * LANES), F32))
    extra = list(side) + list(earlier)
    return pl.pallas_call(
        functools.partial(
            first_stats_kernel, slot, pieces, len(earlier), last, len(tokens)
        ),
        out_shape=tuple(shapes),
        in_specs=[VMEM] * (2 * pieces) + [SMEM] + [VMEM] * len(extra) + [ANY] * len(tokens),
        out_specs=(VMEM,) * len(shapes),
        scratch_shapes=[pltpu.VMEM((rows, LANES), F32)],
        compiler_params=params(),
        cost_estimate=cost(1, 1),
        name="first_stats",
    )(*own, *other, active, *extra, *tokens)


def combine(own_ref, all_ref):
    n = all_ref.shape[0]
    part = lambda d, k: all_ref[d, :, k * LANES : (k + 1) * LANES]
    peaks = [part(d, 0) for d in range(n)]
    peak = functools.reduce(jnp.maximum, peaks)
    scales = [jnp.exp(p - peak) for p in peaks]
    total = sum(part(d, 1) * scales[d] for d in range(n))
    own_scale = jnp.exp(own_ref[:, 0:LANES] - peak)
    return part, peak, scales, total, own_scale


def to_slots(value, line_ref, place):
    n = value.shape[0]
    line_ref[...] = value
    return jnp.concatenate([line_ref[pl.ds(block_of(place, j, n), 1), :] for j in range(n)], axis=0)


def to_columns(lines):
    stacked = jnp.concatenate(lines, axis=0)
    rest = jnp.zeros((LANES - stacked.shape[0], LANES), F32)
    return jnp.concatenate([stacked, rest], axis=0).T


def first_weights_kernel(entries, parts, own_ref, all_ref, *refs):
    e_refs = refs[:parts]
    residual_ref, fisher_ref, damping_ref, target_ref, column_ref, line_ref = refs[parts:]
    n = all_ref.shape[0]
    classes = residual_ref.shape[1]
    place = lax.axis_index("example")
    class_start = place * classes
    part, peak, scales, total, own_scale = combine(own_ref, all_ref)
    square = sum(part(d, 2) * (scales[d] * scales[d]) for d in range(n))
    inverse = 1.0 / total
    spread = 1.0 - square * inverse * inverse
    target = jnp.concatenate([all_ref[d, 0:1, 3 * LANES : 4 * LANES] for d in range(n)], axis=0)
    norm = jnp.concatenate([all_ref[d, 0:1, 4 * LANES : 5 * LANES] for d in range(n)], axis=0)
    valid = (target >= 0.0).astype(F32)
    share = valid / jnp.sum(valid)
    fisher_sum = jnp.sum(norm * share * spread)
    damping_ref[...] = jnp.full(
        damping_ref.shape, DAMPING_SHARE * fisher_sum / entries + EPSILON, F32
    )
    factor = to_slots(own_scale * inverse, line_ref, place)
    share = to_slots(share, line_ref, place)
    target = to_slots(target, line_ref, place)
    target_ref[...] = target
    column_ref[...] = to_columns([factor, share, target])
    index = class_start + lax.broadcasted_iota(jnp.int32, (1, classes), 1)
    done = 0
    for e_ref in e_refs:
        for k in range(e_ref.shape[0] // LANES):
            j = done + k

            def step(i, _, j=j, k=k, e_ref=e_ref):
                start = i * STEP
                at = pl.ds(j * LANES + start, STEP)
                column = column_ref[pl.ds(start, STEP), :]
                e = e_ref[pl.ds(k * LANES + start, STEP), :]
                probability = e * column[:, j : j + 1]
                hit = index == column[:, 2 * n + j : 2 * n + j + 1].astype(jnp.int32)
                part = column[:, n + j : n + j + 1]
                residual_ref[at, :] = (part * (probability - hit.astype(F32))).astype(BF16)
                fisher_ref[at, :] = (part * probability * (1.0 - probability)).astype(BF16)
                return 0

            for i in range(LANES // STEP):
                step(i, 0)
        done += e_ref.shape[0] // LANES


def first_weights(own, every, e_parts, entries):
    n = own.shape[0]
    classes = e_parts[0].shape[1]
    weight = pltpu.VMEM((n * LANES, classes), BF16)
    return pl.pallas_call(
        functools.partial(first_weights_kernel, float(entries), len(e_parts)),
        out_shape=(
            weight,
            weight,
            jax.ShapeDtypeStruct((8, LANES), F32),
            jax.ShapeDtypeStruct((n, LANES), F32),
        ),
        in_specs=[VMEM] * (2 + len(e_parts)),
        out_specs=(VMEM,) * 4,
        scratch_shapes=[pltpu.VMEM((LANES, LANES), F32), pltpu.VMEM((n, LANES), F32)],
        compiler_params=params(),
        cost_estimate=cost(0, 8 * n * LANES * classes),
        name="first_weights",
    )(own, every, *e_parts)


def update_kernel(start, tile, turned_ref, squares_ref, w_ref, residual_ref, fisher_ref,
                  damping_ref, moved_ref, inverse_ref, low_ref):
    features, columns = moved_ref.shape
    damping = damping_ref[0:1, 0:1]
    own = slice(start, start + columns)
    for k in range(features // tile):
        at = slice(k * tile, (k + 1) * tile)
        fisher = jnp.dot(squares_ref[at, :], fisher_ref[:, own], preferred_element_type=F32)
        gradient = jnp.dot(turned_ref[at, :], residual_ref[:, own], preferred_element_type=F32)
        inverse = 1.0 / (fisher + damping)
        change = gradient * inverse
        inverse_ref[at, :] = inverse
        low_ref[at, :] = (w_ref[at, :] - LEARNING_RATE * change).astype(BF16)
        moved_ref[at, :] = -change


def update(turned, squares, weights, residual, fisher_weight, damping, start):
    features, rows = turned.shape
    columns = weights.shape[1]
    return pl.pallas_call(
        functools.partial(update_kernel, start, 512),
        out_shape=(
            pltpu.VMEM((features, columns), F32),
            pltpu.VMEM((features, columns), F32),
            pltpu.VMEM((features, columns), BF16),
        ),
        in_specs=[VMEM] * 6,
        out_specs=(VMEM, VMEM, VMEM),
        input_output_aliases={2: 0},
        compiler_params=params(),
        cost_estimate=cost(4 * rows * features * columns),
        name="update",
    )(turned, squares, weights, residual, fisher_weight, damping)


def next_logits_kernel(start, tile, plain_ref, low_ref, out_ref):
    for first in range(0, out_ref.shape[0], tile):
        out_ref[first : first + tile, :] = jnp.dot(
            plain_ref[start + first : start + first + tile, :],
            low_ref[...],
            preferred_element_type=F32,
        )


def next_logits(plain, low, start, rows):
    features, columns = low.shape
    return pl.pallas_call(
        functools.partial(next_logits_kernel, start, min(512, rows)),
        out_shape=jax.ShapeDtypeStruct((rows, columns), F32),
        in_specs=[VMEM, VMEM],
        out_specs=VMEM,
        compiler_params=params(),
        cost_estimate=cost(2 * rows * features * columns),
        name="next_logits",
    )(plain, low)


def last_stats_kernel(slot, last, pieces, offsets, earlier, *refs):
    own, other = refs[:pieces], refs[pieces : 2 * pieces]
    target_ref, active_ref = refs[2 * pieces : 2 * pieces + 2]
    older = refs[2 * pieces + 2 : 2 * pieces + 2 + earlier]
    outs = refs[2 * pieces + 2 + earlier :]
    e_ref, stats_ref, pack_ref, column_ref = outs[0], outs[1], outs[-2], outs[-1]
    rows, classes = e_ref.shape
    active, place = active_ref[0], lax.axis_index("example")
    class_start = place * classes
    n = stats_ref.shape[0]
    column_ref[...] = to_columns([target_ref[...]])
    index = class_start + lax.broadcasted_iota(jnp.int32, (1, classes), 1)
    live = index < active
    for k in range(rows // LANES):
        def step(i, _, k=k):
            start = i * STEP

            def rows_of(base):
                return pl.ds(base + k * LANES + start, STEP)

            logits = jnp.concatenate(
                [a[rows_of(o), :] + b[rows_of(o), :] for a, b, o in zip(own, other, offsets)],
                axis=1,
            )
            column = column_ref[pl.ds(start, STEP), slot + k : slot + k + 1]
            hit = index == column.astype(jnp.int32)
            label = jnp.sum(jnp.where(hit, logits, 0.0), axis=1, keepdims=True)
            logits = jnp.where(live, logits, NEGATIVE)
            peak = jnp.max(logits, axis=1, keepdims=True)
            e = jnp.exp(logits - peak)
            e_ref[rows_of(0), :] = e
            total = jnp.sum(e, axis=1, keepdims=True)
            pack_ref[rows_of(0), :] = lane_pack((peak, total, label), STEP)
            return 0

        for i in range(LANES // STEP):
            step(i, 0)
    shape = stats_ref.shape
    n = shape[0]
    stats = older[0][...] if earlier else jnp.zeros(shape, F32)
    for k in range(rows // LANES):
        stats += put_stats(pack_ref[k * LANES : (k + 1) * LANES, :], block_of(place, slot + k, n), shape)
    stats_ref[...] = stats
    if last:
        outs[2][...] = jnp.broadcast_to(stats[None], outs[2].shape)


def last_stats(own, other, offsets, target, active, slot, rows, n, earlier):
    classes = sum(c.shape[1] for c in own)
    last = slot + rows // LANES == n
    shapes = [
        jax.ShapeDtypeStruct((rows, classes), F32),
        jax.ShapeDtypeStruct((n, 3 * LANES), F32),
    ]
    if last:
        shapes.append(jax.ShapeDtypeStruct((n, n, 3 * LANES), F32))
    return pl.pallas_call(
        functools.partial(
            last_stats_kernel, slot, last, len(own), tuple(offsets), len(earlier)
        ),
        out_shape=tuple(shapes),
        in_specs=[VMEM] * (2 * len(own) + 1) + [SMEM] + [VMEM] * len(earlier),
        out_specs=(VMEM,) * len(shapes),
        scratch_shapes=[pltpu.VMEM((rows, LANES), F32), pltpu.VMEM((LANES, LANES), F32)],
        compiler_params=params(),
        cost_estimate=cost(0, 24 * rows * classes),
        name="last_stats",
    )(*own, *other, target, active, *earlier)


def finish_kernel(chunks, e_parts, tile, own_ref, all_ref, target_ref, turned_ref, *refs):
    e_refs = refs[:e_parts]
    refs = refs[e_parts:]
    moved_refs, inverse_refs = refs[:chunks], refs[chunks : 2 * chunks]
    out_ref, loss_ref, residual_ref, column_ref, line_ref, held_ref, sems = refs[2 * chunks :]
    n = all_ref.shape[0]
    classes = residual_ref.shape[1]
    place = lax.axis_index("example")
    class_start = place * classes
    part, peak, scales, total, own_scale = combine(own_ref, all_ref)
    label = sum(part(d, 2) for d in range(n))
    target = target_ref[...]
    valid = (target >= 0.0).astype(F32)
    share = valid / jnp.sum(valid)
    losses = to_slots(peak + jnp.log(total) - label, line_ref, place)
    loss_ref[...] = (valid * losses)[0:1, :]
    factor = to_slots(own_scale / total, line_ref, place)
    column_ref[...] = to_columns([factor, share, target])
    index = class_start + lax.broadcasted_iota(jnp.int32, (1, classes), 1)
    done = 0
    for e_ref in e_refs:
        for k in range(e_ref.shape[0] // LANES):
            j = done + k

            def step(i, _, j=j, k=k, e_ref=e_ref):
                start = i * STEP
                at = pl.ds(j * LANES + start, STEP)
                column = column_ref[pl.ds(start, STEP), :]
                e = e_ref[pl.ds(k * LANES + start, STEP), :]
                probability = e * column[:, j : j + 1]
                hit = index == column[:, 2 * n + j : 2 * n + j + 1].astype(jnp.int32)
                part = column[:, n + j : n + j + 1]
                residual_ref[at, :] = (part * (probability - hit.astype(F32))).astype(BF16)
                return 0

            for i in range(LANES // STEP):
                step(i, 0)
        done += e_ref.shape[0] // LANES

    copies = []
    for k in range(out_ref.shape[0] // tile):
        at = slice(k * tile, (k + 1) * tile)
        done = 0
        for moved_ref, inverse_ref in zip(moved_refs, inverse_refs):
            own = slice(done, done + moved_ref.shape[1])
            gradient = jnp.dot(
                turned_ref[at, :], residual_ref[:, own], preferred_element_type=F32
            )
            held_ref[k, :, own] = moved_ref[at, :] - gradient * inverse_ref[at, :]
            done += moved_ref.shape[1]
        copies.append(pltpu.make_async_copy(held_ref.at[k], out_ref.at[at, :], sems.at[k]))
        copies[-1].start()
    for copy in copies:
        copy.wait()


def finish(own, every, target, e_parts, turned, moved, inverse):
    n = own.shape[0]
    features, all_rows = turned.shape
    classes = e_parts[0].shape[1]
    tile = 512
    return pl.pallas_call(
        functools.partial(finish_kernel, len(moved), len(e_parts), tile),
        out_shape=(
            jax.ShapeDtypeStruct((features, classes), F32),
            jax.ShapeDtypeStruct((1, LANES), F32),
        ),
        in_specs=[VMEM] * (4 + len(e_parts) + 2 * len(moved)),
        out_specs=(ANY, VMEM),
        scratch_shapes=[
            pltpu.VMEM((all_rows, classes), BF16),
            pltpu.VMEM((LANES, LANES), F32),
            pltpu.VMEM((n, LANES), F32),
            pltpu.VMEM((features // tile, tile, classes), F32),
            pltpu.SemaphoreType.DMA((features // tile,)),
        ],
        compiler_params=params(16),
        cost_estimate=cost(2 * all_rows * features * classes),
        name="finish",
    )(own, every, target, turned, *e_parts, *moved, *inverse)


def exchange(copies):
    return lax.all_to_all(copies, "example", 0, 0)


def body(n, n_cls, features, weights, labels, counts, active):
    rows = features.shape[0]
    all_rows = rows * n
    feature_count, classes = weights.shape
    entries = feature_count * n_cls * classes * n
    weights = pltpu.with_memory_space_constraint(weights, pltpu.HBM)
    columns = min(512, classes)
    kept, w_low, target, norm = prepare(weights, features, labels, counts, active, columns)
    slots, waits, w_low, gates = gather_blocks(features, n, w_low)
    side = (target, norm, swap(norm, "cls", n_cls, 1))

    groups = [[k, k + 1] for k in range(0, n - 2, 2)] + [[n - 2], [n - 1]]
    count = len(groups)
    behind = max(count - 3, 0)
    plain, buffers, logits, e_parts, stats = (), (), [], [], []

    def statistics(g, tokens):
        last = g == count - 1
        other = [swap(piece, "cls", n_cls, 1) for piece in logits[g]]
        e, found, *copies = first_stats(
            logits[g], other, active, groups[g][0], n, tuple(stats[-1:]),
            side if last else (), tokens,
        )
        e_parts.append(e)
        stats.append(found)
        return copies

    for g in range(count):
        if g == count - 1 and behind:
            logits[behind:], slots[-1] = lax.optimization_barrier((logits[behind:], slots[-1]))
        parts = [part for slot in groups[g] for part in slots[slot]]
        tokens = tuple(stats[-1:]) + tuple(buffers[:1]) + tuple(waits[g] if g < n // 2 else ())
        start = groups[g][0] * rows
        piece = STEP if g < behind else LANES
        block, found = arriving_logits(parts, w_low, plain, start, all_rows, piece, tokens)
        plain = (block,)
        logits.append(found)
        if g < n // 2 - 1:
            buffers = turn(block, start, 2 * rows, buffers)
        if g < behind:
            logits[g], _ = lax.optimization_barrier((logits[g], gates[g]))
            statistics(g, ())
    plain = plain[0]
    turned, squares = turn(plain, (n - 2) * rows, 2 * rows, buffers)
    for g in range(behind, count):
        copies = statistics(g, (logits[-1][0], turned))
    own_stats = stats[-1]
    every = exchange(copies[0])
    residual, fisher_weight, damping, target = first_weights(own_stats, every, e_parts, entries)

    moved, inverse, own, other = [], [], [], []
    for start in range(0, classes, columns):
        a, b, low = update(
            turned, squares, kept[start // columns], residual, fisher_weight, damping, start
        )
        moved.append(a)
        inverse.append(b)
        if start + columns < classes:
            own.append(next_logits(plain, low, 0, all_rows))
            other.append(swap(own[-1], "cls", n_cls, 1))
    half = n // 2
    late = [next_logits(plain, low, first * rows, half * rows) for first in (0, half)]
    late_other = [swap(c, "cls", n_cls, 1) for c in late]
    e_parts, earlier = [], ()
    for first, c, d in zip((0, half), late, late_other):
        offsets = [first * rows] * len(own) + [0]
        e, own_stats, *copies = last_stats(
            own + [c], other + [d], offsets, target, active, first, half * rows, n, earlier
        )
        e_parts.append(e)
        earlier = (own_stats,)
    every = exchange(copies[0])
    out, losses = finish(own_stats, every, target, e_parts, turned, moved, inverse)
    return out, losses.reshape(rows)


def solution(mesh):
    return jax.shard_map(
        functools.partial(body, mesh.shape["example"], mesh.shape["cls"]),
        mesh=mesh,
        in_specs=(
            P(("groups", "example"), "cls"),
            P(("groups", "cls"), "example"),
            P(("groups", "example")),
            P(("groups", "example")),
            P("groups"),
        ),
        out_specs=(P(("groups", "cls"), "example"), P(("groups", "example"))),
        check_vma=False,
    )
```

```python
import functools

import jax
import jax.numpy as jnp
from jax import lax
from jax.experimental import pallas as pl
from jax.experimental.pallas import tpu as pltpu
from jax.sharding import PartitionSpec as P

ITERS = 2
NEGATIVE = -1e30
LEARNING_RATE = 2e-05
DAMPING_SHARE = 0.1
EPSILON = 1e-06

F32 = jnp.float32
BF16 = jnp.bfloat16
VMEM = pl.BlockSpec(memory_space=pltpu.VMEM)
SMEM = pl.BlockSpec(memory_space=pltpu.SMEM)
HBM = pl.BlockSpec(memory_space=pltpu.HBM)
ANY = pl.BlockSpec(memory_space=pl.ANY)
STEP = 64
LANES = 128


def params(mib=10):
    return pltpu.CompilerParams(vmem_limit_bytes=mib << 20)


def cost(flops=0, nbytes=0):
    return pl.CostEstimate(flops=int(flops), bytes_accessed=int(nbytes), transcendentals=0)


def swap(x, axis, n, offset):
    return lax.ppermute(x, axis, [(i, i ^ offset) for i in range(n)])


def gray(v):
    return v ^ (v >> 1)


def block_of(place, slot, n):
    if n != 8:
        return lax.rem(place + n - slot, n)
    z, y = place // 2, place % 2
    return gray((gray(z) + 4 - slot // 2) & 3) * 2 + (y ^ (slot % 2))


def relay_kernel(*refs):
    refs[-1][...] = refs[0][...]


def relay(block, tokens):
    return pl.pallas_call(
        relay_kernel,
        out_shape=pltpu.VMEM(block.shape, block.dtype),
        in_specs=[VMEM] + [ANY] * len(tokens),
        out_specs=VMEM,
        compiler_params=params(),
        cost_estimate=cost(1, 1),
        name="relay",
    )(block, *tokens)


def gather_blocks(x, n, early):
    if n != 8:
        ring = [(i, (i + 1) % n) for i in range(n)]
        slots = [x]
        for _ in range(n - 1):
            slots.append(lax.ppermute(slots[-1], "example", ring))
        return [[slot] for slot in slots], [()] * (n // 2), early, [slot for slot in slots[3::2]]
    hops = ((0, 1), (1, 3), (3, 2), (2, 0))
    ring = [(a * 2 + y, b * 2 + y) for a, b in hops for y in range(2)]
    tie = lax.optimization_barrier
    rows = x.shape[0] // 2
    held, ready = [x[:rows], x[rows:]], [x[:rows], x[rows:]]
    slots = []
    for step in range(3):
        across, later = [], []
        for k in range(2):
            later.append(lax.ppermute(held[k], "example", ring))
            across.append(swap(ready[k], "example", n, 1))
        slots += [held, list(across)]
        if step == 0:
            later[0], early = tie((later[0], early))
        if step < 2:
            ready = [tie((up, over))[0] for up, over in zip(later, across)]
        held = later
    upper = relay(held[0], (held[1], across[0], across[1]))
    lower = relay(across[1], (upper,))
    last = [swap(upper, "example", n, 1), lax.ppermute(lower, "example", ring)]
    slots += [held, last]
    return slots, [tuple(slots[2 * k + 2]) for k in range(3)] + [()], early, [slots[3][1], upper]


def prepare_kernel(tile, chunks, w_ref, x_ref, labels_ref, counts_ref, active_ref, *refs):
    kept = refs[:chunks]
    low_ref, target_ref, norm_ref, block_ref, label_ref, sems = refs[chunks:]
    first = [
        pltpu.make_async_copy(x_ref, block_ref, sems.at[0]),
        pltpu.make_async_copy(labels_ref, label_ref, sems.at[1]),
    ]
    copies = []
    for k in range(w_ref.shape[0] // tile):
        at = slice(k * tile, (k + 1) * tile)
        for c, keep in enumerate(kept):
            own = slice(c * keep.shape[1], (c + 1) * keep.shape[1])
            copy = pltpu.make_async_copy(
                w_ref.at[at, own], keep.at[at, :], sems.at[2 + len(copies)]
            )
            copies.append((copy, keep, at, own))
    for copy in first + [c[0] for c in copies]:
        copy.start()
    for copy in first:
        copy.wait()
    rows = x_ref.shape[0]
    slot = lax.broadcasted_iota(jnp.int32, (1, rows), 1)
    target = jnp.where(slot < counts_ref[0], label_ref[...] % active_ref[0], -1)
    target_ref[...] = target.astype(F32)
    squares = (block_ref[...] * block_ref[...]).astype(F32)
    norm = jnp.sum(squares, axis=1, keepdims=True)
    norm_ref[...] = jnp.broadcast_to(norm, (rows, LANES)).T[0:1, :]
    for copy, keep, at, own in copies:
        copy.wait()
        low_ref[at, own] = keep[at, :].astype(BF16)


def prepare(weights, features, labels, counts, active, columns):
    rows = features.shape[0]
    feature_count, classes = weights.shape
    tile, chunks = 256, classes // columns
    line = jax.ShapeDtypeStruct((1, rows), F32)
    *kept, low, target, norm = pl.pallas_call(
        functools.partial(prepare_kernel, tile, chunks),
        out_shape=(pltpu.VMEM((feature_count, columns), F32),) * chunks
        + (pltpu.VMEM((feature_count, classes), BF16), line, line),
        in_specs=[HBM, HBM, HBM, SMEM, SMEM],
        out_specs=(VMEM,) * (chunks + 3),
        scratch_shapes=[
            pltpu.VMEM(features.shape, BF16),
            pltpu.VMEM((1, rows), jnp.int32),
            pltpu.SemaphoreType.DMA((2 + chunks * (feature_count // tile),)),
        ],
        compiler_params=params(),
        cost_estimate=cost(1, 1),
        name="prepare",
    )(
        weights,
        pltpu.with_memory_space_constraint(features, pltpu.HBM),
        pltpu.with_memory_space_constraint(labels.reshape(1, rows), pltpu.HBM),
        counts,
        active,
    )
    return kept, low, target, norm


def arriving_kernel(count, pieces, start, *refs):
    parts, w_ref = refs[:count], refs[count]
    plain_ref, outs = refs[-pieces - 1], refs[-pieces:]
    done = start
    for part in parts:
        plain_ref[done : done + part.shape[0], :] = part[...]
        done += part.shape[0]
    columns = 256
    for first in range(0, w_ref.shape[1], columns):
        own = slice(first, first + columns)
        found = jnp.dot(plain_ref[start:done, :], w_ref[:, own], preferred_element_type=F32)
        for k, out in enumerate(outs):
            out[:, own] = found[k * out.shape[0] : (k + 1) * out.shape[0], :]


def arriving_logits(parts, w_low, plain, start, all_rows, piece, tokens):
    rows = sum(p.shape[0] for p in parts)
    pieces, count = rows // piece, len(parts)
    plain, *logits = pl.pallas_call(
        functools.partial(arriving_kernel, count, pieces, start),
        out_shape=(pltpu.VMEM((all_rows, w_low.shape[0]), BF16),)
        + (jax.ShapeDtypeStruct((piece, w_low.shape[1]), F32),) * pieces,
        in_specs=[VMEM] * (count + 1 + len(plain)) + [ANY] * len(tokens),
        out_specs=(VMEM,) * (pieces + 1),
        input_output_aliases={count + 1: 0} if plain else {},
        compiler_params=params(),
        cost_estimate=cost(1, 1),
        name="arriving_logits",
    )(*parts, w_low, *plain, *tokens)
    return plain, logits


def turn_kernel(start, rows, plain_ref, *refs):
    turned_ref, squares_ref = refs[-2:]
    at = slice(start, start + rows)
    block = plain_ref[at, :].T
    turned_ref[:, at] = block
    squares_ref[:, at] = block * block


def turn(plain, start, rows, buffers):
    buffer = pltpu.VMEM(plain.shape[::-1], BF16)
    return pl.pallas_call(
        functools.partial(turn_kernel, start, rows),
        out_shape=(buffer, buffer),
        in_specs=[VMEM] * (1 + len(buffers)),
        out_specs=(VMEM, VMEM),
        input_output_aliases={1: 0, 2: 1} if buffers else {},
        compiler_params=params(),
        cost_estimate=cost(1, 1),
        name="turn",
    )(plain, *buffers)


def lane_pack(columns, rows):
    lane = lax.broadcasted_iota(jnp.int32, (rows, LANES), 1)
    packed = jnp.zeros((rows, LANES), F32)
    for k, column in enumerate(columns):
        packed = jnp.where(lane == k, column, packed)
    return packed


def put_stats(packed, place, shape):
    lines = packed.T
    line = jnp.concatenate([lines[k : k + 1, :] for k in range(3)], axis=1)
    here = lax.broadcasted_iota(jnp.int32, shape, 0) == place
    return jnp.where(here, line, 0.0)


def first_stats_kernel(slot, pieces, earlier, last, tokens, *refs):
    own, other = refs[:pieces], refs[pieces : 2 * pieces]
    active_ref, refs = refs[2 * pieces], refs[2 * pieces + 1 :]
    lines = refs[: 3 * last]
    older = refs[3 * last : 3 * last + earlier]
    outs = refs[3 * last + earlier + tokens :]
    e_ref, stats_ref, pack_ref = outs[0], outs[1], outs[-1]
    rows, classes = e_ref.shape
    active, place = active_ref[0], lax.axis_index("example")
    class_start = place * classes
    index = class_start + lax.broadcasted_iota(jnp.int32, (1, classes), 1)
    live = index < active
    for k in range(rows // STEP):
        at = slice(k * STEP, (k + 1) * STEP)
        piece, first = k * STEP // own[0].shape[0], k * STEP % own[0].shape[0]
        here = slice(first, first + STEP)
        logits = jnp.where(live, own[piece][here, :] + other[piece][here, :], NEGATIVE)
        peak = jnp.max(logits, axis=1, keepdims=True)
        e = jnp.exp(logits - peak)
        e_ref[at, :] = e
        total = jnp.sum(e, axis=1, keepdims=True)
        square = jnp.sum(e * e, axis=1, keepdims=True)
        pack_ref[at, :] = lane_pack((peak, total, square), STEP)
    shape = stats_ref.shape
    n = shape[0]
    stats = older[0][...] if earlier else jnp.zeros(shape, F32)
    for k in range(rows // LANES):
        stats += put_stats(pack_ref[k * LANES : (k + 1) * LANES, :], block_of(place, slot + k, n), shape)
    stats_ref[...] = stats
    if last:
        copies_ref = outs[2]
        target, norm = lines[0][...], lines[1][...] + lines[2][...]
        wide = [jnp.broadcast_to(line, (shape[0], LANES)) for line in (target, norm)]
        full = jnp.concatenate([stats] + wide, axis=1)
        copies_ref[...] = jnp.broadcast_to(full[None], copies_ref.shape)


def first_stats(own, other, active, slot, n, earlier, side, tokens):
    pieces, classes = len(own), own[0].shape[1]
    rows = pieces * own[0].shape[0]
    last = len(side) > 0
    shapes = [jax.ShapeDtypeStruct((rows, classes), F32), jax.ShapeDtypeStruct((n, 3 * LANES), F32)]
    if last:
        shapes.append(jax.ShapeDtypeStruct((n, n, 5 * LANES), F32))
    extra = list(side) + list(earlier)
    return pl.pallas_call(
        functools.partial(
            first_stats_kernel, slot, pieces, len(earlier), last, len(tokens)
        ),
        out_shape=tuple(shapes),
        in_specs=[VMEM] * (2 * pieces) + [SMEM] + [VMEM] * len(extra) + [ANY] * len(tokens),
        out_specs=(VMEM,) * len(shapes),
        scratch_shapes=[pltpu.VMEM((rows, LANES), F32)],
        compiler_params=params(),
        cost_estimate=cost(1, 1),
        name="first_stats",
    )(*own, *other, active, *extra, *tokens)


def combine(own_ref, all_ref):
    n = all_ref.shape[0]
    part = lambda d, k: all_ref[d, :, k * LANES : (k + 1) * LANES]
    peaks = [part(d, 0) for d in range(n)]
    peak = functools.reduce(jnp.maximum, peaks)
    scales = [jnp.exp(p - peak) for p in peaks]
    total = sum(part(d, 1) * scales[d] for d in range(n))
    own_scale = jnp.exp(own_ref[:, 0:LANES] - peak)
    return part, peak, scales, total, own_scale


def to_slots(value, line_ref, place):
    n = value.shape[0]
    line_ref[...] = value
    return jnp.concatenate([line_ref[pl.ds(block_of(place, j, n), 1), :] for j in range(n)], axis=0)


def to_columns(lines):
    stacked = jnp.concatenate(lines, axis=0)
    rest = jnp.zeros((LANES - stacked.shape[0], LANES), F32)
    return jnp.concatenate([stacked, rest], axis=0).T


def first_weights_kernel(entries, parts, own_ref, all_ref, *refs):
    e_refs = refs[:parts]
    residual_ref, fisher_ref, damping_ref, target_ref, column_ref, line_ref = refs[parts:]
    n = all_ref.shape[0]
    classes = residual_ref.shape[1]
    place = lax.axis_index("example")
    class_start = place * classes
    part, peak, scales, total, own_scale = combine(own_ref, all_ref)
    square = sum(part(d, 2) * (scales[d] * scales[d]) for d in range(n))
    inverse = 1.0 / total
    spread = 1.0 - square * inverse * inverse
    target = jnp.concatenate([all_ref[d, 0:1, 3 * LANES : 4 * LANES] for d in range(n)], axis=0)
    norm = jnp.concatenate([all_ref[d, 0:1, 4 * LANES : 5 * LANES] for d in range(n)], axis=0)
    valid = (target >= 0.0).astype(F32)
    share = valid / jnp.sum(valid)
    fisher_sum = jnp.sum(norm * share * spread)
    damping_ref[...] = jnp.full(
        damping_ref.shape, DAMPING_SHARE * fisher_sum / entries + EPSILON, F32
    )
    factor = to_slots(own_scale * inverse, line_ref, place)
    share = to_slots(share, line_ref, place)
    target = to_slots(target, line_ref, place)
    target_ref[...] = target
    column_ref[...] = to_columns([factor, share, target])
    index = class_start + lax.broadcasted_iota(jnp.int32, (1, classes), 1)
    done = 0
    for e_ref in e_refs:
        for k in range(e_ref.shape[0] // LANES):
            j = done + k

            def step(i, _, j=j, k=k, e_ref=e_ref):
                start = i * STEP
                at = pl.ds(j * LANES + start, STEP)
                column = column_ref[pl.ds(start, STEP), :]
                e = e_ref[pl.ds(k * LANES + start, STEP), :]
                probability = e * column[:, j : j + 1]
                hit = index == column[:, 2 * n + j : 2 * n + j + 1].astype(jnp.int32)
                part = column[:, n + j : n + j + 1]
                residual_ref[at, :] = (part * (probability - hit.astype(F32))).astype(BF16)
                fisher_ref[at, :] = (part * probability * (1.0 - probability)).astype(BF16)
                return 0

            for i in range(LANES // STEP):
                step(i, 0)
        done += e_ref.shape[0] // LANES


def first_weights(own, every, e_parts, entries):
    n = own.shape[0]
    classes = e_parts[0].shape[1]
    weight = pltpu.VMEM((n * LANES, classes), BF16)
    return pl.pallas_call(
        functools.partial(first_weights_kernel, float(entries), len(e_parts)),
        out_shape=(
            weight,
            weight,
            jax.ShapeDtypeStruct((8, LANES), F32),
            jax.ShapeDtypeStruct((n, LANES), F32),
        ),
        in_specs=[VMEM] * (2 + len(e_parts)),
        out_specs=(VMEM,) * 4,
        scratch_shapes=[pltpu.VMEM((LANES, LANES), F32), pltpu.VMEM((n, LANES), F32)],
        compiler_params=params(),
        cost_estimate=cost(0, 8 * n * LANES * classes),
        name="first_weights",
    )(own, every, *e_parts)


def update_kernel(start, tile, turned_ref, squares_ref, w_ref, residual_ref, fisher_ref,
                  damping_ref, moved_ref, inverse_ref, low_ref):
    features, columns = moved_ref.shape
    damping = damping_ref[0:1, 0:1]
    own = slice(start, start + columns)
    for k in range(features // tile):
        at = slice(k * tile, (k + 1) * tile)
        fisher = jnp.dot(squares_ref[at, :], fisher_ref[:, own], preferred_element_type=F32)
        gradient = jnp.dot(turned_ref[at, :], residual_ref[:, own], preferred_element_type=F32)
        inverse = 1.0 / (fisher + damping)
        change = gradient * inverse
        inverse_ref[at, :] = inverse
        low_ref[at, :] = (w_ref[at, :] - LEARNING_RATE * change).astype(BF16)
        moved_ref[at, :] = -change


def update(turned, squares, weights, residual, fisher_weight, damping, start):
    features, rows = turned.shape
    columns = weights.shape[1]
    return pl.pallas_call(
        functools.partial(update_kernel, start, 512),
        out_shape=(
            pltpu.VMEM((features, columns), F32),
            pltpu.VMEM((features, columns), F32),
            pltpu.VMEM((features, columns), BF16),
        ),
        in_specs=[VMEM] * 6,
        out_specs=(VMEM, VMEM, VMEM),
        input_output_aliases={2: 0},
        compiler_params=params(),
        cost_estimate=cost(4 * rows * features * columns),
        name="update",
    )(turned, squares, weights, residual, fisher_weight, damping)


def next_logits_kernel(start, tile, plain_ref, low_ref, out_ref):
    for first in range(0, out_ref.shape[0], tile):
        out_ref[first : first + tile, :] = jnp.dot(
            plain_ref[start + first : start + first + tile, :],
            low_ref[...],
            preferred_element_type=F32,
        )


def next_logits(plain, low, start, rows):
    features, columns = low.shape
    return pl.pallas_call(
        functools.partial(next_logits_kernel, start, min(512, rows)),
        out_shape=jax.ShapeDtypeStruct((rows, columns), F32),
        in_specs=[VMEM, VMEM],
        out_specs=VMEM,
        compiler_params=params(),
        cost_estimate=cost(2 * rows * features * columns),
        name="next_logits",
    )(plain, low)


def last_stats_kernel(slot, last, pieces, offsets, earlier, *refs):
    own, other = refs[:pieces], refs[pieces : 2 * pieces]
    target_ref, active_ref = refs[2 * pieces : 2 * pieces + 2]
    older = refs[2 * pieces + 2 : 2 * pieces + 2 + earlier]
    outs = refs[2 * pieces + 2 + earlier :]
    e_ref, stats_ref, pack_ref, column_ref = outs[0], outs[1], outs[-2], outs[-1]
    rows, classes = e_ref.shape
    active, place = active_ref[0], lax.axis_index("example")
    class_start = place * classes
    n = stats_ref.shape[0]
    column_ref[...] = to_columns([target_ref[...]])
    index = class_start + lax.broadcasted_iota(jnp.int32, (1, classes), 1)
    live = index < active
    for k in range(rows // LANES):
        def step(i, _, k=k):
            start = i * STEP

            def rows_of(base):
                return pl.ds(base + k * LANES + start, STEP)

            logits = jnp.concatenate(
                [a[rows_of(o), :] + b[rows_of(o), :] for a, b, o in zip(own, other, offsets)],
                axis=1,
            )
            column = column_ref[pl.ds(start, STEP), slot + k : slot + k + 1]
            hit = index == column.astype(jnp.int32)
            label = jnp.sum(jnp.where(hit, logits, 0.0), axis=1, keepdims=True)
            logits = jnp.where(live, logits, NEGATIVE)
            peak = jnp.max(logits, axis=1, keepdims=True)
            e = jnp.exp(logits - peak)
            e_ref[rows_of(0), :] = e
            total = jnp.sum(e, axis=1, keepdims=True)
            pack_ref[rows_of(0), :] = lane_pack((peak, total, label), STEP)
            return 0

        for i in range(LANES // STEP):
            step(i, 0)
    shape = stats_ref.shape
    n = shape[0]
    stats = older[0][...] if earlier else jnp.zeros(shape, F32)
    for k in range(rows // LANES):
        stats += put_stats(pack_ref[k * LANES : (k + 1) * LANES, :], block_of(place, slot + k, n), shape)
    stats_ref[...] = stats
    if last:
        outs[2][...] = jnp.broadcast_to(stats[None], outs[2].shape)


def last_stats(own, other, offsets, target, active, slot, rows, n, earlier):
    classes = sum(c.shape[1] for c in own)
    last = slot + rows // LANES == n
    shapes = [
        jax.ShapeDtypeStruct((rows, classes), F32),
        jax.ShapeDtypeStruct((n, 3 * LANES), F32),
    ]
    if last:
        shapes.append(jax.ShapeDtypeStruct((n, n, 3 * LANES), F32))
    return pl.pallas_call(
        functools.partial(
            last_stats_kernel, slot, last, len(own), tuple(offsets), len(earlier)
        ),
        out_shape=tuple(shapes),
        in_specs=[VMEM] * (2 * len(own) + 1) + [SMEM] + [VMEM] * len(earlier),
        out_specs=(VMEM,) * len(shapes),
        scratch_shapes=[pltpu.VMEM((rows, LANES), F32), pltpu.VMEM((LANES, LANES), F32)],
        compiler_params=params(),
        cost_estimate=cost(0, 24 * rows * classes),
        name="last_stats",
    )(*own, *other, target, active, *earlier)


def finish_kernel(chunks, e_parts, tile, own_ref, all_ref, target_ref, turned_ref, *refs):
    e_refs = refs[:e_parts]
    refs = refs[e_parts:]
    moved_refs, inverse_refs = refs[:chunks], refs[chunks : 2 * chunks]
    out_ref, loss_ref, residual_ref, column_ref, line_ref, held_ref, sems = refs[2 * chunks :]
    n = all_ref.shape[0]
    classes = residual_ref.shape[1]
    place = lax.axis_index("example")
    class_start = place * classes
    part, peak, scales, total, own_scale = combine(own_ref, all_ref)
    label = sum(part(d, 2) for d in range(n))
    target = target_ref[...]
    valid = (target >= 0.0).astype(F32)
    share = valid / jnp.sum(valid)
    losses = to_slots(peak + jnp.log(total) - label, line_ref, place)
    loss_ref[...] = (valid * losses)[0:1, :]
    factor = to_slots(own_scale / total, line_ref, place)
    column_ref[...] = to_columns([factor, share, target])
    index = class_start + lax.broadcasted_iota(jnp.int32, (1, classes), 1)
    done = 0
    for e_ref in e_refs:
        for k in range(e_ref.shape[0] // LANES):
            j = done + k

            def step(i, _, j=j, k=k, e_ref=e_ref):
                start = i * STEP
                at = pl.ds(j * LANES + start, STEP)
                column = column_ref[pl.ds(start, STEP), :]
                e = e_ref[pl.ds(k * LANES + start, STEP), :]
                probability = e * column[:, j : j + 1]
                hit = index == column[:, 2 * n + j : 2 * n + j + 1].astype(jnp.int32)
                part = column[:, n + j : n + j + 1]
                residual_ref[at, :] = (part * (probability - hit.astype(F32))).astype(BF16)
                return 0

            for i in range(LANES // STEP):
                step(i, 0)
        done += e_ref.shape[0] // LANES

    copies = []
    for k in range(out_ref.shape[0] // tile):
        at = slice(k * tile, (k + 1) * tile)
        done = 0
        for moved_ref, inverse_ref in zip(moved_refs, inverse_refs):
            own = slice(done, done + moved_ref.shape[1])
            gradient = jnp.dot(
                turned_ref[at, :], residual_ref[:, own], preferred_element_type=F32
            )
            held_ref[k, :, own] = moved_ref[at, :] - gradient * inverse_ref[at, :]
            done += moved_ref.shape[1]
        copies.append(pltpu.make_async_copy(held_ref.at[k], out_ref.at[at, :], sems.at[k]))
        copies[-1].start()
    for copy in copies:
        copy.wait()


def finish(own, every, target, e_parts, turned, moved, inverse):
    n = own.shape[0]
    features, all_rows = turned.shape
    classes = e_parts[0].shape[1]
    tile = 512
    return pl.pallas_call(
        functools.partial(finish_kernel, len(moved), len(e_parts), tile),
        out_shape=(
            jax.ShapeDtypeStruct((features, classes), F32),
            jax.ShapeDtypeStruct((1, LANES), F32),
        ),
        in_specs=[VMEM] * (4 + len(e_parts) + 2 * len(moved)),
        out_specs=(ANY, VMEM),
        scratch_shapes=[
            pltpu.VMEM((all_rows, classes), BF16),
            pltpu.VMEM((LANES, LANES), F32),
            pltpu.VMEM((n, LANES), F32),
            pltpu.VMEM((features // tile, tile, classes), F32),
            pltpu.SemaphoreType.DMA((features // tile,)),
        ],
        compiler_params=params(16),
        cost_estimate=cost(2 * all_rows * features * classes),
        name="finish",
    )(own, every, target, turned, *e_parts, *moved, *inverse)


def exchange(copies):
    return lax.all_to_all(copies, "example", 0, 0)


def body(n, n_cls, features, weights, labels, counts, active):
    rows = features.shape[0]
    all_rows = rows * n
    feature_count, classes = weights.shape
    entries = feature_count * n_cls * classes * n
    weights = pltpu.with_memory_space_constraint(weights, pltpu.HBM)
    columns = min(512, classes)
    kept, w_low, target, norm = prepare(weights, features, labels, counts, active, columns)
    slots, waits, w_low, gates = gather_blocks(features, n, w_low)
    side = (target, norm, swap(norm, "cls", n_cls, 1))

    groups = [[k, k + 1] for k in range(0, n - 2, 2)] + [[n - 2], [n - 1]]
    count = len(groups)
    behind = max(count - 3, 0)
    plain, buffers, logits, e_parts, stats = (), (), [], [], []

    def statistics(g, tokens):
        last = g == count - 1
        other = [swap(piece, "cls", n_cls, 1) for piece in logits[g]]
        e, found, *copies = first_stats(
            logits[g], other, active, groups[g][0], n, tuple(stats[-1:]),
            side if last else (), tokens,
        )
        e_parts.append(e)
        stats.append(found)
        return copies

    for g in range(count):
        if g == count - 1 and behind:
            logits[behind:], slots[-1] = lax.optimization_barrier((logits[behind:], slots[-1]))
        parts = [part for slot in groups[g] for part in slots[slot]]
        tokens = tuple(stats[-1:]) + tuple(buffers[:1]) + tuple(waits[g] if g < n // 2 else ())
        start = groups[g][0] * rows
        piece = STEP if g < behind else LANES
        block, found = arriving_logits(parts, w_low, plain, start, all_rows, piece, tokens)
        plain = (block,)
        logits.append(found)
        if g < n // 2 - 1:
            buffers = turn(block, start, 2 * rows, buffers)
        if g < behind:
            logits[g], _ = lax.optimization_barrier((logits[g], gates[g]))
            statistics(g, ())
    plain = plain[0]
    turned, squares = turn(plain, (n - 2) * rows, 2 * rows, buffers)
    for g in range(behind, count):
        copies = statistics(g, (logits[-1][0], turned))
    own_stats = stats[-1]
    every = exchange(copies[0])
    residual, fisher_weight, damping, target = first_weights(own_stats, every, e_parts, entries)

    moved, inverse, own, other = [], [], [], []
    for start in range(0, classes, columns):
        a, b, low = update(
            turned, squares, kept[start // columns], residual, fisher_weight, damping, start
        )
        moved.append(a)
        inverse.append(b)
        if start + columns < classes:
            own.append(next_logits(plain, low, 0, all_rows))
            other.append(swap(own[-1], "cls", n_cls, 1))
    half = n // 2
    late = [next_logits(plain, low, first * rows, half * rows) for first in (0, half)]
    late_other = [swap(c, "cls", n_cls, 1) for c in late]
    e_parts, earlier = [], ()
    for first, c, d in zip((0, half), late, late_other):
        offsets = [first * rows] * len(own) + [0]
        e, own_stats, *copies = last_stats(
            own + [c], other + [d], offsets, target, active, first, half * rows, n, earlier
        )
        e_parts.append(e)
        earlier = (own_stats,)
    every = exchange(copies[0])
    out, losses = finish(own_stats, every, target, e_parts, turned, moved, inverse)
    return out, losses.reshape(rows)


def solution(mesh):
    return jax.shard_map(
        functools.partial(body, mesh.shape["example"], mesh.shape["cls"]),
        mesh=mesh,
        in_specs=(
            P(("groups", "example"), "cls"),
            P(("groups", "cls"), "example"),
            P(("groups", "example")),
            P(("groups", "example")),
            P("groups"),
        ),
        out_specs=(P(("groups", "cls"), "example"), P(("groups", "example"))),
        check_vma=False,
    )
```

```python
import functools

import jax
import jax.numpy as jnp
from jax import lax
from jax.experimental import pallas as pl
from jax.experimental.pallas import tpu as pltpu
from jax.sharding import PartitionSpec as P

ITERS = 2
NEGATIVE = -1e30
LEARNING_RATE = 2e-05
DAMPING_SHARE = 0.1
EPSILON = 1e-06

F32 = jnp.float32
BF16 = jnp.bfloat16
VMEM = pl.BlockSpec(memory_space=pltpu.VMEM)
SMEM = pl.BlockSpec(memory_space=pltpu.SMEM)
HBM = pl.BlockSpec(memory_space=pltpu.HBM)
ANY = pl.BlockSpec(memory_space=pl.ANY)
STEP = 64
LANES = 128


def params(mib=10):
    return pltpu.CompilerParams(vmem_limit_bytes=mib << 20)


def cost(flops=0, nbytes=0):
    return pl.CostEstimate(flops=int(flops), bytes_accessed=int(nbytes), transcendentals=0)


def swap(x, axis, n, offset):
    return lax.ppermute(x, axis, [(i, i ^ offset) for i in range(n)])


def gray(v):
    return v ^ (v >> 1)


def block_of(place, slot, n):
    if n != 8:
        return lax.rem(place + n - slot, n)
    z, y = place // 2, place % 2
    return gray((gray(z) + 4 - slot // 2) & 3) * 2 + (y ^ (slot % 2))


def token_kernel(*refs):
    refs[-1][...] = jnp.zeros_like(refs[-1])


def token(values):
    return pl.pallas_call(
        token_kernel,
        out_shape=jax.ShapeDtypeStruct((8, LANES), F32),
        in_specs=[ANY] * len(values),
        out_specs=VMEM,
        compiler_params=params(),
        cost_estimate=cost(1, 1),
        name="token",
    )(*values)


def relay_kernel(*refs):
    refs[-1][...] = refs[0][...]


def relay(block, tokens):
    return pl.pallas_call(
        relay_kernel,
        out_shape=pltpu.VMEM(block.shape, block.dtype),
        in_specs=[VMEM] + [ANY] * len(tokens),
        out_specs=VMEM,
        compiler_params=params(),
        cost_estimate=cost(1, 1),
        name="relay",
    )(block, *tokens)


def gather_blocks(x, n, early):
    if n != 8:
        ring = [(i, (i + 1) % n) for i in range(n)]
        slots = [x]
        for _ in range(n - 1):
            slots.append(lax.ppermute(slots[-1], "example", ring))
        return [[slot] for slot in slots], [()] * (n // 2), early, [slot for slot in slots[3::2]]
    hops = ((0, 1), (1, 3), (3, 2), (2, 0))
    ring = [(a * 2 + y, b * 2 + y) for a, b in hops for y in range(2)]
    tie = lax.optimization_barrier
    rows = x.shape[0] // 2
    held, ready = [x[:rows], x[rows:]], [x[:rows], x[rows:]]
    slots = []
    for step in range(3):
        across, later = [], []
        for k in range(2):
            later.append(lax.ppermute(held[k], "example", ring))
            across.append(swap(ready[k], "example", n, 1))
        slots += [held, list(across)]
        if step == 0:
            later = [tie((up, early))[0] for up in later]
        if step < 2:
            ready = [tie((up, over))[0] for up, over in zip(later, across)]
        held = later
    seen = token((held[0],))
    seen = token((across[0], seen))
    seen = token((held[1], seen))
    seen = token((across[1], seen))
    lower = relay(across[1], (seen,))
    upper = relay(held[0], (seen,))
    last = [swap(upper, "example", n, 1), lax.ppermute(lower, "example", ring)]
    slots += [held, last]
    return slots, [tuple(slots[2 * k + 2]) for k in range(3)] + [()], early, [slots[3][1], upper]


def prepare_kernel(tile, chunks, w_ref, x_ref, labels_ref, counts_ref, active_ref, *refs):
    kept = refs[:chunks]
    low_ref, target_ref, norm_ref, block_ref, label_ref, sems = refs[chunks:]
    first = [
        pltpu.make_async_copy(x_ref, block_ref, sems.at[0]),
        pltpu.make_async_copy(labels_ref, label_ref, sems.at[1]),
    ]
    copies = []
    for k in range(w_ref.shape[0] // tile):
        at = slice(k * tile, (k + 1) * tile)
        for c, keep in enumerate(kept):
            own = slice(c * keep.shape[1], (c + 1) * keep.shape[1])
            copy = pltpu.make_async_copy(
                w_ref.at[at, own], keep.at[at, :], sems.at[2 + len(copies)]
            )
            copies.append((copy, keep, at, own))
    for copy in first + [c[0] for c in copies]:
        copy.start()
    for copy in first:
        copy.wait()
    rows = x_ref.shape[0]
    slot = lax.broadcasted_iota(jnp.int32, (1, rows), 1)
    target = jnp.where(slot < counts_ref[0], label_ref[...] % active_ref[0], -1)
    target_ref[...] = target.astype(F32)
    squares = (block_ref[...] * block_ref[...]).astype(F32)
    norm = jnp.sum(squares, axis=1, keepdims=True)
    norm_ref[...] = jnp.broadcast_to(norm, (rows, LANES)).T[0:1, :]
    for copy, keep, at, own in copies:
        copy.wait()
        low_ref[at, own] = keep[at, :].astype(BF16)


def prepare(weights, features, labels, counts, active, columns):
    rows = features.shape[0]
    feature_count, classes = weights.shape
    tile, chunks = 256, classes // columns
    line = jax.ShapeDtypeStruct((1, rows), F32)
    *kept, low, target, norm = pl.pallas_call(
        functools.partial(prepare_kernel, tile, chunks),
        out_shape=(pltpu.VMEM((feature_count, columns), F32),) * chunks
        + (pltpu.VMEM((feature_count, classes), BF16), line, line),
        in_specs=[HBM, HBM, HBM, SMEM, SMEM],
        out_specs=(VMEM,) * (chunks + 3),
        scratch_shapes=[
            pltpu.VMEM(features.shape, BF16),
            pltpu.VMEM((1, rows), jnp.int32),
            pltpu.SemaphoreType.DMA((2 + chunks * (feature_count // tile),)),
        ],
        compiler_params=params(),
        cost_estimate=cost(1, 1),
        name="prepare",
    )(
        weights,
        pltpu.with_memory_space_constraint(features, pltpu.HBM),
        pltpu.with_memory_space_constraint(labels.reshape(1, rows), pltpu.HBM),
        counts,
        active,
    )
    return kept, low, target, norm


def arriving_kernel(count, pieces, start, *refs):
    parts, w_ref = refs[:count], refs[count]
    plain_ref, outs = refs[-pieces - 1], refs[-pieces:]
    done = start
    for part in parts:
        plain_ref[done : done + part.shape[0], :] = part[...]
        done += part.shape[0]
    columns = 256
    for first in range(0, w_ref.shape[1], columns):
        own = slice(first, first + columns)
        found = jnp.dot(plain_ref[start:done, :], w_ref[:, own], preferred_element_type=F32)
        for k, out in enumerate(outs):
            out[:, own] = found[k * out.shape[0] : (k + 1) * out.shape[0], :]


def arriving_logits(parts, w_low, plain, start, all_rows, piece, tokens):
    rows = sum(p.shape[0] for p in parts)
    pieces, count = rows // piece, len(parts)
    plain, *logits = pl.pallas_call(
        functools.partial(arriving_kernel, count, pieces, start),
        out_shape=(pltpu.VMEM((all_rows, w_low.shape[0]), BF16),)
        + (jax.ShapeDtypeStruct((piece, w_low.shape[1]), F32),) * pieces,
        in_specs=[VMEM] * (count + 1 + len(plain)) + [ANY] * len(tokens),
        out_specs=(VMEM,) * (pieces + 1),
        input_output_aliases={count + 1: 0} if plain else {},
        compiler_params=params(),
        cost_estimate=cost(1, 1),
        name="arriving_logits",
    )(*parts, w_low, *plain, *tokens)
    return plain, logits


def turn_kernel(start, rows, plain_ref, *refs):
    turned_ref, squares_ref = refs[-2:]
    at = slice(start, start + rows)
    block = plain_ref[at, :].T
    turned_ref[:, at] = block
    squares_ref[:, at] = block * block


def turn(plain, start, rows, buffers):
    buffer = pltpu.VMEM(plain.shape[::-1], BF16)
    return pl.pallas_call(
        functools.partial(turn_kernel, start, rows),
        out_shape=(buffer, buffer),
        in_specs=[VMEM] * (1 + len(buffers)),
        out_specs=(VMEM, VMEM),
        input_output_aliases={1: 0, 2: 1} if buffers else {},
        compiler_params=params(),
        cost_estimate=cost(1, 1),
        name="turn",
    )(plain, *buffers)


def lane_pack(columns, rows):
    lane = lax.broadcasted_iota(jnp.int32, (rows, LANES), 1)
    packed = jnp.zeros((rows, LANES), F32)
    for k, column in enumerate(columns):
        packed = jnp.where(lane == k, column, packed)
    return packed


def put_stats(packed, place, shape):
    lines = packed.T
    line = jnp.concatenate([lines[k : k + 1, :] for k in range(3)], axis=1)
    here = lax.broadcasted_iota(jnp.int32, shape, 0) == place
    return jnp.where(here, line, 0.0)


def first_stats_kernel(slot, pieces, earlier, last, tokens, *refs):
    own, other = refs[:pieces], refs[pieces : 2 * pieces]
    active_ref, refs = refs[2 * pieces], refs[2 * pieces + 1 :]
    lines = refs[: 3 * last]
    older = refs[3 * last : 3 * last + earlier]
    outs = refs[3 * last + earlier + tokens :]
    e_ref, stats_ref, pack_ref = outs[0], outs[1], outs[-1]
    rows, classes = e_ref.shape
    active, place = active_ref[0], lax.axis_index("example")
    class_start = place * classes
    index = class_start + lax.broadcasted_iota(jnp.int32, (1, classes), 1)
    live = index < active
    for k in range(rows // STEP):
        at = slice(k * STEP, (k + 1) * STEP)
        piece, first = k * STEP // own[0].shape[0], k * STEP % own[0].shape[0]
        here = slice(first, first + STEP)
        logits = jnp.where(live, own[piece][here, :] + other[piece][here, :], NEGATIVE)
        peak = jnp.max(logits, axis=1, keepdims=True)
        e = jnp.exp(logits - peak)
        e_ref[at, :] = e
        total = jnp.sum(e, axis=1, keepdims=True)
        square = jnp.sum(e * e, axis=1, keepdims=True)
        pack_ref[at, :] = lane_pack((peak, total, square), STEP)
    shape = stats_ref.shape
    n = shape[0]
    stats = older[0][...] if earlier else jnp.zeros(shape, F32)
    for k in range(rows // LANES):
        stats += put_stats(pack_ref[k * LANES : (k + 1) * LANES, :], block_of(place, slot + k, n), shape)
    stats_ref[...] = stats
    if last:
        copies_ref = outs[2]
        target, norm = lines[0][...], lines[1][...] + lines[2][...]
        wide = [jnp.broadcast_to(line, (shape[0], LANES)) for line in (target, norm)]
        full = jnp.concatenate([stats] + wide, axis=1)
        copies_ref[...] = jnp.broadcast_to(full[None], copies_ref.shape)


def first_stats(own, other, active, slot, n, earlier, side, tokens):
    pieces, classes = len(own), own[0].shape[1]
    rows = pieces * own[0].shape[0]
    last = len(side) > 0
    shapes = [jax.ShapeDtypeStruct((rows, classes), F32), jax.ShapeDtypeStruct((n, 3 * LANES), F32)]
    if last:
        shapes.append(jax.ShapeDtypeStruct((n, n, 5 * LANES), F32))
    extra = list(side) + list(earlier)
    return pl.pallas_call(
        functools.partial(
            first_stats_kernel, slot, pieces, len(earlier), last, len(tokens)
        ),
        out_shape=tuple(shapes),
        in_specs=[VMEM] * (2 * pieces) + [SMEM] + [VMEM] * len(extra) + [ANY] * len(tokens),
        out_specs=(VMEM,) * len(shapes),
        scratch_shapes=[pltpu.VMEM((rows, LANES), F32)],
        compiler_params=params(),
        cost_estimate=cost(1, 1),
        name="first_stats",
    )(*own, *other, active, *extra, *tokens)


def combine(own_ref, all_ref):
    n = all_ref.shape[0]
    part = lambda d, k: all_ref[d, :, k * LANES : (k + 1) * LANES]
    peaks = [part(d, 0) for d in range(n)]
    peak = functools.reduce(jnp.maximum, peaks)
    scales = [jnp.exp(p - peak) for p in peaks]
    total = sum(part(d, 1) * scales[d] for d in range(n))
    own_scale = jnp.exp(own_ref[:, 0:LANES] - peak)
    return part, peak, scales, total, own_scale


def to_slots(value, line_ref, place):
    n = value.shape[0]
    line_ref[...] = value
    return jnp.concatenate([line_ref[pl.ds(block_of(place, j, n), 1), :] for j in range(n)], axis=0)


def to_columns(lines):
    stacked = jnp.concatenate(lines, axis=0)
    rest = jnp.zeros((LANES - stacked.shape[0], LANES), F32)
    return jnp.concatenate([stacked, rest], axis=0).T


def first_weights_kernel(entries, parts, own_ref, all_ref, *refs):
    e_refs = refs[:parts]
    residual_ref, fisher_ref, damping_ref, target_ref, column_ref, line_ref = refs[parts:]
    n = all_ref.shape[0]
    classes = residual_ref.shape[1]
    place = lax.axis_index("example")
    class_start = place * classes
    part, peak, scales, total, own_scale = combine(own_ref, all_ref)
    square = sum(part(d, 2) * (scales[d] * scales[d]) for d in range(n))
    inverse = 1.0 / total
    spread = 1.0 - square * inverse * inverse
    target = jnp.concatenate([all_ref[d, 0:1, 3 * LANES : 4 * LANES] for d in range(n)], axis=0)
    norm = jnp.concatenate([all_ref[d, 0:1, 4 * LANES : 5 * LANES] for d in range(n)], axis=0)
    valid = (target >= 0.0).astype(F32)
    share = valid / jnp.sum(valid)
    fisher_sum = jnp.sum(norm * share * spread)
    damping_ref[...] = jnp.full(
        damping_ref.shape, DAMPING_SHARE * fisher_sum / entries + EPSILON, F32
    )
    factor = to_slots(own_scale * inverse, line_ref, place)
    share = to_slots(share, line_ref, place)
    target = to_slots(target, line_ref, place)
    target_ref[...] = target
    column_ref[...] = to_columns([factor, share, target])
    index = class_start + lax.broadcasted_iota(jnp.int32, (1, classes), 1)
    done = 0
    for e_ref in e_refs:
        for k in range(e_ref.shape[0] // LANES):
            j = done + k

            def step(i, _, j=j, k=k, e_ref=e_ref):
                start = i * STEP
                at = pl.ds(j * LANES + start, STEP)
                column = column_ref[pl.ds(start, STEP), :]
                e = e_ref[pl.ds(k * LANES + start, STEP), :]
                probability = e * column[:, j : j + 1]
                hit = index == column[:, 2 * n + j : 2 * n + j + 1].astype(jnp.int32)
                part = column[:, n + j : n + j + 1]
                residual_ref[at, :] = (part * (probability - hit.astype(F32))).astype(BF16)
                fisher_ref[at, :] = (part * probability * (1.0 - probability)).astype(BF16)
                return 0

            for i in range(LANES // STEP):
                step(i, 0)
        done += e_ref.shape[0] // LANES


def first_weights(own, every, e_parts, entries):
    n = own.shape[0]
    classes = e_parts[0].shape[1]
    weight = pltpu.VMEM((n * LANES, classes), BF16)
    return pl.pallas_call(
        functools.partial(first_weights_kernel, float(entries), len(e_parts)),
        out_shape=(
            weight,
            weight,
            jax.ShapeDtypeStruct((8, LANES), F32),
            jax.ShapeDtypeStruct((n, LANES), F32),
        ),
        in_specs=[VMEM] * (2 + len(e_parts)),
        out_specs=(VMEM,) * 4,
        scratch_shapes=[pltpu.VMEM((LANES, LANES), F32), pltpu.VMEM((n, LANES), F32)],
        compiler_params=params(),
        cost_estimate=cost(0, 8 * n * LANES * classes),
        name="first_weights",
    )(own, every, *e_parts)


def update_kernel(start, tile, turned_ref, squares_ref, w_ref, residual_ref, fisher_ref,
                  damping_ref, moved_ref, inverse_ref, low_ref):
    features, columns = moved_ref.shape
    damping = damping_ref[0:1, 0:1]
    own = slice(start, start + columns)
    for k in range(features // tile):
        at = slice(k * tile, (k + 1) * tile)
        fisher = jnp.dot(squares_ref[at, :], fisher_ref[:, own], preferred_element_type=F32)
        gradient = jnp.dot(turned_ref[at, :], residual_ref[:, own], preferred_element_type=F32)
        inverse = 1.0 / (fisher + damping)
        change = gradient * inverse
        inverse_ref[at, :] = inverse
        low_ref[at, :] = (w_ref[at, :] - LEARNING_RATE * change).astype(BF16)
        moved_ref[at, :] = -change


def update(turned, squares, weights, residual, fisher_weight, damping, start):
    features, rows = turned.shape
    columns = weights.shape[1]
    return pl.pallas_call(
        functools.partial(update_kernel, start, 512),
        out_shape=(
            pltpu.VMEM((features, columns), F32),
            pltpu.VMEM((features, columns), F32),
            pltpu.VMEM((features, columns), BF16),
        ),
        in_specs=[VMEM] * 6,
        out_specs=(VMEM, VMEM, VMEM),
        input_output_aliases={2: 0},
        compiler_params=params(),
        cost_estimate=cost(4 * rows * features * columns),
        name="update",
    )(turned, squares, weights, residual, fisher_weight, damping)


def next_logits_kernel(start, tile, plain_ref, low_ref, out_ref):
    for first in range(0, out_ref.shape[0], tile):
        out_ref[first : first + tile, :] = jnp.dot(
            plain_ref[start + first : start + first + tile, :],
            low_ref[...],
            preferred_element_type=F32,
        )


def next_logits(plain, low, start, rows):
    features, columns = low.shape
    return pl.pallas_call(
        functools.partial(next_logits_kernel, start, min(512, rows)),
        out_shape=jax.ShapeDtypeStruct((rows, columns), F32),
        in_specs=[VMEM, VMEM],
        out_specs=VMEM,
        compiler_params=params(),
        cost_estimate=cost(2 * rows * features * columns),
        name="next_logits",
    )(plain, low)


def last_stats_kernel(slot, last, pieces, offsets, earlier, *refs):
    own, other = refs[:pieces], refs[pieces : 2 * pieces]
    target_ref, active_ref = refs[2 * pieces : 2 * pieces + 2]
    older = refs[2 * pieces + 2 : 2 * pieces + 2 + earlier]
    outs = refs[2 * pieces + 2 + earlier :]
    e_ref, stats_ref, pack_ref, column_ref = outs[0], outs[1], outs[-2], outs[-1]
    rows, classes = e_ref.shape
    active, place = active_ref[0], lax.axis_index("example")
    class_start = place * classes
    n = stats_ref.shape[0]
    column_ref[...] = to_columns([target_ref[...]])
    index = class_start + lax.broadcasted_iota(jnp.int32, (1, classes), 1)
    live = index < active
    for k in range(rows // LANES):
        def step(i, _, k=k):
            start = i * STEP

            def rows_of(base):
                return pl.ds(base + k * LANES + start, STEP)

            logits = jnp.concatenate(
                [a[rows_of(o), :] + b[rows_of(o), :] for a, b, o in zip(own, other, offsets)],
                axis=1,
            )
            column = column_ref[pl.ds(start, STEP), slot + k : slot + k + 1]
            hit = index == column.astype(jnp.int32)
            label = jnp.sum(jnp.where(hit, logits, 0.0), axis=1, keepdims=True)
            logits = jnp.where(live, logits, NEGATIVE)
            peak = jnp.max(logits, axis=1, keepdims=True)
            e = jnp.exp(logits - peak)
            e_ref[rows_of(0), :] = e
            total = jnp.sum(e, axis=1, keepdims=True)
            pack_ref[rows_of(0), :] = lane_pack((peak, total, label), STEP)
            return 0

        for i in range(LANES // STEP):
            step(i, 0)
    shape = stats_ref.shape
    n = shape[0]
    stats = older[0][...] if earlier else jnp.zeros(shape, F32)
    for k in range(rows // LANES):
        stats += put_stats(pack_ref[k * LANES : (k + 1) * LANES, :], block_of(place, slot + k, n), shape)
    stats_ref[...] = stats
    if last:
        outs[2][...] = jnp.broadcast_to(stats[None], outs[2].shape)


def last_stats(own, other, offsets, target, active, slot, rows, n, earlier):
    classes = sum(c.shape[1] for c in own)
    last = slot + rows // LANES == n
    shapes = [
        jax.ShapeDtypeStruct((rows, classes), F32),
        jax.ShapeDtypeStruct((n, 3 * LANES), F32),
    ]
    if last:
        shapes.append(jax.ShapeDtypeStruct((n, n, 3 * LANES), F32))
    return pl.pallas_call(
        functools.partial(
            last_stats_kernel, slot, last, len(own), tuple(offsets), len(earlier)
        ),
        out_shape=tuple(shapes),
        in_specs=[VMEM] * (2 * len(own) + 1) + [SMEM] + [VMEM] * len(earlier),
        out_specs=(VMEM,) * len(shapes),
        scratch_shapes=[pltpu.VMEM((rows, LANES), F32), pltpu.VMEM((LANES, LANES), F32)],
        compiler_params=params(),
        cost_estimate=cost(0, 24 * rows * classes),
        name="last_stats",
    )(*own, *other, target, active, *earlier)


def finish_kernel(chunks, e_parts, tile, own_ref, all_ref, target_ref, turned_ref, *refs):
    e_refs = refs[:e_parts]
    refs = refs[e_parts:]
    moved_refs, inverse_refs = refs[:chunks], refs[chunks : 2 * chunks]
    out_ref, loss_ref, residual_ref, column_ref, line_ref, held_ref, sems = refs[2 * chunks :]
    n = all_ref.shape[0]
    classes = residual_ref.shape[1]
    place = lax.axis_index("example")
    class_start = place * classes
    part, peak, scales, total, own_scale = combine(own_ref, all_ref)
    label = sum(part(d, 2) for d in range(n))
    target = target_ref[...]
    valid = (target >= 0.0).astype(F32)
    share = valid / jnp.sum(valid)
    losses = to_slots(peak + jnp.log(total) - label, line_ref, place)
    loss_ref[...] = (valid * losses)[0:1, :]
    factor = to_slots(own_scale / total, line_ref, place)
    column_ref[...] = to_columns([factor, share, target])
    index = class_start + lax.broadcasted_iota(jnp.int32, (1, classes), 1)
    done = 0
    for e_ref in e_refs:
        for k in range(e_ref.shape[0] // LANES):
            j = done + k

            def step(i, _, j=j, k=k, e_ref=e_ref):
                start = i * STEP
                at = pl.ds(j * LANES + start, STEP)
                column = column_ref[pl.ds(start, STEP), :]
                e = e_ref[pl.ds(k * LANES + start, STEP), :]
                probability = e * column[:, j : j + 1]
                hit = index == column[:, 2 * n + j : 2 * n + j + 1].astype(jnp.int32)
                part = column[:, n + j : n + j + 1]
                residual_ref[at, :] = (part * (probability - hit.astype(F32))).astype(BF16)
                return 0

            for i in range(LANES // STEP):
                step(i, 0)
        done += e_ref.shape[0] // LANES

    copies = []
    for k in range(out_ref.shape[0] // tile):
        at = slice(k * tile, (k + 1) * tile)
        done = 0
        for moved_ref, inverse_ref in zip(moved_refs, inverse_refs):
            own = slice(done, done + moved_ref.shape[1])
            gradient = jnp.dot(
                turned_ref[at, :], residual_ref[:, own], preferred_element_type=F32
            )
            held_ref[k, :, own] = moved_ref[at, :] - gradient * inverse_ref[at, :]
            done += moved_ref.shape[1]
        copies.append(pltpu.make_async_copy(held_ref.at[k], out_ref.at[at, :], sems.at[k]))
        copies[-1].start()
    for copy in copies:
        copy.wait()


def finish(own, every, target, e_parts, turned, moved, inverse):
    n = own.shape[0]
    features, all_rows = turned.shape
    classes = e_parts[0].shape[1]
    tile = 512
    return pl.pallas_call(
        functools.partial(finish_kernel, len(moved), len(e_parts), tile),
        out_shape=(
            jax.ShapeDtypeStruct((features, classes), F32),
            jax.ShapeDtypeStruct((1, LANES), F32),
        ),
        in_specs=[VMEM] * (4 + len(e_parts) + 2 * len(moved)),
        out_specs=(ANY, VMEM),
        scratch_shapes=[
            pltpu.VMEM((all_rows, classes), BF16),
            pltpu.VMEM((LANES, LANES), F32),
            pltpu.VMEM((n, LANES), F32),
            pltpu.VMEM((features // tile, tile, classes), F32),
            pltpu.SemaphoreType.DMA((features // tile,)),
        ],
        compiler_params=params(16),
        cost_estimate=cost(2 * all_rows * features * classes),
        name="finish",
    )(own, every, target, turned, *e_parts, *moved, *inverse)


def exchange(copies):
    return lax.all_to_all(copies, "example", 0, 0)


def body(n, n_cls, features, weights, labels, counts, active):
    rows = features.shape[0]
    all_rows = rows * n
    feature_count, classes = weights.shape
    entries = feature_count * n_cls * classes * n
    weights = pltpu.with_memory_space_constraint(weights, pltpu.HBM)
    columns = min(512, classes)
    kept, w_low, target, norm = prepare(weights, features, labels, counts, active, columns)
    slots, waits, w_low, gates = gather_blocks(features, n, w_low)
    side = (target, norm, swap(norm, "cls", n_cls, 1))

    groups = [[k, k + 1] for k in range(0, n - 2, 2)] + [[n - 2], [n - 1]]
    count = len(groups)
    behind = max(count - 3, 0)
    plain, buffers, logits, e_parts, stats = (), (), [], [], []

    def statistics(g, tokens):
        last = g == count - 1
        other = [swap(piece, "cls", n_cls, 1) for piece in logits[g]]
        e, found, *copies = first_stats(
            logits[g], other, active, groups[g][0], n, tuple(stats[-1:]),
            side if last else (), tokens,
        )
        e_parts.append(e)
        stats.append(found)
        return copies

    for g in range(count):
        if g == count - 1 and behind:
            logits[behind:], slots[-1] = lax.optimization_barrier((logits[behind:], slots[-1]))
        parts = [part for slot in groups[g] for part in slots[slot]]
        tokens = tuple(stats[-1:]) + tuple(buffers[:1]) + tuple(waits[g] if g < n // 2 else ())
        start = groups[g][0] * rows
        piece = STEP if g < behind else LANES
        block, found = arriving_logits(parts, w_low, plain, start, all_rows, piece, tokens)
        plain = (block,)
        logits.append(found)
        if g < n // 2 - 1:
            buffers = turn(block, start, 2 * rows, buffers)
        if g < behind:
            logits[g], _ = lax.optimization_barrier((logits[g], gates[g]))
        if g < behind - 1:
            statistics(g, ())
    plain = plain[0]
    turned, squares = turn(plain, (n - 2) * rows, 2 * rows, buffers)
    for g in range(max(behind - 1, 0), count):
        copies = statistics(g, (logits[-1][0], turned))
    own_stats = stats[-1]
    every = exchange(copies[0])
    residual, fisher_weight, damping, target = first_weights(own_stats, every, e_parts, entries)

    moved, inverse, own, other = [], [], [], []
    for start in range(0, classes, columns):
        a, b, low = update(
            turned, squares, kept[start // columns], residual, fisher_weight, damping, start
        )
        moved.append(a)
        inverse.append(b)
        if start + columns < classes:
            own.append(next_logits(plain, low, 0, all_rows))
            other.append(swap(own[-1], "cls", n_cls, 1))
    half = n // 2
    late = [next_logits(plain, low, first * rows, half * rows) for first in (0, half)]
    late_other = [swap(c, "cls", n_cls, 1) for c in late]
    e_parts, earlier = [], ()
    for first, c, d in zip((0, half), late, late_other):
        offsets = [first * rows] * len(own) + [0]
        e, own_stats, *copies = last_stats(
            own + [c], other + [d], offsets, target, active, first, half * rows, n, earlier
        )
        e_parts.append(e)
        earlier = (own_stats,)
    every = exchange(copies[0])
    out, losses = finish(own_stats, every, target, e_parts, turned, moved, inverse)
    return out, losses.reshape(rows)


def solution(mesh):
    return jax.shard_map(
        functools.partial(body, mesh.shape["example"], mesh.shape["cls"]),
        mesh=mesh,
        in_specs=(
            P(("groups", "example"), "cls"),
            P(("groups", "cls"), "example"),
            P(("groups", "example")),
            P(("groups", "example")),
            P("groups"),
        ),
        out_specs=(P(("groups", "cls"), "example"), P(("groups", "example"))),
        check_vma=False,
    )
```

```python
import functools

import jax
import jax.numpy as jnp
from jax import lax
from jax.experimental import pallas as pl
from jax.experimental.pallas import tpu as pltpu
from jax.sharding import PartitionSpec as P

ITERS = 2
NEGATIVE = -1e30
LEARNING_RATE = 2e-05
DAMPING_SHARE = 0.1
EPSILON = 1e-06

F32 = jnp.float32
BF16 = jnp.bfloat16
VMEM = pl.BlockSpec(memory_space=pltpu.VMEM)
SMEM = pl.BlockSpec(memory_space=pltpu.SMEM)
HBM = pl.BlockSpec(memory_space=pltpu.HBM)
ANY = pl.BlockSpec(memory_space=pl.ANY)
STEP = 64
LANES = 128


def params(mib=10):
    return pltpu.CompilerParams(vmem_limit_bytes=mib << 20)


def cost(flops=0, nbytes=0):
    return pl.CostEstimate(flops=int(flops), bytes_accessed=int(nbytes), transcendentals=0)


def swap(x, axis, n, offset):
    return lax.ppermute(x, axis, [(i, i ^ offset) for i in range(n)])


def gray(v):
    return v ^ (v >> 1)


def block_of(place, slot, n):
    if n != 8:
        return lax.rem(place + n - slot, n)
    z, y = place // 2, place % 2
    return gray((gray(z) + 4 - slot // 2) & 3) * 2 + (y ^ (slot % 2))


def token_kernel(*refs):
    refs[-1][...] = jnp.zeros_like(refs[-1])


def token(values):
    return pl.pallas_call(
        token_kernel,
        out_shape=jax.ShapeDtypeStruct((8, LANES), F32),
        in_specs=[ANY] * len(values),
        out_specs=VMEM,
        compiler_params=params(),
        cost_estimate=cost(1, 1),
        name="token",
    )(*values)


def relay_kernel(*refs):
    refs[-1][...] = refs[0][...]


def relay(block, tokens):
    return pl.pallas_call(
        relay_kernel,
        out_shape=pltpu.VMEM(block.shape, block.dtype),
        in_specs=[VMEM] + [ANY] * len(tokens),
        out_specs=VMEM,
        compiler_params=params(),
        cost_estimate=cost(1, 1),
        name="relay",
    )(block, *tokens)


def gather_blocks(x, n, early):
    if n != 8:
        ring = [(i, (i + 1) % n) for i in range(n)]
        slots = [x]
        for _ in range(n - 1):
            slots.append(lax.ppermute(slots[-1], "example", ring))
        return [[slot] for slot in slots], [()] * (n // 2), early, [slot for slot in slots[3::2]]
    hops = ((0, 1), (1, 3), (3, 2), (2, 0))
    ring = [(a * 2 + y, b * 2 + y) for a, b in hops for y in range(2)]
    tie = lax.optimization_barrier
    rows = x.shape[0] // 2
    held, ready = [x[:rows], x[rows:]], [x[:rows], x[rows:]]
    slots = []
    for step in range(3):
        across, later = [], []
        for k in range(2):
            later.append(lax.ppermute(held[k], "example", ring))
            across.append(swap(ready[k], "example", n, 1))
        slots += [held, list(across)]
        if step == 0:
            later = [tie((up, early))[0] for up in later]
        if step < 2:
            ready = [tie((up, over))[0] for up, over in zip(later, across)]
        held = later
    seen = token((held[0],))
    seen = token((across[0], seen))
    seen = token((held[1], seen))
    seen = token((across[1], seen))
    lower = relay(across[1], (seen,))
    upper = relay(held[0], (seen,))
    last = [swap(upper, "example", n, 1), lax.ppermute(lower, "example", ring)]
    slots += [held, last]
    return slots, [tuple(slots[2 * k + 2]) for k in range(3)] + [()], early, [slots[3][1], upper]


def prepare_kernel(tile, chunks, w_ref, x_ref, labels_ref, counts_ref, active_ref, *refs):
    kept = refs[:chunks]
    low_ref, target_ref, norm_ref, block_ref, label_ref, sems = refs[chunks:]
    first = [
        pltpu.make_async_copy(x_ref, block_ref, sems.at[0]),
        pltpu.make_async_copy(labels_ref, label_ref, sems.at[1]),
    ]
    copies = []
    for k in range(w_ref.shape[0] // tile):
        at = slice(k * tile, (k + 1) * tile)
        for c, keep in enumerate(kept):
            own = slice(c * keep.shape[1], (c + 1) * keep.shape[1])
            copy = pltpu.make_async_copy(
                w_ref.at[at, own], keep.at[at, :], sems.at[2 + len(copies)]
            )
            copies.append((copy, keep, at, own))
    for copy in first + [c[0] for c in copies]:
        copy.start()
    for copy in first:
        copy.wait()
    rows = x_ref.shape[0]
    slot = lax.broadcasted_iota(jnp.int32, (1, rows), 1)
    target = jnp.where(slot < counts_ref[0], label_ref[...] % active_ref[0], -1)
    target_ref[...] = target.astype(F32)
    squares = (block_ref[...] * block_ref[...]).astype(F32)
    norm = jnp.sum(squares, axis=1, keepdims=True)
    norm_ref[...] = jnp.broadcast_to(norm, (rows, LANES)).T[0:1, :]
    for copy, keep, at, own in copies:
        copy.wait()
        low_ref[at, own] = keep[at, :].astype(BF16)


def prepare(weights, features, labels, counts, active, columns):
    rows = features.shape[0]
    feature_count, classes = weights.shape
    tile, chunks = 256, classes // columns
    line = jax.ShapeDtypeStruct((1, rows), F32)
    *kept, low, target, norm = pl.pallas_call(
        functools.partial(prepare_kernel, tile, chunks),
        out_shape=(pltpu.VMEM((feature_count, columns), F32),) * chunks
        + (pltpu.VMEM((feature_count, classes), BF16), line, line),
        in_specs=[HBM, HBM, HBM, SMEM, SMEM],
        out_specs=(VMEM,) * (chunks + 3),
        scratch_shapes=[
            pltpu.VMEM(features.shape, BF16),
            pltpu.VMEM((1, rows), jnp.int32),
            pltpu.SemaphoreType.DMA((2 + chunks * (feature_count // tile),)),
        ],
        compiler_params=params(),
        cost_estimate=cost(1, 1),
        name="prepare",
    )(
        weights,
        pltpu.with_memory_space_constraint(features, pltpu.HBM),
        pltpu.with_memory_space_constraint(labels.reshape(1, rows), pltpu.HBM),
        counts,
        active,
    )
    return kept, low, target, norm


def arriving_kernel(count, pieces, start, *refs):
    parts, w_ref = refs[:count], refs[count]
    plain_ref, outs = refs[-pieces - 1], refs[-pieces:]
    done = start
    for part in parts:
        plain_ref[done : done + part.shape[0], :] = part[...]
        done += part.shape[0]
    columns = 256
    for first in range(0, w_ref.shape[1], columns):
        own = slice(first, first + columns)
        found = jnp.dot(plain_ref[start:done, :], w_ref[:, own], preferred_element_type=F32)
        for k, out in enumerate(outs):
            out[:, own] = found[k * out.shape[0] : (k + 1) * out.shape[0], :]


def arriving_logits(parts, w_low, plain, start, all_rows, piece, tokens):
    rows = sum(p.shape[0] for p in parts)
    pieces, count = rows // piece, len(parts)
    plain, *logits = pl.pallas_call(
        functools.partial(arriving_kernel, count, pieces, start),
        out_shape=(pltpu.VMEM((all_rows, w_low.shape[0]), BF16),)
        + (jax.ShapeDtypeStruct((piece, w_low.shape[1]), F32),) * pieces,
        in_specs=[VMEM] * (count + 1 + len(plain)) + [ANY] * len(tokens),
        out_specs=(VMEM,) * (pieces + 1),
        input_output_aliases={count + 1: 0} if plain else {},
        compiler_params=params(),
        cost_estimate=cost(1, 1),
        name="arriving_logits",
    )(*parts, w_low, *plain, *tokens)
    return plain, logits


def turn_kernel(start, rows, plain_ref, *refs):
    turned_ref, squares_ref = refs[-2:]
    at = slice(start, start + rows)
    block = plain_ref[at, :].T
    turned_ref[:, at] = block
    squares_ref[:, at] = block * block


def turn(plain, start, rows, buffers):
    buffer = pltpu.VMEM(plain.shape[::-1], BF16)
    return pl.pallas_call(
        functools.partial(turn_kernel, start, rows),
        out_shape=(buffer, buffer),
        in_specs=[VMEM] * (1 + len(buffers)),
        out_specs=(VMEM, VMEM),
        input_output_aliases={1: 0, 2: 1} if buffers else {},
        compiler_params=params(),
        cost_estimate=cost(1, 1),
        name="turn",
    )(plain, *buffers)


def lane_pack(columns, rows):
    lane = lax.broadcasted_iota(jnp.int32, (rows, LANES), 1)
    packed = jnp.zeros((rows, LANES), F32)
    for k, column in enumerate(columns):
        packed = jnp.where(lane == k, column, packed)
    return packed


def put_stats(packed, place, shape):
    lines = packed.T
    line = jnp.concatenate([lines[k : k + 1, :] for k in range(3)], axis=1)
    here = lax.broadcasted_iota(jnp.int32, shape, 0) == place
    return jnp.where(here, line, 0.0)


def first_stats_kernel(slot, pieces, earlier, last, tokens, *refs):
    own, other = refs[:pieces], refs[pieces : 2 * pieces]
    active_ref, refs = refs[2 * pieces], refs[2 * pieces + 1 :]
    lines = refs[: 3 * last]
    older = refs[3 * last : 3 * last + earlier]
    outs = refs[3 * last + earlier + tokens :]
    e_ref, stats_ref, pack_ref = outs[0], outs[1], outs[-1]
    rows, classes = e_ref.shape
    active, place = active_ref[0], lax.axis_index("example")
    class_start = place * classes
    index = class_start + lax.broadcasted_iota(jnp.int32, (1, classes), 1)
    live = index < active
    for k in range(rows // STEP):
        at = slice(k * STEP, (k + 1) * STEP)
        piece, first = k * STEP // own[0].shape[0], k * STEP % own[0].shape[0]
        here = slice(first, first + STEP)
        logits = jnp.where(live, own[piece][here, :] + other[piece][here, :], NEGATIVE)
        peak = jnp.max(logits, axis=1, keepdims=True)
        e = jnp.exp(logits - peak)
        e_ref[at, :] = e
        total = jnp.sum(e, axis=1, keepdims=True)
        square = jnp.sum(e * e, axis=1, keepdims=True)
        pack_ref[at, :] = lane_pack((peak, total, square), STEP)
    shape = stats_ref.shape
    n = shape[0]
    stats = older[0][...] if earlier else jnp.zeros(shape, F32)
    for k in range(rows // LANES):
        stats += put_stats(pack_ref[k * LANES : (k + 1) * LANES, :], block_of(place, slot + k, n), shape)
    stats_ref[...] = stats
    if last:
        copies_ref = outs[2]
        target, norm = lines[0][...], lines[1][...] + lines[2][...]
        wide = [jnp.broadcast_to(line, (shape[0], LANES)) for line in (target, norm)]
        full = jnp.concatenate([stats] + wide, axis=1)
        copies_ref[...] = jnp.broadcast_to(full[None], copies_ref.shape)


def first_stats(own, other, active, slot, n, earlier, side, tokens):
    pieces, classes = len(own), own[0].shape[1]
    rows = pieces * own[0].shape[0]
    last = len(side) > 0
    shapes = [jax.ShapeDtypeStruct((rows, classes), F32), jax.ShapeDtypeStruct((n, 3 * LANES), F32)]
    if last:
        shapes.append(jax.ShapeDtypeStruct((n, n, 5 * LANES), F32))
    extra = list(side) + list(earlier)
    return pl.pallas_call(
        functools.partial(
            first_stats_kernel, slot, pieces, len(earlier), last, len(tokens)
        ),
        out_shape=tuple(shapes),
        in_specs=[VMEM] * (2 * pieces) + [SMEM] + [VMEM] * len(extra) + [ANY] * len(tokens),
        out_specs=(VMEM,) * len(shapes),
        scratch_shapes=[pltpu.VMEM((rows, LANES), F32)],
        compiler_params=params(),
        cost_estimate=cost(1, 1),
        name="first_stats",
    )(*own, *other, active, *extra, *tokens)


def combine(own_ref, all_ref):
    n = all_ref.shape[0]
    part = lambda d, k: all_ref[d, :, k * LANES : (k + 1) * LANES]
    peaks = [part(d, 0) for d in range(n)]
    peak = functools.reduce(jnp.maximum, peaks)
    scales = [jnp.exp(p - peak) for p in peaks]
    total = sum(part(d, 1) * scales[d] for d in range(n))
    own_scale = jnp.exp(own_ref[:, 0:LANES] - peak)
    return part, peak, scales, total, own_scale


def to_slots(value, line_ref, place):
    n = value.shape[0]
    line_ref[...] = value
    return jnp.concatenate([line_ref[pl.ds(block_of(place, j, n), 1), :] for j in range(n)], axis=0)


def to_columns(lines):
    stacked = jnp.concatenate(lines, axis=0)
    rest = jnp.zeros((LANES - stacked.shape[0], LANES), F32)
    return jnp.concatenate([stacked, rest], axis=0).T


def first_weights_kernel(entries, parts, own_ref, all_ref, *refs):
    e_refs = refs[:parts]
    residual_ref, fisher_ref, damping_ref, target_ref, column_ref, line_ref = refs[parts:]
    n = all_ref.shape[0]
    classes = residual_ref.shape[1]
    place = lax.axis_index("example")
    class_start = place * classes
    part, peak, scales, total, own_scale = combine(own_ref, all_ref)
    square = sum(part(d, 2) * (scales[d] * scales[d]) for d in range(n))
    inverse = 1.0 / total
    spread = 1.0 - square * inverse * inverse
    target = jnp.concatenate([all_ref[d, 0:1, 3 * LANES : 4 * LANES] for d in range(n)], axis=0)
    norm = jnp.concatenate([all_ref[d, 0:1, 4 * LANES : 5 * LANES] for d in range(n)], axis=0)
    valid = (target >= 0.0).astype(F32)
    share = valid / jnp.sum(valid)
    fisher_sum = jnp.sum(norm * share * spread)
    damping_ref[...] = jnp.full(
        damping_ref.shape, DAMPING_SHARE * fisher_sum / entries + EPSILON, F32
    )
    factor = to_slots(own_scale * inverse, line_ref, place)
    share = to_slots(share, line_ref, place)
    target = to_slots(target, line_ref, place)
    target_ref[...] = target
    column_ref[...] = to_columns([factor, share, target])
    index = class_start + lax.broadcasted_iota(jnp.int32, (1, classes), 1)
    done = 0
    for e_ref in e_refs:
        for k in range(e_ref.shape[0] // LANES):
            j = done + k

            def step(i, _, j=j, k=k, e_ref=e_ref):
                start = i * STEP
                at = pl.ds(j * LANES + start, STEP)
                column = column_ref[pl.ds(start, STEP), :]
                e = e_ref[pl.ds(k * LANES + start, STEP), :]
                probability = e * column[:, j : j + 1]
                hit = index == column[:, 2 * n + j : 2 * n + j + 1].astype(jnp.int32)
                part = column[:, n + j : n + j + 1]
                residual_ref[at, :] = (part * (probability - hit.astype(F32))).astype(BF16)
                fisher_ref[at, :] = (part * probability * (1.0 - probability)).astype(BF16)
                return 0

            for i in range(LANES // STEP):
                step(i, 0)
        done += e_ref.shape[0] // LANES


def first_weights(own, every, e_parts, entries):
    n = own.shape[0]
    classes = e_parts[0].shape[1]
    weight = pltpu.VMEM((n * LANES, classes), BF16)
    return pl.pallas_call(
        functools.partial(first_weights_kernel, float(entries), len(e_parts)),
        out_shape=(
            weight,
            weight,
            jax.ShapeDtypeStruct((8, LANES), F32),
            jax.ShapeDtypeStruct((n, LANES), F32),
        ),
        in_specs=[VMEM] * (2 + len(e_parts)),
        out_specs=(VMEM,) * 4,
        scratch_shapes=[pltpu.VMEM((LANES, LANES), F32), pltpu.VMEM((n, LANES), F32)],
        compiler_params=params(),
        cost_estimate=cost(0, 8 * n * LANES * classes),
        name="first_weights",
    )(own, every, *e_parts)


def update_kernel(start, tile, turned_ref, squares_ref, w_ref, residual_ref, fisher_ref,
                  damping_ref, moved_ref, inverse_ref, low_ref):
    features, columns = moved_ref.shape
    damping = damping_ref[0:1, 0:1]
    own = slice(start, start + columns)
    for k in range(features // tile):
        at = slice(k * tile, (k + 1) * tile)
        fisher = jnp.dot(squares_ref[at, :], fisher_ref[:, own], preferred_element_type=F32)
        gradient = jnp.dot(turned_ref[at, :], residual_ref[:, own], preferred_element_type=F32)
        inverse = 1.0 / (fisher + damping)
        change = gradient * inverse
        inverse_ref[at, :] = inverse
        low_ref[at, :] = (w_ref[at, :] - LEARNING_RATE * change).astype(BF16)
        moved_ref[at, :] = -change


def update(turned, squares, weights, residual, fisher_weight, damping, start):
    features, rows = turned.shape
    columns = weights.shape[1]
    return pl.pallas_call(
        functools.partial(update_kernel, start, 512),
        out_shape=(
            pltpu.VMEM((features, columns), F32),
            pltpu.VMEM((features, columns), F32),
            pltpu.VMEM((features, columns), BF16),
        ),
        in_specs=[VMEM] * 6,
        out_specs=(VMEM, VMEM, VMEM),
        input_output_aliases={2: 0},
        compiler_params=params(),
        cost_estimate=cost(4 * rows * features * columns),
        name="update",
    )(turned, squares, weights, residual, fisher_weight, damping)


def next_logits_kernel(start, tile, plain_ref, low_ref, out_ref):
    for first in range(0, out_ref.shape[0], tile):
        out_ref[first : first + tile, :] = jnp.dot(
            plain_ref[start + first : start + first + tile, :],
            low_ref[...],
            preferred_element_type=F32,
        )


def next_logits(plain, low, start, rows):
    features, columns = low.shape
    return pl.pallas_call(
        functools.partial(next_logits_kernel, start, min(512, rows)),
        out_shape=jax.ShapeDtypeStruct((rows, columns), F32),
        in_specs=[VMEM, VMEM],
        out_specs=VMEM,
        compiler_params=params(),
        cost_estimate=cost(2 * rows * features * columns),
        name="next_logits",
    )(plain, low)


def last_stats_kernel(slot, last, pieces, offsets, earlier, *refs):
    own, other = refs[:pieces], refs[pieces : 2 * pieces]
    target_ref, active_ref = refs[2 * pieces : 2 * pieces + 2]
    older = refs[2 * pieces + 2 : 2 * pieces + 2 + earlier]
    outs = refs[2 * pieces + 2 + earlier :]
    e_ref, stats_ref, pack_ref, column_ref = outs[0], outs[1], outs[-2], outs[-1]
    rows, classes = e_ref.shape
    active, place = active_ref[0], lax.axis_index("example")
    class_start = place * classes
    n = stats_ref.shape[0]
    column_ref[...] = to_columns([target_ref[...]])
    index = class_start + lax.broadcasted_iota(jnp.int32, (1, classes), 1)
    live = index < active
    for k in range(rows // LANES):
        def step(i, _, k=k):
            start = i * STEP

            def rows_of(base):
                return pl.ds(base + k * LANES + start, STEP)

            logits = jnp.concatenate(
                [a[rows_of(o), :] + b[rows_of(o), :] for a, b, o in zip(own, other, offsets)],
                axis=1,
            )
            column = column_ref[pl.ds(start, STEP), slot + k : slot + k + 1]
            hit = index == column.astype(jnp.int32)
            label = jnp.sum(jnp.where(hit, logits, 0.0), axis=1, keepdims=True)
            logits = jnp.where(live, logits, NEGATIVE)
            peak = jnp.max(logits, axis=1, keepdims=True)
            e = jnp.exp(logits - peak)
            e_ref[rows_of(0), :] = e
            total = jnp.sum(e, axis=1, keepdims=True)
            pack_ref[rows_of(0), :] = lane_pack((peak, total, label), STEP)
            return 0

        for i in range(LANES // STEP):
            step(i, 0)
    shape = stats_ref.shape
    n = shape[0]
    stats = older[0][...] if earlier else jnp.zeros(shape, F32)
    for k in range(rows // LANES):
        stats += put_stats(pack_ref[k * LANES : (k + 1) * LANES, :], block_of(place, slot + k, n), shape)
    stats_ref[...] = stats
    if last:
        outs[2][...] = jnp.broadcast_to(stats[None], outs[2].shape)


def last_stats(own, other, offsets, target, active, slot, rows, n, earlier):
    classes = sum(c.shape[1] for c in own)
    last = slot + rows // LANES == n
    shapes = [
        jax.ShapeDtypeStruct((rows, classes), F32),
        jax.ShapeDtypeStruct((n, 3 * LANES), F32),
    ]
    if last:
        shapes.append(jax.ShapeDtypeStruct((n, n, 3 * LANES), F32))
    return pl.pallas_call(
        functools.partial(
            last_stats_kernel, slot, last, len(own), tuple(offsets), len(earlier)
        ),
        out_shape=tuple(shapes),
        in_specs=[VMEM] * (2 * len(own) + 1) + [SMEM] + [VMEM] * len(earlier),
        out_specs=(VMEM,) * len(shapes),
        scratch_shapes=[pltpu.VMEM((rows, LANES), F32), pltpu.VMEM((LANES, LANES), F32)],
        compiler_params=params(),
        cost_estimate=cost(0, 24 * rows * classes),
        name="last_stats",
    )(*own, *other, target, active, *earlier)


def finish_kernel(chunks, e_parts, tile, own_ref, all_ref, target_ref, turned_ref, *refs):
    e_refs = refs[:e_parts]
    refs = refs[e_parts:]
    moved_refs, inverse_refs = refs[:chunks], refs[chunks : 2 * chunks]
    out_ref, loss_ref, residual_ref, column_ref, line_ref, held_ref, sems = refs[2 * chunks :]
    n = all_ref.shape[0]
    classes = residual_ref.shape[1]
    place = lax.axis_index("example")
    class_start = place * classes
    part, peak, scales, total, own_scale = combine(own_ref, all_ref)
    label = sum(part(d, 2) for d in range(n))
    target = target_ref[...]
    valid = (target >= 0.0).astype(F32)
    share = valid / jnp.sum(valid)
    losses = to_slots(peak + jnp.log(total) - label, line_ref, place)
    loss_ref[...] = (valid * losses)[0:1, :]
    factor = to_slots(own_scale / total, line_ref, place)
    column_ref[...] = to_columns([factor, share, target])
    index = class_start + lax.broadcasted_iota(jnp.int32, (1, classes), 1)
    done = 0
    for e_ref in e_refs:
        for k in range(e_ref.shape[0] // LANES):
            j = done + k

            def step(i, _, j=j, k=k, e_ref=e_ref):
                start = i * STEP
                at = pl.ds(j * LANES + start, STEP)
                column = column_ref[pl.ds(start, STEP), :]
                e = e_ref[pl.ds(k * LANES + start, STEP), :]
                probability = e * column[:, j : j + 1]
                hit = index == column[:, 2 * n + j : 2 * n + j + 1].astype(jnp.int32)
                part = column[:, n + j : n + j + 1]
                residual_ref[at, :] = (part * (probability - hit.astype(F32))).astype(BF16)
                return 0

            for i in range(LANES // STEP):
                step(i, 0)
        done += e_ref.shape[0] // LANES

    copies = []
    for k in range(out_ref.shape[0] // tile):
        at = slice(k * tile, (k + 1) * tile)
        done = 0
        for moved_ref, inverse_ref in zip(moved_refs, inverse_refs):
            own = slice(done, done + moved_ref.shape[1])
            gradient = jnp.dot(
                turned_ref[at, :], residual_ref[:, own], preferred_element_type=F32
            )
            held_ref[k, :, own] = moved_ref[at, :] - gradient * inverse_ref[at, :]
            done += moved_ref.shape[1]
        copies.append(pltpu.make_async_copy(held_ref.at[k], out_ref.at[at, :], sems.at[k]))
        copies[-1].start()
    for copy in copies:
        copy.wait()


def finish(own, every, target, e_parts, turned, moved, inverse):
    n = own.shape[0]
    features, all_rows = turned.shape
    classes = e_parts[0].shape[1]
    tile = 512
    return pl.pallas_call(
        functools.partial(finish_kernel, len(moved), len(e_parts), tile),
        out_shape=(
            jax.ShapeDtypeStruct((features, classes), F32),
            jax.ShapeDtypeStruct((1, LANES), F32),
        ),
        in_specs=[VMEM] * (4 + len(e_parts) + 2 * len(moved)),
        out_specs=(ANY, VMEM),
        scratch_shapes=[
            pltpu.VMEM((all_rows, classes), BF16),
            pltpu.VMEM((LANES, LANES), F32),
            pltpu.VMEM((n, LANES), F32),
            pltpu.VMEM((features // tile, tile, classes), F32),
            pltpu.SemaphoreType.DMA((features // tile,)),
        ],
        compiler_params=params(16),
        cost_estimate=cost(2 * all_rows * features * classes),
        name="finish",
    )(own, every, target, turned, *e_parts, *moved, *inverse)


def exchange(copies):
    return lax.all_to_all(copies, "example", 0, 0)


def body(n, n_cls, features, weights, labels, counts, active):
    rows = features.shape[0]
    all_rows = rows * n
    feature_count, classes = weights.shape
    entries = feature_count * n_cls * classes * n
    weights = pltpu.with_memory_space_constraint(weights, pltpu.HBM)
    columns = min(512, classes)
    kept, w_low, target, norm = prepare(weights, features, labels, counts, active, columns)
    slots, waits, w_low, gates = gather_blocks(features, n, w_low)
    side = (target, norm, swap(norm, "cls", n_cls, 1))

    groups = [[k, k + 1] for k in range(0, n - 2, 2)] + [[n - 2], [n - 1]]
    count = len(groups)
    behind = max(count - 3, 0)
    plain, buffers, logits, e_parts, stats = (), (), [], [], []

    def statistics(g, tokens):
        last = g == count - 1
        other = [swap(piece, "cls", n_cls, 1) for piece in logits[g]]
        e, found, *copies = first_stats(
            logits[g], other, active, groups[g][0], n, tuple(stats[-1:]),
            side if last else (), tokens,
        )
        e_parts.append(e)
        stats.append(found)
        return copies

    for g in range(count):
        if g == count - 1 and behind:
            logits[behind:], slots[-1] = lax.optimization_barrier((logits[behind:], slots[-1]))
        parts = [part for slot in groups[g] for part in slots[slot]]
        tokens = tuple(stats[-1:]) + tuple(buffers[:1]) + tuple(waits[g] if g < n // 2 else ())
        start = groups[g][0] * rows
        piece = (64,256,256,128,128)[g] if count == 5 else LANES
        block, found = arriving_logits(parts, w_low, plain, start, all_rows, piece, tokens)
        plain = (block,)
        logits.append(found)
        if g < n // 2 - 1:
            buffers = turn(block, start, 2 * rows, buffers)
        if g < behind:
            logits[g], _ = lax.optimization_barrier((logits[g], gates[g]))
        if g < behind - 1:
            statistics(g, ())
    plain = plain[0]
    turned, squares = turn(plain, (n - 2) * rows, 2 * rows, buffers)
    for g in range(max(behind - 1, 0), count):
        copies = statistics(g, (logits[-1][0], turned))
    own_stats = stats[-1]
    every = exchange(copies[0])
    residual, fisher_weight, damping, target = first_weights(own_stats, every, e_parts, entries)

    moved, inverse, own, other = [], [], [], []
    for start in range(0, classes, columns):
        a, b, low = update(
            turned, squares, kept[start // columns], residual, fisher_weight, damping, start
        )
        moved.append(a)
        inverse.append(b)
        if start + columns < classes:
            own.append(next_logits(plain, low, 0, all_rows))
            other.append(swap(own[-1], "cls", n_cls, 1))
    half = n // 2
    late = [next_logits(plain, low, first * rows, half * rows) for first in (0, half)]
    late_other = [swap(c, "cls", n_cls, 1) for c in late]
    e_parts, earlier = [], ()
    for first, c, d in zip((0, half), late, late_other):
        offsets = [first * rows] * len(own) + [0]
        e, own_stats, *copies = last_stats(
            own + [c], other + [d], offsets, target, active, first, half * rows, n, earlier
        )
        e_parts.append(e)
        earlier = (own_stats,)
    every = exchange(copies[0])
    out, losses = finish(own_stats, every, target, e_parts, turned, moved, inverse)
    return out, losses.reshape(rows)


def solution(mesh):
    return jax.shard_map(
        functools.partial(body, mesh.shape["example"], mesh.shape["cls"]),
        mesh=mesh,
        in_specs=(
            P(("groups", "example"), "cls"),
            P(("groups", "cls"), "example"),
            P(("groups", "example")),
            P(("groups", "example")),
            P("groups"),
        ),
        out_specs=(P(("groups", "cls"), "example"), P(("groups", "example"))),
        check_vma=False,
    )
```

```python
import functools

import jax
import jax.numpy as jnp
from jax import lax
from jax.experimental import pallas as pl
from jax.experimental.pallas import tpu as pltpu
from jax.sharding import PartitionSpec as P

ITERS = 2
NEGATIVE = -1e30
LEARNING_RATE = 2e-05
DAMPING_SHARE = 0.1
EPSILON = 1e-06

F32 = jnp.float32
BF16 = jnp.bfloat16
VMEM = pl.BlockSpec(memory_space=pltpu.VMEM)
SMEM = pl.BlockSpec(memory_space=pltpu.SMEM)
HBM = pl.BlockSpec(memory_space=pltpu.HBM)
ANY = pl.BlockSpec(memory_space=pl.ANY)
STEP = 64
LANES = 128


def params(mib=10):
    return pltpu.CompilerParams(vmem_limit_bytes=mib << 20)


def cost(flops=0, nbytes=0):
    return pl.CostEstimate(flops=int(flops), bytes_accessed=int(nbytes), transcendentals=0)


def swap(x, axis, n, offset):
    return lax.ppermute(x, axis, [(i, i ^ offset) for i in range(n)])


def gray(v):
    return v ^ (v >> 1)


def block_of(place, slot, n):
    if n != 8:
        return lax.rem(place + n - slot, n)
    z, y = place // 2, place % 2
    return gray((gray(z) + 4 - slot // 2) & 3) * 2 + (y ^ (slot % 2))


def token_kernel(*refs):
    refs[-1][...] = jnp.zeros_like(refs[-1])


def token(values):
    return pl.pallas_call(
        token_kernel,
        out_shape=jax.ShapeDtypeStruct((8, LANES), F32),
        in_specs=[ANY] * len(values),
        out_specs=VMEM,
        compiler_params=params(),
        cost_estimate=cost(1, 1),
        name="token",
    )(*values)


def relay_kernel(*refs):
    refs[-1][...] = refs[0][...]


def relay(block, tokens):
    return pl.pallas_call(
        relay_kernel,
        out_shape=pltpu.VMEM(block.shape, block.dtype),
        in_specs=[VMEM] + [ANY] * len(tokens),
        out_specs=VMEM,
        compiler_params=params(),
        cost_estimate=cost(1, 1),
        name="relay",
    )(block, *tokens)


def gather_blocks(x, n, early):
    if n != 8:
        ring = [(i, (i + 1) % n) for i in range(n)]
        slots = [x]
        for _ in range(n - 1):
            slots.append(lax.ppermute(slots[-1], "example", ring))
        return [[slot] for slot in slots], [()] * (n // 2), early, [slot for slot in slots[3::2]]
    hops = ((0, 1), (1, 3), (3, 2), (2, 0))
    ring = [(a * 2 + y, b * 2 + y) for a, b in hops for y in range(2)]
    tie = lax.optimization_barrier
    rows = x.shape[0] // 2
    held, ready = [x[:rows], x[rows:]], [x[:rows], x[rows:]]
    slots = []
    for step in range(3):
        across, later = [], []
        for k in range(2):
            later.append(lax.ppermute(held[k], "example", ring))
            across.append(swap(ready[k], "example", n, 1))
        slots += [held, list(across)]
        if step == 0:
            later = [tie((up, early))[0] for up in later]
        if step < 2:
            ready = [tie((up, over))[0] for up, over in zip(later, across)]
        held = later
    seen = token((held[0],))
    seen = token((across[0], seen))
    seen = token((held[1], seen))
    seen = token((across[1], seen))
    lower = relay(across[1], (seen,))
    upper = relay(held[0], (seen,))
    last = [swap(upper, "example", n, 1), lax.ppermute(lower, "example", ring)]
    slots += [held, last]
    return slots, [tuple(slots[2 * k + 2]) for k in range(3)] + [()], early, [slots[3][1], upper]


def prepare_kernel(tile, chunks, w_ref, x_ref, labels_ref, counts_ref, active_ref, *refs):
    kept = refs[:chunks]
    low_ref, target_ref, norm_ref, block_ref, label_ref, sems = refs[chunks:]
    first = [
        pltpu.make_async_copy(x_ref, block_ref, sems.at[0]),
        pltpu.make_async_copy(labels_ref, label_ref, sems.at[1]),
    ]
    copies = []
    for k in range(w_ref.shape[0] // tile):
        at = slice(k * tile, (k + 1) * tile)
        for c, keep in enumerate(kept):
            own = slice(c * keep.shape[1], (c + 1) * keep.shape[1])
            copy = pltpu.make_async_copy(
                w_ref.at[at, own], keep.at[at, :], sems.at[2 + len(copies)]
            )
            copies.append((copy, keep, at, own))
    for copy in first + [c[0] for c in copies]:
        copy.start()
    for copy in first:
        copy.wait()
    rows = x_ref.shape[0]
    slot = lax.broadcasted_iota(jnp.int32, (1, rows), 1)
    target = jnp.where(slot < counts_ref[0], label_ref[...] % active_ref[0], -1)
    target_ref[...] = target.astype(F32)
    squares = (block_ref[...] * block_ref[...]).astype(F32)
    norm = jnp.sum(squares, axis=1, keepdims=True)
    norm_ref[...] = jnp.broadcast_to(norm, (rows, LANES)).T[0:1, :]
    for copy, keep, at, own in copies:
        copy.wait()
        low_ref[at, own] = keep[at, :].astype(BF16)


def prepare(weights, features, labels, counts, active, columns):
    rows = features.shape[0]
    feature_count, classes = weights.shape
    tile, chunks = 256, classes // columns
    line = jax.ShapeDtypeStruct((1, rows), F32)
    *kept, low, target, norm = pl.pallas_call(
        functools.partial(prepare_kernel, tile, chunks),
        out_shape=(pltpu.VMEM((feature_count, columns), F32),) * chunks
        + (pltpu.VMEM((feature_count, classes), BF16), line, line),
        in_specs=[HBM, HBM, HBM, SMEM, SMEM],
        out_specs=(VMEM,) * (chunks + 3),
        scratch_shapes=[
            pltpu.VMEM(features.shape, BF16),
            pltpu.VMEM((1, rows), jnp.int32),
            pltpu.SemaphoreType.DMA((2 + chunks * (feature_count // tile),)),
        ],
        compiler_params=params(),
        cost_estimate=cost(1, 1),
        name="prepare",
    )(
        weights,
        pltpu.with_memory_space_constraint(features, pltpu.HBM),
        pltpu.with_memory_space_constraint(labels.reshape(1, rows), pltpu.HBM),
        counts,
        active,
    )
    return kept, low, target, norm


def arriving_kernel(count, pieces, start, *refs):
    parts, w_ref = refs[:count], refs[count]
    plain_ref, outs = refs[-pieces - 1], refs[-pieces:]
    done = start
    for part in parts:
        plain_ref[done : done + part.shape[0], :] = part[...]
        done += part.shape[0]
    columns = 256
    for first in range(0, w_ref.shape[1], columns):
        own = slice(first, first + columns)
        found = jnp.dot(plain_ref[start:done, :], w_ref[:, own], preferred_element_type=F32)
        for k, out in enumerate(outs):
            out[:, own] = found[k * out.shape[0] : (k + 1) * out.shape[0], :]


def arriving_logits(parts, w_low, plain, start, all_rows, piece, tokens):
    rows = sum(p.shape[0] for p in parts)
    pieces, count = rows // piece, len(parts)
    plain, *logits = pl.pallas_call(
        functools.partial(arriving_kernel, count, pieces, start),
        out_shape=(pltpu.VMEM((all_rows, w_low.shape[0]), BF16),)
        + (jax.ShapeDtypeStruct((piece, w_low.shape[1]), F32),) * pieces,
        in_specs=[VMEM] * (count + 1 + len(plain)) + [ANY] * len(tokens),
        out_specs=(VMEM,) * (pieces + 1),
        input_output_aliases={count + 1: 0} if plain else {},
        compiler_params=params(),
        cost_estimate=cost(1, 1),
        name="arriving_logits",
    )(*parts, w_low, *plain, *tokens)
    return plain, logits


def turn_kernel(start, rows, plain_ref, *refs):
    turned_ref, squares_ref = refs[-2:]
    at = slice(start, start + rows)
    block = plain_ref[at, :].T
    turned_ref[:, at] = block
    squares_ref[:, at] = block * block


def turn(plain, start, rows, buffers):
    buffer = pltpu.VMEM(plain.shape[::-1], BF16)
    return pl.pallas_call(
        functools.partial(turn_kernel, start, rows),
        out_shape=(buffer, buffer),
        in_specs=[VMEM] * (1 + len(buffers)),
        out_specs=(VMEM, VMEM),
        input_output_aliases={1: 0, 2: 1} if buffers else {},
        compiler_params=params(),
        cost_estimate=cost(1, 1),
        name="turn",
    )(plain, *buffers)


def lane_pack(columns, rows):
    lane = lax.broadcasted_iota(jnp.int32, (rows, LANES), 1)
    packed = jnp.zeros((rows, LANES), F32)
    for k, column in enumerate(columns):
        packed = jnp.where(lane == k, column, packed)
    return packed


def put_stats(packed, place, shape):
    lines = packed.T
    line = jnp.concatenate([lines[k : k + 1, :] for k in range(3)], axis=1)
    here = lax.broadcasted_iota(jnp.int32, shape, 0) == place
    return jnp.where(here, line, 0.0)


def first_stats_kernel(slot, pieces, earlier, last, tokens, *refs):
    own, other = refs[:pieces], refs[pieces : 2 * pieces]
    active_ref, refs = refs[2 * pieces], refs[2 * pieces + 1 :]
    lines = refs[: 3 * last]
    older = refs[3 * last : 3 * last + earlier]
    outs = refs[3 * last + earlier + tokens :]
    e_ref, stats_ref, pack_ref = outs[0], outs[1], outs[-1]
    rows, classes = e_ref.shape
    active, place = active_ref[0], lax.axis_index("example")
    class_start = place * classes
    index = class_start + lax.broadcasted_iota(jnp.int32, (1, classes), 1)
    live = index < active
    for k in range(rows // STEP):
        at = slice(k * STEP, (k + 1) * STEP)
        piece, first = k * STEP // own[0].shape[0], k * STEP % own[0].shape[0]
        here = slice(first, first + STEP)
        logits = jnp.where(live, own[piece][here, :] + other[piece][here, :], NEGATIVE)
        peak = jnp.max(logits, axis=1, keepdims=True)
        e = jnp.exp(logits - peak)
        e_ref[at, :] = e
        total = jnp.sum(e, axis=1, keepdims=True)
        square = jnp.sum(e * e, axis=1, keepdims=True)
        pack_ref[at, :] = lane_pack((peak, total, square), STEP)
    shape = stats_ref.shape
    n = shape[0]
    stats = older[0][...] if earlier else jnp.zeros(shape, F32)
    for k in range(rows // LANES):
        stats += put_stats(pack_ref[k * LANES : (k + 1) * LANES, :], block_of(place, slot + k, n), shape)
    stats_ref[...] = stats
    if last:
        copies_ref = outs[2]
        target, norm = lines[0][...], lines[1][...] + lines[2][...]
        wide = [jnp.broadcast_to(line, (shape[0], LANES)) for line in (target, norm)]
        full = jnp.concatenate([stats] + wide, axis=1)
        copies_ref[...] = jnp.broadcast_to(full[None], copies_ref.shape)


def first_stats(own, other, active, slot, n, earlier, side, tokens):
    pieces, classes = len(own), own[0].shape[1]
    rows = pieces * own[0].shape[0]
    last = len(side) > 0
    shapes = [jax.ShapeDtypeStruct((rows, classes), F32), jax.ShapeDtypeStruct((n, 3 * LANES), F32)]
    if last:
        shapes.append(jax.ShapeDtypeStruct((lines_of(n)[0], n, 5 * LANES), F32))
    extra = list(side) + list(earlier)
    return pl.pallas_call(
        functools.partial(
            first_stats_kernel, slot, pieces, len(earlier), last, len(tokens)
        ),
        out_shape=tuple(shapes),
        in_specs=[VMEM] * (2 * pieces) + [SMEM] + [VMEM] * len(extra) + [ANY] * len(tokens),
        out_specs=(VMEM,) * len(shapes),
        scratch_shapes=[pltpu.VMEM((rows, LANES), F32)],
        compiler_params=params(),
        cost_estimate=cost(1, 1),
        name="first_stats",
    )(*own, *other, active, *extra, *tokens)


def lines_of(n):
    return (4, 2) if n == 8 else (n, 1)


def merge_kernel(squares, across, all_ref, out_ref):
    count, n, width = all_ref.shape
    first = lax.rem(lax.axis_index("example"), across)
    part = lambda d, k: all_ref[d, :, k * LANES : (k + 1) * LANES]
    peak = functools.reduce(jnp.maximum, [part(d, 0) for d in range(count)])
    scales = [jnp.exp(part(d, 0) - peak) for d in range(count)]
    weights = [x * x if squares else 1.0 for x in scales]
    out_ref[:, 0:LANES] = peak
    out_ref[:, LANES : 2 * LANES] = sum(part(d, 1) * scales[d] for d in range(count))
    out_ref[:, 2 * LANES : 3 * LANES] = sum(part(d, 2) * weights[d] for d in range(count))
    row = lax.broadcasted_iota(jnp.int32, (n, LANES), 0)
    for k in range(3, width // LANES):
        own = [jnp.where(row == d * across + first, part(d, k), 0.0) for d in range(count)]
        out_ref[:, k * LANES : (k + 1) * LANES] = sum(own)


def exchange(copies, squares):
    count, n, width = copies.shape
    across = lines_of(n)[1]
    groups = [[d * across + y for d in range(count)] for y in range(across)]
    every = lax.all_to_all(copies, "example", 0, 0, axis_index_groups=groups)
    merged = pl.pallas_call(
        functools.partial(merge_kernel, squares, across),
        out_shape=jax.ShapeDtypeStruct((n, width), F32),
        in_specs=[VMEM],
        out_specs=VMEM,
        compiler_params=params(),
        cost_estimate=cost(1, 1),
        name="merge",
    )(every)
    return [merged] + [swap(merged, "example", n, 1)] * (across - 1)


def combine(own_ref, sources):
    part = lambda d, k: sources[d][:, k * LANES : (k + 1) * LANES]
    count = len(sources)
    peak = functools.reduce(jnp.maximum, [part(d, 0) for d in range(count)])
    scales = [jnp.exp(part(d, 0) - peak) for d in range(count)]
    total = sum(part(d, 1) * scales[d] for d in range(count))
    own_scale = jnp.exp(own_ref[:, 0:LANES] - peak)
    return part, peak, scales, total, own_scale


def to_slots(value, line_ref, place):
    n = value.shape[0]
    line_ref[...] = value
    return jnp.concatenate([line_ref[pl.ds(block_of(place, j, n), 1), :] for j in range(n)], axis=0)


def to_columns(lines):
    stacked = jnp.concatenate(lines, axis=0)
    rest = jnp.zeros((LANES - stacked.shape[0], LANES), F32)
    return jnp.concatenate([stacked, rest], axis=0).T


def first_weights_kernel(entries, parts, count, own_ref, *refs):
    sources, refs = refs[:count], refs[count:]
    e_refs = refs[:parts]
    residual_ref, fisher_ref, damping_ref, target_ref, column_ref, line_ref = refs[parts:]
    n = own_ref.shape[0]
    classes = residual_ref.shape[1]
    place = lax.axis_index("example")
    class_start = place * classes
    part, peak, scales, total, own_scale = combine(own_ref, sources)
    square = sum(part(d, 2) * (scales[d] * scales[d]) for d in range(count))
    inverse = 1.0 / total
    spread = 1.0 - square * inverse * inverse
    target = sum(part(d, 3) for d in range(count))
    norm = sum(part(d, 4) for d in range(count))
    valid = (target >= 0.0).astype(F32)
    share = valid / jnp.sum(valid)
    fisher_sum = jnp.sum(norm * share * spread)
    damping_ref[...] = jnp.full(
        damping_ref.shape, DAMPING_SHARE * fisher_sum / entries + EPSILON, F32
    )
    factor = to_slots(own_scale * inverse, line_ref, place)
    share = to_slots(share, line_ref, place)
    target = to_slots(target, line_ref, place)
    target_ref[...] = target
    column_ref[...] = to_columns([factor, share, target])
    index = class_start + lax.broadcasted_iota(jnp.int32, (1, classes), 1)
    done = 0
    for e_ref in e_refs:
        for k in range(e_ref.shape[0] // LANES):
            j = done + k

            def step(i, _, j=j, k=k, e_ref=e_ref):
                start = i * STEP
                at = pl.ds(j * LANES + start, STEP)
                column = column_ref[pl.ds(start, STEP), :]
                e = e_ref[pl.ds(k * LANES + start, STEP), :]
                probability = e * column[:, j : j + 1]
                hit = index == column[:, 2 * n + j : 2 * n + j + 1].astype(jnp.int32)
                part = column[:, n + j : n + j + 1]
                residual_ref[at, :] = (part * (probability - hit.astype(F32))).astype(BF16)
                fisher_ref[at, :] = (part * probability * (1.0 - probability)).astype(BF16)
                return 0

            for i in range(LANES // STEP):
                step(i, 0)
        done += e_ref.shape[0] // LANES


def first_weights(own, every, e_parts, entries):
    n = own.shape[0]
    classes = e_parts[0].shape[1]
    weight = pltpu.VMEM((n * LANES, classes), BF16)
    return pl.pallas_call(
        functools.partial(first_weights_kernel, float(entries), len(e_parts), len(every)),
        out_shape=(
            weight,
            weight,
            jax.ShapeDtypeStruct((8, LANES), F32),
            jax.ShapeDtypeStruct((n, LANES), F32),
        ),
        in_specs=[VMEM] * (1 + len(every) + len(e_parts)),
        out_specs=(VMEM,) * 4,
        scratch_shapes=[pltpu.VMEM((LANES, LANES), F32), pltpu.VMEM((n, LANES), F32)],
        compiler_params=params(),
        cost_estimate=cost(0, 8 * n * LANES * classes),
        name="first_weights",
    )(own, *every, *e_parts)


def update_kernel(start, tile, turned_ref, squares_ref, w_ref, residual_ref, fisher_ref,
                  damping_ref, moved_ref, inverse_ref, low_ref):
    features, columns = moved_ref.shape
    damping = damping_ref[0:1, 0:1]
    own = slice(start, start + columns)

    def settle(k, gradient, fisher):
        at = slice(k * tile, (k + 1) * tile)
        inverse = 1.0 / (fisher + damping)
        change = gradient * inverse
        inverse_ref[at, :] = inverse
        low_ref[at, :] = (w_ref[at, :] - LEARNING_RATE * change).astype(BF16)
        moved_ref[at, :] = -change

    before = None
    for k in range(features // tile):
        at = slice(k * tile, (k + 1) * tile)
        fisher = jnp.dot(squares_ref[at, :], fisher_ref[:, own], preferred_element_type=F32)
        if before is not None:
            settle(*before)
        gradient = jnp.dot(turned_ref[at, :], residual_ref[:, own], preferred_element_type=F32)
        before = (k, gradient, fisher)
    settle(*before)


def update(turned, squares, weights, residual, fisher_weight, damping, start):
    features, rows = turned.shape
    columns = weights.shape[1]
    return pl.pallas_call(
        functools.partial(update_kernel, start, 512),
        out_shape=(
            pltpu.VMEM((features, columns), F32),
            pltpu.VMEM((features, columns), F32),
            pltpu.VMEM((features, columns), BF16),
        ),
        in_specs=[VMEM] * 6,
        out_specs=(VMEM, VMEM, VMEM),
        input_output_aliases={2: 0},
        compiler_params=params(),
        cost_estimate=cost(4 * rows * features * columns),
        name="update",
    )(turned, squares, weights, residual, fisher_weight, damping)


def next_logits_kernel(start, tile, plain_ref, low_ref, out_ref):
    for first in range(0, out_ref.shape[0], tile):
        out_ref[first : first + tile, :] = jnp.dot(
            plain_ref[start + first : start + first + tile, :],
            low_ref[...],
            preferred_element_type=F32,
        )


def next_logits(plain, low, start, rows):
    features, columns = low.shape
    return pl.pallas_call(
        functools.partial(next_logits_kernel, start, min(512, rows)),
        out_shape=jax.ShapeDtypeStruct((rows, columns), F32),
        in_specs=[VMEM, VMEM],
        out_specs=VMEM,
        compiler_params=params(),
        cost_estimate=cost(2 * rows * features * columns),
        name="next_logits",
    )(plain, low)


def last_stats_kernel(slot, last, pieces, offsets, earlier, *refs):
    own, other = refs[:pieces], refs[pieces : 2 * pieces]
    target_ref, active_ref = refs[2 * pieces : 2 * pieces + 2]
    older = refs[2 * pieces + 2 : 2 * pieces + 2 + earlier]
    outs = refs[2 * pieces + 2 + earlier :]
    e_ref, stats_ref, pack_ref, column_ref = outs[0], outs[1], outs[-2], outs[-1]
    rows, classes = e_ref.shape
    active, place = active_ref[0], lax.axis_index("example")
    class_start = place * classes
    n = stats_ref.shape[0]
    column_ref[...] = to_columns([target_ref[...]])
    index = class_start + lax.broadcasted_iota(jnp.int32, (1, classes), 1)
    live = index < active
    for k in range(rows // LANES):
        def step(i, _, k=k):
            start = i * STEP

            def rows_of(base):
                return pl.ds(base + k * LANES + start, STEP)

            logits = jnp.concatenate(
                [a[rows_of(o), :] + b[rows_of(o), :] for a, b, o in zip(own, other, offsets)],
                axis=1,
            )
            column = column_ref[pl.ds(start, STEP), slot + k : slot + k + 1]
            hit = index == column.astype(jnp.int32)
            label = jnp.sum(jnp.where(hit, logits, 0.0), axis=1, keepdims=True)
            logits = jnp.where(live, logits, NEGATIVE)
            peak = jnp.max(logits, axis=1, keepdims=True)
            e = jnp.exp(logits - peak)
            e_ref[rows_of(0), :] = e
            total = jnp.sum(e, axis=1, keepdims=True)
            pack_ref[rows_of(0), :] = lane_pack((peak, total, label), STEP)
            return 0

        for i in range(LANES // STEP):
            step(i, 0)
    shape = stats_ref.shape
    n = shape[0]
    stats = older[0][...] if earlier else jnp.zeros(shape, F32)
    for k in range(rows // LANES):
        stats += put_stats(pack_ref[k * LANES : (k + 1) * LANES, :], block_of(place, slot + k, n), shape)
    stats_ref[...] = stats
    if last:
        outs[2][...] = jnp.broadcast_to(stats[None], outs[2].shape)


def last_stats(own, other, offsets, target, active, slot, rows, n, earlier):
    classes = sum(c.shape[1] for c in own)
    last = slot + rows // LANES == n
    shapes = [
        jax.ShapeDtypeStruct((rows, classes), F32),
        jax.ShapeDtypeStruct((n, 3 * LANES), F32),
    ]
    if last:
        shapes.append(jax.ShapeDtypeStruct((lines_of(n)[0], n, 3 * LANES), F32))
    return pl.pallas_call(
        functools.partial(
            last_stats_kernel, slot, last, len(own), tuple(offsets), len(earlier)
        ),
        out_shape=tuple(shapes),
        in_specs=[VMEM] * (2 * len(own) + 1) + [SMEM] + [VMEM] * len(earlier),
        out_specs=(VMEM,) * len(shapes),
        scratch_shapes=[pltpu.VMEM((rows, LANES), F32), pltpu.VMEM((LANES, LANES), F32)],
        compiler_params=params(),
        cost_estimate=cost(0, 24 * rows * classes),
        name="last_stats",
    )(*own, *other, target, active, *earlier)


def finish_kernel(chunks, e_parts, tile, count, own_ref, target_ref, turned_ref, *refs):
    sources, refs = refs[:count], refs[count:]
    e_refs = refs[:e_parts]
    refs = refs[e_parts:]
    moved_refs, inverse_refs = refs[:chunks], refs[chunks : 2 * chunks]
    out_ref, loss_ref, residual_ref, column_ref, line_ref, held_ref, sems = refs[2 * chunks :]
    n = own_ref.shape[0]
    classes = residual_ref.shape[1]
    place = lax.axis_index("example")
    class_start = place * classes
    part, peak, scales, total, own_scale = combine(own_ref, sources)
    label = sum(part(d, 2) for d in range(count))
    target = target_ref[...]
    valid = (target >= 0.0).astype(F32)
    share = valid / jnp.sum(valid)
    losses = to_slots(peak + jnp.log(total) - label, line_ref, place)
    loss_ref[...] = (valid * losses)[0:1, :]
    factor = to_slots(own_scale / total, line_ref, place)
    column_ref[...] = to_columns([factor, share, target])
    index = class_start + lax.broadcasted_iota(jnp.int32, (1, classes), 1)
    done = 0
    for e_ref in e_refs:
        for k in range(e_ref.shape[0] // LANES):
            j = done + k

            def step(i, _, j=j, k=k, e_ref=e_ref):
                start = i * STEP
                at = pl.ds(j * LANES + start, STEP)
                column = column_ref[pl.ds(start, STEP), :]
                e = e_ref[pl.ds(k * LANES + start, STEP), :]
                probability = e * column[:, j : j + 1]
                hit = index == column[:, 2 * n + j : 2 * n + j + 1].astype(jnp.int32)
                part = column[:, n + j : n + j + 1]
                residual_ref[at, :] = (part * (probability - hit.astype(F32))).astype(BF16)
                return 0

            for i in range(LANES // STEP):
                step(i, 0)
        done += e_ref.shape[0] // LANES

    copies = []
    for k in range(out_ref.shape[0] // tile):
        at = slice(k * tile, (k + 1) * tile)
        done = 0
        for moved_ref, inverse_ref in zip(moved_refs, inverse_refs):
            own = slice(done, done + moved_ref.shape[1])
            gradient = jnp.dot(
                turned_ref[at, :], residual_ref[:, own], preferred_element_type=F32
            )
            held_ref[k, :, own] = moved_ref[at, :] - gradient * inverse_ref[at, :]
            done += moved_ref.shape[1]
        copies.append(pltpu.make_async_copy(held_ref.at[k], out_ref.at[at, :], sems.at[k]))
        copies[-1].start()
    for copy in copies:
        copy.wait()


def finish(own, every, target, e_parts, turned, moved, inverse):
    n = own.shape[0]
    features, all_rows = turned.shape
    classes = e_parts[0].shape[1]
    tile = 512
    return pl.pallas_call(
        functools.partial(finish_kernel, len(moved), len(e_parts), tile, len(every)),
        out_shape=(
            jax.ShapeDtypeStruct((features, classes), F32),
            jax.ShapeDtypeStruct((1, LANES), F32),
        ),
        in_specs=[VMEM] * (3 + len(every) + len(e_parts) + 2 * len(moved)),
        out_specs=(ANY, VMEM),
        scratch_shapes=[
            pltpu.VMEM((all_rows, classes), BF16),
            pltpu.VMEM((LANES, LANES), F32),
            pltpu.VMEM((n, LANES), F32),
            pltpu.VMEM((features // tile, tile, classes), F32),
            pltpu.SemaphoreType.DMA((features // tile,)),
        ],
        compiler_params=params(16),
        cost_estimate=cost(2 * all_rows * features * classes),
        name="finish",
    )(own, target, turned, *every, *e_parts, *moved, *inverse)


def body(n, n_cls, features, weights, labels, counts, active):
    rows = features.shape[0]
    all_rows = rows * n
    feature_count, classes = weights.shape
    entries = feature_count * n_cls * classes * n
    weights = pltpu.with_memory_space_constraint(weights, pltpu.HBM)
    columns = min(512, classes)
    kept, w_low, target, norm = prepare(weights, features, labels, counts, active, columns)
    slots, waits, w_low, gates = gather_blocks(features, n, w_low)
    side = (target, norm, swap(norm, "cls", n_cls, 1))

    groups = [[k, k + 1] for k in range(0, n - 2, 2)] + [[n - 2], [n - 1]]
    count = len(groups)
    behind = max(count - 3, 0)
    plain, buffers, logits, e_parts, stats = (), (), [], [], []

    def statistics(g, tokens):
        last = g == count - 1
        other = [swap(piece, "cls", n_cls, 1) for piece in logits[g]]
        e, found, *copies = first_stats(
            logits[g], other, active, groups[g][0], n, tuple(stats[-1:]),
            side if last else (), tokens,
        )
        e_parts.append(e)
        stats.append(found)
        return copies

    for g in range(count):
        if g == count - 1 and behind:
            logits[behind:], slots[-1] = lax.optimization_barrier((logits[behind:], slots[-1]))
        parts = [part for slot in groups[g] for part in slots[slot]]
        tokens = tuple(stats[-1:]) + tuple(buffers[:1]) + tuple(waits[g] if g < n // 2 else ())
        start = groups[g][0] * rows
        piece = (64,256,256,128,128)[g] if count == 5 else LANES
        block, found = arriving_logits(parts, w_low, plain, start, all_rows, piece, tokens)
        plain = (block,)
        logits.append(found)
        if g < n // 2 - 1:
            buffers = turn(block, start, 2 * rows, buffers)
        if g < behind:
            logits[g], _ = lax.optimization_barrier((logits[g], gates[g]))
        if g < behind - 1:
            statistics(g, ())
    plain = plain[0]
    turned, squares = turn(plain, (n - 2) * rows, 2 * rows, buffers)
    for g in range(max(behind - 1, 0), count):
        copies = statistics(g, (logits[-1][0], turned))
    own_stats = stats[-1]
    every = exchange(copies[0], True)
    residual, fisher_weight, damping, target = first_weights(own_stats, every, e_parts, entries)

    moved, inverse, own, other = [], [], [], []
    for start in range(0, classes, columns):
        a, b, low = update(
            turned, squares, kept[start // columns], residual, fisher_weight, damping, start
        )
        moved.append(a)
        inverse.append(b)
        if start + columns < classes:
            own.append(next_logits(plain, low, 0, all_rows))
            other.append(swap(own[-1], "cls", n_cls, 1))
    half = n // 2
    late = [next_logits(plain, low, first * rows, half * rows) for first in (0, half)]
    late_other = [swap(c, "cls", n_cls, 1) for c in late]
    e_parts, earlier = [], ()
    for first, c, d in zip((0, half), late, late_other):
        offsets = [first * rows] * len(own) + [0]
        e, own_stats, *copies = last_stats(
            own + [c], other + [d], offsets, target, active, first, half * rows, n, earlier
        )
        e_parts.append(e)
        earlier = (own_stats,)
    every = exchange(copies[0], False)
    out, losses = finish(own_stats, every, target, e_parts, turned, moved, inverse)
    return out, losses.reshape(rows)


def solution(mesh):
    return jax.shard_map(
        functools.partial(body, mesh.shape["example"], mesh.shape["cls"]),
        mesh=mesh,
        in_specs=(
            P(("groups", "example"), "cls"),
            P(("groups", "cls"), "example"),
            P(("groups", "example")),
            P(("groups", "example")),
            P("groups"),
        ),
        out_specs=(P(("groups", "cls"), "example"), P(("groups", "example"))),
        check_vma=False,
    )
```

```python
import functools

import jax
import jax.numpy as jnp
from jax import lax
from jax.experimental import pallas as pl
from jax.experimental.pallas import tpu as pltpu
from jax.sharding import PartitionSpec as P

ITERS = 2
NEGATIVE = -1e30
LEARNING_RATE = 2e-05
DAMPING_SHARE = 0.1
EPSILON = 1e-06

F32 = jnp.float32
BF16 = jnp.bfloat16
VMEM = pl.BlockSpec(memory_space=pltpu.VMEM)
SMEM = pl.BlockSpec(memory_space=pltpu.SMEM)
HBM = pl.BlockSpec(memory_space=pltpu.HBM)
ANY = pl.BlockSpec(memory_space=pl.ANY)
STEP = 64
LANES = 128


def params(mib=10):
    return pltpu.CompilerParams(vmem_limit_bytes=mib << 20)


def cost(flops=0, nbytes=0):
    return pl.CostEstimate(flops=int(flops), bytes_accessed=int(nbytes), transcendentals=0)


def swap(x, axis, n, offset):
    return lax.ppermute(x, axis, [(i, i ^ offset) for i in range(n)])


def gray(v):
    return v ^ (v >> 1)


def block_of(place, slot, n):
    if n != 8:
        return lax.rem(place + n - slot, n)
    z, y = place // 2, place % 2
    return gray((gray(z) + 4 - slot // 2) & 3) * 2 + (y ^ (slot % 2))


def split_kernel(x_ref, upper_ref, lower_ref, sems):
    rows = upper_ref.shape[0]
    copies = [
        pltpu.make_async_copy(x_ref.at[k * rows : (k + 1) * rows, :], ref, sems.at[k])
        for k, ref in enumerate((upper_ref, lower_ref))
    ]
    for copy in copies:
        copy.start()
    for copy in copies:
        copy.wait()


def split(x):
    half = pltpu.VMEM((x.shape[0] // 2, x.shape[1]), x.dtype)
    return pl.pallas_call(
        split_kernel,
        out_shape=(half, half),
        in_specs=[HBM],
        out_specs=(VMEM, VMEM),
        scratch_shapes=[pltpu.SemaphoreType.DMA((2,))],
        compiler_params=params(),
        cost_estimate=cost(1, 1),
        name="split",
    )(pltpu.with_memory_space_constraint(x, pltpu.HBM))


def token_kernel(*refs):
    refs[-1][...] = jnp.zeros_like(refs[-1])


def token(values):
    return pl.pallas_call(
        token_kernel,
        out_shape=jax.ShapeDtypeStruct((8, LANES), F32),
        in_specs=[ANY] * len(values),
        out_specs=VMEM,
        compiler_params=params(),
        cost_estimate=cost(1, 1),
        name="token",
    )(*values)


def relay_kernel(*refs):
    refs[-1][...] = refs[0][...]


def relay(block, tokens):
    return pl.pallas_call(
        relay_kernel,
        out_shape=pltpu.VMEM(block.shape, block.dtype),
        in_specs=[VMEM] + [ANY] * len(tokens),
        out_specs=VMEM,
        compiler_params=params(),
        cost_estimate=cost(1, 1),
        name="relay",
    )(block, *tokens)


def gather_blocks(x, n, early):
    if n != 8:
        ring = [(i, (i + 1) % n) for i in range(n)]
        slots = [x]
        for _ in range(n - 1):
            slots.append(lax.ppermute(slots[-1], "example", ring))
        return [[slot] for slot in slots], [()] * (n // 2), early, [slot for slot in slots[3::2]]
    hops = ((0, 1), (1, 3), (3, 2), (2, 0))
    ring = [(a * 2 + y, b * 2 + y) for a, b in hops for y in range(2)]
    tie = lax.optimization_barrier
    held = list(split(x))
    ready = list(held)
    slots = []
    for step in range(3):
        across, later = [], []
        for k in range(2):
            later.append(lax.ppermute(held[k], "example", ring))
            across.append(swap(ready[k], "example", n, 1))
        slots += [held, list(across)]
        if step == 0:
            later = [tie((up, early))[0] for up in later]
        if step < 2:
            ready = [tie((up, over))[0] for up, over in zip(later, across)]
        held = later
    seen = token((held[0],))
    seen = token((across[0], seen))
    seen = token((held[1], seen))
    seen = token((across[1], seen))
    lower = relay(across[1], (seen,))
    upper = relay(held[0], (seen,))
    last = [swap(upper, "example", n, 1), lax.ppermute(lower, "example", ring)]
    slots += [held, last]
    return slots, [tuple(slots[2 * k + 2]) for k in range(3)] + [()], early, [slots[3][1], upper]


def prepare_kernel(tile, chunks, w_ref, x_ref, labels_ref, counts_ref, active_ref, *refs):
    kept = refs[:chunks]
    low_ref, target_ref, norm_ref, block_ref, label_ref, sems = refs[chunks:]
    first = [
        pltpu.make_async_copy(x_ref, block_ref, sems.at[0]),
        pltpu.make_async_copy(labels_ref, label_ref, sems.at[1]),
    ]
    copies = []
    for k in range(w_ref.shape[0] // tile):
        at = slice(k * tile, (k + 1) * tile)
        for c, keep in enumerate(kept):
            own = slice(c * keep.shape[1], (c + 1) * keep.shape[1])
            copy = pltpu.make_async_copy(
                w_ref.at[at, own], keep.at[at, :], sems.at[2 + len(copies)]
            )
            copies.append((copy, keep, at, own))
    for copy in first + [c[0] for c in copies]:
        copy.start()
    for copy in first:
        copy.wait()
    rows = x_ref.shape[0]
    slot = lax.broadcasted_iota(jnp.int32, (1, rows), 1)
    target = jnp.where(slot < counts_ref[0], label_ref[...] % active_ref[0], -1)
    target_ref[...] = target.astype(F32)
    squares = (block_ref[...] * block_ref[...]).astype(F32)
    norm = jnp.sum(squares, axis=1, keepdims=True)
    norm_ref[...] = jnp.broadcast_to(norm, (rows, LANES)).T[0:1, :]
    for copy, keep, at, own in copies:
        copy.wait()
        low_ref[at, own] = keep[at, :].astype(BF16)


def prepare(weights, features, labels, counts, active, columns):
    rows = features.shape[0]
    feature_count, classes = weights.shape
    tile, chunks = 256, classes // columns
    line = jax.ShapeDtypeStruct((1, rows), F32)
    *kept, low, target, norm = pl.pallas_call(
        functools.partial(prepare_kernel, tile, chunks),
        out_shape=(pltpu.VMEM((feature_count, columns), F32),) * chunks
        + (pltpu.VMEM((feature_count, classes), BF16), line, line),
        in_specs=[HBM, HBM, HBM, SMEM, SMEM],
        out_specs=(VMEM,) * (chunks + 3),
        scratch_shapes=[
            pltpu.VMEM(features.shape, BF16),
            pltpu.VMEM((1, rows), jnp.int32),
            pltpu.SemaphoreType.DMA((2 + chunks * (feature_count // tile),)),
        ],
        compiler_params=params(),
        cost_estimate=cost(1, 1),
        name="prepare",
    )(
        weights,
        pltpu.with_memory_space_constraint(features, pltpu.HBM),
        pltpu.with_memory_space_constraint(labels.reshape(1, rows), pltpu.HBM),
        counts,
        active,
    )
    return kept, low, target, norm


def arriving_kernel(count, pieces, start, *refs):
    parts, w_ref = refs[:count], refs[count]
    plain_ref, outs = refs[-pieces - 1], refs[-pieces:]
    done = start
    for part in parts:
        plain_ref[done : done + part.shape[0], :] = part[...]
        done += part.shape[0]
    columns = 256
    for first in range(0, w_ref.shape[1], columns):
        own = slice(first, first + columns)
        found = jnp.dot(plain_ref[start:done, :], w_ref[:, own], preferred_element_type=F32)
        for k, out in enumerate(outs):
            out[:, own] = found[k * out.shape[0] : (k + 1) * out.shape[0], :]


def arriving_logits(parts, w_low, plain, start, all_rows, piece, tokens):
    rows = sum(p.shape[0] for p in parts)
    pieces, count = rows // piece, len(parts)
    plain, *logits = pl.pallas_call(
        functools.partial(arriving_kernel, count, pieces, start),
        out_shape=(pltpu.VMEM((all_rows, w_low.shape[0]), BF16),)
        + (jax.ShapeDtypeStruct((piece, w_low.shape[1]), F32),) * pieces,
        in_specs=[VMEM] * (count + 1 + len(plain)) + [ANY] * len(tokens),
        out_specs=(VMEM,) * (pieces + 1),
        input_output_aliases={count + 1: 0} if plain else {},
        compiler_params=params(),
        cost_estimate=cost(1, 1),
        name="arriving_logits",
    )(*parts, w_low, *plain, *tokens)
    return plain, logits


def turn_kernel(start, rows, plain_ref, *refs):
    turned_ref, squares_ref = refs[-2:]
    at = slice(start, start + rows)
    block = plain_ref[at, :].T
    turned_ref[:, at] = block
    squares_ref[:, at] = block * block


def turn(plain, start, rows, buffers):
    buffer = pltpu.VMEM(plain.shape[::-1], BF16)
    return pl.pallas_call(
        functools.partial(turn_kernel, start, rows),
        out_shape=(buffer, buffer),
        in_specs=[VMEM] * (1 + len(buffers)),
        out_specs=(VMEM, VMEM),
        input_output_aliases={1: 0, 2: 1} if buffers else {},
        compiler_params=params(),
        cost_estimate=cost(1, 1),
        name="turn",
    )(plain, *buffers)


def lane_pack(columns, rows):
    lane = lax.broadcasted_iota(jnp.int32, (rows, LANES), 1)
    packed = jnp.zeros((rows, LANES), F32)
    for k, column in enumerate(columns):
        packed = jnp.where(lane == k, column, packed)
    return packed


def put_stats(packed, place, shape):
    lines = packed.T
    line = jnp.concatenate([lines[k : k + 1, :] for k in range(3)], axis=1)
    here = lax.broadcasted_iota(jnp.int32, shape, 0) == place
    return jnp.where(here, line, 0.0)


def first_stats_kernel(slot, pieces, earlier, last, tokens, *refs):
    own, other = refs[:pieces], refs[pieces : 2 * pieces]
    active_ref, refs = refs[2 * pieces], refs[2 * pieces + 1 :]
    lines = refs[: 3 * last]
    older = refs[3 * last : 3 * last + earlier]
    outs = refs[3 * last + earlier + tokens :]
    e_ref, stats_ref, pack_ref = outs[0], outs[1], outs[-1]
    rows, classes = e_ref.shape
    active, place = active_ref[0], lax.axis_index("example")
    class_start = place * classes
    index = class_start + lax.broadcasted_iota(jnp.int32, (1, classes), 1)
    live = index < active
    for k in range(rows // STEP):
        at = slice(k * STEP, (k + 1) * STEP)
        piece, first = k * STEP // own[0].shape[0], k * STEP % own[0].shape[0]
        here = slice(first, first + STEP)
        logits = jnp.where(live, own[piece][here, :] + other[piece][here, :], NEGATIVE)
        peak = jnp.max(logits, axis=1, keepdims=True)
        e = jnp.exp(logits - peak)
        e_ref[at, :] = e
        total = jnp.sum(e, axis=1, keepdims=True)
        square = jnp.sum(e * e, axis=1, keepdims=True)
        pack_ref[at, :] = lane_pack((peak, total, square), STEP)
    shape = stats_ref.shape
    n = shape[0]
    stats = older[0][...] if earlier else jnp.zeros(shape, F32)
    for k in range(rows // LANES):
        stats += put_stats(pack_ref[k * LANES : (k + 1) * LANES, :], block_of(place, slot + k, n), shape)
    stats_ref[...] = stats
    if last:
        copies_ref = outs[2]
        target, norm = lines[0][...], lines[1][...] + lines[2][...]
        wide = [jnp.broadcast_to(line, (shape[0], LANES)) for line in (target, norm)]
        full = jnp.concatenate([stats] + wide, axis=1)
        copies_ref[...] = jnp.broadcast_to(full[None], copies_ref.shape)


def first_stats(own, other, active, slot, n, earlier, side, tokens):
    pieces, classes = len(own), own[0].shape[1]
    rows = pieces * own[0].shape[0]
    last = len(side) > 0
    shapes = [jax.ShapeDtypeStruct((rows, classes), F32), jax.ShapeDtypeStruct((n, 3 * LANES), F32)]
    if last:
        shapes.append(jax.ShapeDtypeStruct((n, n, 5 * LANES), F32))
    extra = list(side) + list(earlier)
    return pl.pallas_call(
        functools.partial(
            first_stats_kernel, slot, pieces, len(earlier), last, len(tokens)
        ),
        out_shape=tuple(shapes),
        in_specs=[VMEM] * (2 * pieces) + [SMEM] + [VMEM] * len(extra) + [ANY] * len(tokens),
        out_specs=(VMEM,) * len(shapes),
        scratch_shapes=[pltpu.VMEM((rows, LANES), F32)],
        compiler_params=params(),
        cost_estimate=cost(1, 1),
        name="first_stats",
    )(*own, *other, active, *extra, *tokens)


def combine(own_ref, all_ref):
    n = all_ref.shape[0]
    part = lambda d, k: all_ref[d, :, k * LANES : (k + 1) * LANES]
    peaks = [part(d, 0) for d in range(n)]
    peak = functools.reduce(jnp.maximum, peaks)
    scales = [jnp.exp(p - peak) for p in peaks]
    total = sum(part(d, 1) * scales[d] for d in range(n))
    own_scale = jnp.exp(own_ref[:, 0:LANES] - peak)
    return part, peak, scales, total, own_scale


def to_slots(value, line_ref, place):
    n = value.shape[0]
    line_ref[...] = value
    return jnp.concatenate([line_ref[pl.ds(block_of(place, j, n), 1), :] for j in range(n)], axis=0)


def to_columns(lines):
    stacked = jnp.concatenate(lines, axis=0)
    rest = jnp.zeros((LANES - stacked.shape[0], LANES), F32)
    return jnp.concatenate([stacked, rest], axis=0).T


def first_weights_kernel(entries, parts, own_ref, all_ref, *refs):
    e_refs = refs[:parts]
    residual_ref, fisher_ref, damping_ref, target_ref, column_ref, line_ref = refs[parts:]
    n = all_ref.shape[0]
    classes = residual_ref.shape[1]
    place = lax.axis_index("example")
    class_start = place * classes
    part, peak, scales, total, own_scale = combine(own_ref, all_ref)
    square = sum(part(d, 2) * (scales[d] * scales[d]) for d in range(n))
    inverse = 1.0 / total
    spread = 1.0 - square * inverse * inverse
    target = jnp.concatenate([all_ref[d, 0:1, 3 * LANES : 4 * LANES] for d in range(n)], axis=0)
    norm = jnp.concatenate([all_ref[d, 0:1, 4 * LANES : 5 * LANES] for d in range(n)], axis=0)
    valid = (target >= 0.0).astype(F32)
    share = valid / jnp.sum(valid)
    fisher_sum = jnp.sum(norm * share * spread)
    damping_ref[...] = jnp.full(
        damping_ref.shape, DAMPING_SHARE * fisher_sum / entries + EPSILON, F32
    )
    factor = to_slots(own_scale * inverse, line_ref, place)
    share = to_slots(share, line_ref, place)
    target = to_slots(target, line_ref, place)
    target_ref[...] = target
    column_ref[...] = to_columns([factor, share, target])
    index = class_start + lax.broadcasted_iota(jnp.int32, (1, classes), 1)
    done = 0
    for e_ref in e_refs:
        for k in range(e_ref.shape[0] // LANES):
            j = done + k

            def step(i, _, j=j, k=k, e_ref=e_ref):
                start = i * STEP
                at = pl.ds(j * LANES + start, STEP)
                column = column_ref[pl.ds(start, STEP), :]
                e = e_ref[pl.ds(k * LANES + start, STEP), :]
                probability = e * column[:, j : j + 1]
                hit = index == column[:, 2 * n + j : 2 * n + j + 1].astype(jnp.int32)
                part = column[:, n + j : n + j + 1]
                residual_ref[at, :] = (part * (probability - hit.astype(F32))).astype(BF16)
                fisher_ref[at, :] = (part * probability * (1.0 - probability)).astype(BF16)
                return 0

            for i in range(LANES // STEP):
                step(i, 0)
        done += e_ref.shape[0] // LANES


def first_weights(own, every, e_parts, entries):
    n = own.shape[0]
    classes = e_parts[0].shape[1]
    weight = pltpu.VMEM((n * LANES, classes), BF16)
    return pl.pallas_call(
        functools.partial(first_weights_kernel, float(entries), len(e_parts)),
        out_shape=(
            weight,
            weight,
            jax.ShapeDtypeStruct((8, LANES), F32),
            jax.ShapeDtypeStruct((n, LANES), F32),
        ),
        in_specs=[VMEM] * (2 + len(e_parts)),
        out_specs=(VMEM,) * 4,
        scratch_shapes=[pltpu.VMEM((LANES, LANES), F32), pltpu.VMEM((n, LANES), F32)],
        compiler_params=params(),
        cost_estimate=cost(0, 8 * n * LANES * classes),
        name="first_weights",
    )(own, every, *e_parts)


def update_kernel(start, tile, turned_ref, squares_ref, w_ref, residual_ref, fisher_ref,
                  damping_ref, moved_ref, inverse_ref, low_ref):
    features, columns = moved_ref.shape
    damping = damping_ref[0:1, 0:1]
    own = slice(start, start + columns)
    for k in range(features // tile):
        at = slice(k * tile, (k + 1) * tile)
        fisher = jnp.dot(squares_ref[at, :], fisher_ref[:, own], preferred_element_type=F32)
        gradient = jnp.dot(turned_ref[at, :], residual_ref[:, own], preferred_element_type=F32)
        denominator = fisher + damping
        inverse = pl.reciprocal(denominator, approx=True)
        inverse = inverse * (2.0 - denominator * inverse)
        change = gradient * inverse
        inverse_ref[at, :] = inverse
        low_ref[at, :] = (w_ref[at, :] - LEARNING_RATE * change).astype(BF16)
        moved_ref[at, :] = -change


def update(turned, squares, weights, residual, fisher_weight, damping, start):
    features, rows = turned.shape
    columns = weights.shape[1]
    return pl.pallas_call(
        functools.partial(update_kernel, start, 512 if start else 1024),
        out_shape=(
            pltpu.VMEM((features, columns), F32),
            pltpu.VMEM((features, columns), F32),
            pltpu.VMEM((features, columns), BF16),
        ),
        in_specs=[VMEM] * 6,
        out_specs=(VMEM, VMEM, VMEM),
        input_output_aliases={2: 0},
        compiler_params=params(16),
        cost_estimate=cost(4 * rows * features * columns),
        name="update",
    )(turned, squares, weights, residual, fisher_weight, damping)


def next_logits_kernel(start, tile, plain_ref, low_ref, out_ref):
    for first in range(0, out_ref.shape[0], tile):
        out_ref[first : first + tile, :] = jnp.dot(
            plain_ref[start + first : start + first + tile, :],
            low_ref[...],
            preferred_element_type=F32,
        )


def next_logits(plain, low, start, rows):
    features, columns = low.shape
    return pl.pallas_call(
        functools.partial(next_logits_kernel, start, min(512, rows)),
        out_shape=jax.ShapeDtypeStruct((rows, columns), F32),
        in_specs=[VMEM, VMEM],
        out_specs=VMEM,
        compiler_params=params(),
        cost_estimate=cost(2 * rows * features * columns),
        name="next_logits",
    )(plain, low)


def last_stats_kernel(slot, last, pieces, offsets, earlier, *refs):
    own, other = refs[:pieces], refs[pieces : 2 * pieces]
    target_ref, active_ref = refs[2 * pieces : 2 * pieces + 2]
    older = refs[2 * pieces + 2 : 2 * pieces + 2 + earlier]
    outs = refs[2 * pieces + 2 + earlier :]
    e_ref, stats_ref, pack_ref, column_ref = outs[0], outs[1], outs[-2], outs[-1]
    rows, classes = e_ref.shape
    active, place = active_ref[0], lax.axis_index("example")
    class_start = place * classes
    n = stats_ref.shape[0]
    column_ref[...] = to_columns([target_ref[...]])
    index = class_start + lax.broadcasted_iota(jnp.int32, (1, classes), 1)
    live = index < active
    for k in range(rows // LANES):
        def step(i, _, k=k):
            start = i * STEP

            def rows_of(base):
                return pl.ds(base + k * LANES + start, STEP)

            logits = jnp.concatenate(
                [a[rows_of(o), :] + b[rows_of(o), :] for a, b, o in zip(own, other, offsets)],
                axis=1,
            )
            column = column_ref[pl.ds(start, STEP), slot + k : slot + k + 1]
            hit = index == column.astype(jnp.int32)
            label = jnp.sum(jnp.where(hit, logits, 0.0), axis=1, keepdims=True)
            logits = jnp.where(live, logits, NEGATIVE)
            peak = jnp.max(logits, axis=1, keepdims=True)
            e = jnp.exp(logits - peak)
            e_ref[rows_of(0), :] = e
            total = jnp.sum(e, axis=1, keepdims=True)
            pack_ref[rows_of(0), :] = lane_pack((peak, total, label), STEP)
            return 0

        for i in range(LANES // STEP):
            step(i, 0)
    shape = stats_ref.shape
    n = shape[0]
    stats = older[0][...] if earlier else jnp.zeros(shape, F32)
    for k in range(rows // LANES):
        stats += put_stats(pack_ref[k * LANES : (k + 1) * LANES, :], block_of(place, slot + k, n), shape)
    stats_ref[...] = stats
    if last:
        outs[2][...] = jnp.broadcast_to(stats[None], outs[2].shape)


def last_stats(own, other, offsets, target, active, slot, rows, n, earlier):
    classes = sum(c.shape[1] for c in own)
    last = slot + rows // LANES == n
    shapes = [
        jax.ShapeDtypeStruct((rows, classes), F32),
        jax.ShapeDtypeStruct((n, 3 * LANES), F32),
    ]
    if last:
        shapes.append(jax.ShapeDtypeStruct((n, n, 3 * LANES), F32))
    return pl.pallas_call(
        functools.partial(
            last_stats_kernel, slot, last, len(own), tuple(offsets), len(earlier)
        ),
        out_shape=tuple(shapes),
        in_specs=[VMEM] * (2 * len(own) + 1) + [SMEM] + [VMEM] * len(earlier),
        out_specs=(VMEM,) * len(shapes),
        scratch_shapes=[pltpu.VMEM((rows, LANES), F32), pltpu.VMEM((LANES, LANES), F32)],
        compiler_params=params(),
        cost_estimate=cost(0, 24 * rows * classes),
        name="last_stats",
    )(*own, *other, target, active, *earlier)


def finish_kernel(chunks, e_parts, tile, own_ref, all_ref, target_ref, turned_ref, *refs):
    e_refs = refs[:e_parts]
    refs = refs[e_parts:]
    moved_refs, inverse_refs = refs[:chunks], refs[chunks : 2 * chunks]
    out_ref, loss_ref, residual_ref, column_ref, line_ref, held_ref, sems = refs[2 * chunks :]
    n = all_ref.shape[0]
    classes = residual_ref.shape[1]
    place = lax.axis_index("example")
    class_start = place * classes
    part, peak, scales, total, own_scale = combine(own_ref, all_ref)
    label = sum(part(d, 2) for d in range(n))
    target = target_ref[...]
    valid = (target >= 0.0).astype(F32)
    share = valid / jnp.sum(valid)
    losses = to_slots(peak + jnp.log(total) - label, line_ref, place)
    loss_ref[...] = (valid * losses)[0:1, :]
    factor = to_slots(own_scale / total, line_ref, place)
    column_ref[...] = to_columns([factor, share, target])
    index = class_start + lax.broadcasted_iota(jnp.int32, (1, classes), 1)
    done = 0
    for e_ref in e_refs:
        for k in range(e_ref.shape[0] // LANES):
            j = done + k

            def step(i, _, j=j, k=k, e_ref=e_ref):
                start = i * STEP
                at = pl.ds(j * LANES + start, STEP)
                column = column_ref[pl.ds(start, STEP), :]
                e = e_ref[pl.ds(k * LANES + start, STEP), :]
                probability = e * column[:, j : j + 1]
                hit = index == column[:, 2 * n + j : 2 * n + j + 1].astype(jnp.int32)
                part = column[:, n + j : n + j + 1]
                residual_ref[at, :] = (part * (probability - hit.astype(F32))).astype(BF16)
                return 0

            for i in range(LANES // STEP):
                step(i, 0)
        done += e_ref.shape[0] // LANES

    copies = []
    for k in range(out_ref.shape[0] // tile):
        at = slice(k * tile, (k + 1) * tile)
        done = 0
        for moved_ref, inverse_ref in zip(moved_refs, inverse_refs):
            own = slice(done, done + moved_ref.shape[1])
            gradient = jnp.dot(
                turned_ref[at, :], residual_ref[:, own], preferred_element_type=F32
            )
            held_ref[k, :, own] = moved_ref[at, :] - gradient * inverse_ref[at, :]
            done += moved_ref.shape[1]
            copies.append(
                pltpu.make_async_copy(
                    held_ref.at[k, :, own], out_ref.at[at, own], sems.at[len(copies)]
                )
            )
            copies[-1].start()
    for copy in copies:
        copy.wait()


def finish(own, every, target, e_parts, turned, moved, inverse):
    n = own.shape[0]
    features, all_rows = turned.shape
    classes = e_parts[0].shape[1]
    tile = 512
    return pl.pallas_call(
        functools.partial(finish_kernel, len(moved), len(e_parts), tile),
        out_shape=(
            jax.ShapeDtypeStruct((features, classes), F32),
            jax.ShapeDtypeStruct((1, LANES), F32),
        ),
        in_specs=[VMEM] * (4 + len(e_parts) + 2 * len(moved)),
        out_specs=(ANY, VMEM),
        scratch_shapes=[
            pltpu.VMEM((all_rows, classes), BF16),
            pltpu.VMEM((LANES, LANES), F32),
            pltpu.VMEM((n, LANES), F32),
            pltpu.VMEM((features // tile, tile, classes), F32),
            pltpu.SemaphoreType.DMA((features // tile * len(moved),)),
        ],
        compiler_params=params(16),
        cost_estimate=cost(2 * all_rows * features * classes),
        name="finish",
    )(own, every, target, turned, *e_parts, *moved, *inverse)


def exchange(copies):
    return lax.all_to_all(copies, "example", 0, 0)


def body(n, n_cls, features, weights, labels, counts, active):
    rows = features.shape[0]
    all_rows = rows * n
    feature_count, classes = weights.shape
    entries = feature_count * n_cls * classes * n
    weights = pltpu.with_memory_space_constraint(weights, pltpu.HBM)
    columns = min(512, classes)
    kept, w_low, target, norm = prepare(weights, features, labels, counts, active, columns)
    slots, waits, w_low, gates = gather_blocks(features, n, w_low)
    side = (target, norm, swap(norm, "cls", n_cls, 1))

    groups = [[k, k + 1] for k in range(0, n - 2, 2)] + [[n - 2], [n - 1]]
    count = len(groups)
    behind = max(count - 3, 0)
    plain, buffers, logits, e_parts, stats = (), (), [], [], []

    def statistics(g, tokens):
        last = g == count - 1
        other = [swap(piece, "cls", n_cls, 1) for piece in logits[g]]
        e, found, *copies = first_stats(
            logits[g], other, active, groups[g][0], n, tuple(stats[-1:]),
            side if last else (), tokens,
        )
        e_parts.append(e)
        stats.append(found)
        return copies

    for g in range(count):
        if g == count - 1 and behind:
            logits[behind:], slots[-1] = lax.optimization_barrier((logits[behind:], slots[-1]))
        parts = [part for slot in groups[g] for part in slots[slot]]
        tokens = tuple(stats[-1:]) + tuple(buffers[:1]) + tuple(waits[g] if g < n // 2 else ())
        start = groups[g][0] * rows
        piece = (64,256,256,128,128)[g] if count == 5 else LANES
        block, found = arriving_logits(parts, w_low, plain, start, all_rows, piece, tokens)
        plain = (block,)
        logits.append(found)
        if g < n // 2 - 1:
            buffers = turn(block, start, 2 * rows, buffers)
        if g < behind:
            logits[g], _ = lax.optimization_barrier((logits[g], gates[g]))
        if g < behind - 1:
            statistics(g, ())
    plain = plain[0]
    turned, squares = turn(plain, (n - 2) * rows, 2 * rows, buffers)
    for g in range(max(behind - 1, 0), count):
        copies = statistics(g, (logits[-2 if g < behind else -1][0], turned if g >= behind else buffers[0]))
    own_stats = stats[-1]
    every = exchange(copies[0])
    residual, fisher_weight, damping, target = first_weights(own_stats, every, e_parts, entries)

    moved, inverse, own, other = [], [], [], []
    for start in range(0, classes, columns):
        a, b, low = update(
            turned, squares, kept[start // columns], residual, fisher_weight, damping, start
        )
        moved.append(a)
        inverse.append(b)
        if start + columns < classes:
            own.append(next_logits(plain, low, 0, all_rows))
            other.append(swap(own[-1], "cls", n_cls, 1))
    half = n // 2
    late = [next_logits(plain, low, first * rows, half * rows) for first in (0, half)]
    late_other = [swap(c, "cls", n_cls, 1) for c in late]
    e_parts, earlier = [], ()
    for first, c, d in zip((0, half), late, late_other):
        offsets = [first * rows] * len(own) + [0]
        e, own_stats, *copies = last_stats(
            own + [c], other + [d], offsets, target, active, first, half * rows, n, earlier
        )
        e_parts.append(e)
        earlier = (own_stats,)
    every = exchange(copies[0])
    out, losses = finish(own_stats, every, target, e_parts, turned, moved, inverse)
    return out, losses.reshape(rows)


def solution(mesh):
    return jax.shard_map(
        functools.partial(body, mesh.shape["example"], mesh.shape["cls"]),
        mesh=mesh,
        in_specs=(
            P(("groups", "example"), "cls"),
            P(("groups", "cls"), "example"),
            P(("groups", "example")),
            P(("groups", "example")),
            P("groups"),
        ),
        out_specs=(P(("groups", "cls"), "example"), P(("groups", "example"))),
        check_vma=False,
    )
```

```python
import functools

import jax
import jax.numpy as jnp
from jax import lax
from jax.experimental import pallas as pl
from jax.experimental.pallas import tpu as pltpu
from jax.sharding import PartitionSpec as P

ITERS = 2
NEGATIVE = -1e30
LEARNING_RATE = 2e-05
DAMPING_SHARE = 0.1
EPSILON = 1e-06

F32 = jnp.float32
BF16 = jnp.bfloat16
VMEM = pl.BlockSpec(memory_space=pltpu.VMEM)
SMEM = pl.BlockSpec(memory_space=pltpu.SMEM)
HBM = pl.BlockSpec(memory_space=pltpu.HBM)
ANY = pl.BlockSpec(memory_space=pl.ANY)
STEP = 64
LANES = 128


def params(mib=10):
    return pltpu.CompilerParams(vmem_limit_bytes=mib << 20)


def cost(flops=0, nbytes=0):
    return pl.CostEstimate(flops=int(flops), bytes_accessed=int(nbytes), transcendentals=0)


def swap(x, axis, n, offset):
    return lax.ppermute(x, axis, [(i, i ^ offset) for i in range(n)])


def gray(v):
    return v ^ (v >> 1)


def block_of(place, slot, n):
    if n != 8:
        return lax.rem(place + n - slot, n)
    z, y = place // 2, place % 2
    return gray((gray(z) + 4 - slot // 2) & 3) * 2 + (y ^ (slot % 2))


def token_kernel(*refs):
    refs[-1][...] = jnp.zeros_like(refs[-1])


def token(values):
    return pl.pallas_call(
        token_kernel,
        out_shape=jax.ShapeDtypeStruct((8, LANES), F32),
        in_specs=[ANY] * len(values),
        out_specs=VMEM,
        compiler_params=params(),
        cost_estimate=cost(1, 1),
        name="token",
    )(*values)


def relay_kernel(*refs):
    refs[-1][...] = refs[0][...]


def relay(block, tokens):
    return pl.pallas_call(
        relay_kernel,
        out_shape=pltpu.VMEM(block.shape, block.dtype),
        in_specs=[VMEM] + [ANY] * len(tokens),
        out_specs=VMEM,
        compiler_params=params(),
        cost_estimate=cost(1, 1),
        name="relay",
    )(block, *tokens)


def gather_blocks(x, n, early, first_logits):
    if n != 8:
        ring = [(i, (i + 1) % n) for i in range(n)]
        slots = [x]
        for _ in range(n - 1):
            slots.append(lax.ppermute(slots[-1], "example", ring))
        return [[slot] for slot in slots], [()] * (n // 2), early, [slot for slot in slots[3::2]], None
    hops = ((0, 1), (1, 3), (3, 2), (2, 0))
    ring = [(a * 2 + y, b * 2 + y) for a, b in hops for y in range(2)]
    tie = lax.optimization_barrier
    rows = x.shape[0] // 2
    held, ready = [x[:rows], x[rows:]], [x[:rows], x[rows:]]
    slots = []
    for step in range(3):
        across, later = [], []
        for k in range(2):
            if step == 2 and k == 1:
                begun = first_logits(slots[0] + slots[1], early, tuple(slots[2]))
                held[k], *begun[1] = tie((held[k], *begun[1]))
            later.append(lax.ppermute(held[k], "example", ring))
            across.append(swap(ready[k], "example", n, 1))
        slots += [held, list(across)]
        if step == 0:
            later = [tie((up, early))[0] for up in later]
        if step < 2:
            ready = [tie((up, over))[0] for up, over in zip(later, across)]
        held = later
    seen = token((held[0],))
    seen = token((across[0], seen))
    seen = token((held[1], seen))
    seen = token((across[1], seen))
    lower = relay(across[1], (seen,))
    upper = relay(held[0], (seen,))
    last = [swap(upper, "example", n, 1), lax.ppermute(lower, "example", ring)]
    slots += [held, last]
    return slots, [tuple(slots[2 * k + 2]) for k in range(3)] + [()], early, [slots[3][1], upper], begun


def prepare_kernel(tile, chunks, w_ref, x_ref, labels_ref, counts_ref, active_ref, *refs):
    kept = refs[:chunks]
    low_ref, target_ref, norm_ref, block_ref, label_ref, sems = refs[chunks:]
    first = [
        pltpu.make_async_copy(x_ref, block_ref, sems.at[0]),
        pltpu.make_async_copy(labels_ref, label_ref, sems.at[1]),
    ]
    copies = []
    for k in range(w_ref.shape[0] // tile):
        at = slice(k * tile, (k + 1) * tile)
        for c, keep in enumerate(kept):
            own = slice(c * keep.shape[1], (c + 1) * keep.shape[1])
            copy = pltpu.make_async_copy(
                w_ref.at[at, own], keep.at[at, :], sems.at[2 + len(copies)]
            )
            copies.append((copy, keep, at, own))
    for copy in first + [c[0] for c in copies]:
        copy.start()
    for copy in first:
        copy.wait()
    rows = x_ref.shape[0]
    slot = lax.broadcasted_iota(jnp.int32, (1, rows), 1)
    target = jnp.where(slot < counts_ref[0], label_ref[...] % active_ref[0], -1)
    target_ref[...] = target.astype(F32)
    squares = (block_ref[...] * block_ref[...]).astype(F32)
    norm = jnp.sum(squares, axis=1, keepdims=True)
    norm_ref[...] = jnp.broadcast_to(norm, (rows, LANES)).T[0:1, :]
    for copy, keep, at, own in copies:
        copy.wait()
        low_ref[at, own] = keep[at, :].astype(BF16)


def prepare(weights, features, labels, counts, active, columns):
    rows = features.shape[0]
    feature_count, classes = weights.shape
    tile, chunks = 256, classes // columns
    line = jax.ShapeDtypeStruct((1, rows), F32)
    *kept, low, target, norm = pl.pallas_call(
        functools.partial(prepare_kernel, tile, chunks),
        out_shape=(pltpu.VMEM((feature_count, columns), F32),) * chunks
        + (pltpu.VMEM((feature_count, classes), BF16), line, line),
        in_specs=[HBM, HBM, HBM, SMEM, SMEM],
        out_specs=(VMEM,) * (chunks + 3),
        scratch_shapes=[
            pltpu.VMEM(features.shape, BF16),
            pltpu.VMEM((1, rows), jnp.int32),
            pltpu.SemaphoreType.DMA((2 + chunks * (feature_count // tile),)),
        ],
        compiler_params=params(),
        cost_estimate=cost(1, 1),
        name="prepare",
    )(
        weights,
        pltpu.with_memory_space_constraint(features, pltpu.HBM),
        pltpu.with_memory_space_constraint(labels.reshape(1, rows), pltpu.HBM),
        counts,
        active,
    )
    return kept, low, target, norm


def arriving_kernel(count, pieces, start, *refs):
    parts, w_ref = refs[:count], refs[count]
    plain_ref, outs = refs[-pieces - 1], refs[-pieces:]
    done = start
    for part in parts:
        plain_ref[done : done + part.shape[0], :] = part[...]
        done += part.shape[0]
    columns = 256
    for first in range(0, w_ref.shape[1], columns):
        own = slice(first, first + columns)
        found = jnp.dot(plain_ref[start:done, :], w_ref[:, own], preferred_element_type=F32)
        for k, out in enumerate(outs):
            out[:, own] = found[k * out.shape[0] : (k + 1) * out.shape[0], :]


def arriving_logits(parts, w_low, plain, start, all_rows, piece, tokens):
    rows = sum(p.shape[0] for p in parts)
    pieces, count = rows // piece, len(parts)
    plain, *logits = pl.pallas_call(
        functools.partial(arriving_kernel, count, pieces, start),
        out_shape=(pltpu.VMEM((all_rows, w_low.shape[0]), BF16),)
        + (jax.ShapeDtypeStruct((piece, w_low.shape[1]), F32),) * pieces,
        in_specs=[VMEM] * (count + 1 + len(plain)) + [ANY] * len(tokens),
        out_specs=(VMEM,) * (pieces + 1),
        input_output_aliases={count + 1: 0} if plain else {},
        compiler_params=params(),
        cost_estimate=cost(1, 1),
        name="arriving_logits",
    )(*parts, w_low, *plain, *tokens)
    return plain, logits


def turn_kernel(start, rows, plain_ref, *refs):
    turned_ref, squares_ref = refs[-2:]
    at = slice(start, start + rows)
    block = plain_ref[at, :].T
    turned_ref[:, at] = block
    squares_ref[:, at] = block * block


def turn(plain, start, rows, buffers):
    buffer = pltpu.VMEM(plain.shape[::-1], BF16)
    return pl.pallas_call(
        functools.partial(turn_kernel, start, rows),
        out_shape=(buffer, buffer),
        in_specs=[VMEM] * (1 + len(buffers)),
        out_specs=(VMEM, VMEM),
        input_output_aliases={1: 0, 2: 1} if buffers else {},
        compiler_params=params(),
        cost_estimate=cost(1, 1),
        name="turn",
    )(plain, *buffers)


def lane_pack(columns, rows):
    lane = lax.broadcasted_iota(jnp.int32, (rows, LANES), 1)
    packed = jnp.zeros((rows, LANES), F32)
    for k, column in enumerate(columns):
        packed = jnp.where(lane == k, column, packed)
    return packed


def put_stats(packed, place, shape):
    lines = packed.T
    line = jnp.concatenate([lines[k : k + 1, :] for k in range(3)], axis=1)
    here = lax.broadcasted_iota(jnp.int32, shape, 0) == place
    return jnp.where(here, line, 0.0)


def first_stats_kernel(slot, pieces, earlier, last, tokens, *refs):
    own, other = refs[:pieces], refs[pieces : 2 * pieces]
    active_ref, refs = refs[2 * pieces], refs[2 * pieces + 1 :]
    lines = refs[: 3 * last]
    older = refs[3 * last : 3 * last + earlier]
    outs = refs[3 * last + earlier + tokens :]
    e_ref, stats_ref, pack_ref = outs[0], outs[1], outs[-1]
    rows, classes = e_ref.shape
    active, place = active_ref[0], lax.axis_index("example")
    class_start = place * classes
    index = class_start + lax.broadcasted_iota(jnp.int32, (1, classes), 1)
    live = index < active
    for k in range(rows // STEP):
        at = slice(k * STEP, (k + 1) * STEP)
        piece, first = k * STEP // own[0].shape[0], k * STEP % own[0].shape[0]
        here = slice(first, first + STEP)
        logits = jnp.where(live, own[piece][here, :] + other[piece][here, :], NEGATIVE)
        peak = jnp.max(logits, axis=1, keepdims=True)
        e = jnp.exp(logits - peak)
        e_ref[at, :] = e
        total = jnp.sum(e, axis=1, keepdims=True)
        square = jnp.sum(e * e, axis=1, keepdims=True)
        pack_ref[at, :] = lane_pack((peak, total, square), STEP)
    shape = stats_ref.shape
    n = shape[0]
    stats = older[0][...] if earlier else jnp.zeros(shape, F32)
    for k in range(rows // LANES):
        stats += put_stats(pack_ref[k * LANES : (k + 1) * LANES, :], block_of(place, slot + k, n), shape)
    stats_ref[...] = stats
    if last:
        copies_ref = outs[2]
        target, norm = lines[0][...], lines[1][...] + lines[2][...]
        wide = [jnp.broadcast_to(line, (shape[0], LANES)) for line in (target, norm)]
        full = jnp.concatenate([stats] + wide, axis=1)
        copies_ref[...] = jnp.broadcast_to(full[None], copies_ref.shape)


def first_stats(own, other, active, slot, n, earlier, side, tokens):
    pieces, classes = len(own), own[0].shape[1]
    rows = pieces * own[0].shape[0]
    last = len(side) > 0
    shapes = [jax.ShapeDtypeStruct((rows, classes), F32), jax.ShapeDtypeStruct((n, 3 * LANES), F32)]
    if last:
        shapes.append(jax.ShapeDtypeStruct((n, n, 5 * LANES), F32))
    extra = list(side) + list(earlier)
    return pl.pallas_call(
        functools.partial(
            first_stats_kernel, slot, pieces, len(earlier), last, len(tokens)
        ),
        out_shape=tuple(shapes),
        in_specs=[VMEM] * (2 * pieces) + [SMEM] + [VMEM] * len(extra) + [ANY] * len(tokens),
        out_specs=(VMEM,) * len(shapes),
        scratch_shapes=[pltpu.VMEM((rows, LANES), F32)],
        compiler_params=params(),
        cost_estimate=cost(1, 1),
        name="first_stats",
    )(*own, *other, active, *extra, *tokens)


def combine(own_ref, all_ref):
    n = all_ref.shape[0]
    part = lambda d, k: all_ref[d, :, k * LANES : (k + 1) * LANES]
    peaks = [part(d, 0) for d in range(n)]
    peak = functools.reduce(jnp.maximum, peaks)
    scales = [jnp.exp(p - peak) for p in peaks]
    total = sum(part(d, 1) * scales[d] for d in range(n))
    own_scale = jnp.exp(own_ref[:, 0:LANES] - peak)
    return part, peak, scales, total, own_scale


def to_slots(value, line_ref, place):
    n = value.shape[0]
    line_ref[...] = value
    return jnp.concatenate([line_ref[pl.ds(block_of(place, j, n), 1), :] for j in range(n)], axis=0)


def to_columns(lines):
    stacked = jnp.concatenate(lines, axis=0)
    rest = jnp.zeros((LANES - stacked.shape[0], LANES), F32)
    return jnp.concatenate([stacked, rest], axis=0).T


def first_weights_kernel(entries, parts, own_ref, all_ref, *refs):
    e_refs = refs[:parts]
    residual_ref, fisher_ref, damping_ref, target_ref, column_ref, line_ref = refs[parts:]
    n = all_ref.shape[0]
    classes = residual_ref.shape[1]
    place = lax.axis_index("example")
    class_start = place * classes
    part, peak, scales, total, own_scale = combine(own_ref, all_ref)
    square = sum(part(d, 2) * (scales[d] * scales[d]) for d in range(n))
    inverse = 1.0 / total
    spread = 1.0 - square * inverse * inverse
    target = jnp.concatenate([all_ref[d, 0:1, 3 * LANES : 4 * LANES] for d in range(n)], axis=0)
    norm = jnp.concatenate([all_ref[d, 0:1, 4 * LANES : 5 * LANES] for d in range(n)], axis=0)
    valid = (target >= 0.0).astype(F32)
    share = valid / jnp.sum(valid)
    fisher_sum = jnp.sum(norm * share * spread)
    damping_ref[...] = jnp.full(
        damping_ref.shape, DAMPING_SHARE * fisher_sum / entries + EPSILON, F32
    )
    factor = to_slots(own_scale * inverse, line_ref, place)
    share = to_slots(share, line_ref, place)
    target = to_slots(target, line_ref, place)
    target_ref[...] = target
    column_ref[...] = to_columns([factor, share, target])
    index = class_start + lax.broadcasted_iota(jnp.int32, (1, classes), 1)
    done = 0
    for e_ref in e_refs:
        for k in range(e_ref.shape[0] // LANES):
            j = done + k

            def step(i, _, j=j, k=k, e_ref=e_ref):
                start = i * STEP
                at = pl.ds(j * LANES + start, STEP)
                column = column_ref[pl.ds(start, STEP), :]
                e = e_ref[pl.ds(k * LANES + start, STEP), :]
                probability = e * column[:, j : j + 1]
                hit = index == column[:, 2 * n + j : 2 * n + j + 1].astype(jnp.int32)
                part = column[:, n + j : n + j + 1]
                residual_ref[at, :] = (part * (probability - hit.astype(F32))).astype(BF16)
                fisher_ref[at, :] = (part * probability * (1.0 - probability)).astype(BF16)
                return 0

            for i in range(LANES // STEP):
                step(i, 0)
        done += e_ref.shape[0] // LANES


def first_weights(own, every, e_parts, entries):
    n = own.shape[0]
    classes = e_parts[0].shape[1]
    weight = pltpu.VMEM((n * LANES, classes), BF16)
    return pl.pallas_call(
        functools.partial(first_weights_kernel, float(entries), len(e_parts)),
        out_shape=(
            weight,
            weight,
            jax.ShapeDtypeStruct((8, LANES), F32),
            jax.ShapeDtypeStruct((n, LANES), F32),
        ),
        in_specs=[VMEM] * (2 + len(e_parts)),
        out_specs=(VMEM,) * 4,
        scratch_shapes=[pltpu.VMEM((LANES, LANES), F32), pltpu.VMEM((n, LANES), F32)],
        compiler_params=params(),
        cost_estimate=cost(0, 8 * n * LANES * classes),
        name="first_weights",
    )(own, every, *e_parts)


def update_kernel(start, tile, turned_ref, squares_ref, w_ref, residual_ref, fisher_ref,
                  damping_ref, moved_ref, inverse_ref, low_ref):
    features, columns = moved_ref.shape
    damping = damping_ref[0:1, 0:1]
    own = slice(start, start + columns)
    for k in range(features // tile):
        at = slice(k * tile, (k + 1) * tile)
        fisher = jnp.dot(squares_ref[at, :], fisher_ref[:, own], preferred_element_type=F32)
        gradient = jnp.dot(turned_ref[at, :], residual_ref[:, own], preferred_element_type=F32)
        inverse = 1.0 / (fisher + damping)
        change = gradient * inverse
        inverse_ref[at, :] = inverse
        low_ref[at, :] = (w_ref[at, :] - LEARNING_RATE * change).astype(BF16)
        moved_ref[at, :] = -change


def update(turned, squares, weights, residual, fisher_weight, damping, start):
    features, rows = turned.shape
    columns = weights.shape[1]
    return pl.pallas_call(
        functools.partial(update_kernel, start, 512),
        out_shape=(
            pltpu.VMEM((features, columns), F32),
            pltpu.VMEM((features, columns), F32),
            pltpu.VMEM((features, columns), BF16),
        ),
        in_specs=[VMEM] * 6,
        out_specs=(VMEM, VMEM, VMEM),
        input_output_aliases={2: 0},
        compiler_params=params(),
        cost_estimate=cost(4 * rows * features * columns),
        name="update",
    )(turned, squares, weights, residual, fisher_weight, damping)


def next_logits_kernel(start, tile, plain_ref, low_ref, out_ref):
    for first in range(0, out_ref.shape[0], tile):
        out_ref[first : first + tile, :] = jnp.dot(
            plain_ref[start + first : start + first + tile, :],
            low_ref[...],
            preferred_element_type=F32,
        )


def next_logits(plain, low, start, rows):
    features, columns = low.shape
    return pl.pallas_call(
        functools.partial(next_logits_kernel, start, min(512, rows)),
        out_shape=jax.ShapeDtypeStruct((rows, columns), F32),
        in_specs=[VMEM, VMEM],
        out_specs=VMEM,
        compiler_params=params(),
        cost_estimate=cost(2 * rows * features * columns),
        name="next_logits",
    )(plain, low)


def last_stats_kernel(slot, last, pieces, offsets, earlier, *refs):
    own, other = refs[:pieces], refs[pieces : 2 * pieces]
    target_ref, active_ref = refs[2 * pieces : 2 * pieces + 2]
    older = refs[2 * pieces + 2 : 2 * pieces + 2 + earlier]
    outs = refs[2 * pieces + 2 + earlier :]
    e_ref, stats_ref, pack_ref, column_ref = outs[0], outs[1], outs[-2], outs[-1]
    rows, classes = e_ref.shape
    active, place = active_ref[0], lax.axis_index("example")
    class_start = place * classes
    n = stats_ref.shape[0]
    column_ref[...] = to_columns([target_ref[...]])
    index = class_start + lax.broadcasted_iota(jnp.int32, (1, classes), 1)
    live = index < active
    for k in range(rows // LANES):
        def step(i, _, k=k):
            start = i * STEP

            def rows_of(base):
                return pl.ds(base + k * LANES + start, STEP)

            logits = jnp.concatenate(
                [a[rows_of(o), :] + b[rows_of(o), :] for a, b, o in zip(own, other, offsets)],
                axis=1,
            )
            column = column_ref[pl.ds(start, STEP), slot + k : slot + k + 1]
            hit = index == column.astype(jnp.int32)
            label = jnp.sum(jnp.where(hit, logits, 0.0), axis=1, keepdims=True)
            logits = jnp.where(live, logits, NEGATIVE)
            peak = jnp.max(logits, axis=1, keepdims=True)
            e = jnp.exp(logits - peak)
            e_ref[rows_of(0), :] = e
            total = jnp.sum(e, axis=1, keepdims=True)
            pack_ref[rows_of(0), :] = lane_pack((peak, total, label), STEP)
            return 0

        for i in range(LANES // STEP):
            step(i, 0)
    shape = stats_ref.shape
    n = shape[0]
    stats = older[0][...] if earlier else jnp.zeros(shape, F32)
    for k in range(rows // LANES):
        stats += put_stats(pack_ref[k * LANES : (k + 1) * LANES, :], block_of(place, slot + k, n), shape)
    stats_ref[...] = stats
    if last:
        outs[2][...] = jnp.broadcast_to(stats[None], outs[2].shape)


def last_stats(own, other, offsets, target, active, slot, rows, n, earlier):
    classes = sum(c.shape[1] for c in own)
    last = slot + rows // LANES == n
    shapes = [
        jax.ShapeDtypeStruct((rows, classes), F32),
        jax.ShapeDtypeStruct((n, 3 * LANES), F32),
    ]
    if last:
        shapes.append(jax.ShapeDtypeStruct((n, n, 3 * LANES), F32))
    return pl.pallas_call(
        functools.partial(
            last_stats_kernel, slot, last, len(own), tuple(offsets), len(earlier)
        ),
        out_shape=tuple(shapes),
        in_specs=[VMEM] * (2 * len(own) + 1) + [SMEM] + [VMEM] * len(earlier),
        out_specs=(VMEM,) * len(shapes),
        scratch_shapes=[pltpu.VMEM((rows, LANES), F32), pltpu.VMEM((LANES, LANES), F32)],
        compiler_params=params(),
        cost_estimate=cost(0, 24 * rows * classes),
        name="last_stats",
    )(*own, *other, target, active, *earlier)


def finish_kernel(chunks, e_parts, tile, own_ref, all_ref, target_ref, turned_ref, *refs):
    e_refs = refs[:e_parts]
    refs = refs[e_parts:]
    moved_refs, inverse_refs = refs[:chunks], refs[chunks : 2 * chunks]
    out_ref, loss_ref, residual_ref, column_ref, line_ref, held_ref, sems = refs[2 * chunks :]
    n = all_ref.shape[0]
    classes = residual_ref.shape[1]
    place = lax.axis_index("example")
    class_start = place * classes
    part, peak, scales, total, own_scale = combine(own_ref, all_ref)
    label = sum(part(d, 2) for d in range(n))
    target = target_ref[...]
    valid = (target >= 0.0).astype(F32)
    share = valid / jnp.sum(valid)
    losses = to_slots(peak + jnp.log(total) - label, line_ref, place)
    loss_ref[...] = (valid * losses)[0:1, :]
    factor = to_slots(own_scale / total, line_ref, place)
    column_ref[...] = to_columns([factor, share, target])
    index = class_start + lax.broadcasted_iota(jnp.int32, (1, classes), 1)
    done = 0
    for e_ref in e_refs:
        for k in range(e_ref.shape[0] // LANES):
            j = done + k

            def step(i, _, j=j, k=k, e_ref=e_ref):
                start = i * STEP
                at = pl.ds(j * LANES + start, STEP)
                column = column_ref[pl.ds(start, STEP), :]
                e = e_ref[pl.ds(k * LANES + start, STEP), :]
                probability = e * column[:, j : j + 1]
                hit = index == column[:, 2 * n + j : 2 * n + j + 1].astype(jnp.int32)
                part = column[:, n + j : n + j + 1]
                residual_ref[at, :] = (part * (probability - hit.astype(F32))).astype(BF16)
                return 0

            for i in range(LANES // STEP):
                step(i, 0)
        done += e_ref.shape[0] // LANES

    copies = []
    for k in range(out_ref.shape[0] // tile):
        at = slice(k * tile, (k + 1) * tile)
        done = 0
        for moved_ref, inverse_ref in zip(moved_refs, inverse_refs):
            own = slice(done, done + moved_ref.shape[1])
            gradient = jnp.dot(
                turned_ref[at, :], residual_ref[:, own], preferred_element_type=F32
            )
            held_ref[k, :, own] = moved_ref[at, :] - gradient * inverse_ref[at, :]
            done += moved_ref.shape[1]
            copies.append(
                pltpu.make_async_copy(
                    held_ref.at[k, :, own], out_ref.at[at, own], sems.at[len(copies)]
                )
            )
            copies[-1].start()
    for copy in copies:
        copy.wait()


def finish(own, every, target, e_parts, turned, moved, inverse):
    n = own.shape[0]
    features, all_rows = turned.shape
    classes = e_parts[0].shape[1]
    tile = 512
    return pl.pallas_call(
        functools.partial(finish_kernel, len(moved), len(e_parts), tile),
        out_shape=(
            jax.ShapeDtypeStruct((features, classes), F32),
            jax.ShapeDtypeStruct((1, LANES), F32),
        ),
        in_specs=[VMEM] * (4 + len(e_parts) + 2 * len(moved)),
        out_specs=(ANY, VMEM),
        scratch_shapes=[
            pltpu.VMEM((all_rows, classes), BF16),
            pltpu.VMEM((LANES, LANES), F32),
            pltpu.VMEM((n, LANES), F32),
            pltpu.VMEM((features // tile, tile, classes), F32),
            pltpu.SemaphoreType.DMA((features // tile * len(moved),)),
        ],
        compiler_params=params(16),
        cost_estimate=cost(2 * all_rows * features * classes),
        name="finish",
    )(own, every, target, turned, *e_parts, *moved, *inverse)


def exchange(copies):
    return lax.all_to_all(copies, "example", 0, 0)


def body(n, n_cls, features, weights, labels, counts, active):
    rows = features.shape[0]
    all_rows = rows * n
    feature_count, classes = weights.shape
    entries = feature_count * n_cls * classes * n
    weights = pltpu.with_memory_space_constraint(weights, pltpu.HBM)
    columns = min(512, classes)
    kept, w_low, target, norm = prepare(weights, features, labels, counts, active, columns)
    def first_logits(parts, low, tokens):
        return list(arriving_logits(parts, low, (), 0, all_rows, STEP, tokens))

    slots, waits, w_low, gates, begun = gather_blocks(features, n, w_low, first_logits)
    side = (target, norm, swap(norm, "cls", n_cls, 1))

    groups = [[k, k + 1] for k in range(0, n - 2, 2)] + [[n - 2], [n - 1]]
    count = len(groups)
    behind = max(count - 3, 0)
    plain, buffers, logits, e_parts, stats = (), (), [], [], []

    def statistics(g, tokens):
        last = g == count - 1
        other = [swap(piece, "cls", n_cls, 1) for piece in logits[g]]
        e, found, *copies = first_stats(
            logits[g], other, active, groups[g][0], n, tuple(stats[-1:]),
            side if last else (), tokens,
        )
        e_parts.append(e)
        stats.append(found)
        return copies

    for g in range(count):
        if g == count - 1 and behind:
            logits[behind:], slots[-1] = lax.optimization_barrier((logits[behind:], slots[-1]))
        parts = [part for slot in groups[g] for part in slots[slot]]
        tokens = tuple(stats[-1:]) + tuple(buffers[:1]) + tuple(waits[g] if g < n // 2 else ())
        if g == 2:
            tokens += side[2:]
        start = groups[g][0] * rows
        piece = (64,256,256,128,128)[g] if count == 5 else LANES
        if g == 0 and begun is not None:
            block, found = begun
        else:
            block, found = arriving_logits(parts, w_low, plain, start, all_rows, piece, tokens)
        plain = (block,)
        logits.append(found)
        if g < n // 2 - 1:
            buffers = turn(block, start, 2 * rows, buffers)
        if g < behind:
            logits[g], _ = lax.optimization_barrier((logits[g], gates[g]))
        if g < behind - 1:
            statistics(g, ())
    plain = plain[0]
    turned, squares = turn(plain, (n - 2) * rows, 2 * rows, buffers)
    for g in range(max(behind - 1, 0), count):
        copies = statistics(g, (logits[-1][0], turned))
    own_stats = stats[-1]
    every = exchange(copies[0])
    residual, fisher_weight, damping, target = first_weights(own_stats, every, e_parts, entries)

    moved, inverse, own, other = [], [], [], []
    for start in range(0, classes, columns):
        a, b, low = update(
            turned, squares, kept[start // columns], residual, fisher_weight, damping, start
        )
        moved.append(a)
        inverse.append(b)
        if start + columns < classes:
            own.append(next_logits(plain, low, 0, all_rows))
            other.append(swap(own[-1], "cls", n_cls, 1))
    half = n // 2
    late = [next_logits(plain, low, first * rows, half * rows) for first in (0, half)]
    late_other = [swap(c, "cls", n_cls, 1) for c in late]
    e_parts, earlier = [], ()
    for first, c, d in zip((0, half), late, late_other):
        offsets = [first * rows] * len(own) + [0]
        e, own_stats, *copies = last_stats(
            own + [c], other + [d], offsets, target, active, first, half * rows, n, earlier
        )
        e_parts.append(e)
        earlier = (own_stats,)
    every = exchange(copies[0])
    out, losses = finish(own_stats, every, target, e_parts, turned, moved, inverse)
    return out, losses.reshape(rows)


def solution(mesh):
    return jax.shard_map(
        functools.partial(body, mesh.shape["example"], mesh.shape["cls"]),
        mesh=mesh,
        in_specs=(
            P(("groups", "example"), "cls"),
            P(("groups", "cls"), "example"),
            P(("groups", "example")),
            P(("groups", "example")),
            P("groups"),
        ),
        out_specs=(P(("groups", "cls"), "example"), P(("groups", "example"))),
        check_vma=False,
    )
```

```python
import functools

import jax
import jax.numpy as jnp
from jax import lax
from jax.experimental import pallas as pl
from jax.experimental.pallas import tpu as pltpu
from jax.sharding import PartitionSpec as P

ITERS = 2
NEGATIVE = -1e30
LEARNING_RATE = 2e-05
DAMPING_SHARE = 0.1
EPSILON = 1e-06

F32 = jnp.float32
BF16 = jnp.bfloat16
VMEM = pl.BlockSpec(memory_space=pltpu.VMEM)
SMEM = pl.BlockSpec(memory_space=pltpu.SMEM)
HBM = pl.BlockSpec(memory_space=pltpu.HBM)
ANY = pl.BlockSpec(memory_space=pl.ANY)
STEP = 64
LANES = 128


def params(mib=10):
    return pltpu.CompilerParams(vmem_limit_bytes=mib << 20)


def cost(flops=0, nbytes=0):
    return pl.CostEstimate(flops=int(flops), bytes_accessed=int(nbytes), transcendentals=0)


def swap(x, axis, n, offset):
    return lax.ppermute(x, axis, [(i, i ^ offset) for i in range(n)])


def gray(v):
    return v ^ (v >> 1)


def block_of(place, slot, n):
    if n != 8:
        return lax.rem(place + n - slot, n)
    z, y = place // 2, place % 2
    return gray((gray(z) + 4 - slot // 2) & 3) * 2 + (y ^ (slot % 2))


def token_kernel(*refs):
    refs[-1][...] = jnp.zeros_like(refs[-1])


def token(values):
    return pl.pallas_call(
        token_kernel,
        out_shape=jax.ShapeDtypeStruct((8, LANES), F32),
        in_specs=[ANY] * len(values),
        out_specs=VMEM,
        compiler_params=params(),
        cost_estimate=cost(1, 1),
        name="token",
    )(*values)


def relay_kernel(*refs):
    refs[-1][...] = refs[0][...]


def relay(block, tokens):
    return pl.pallas_call(
        relay_kernel,
        out_shape=pltpu.VMEM(block.shape, block.dtype),
        in_specs=[VMEM] + [ANY] * len(tokens),
        out_specs=VMEM,
        compiler_params=params(),
        cost_estimate=cost(1, 1),
        name="relay",
    )(block, *tokens)


def gather_blocks(x, n, early, first_logits):
    if n != 8:
        ring = [(i, (i + 1) % n) for i in range(n)]
        slots = [x]
        for _ in range(n - 1):
            slots.append(lax.ppermute(slots[-1], "example", ring))
        return [[slot] for slot in slots], [()] * (n // 2), early, [slot for slot in slots[3::2]], None
    hops = ((0, 1), (1, 3), (3, 2), (2, 0))
    ring = [(a * 2 + y, b * 2 + y) for a, b in hops for y in range(2)]
    tie = lax.optimization_barrier
    rows = x.shape[0] // 2
    held, ready = [x[:rows], x[rows:]], [x[:rows], x[rows:]]
    slots = []
    for step in range(3):
        across, later = [], []
        for k in range(2):
            if step == 2 and k == 1:
                begun = first_logits(slots[0] + slots[1], early, tuple(slots[2]))
                held[k], *begun[1] = tie((held[k], *begun[1]))
            later.append(lax.ppermute(held[k], "example", ring))
            across.append(swap(ready[k], "example", n, 1))
        slots += [held, list(across)]
        if step == 0:
            later = [tie((up, early))[0] for up in later]
        if step < 2:
            ready = [tie((up, over))[0] for up, over in zip(later, across)]
        held = later
    seen = token((held[0],))
    seen = token((across[0], seen))
    upper = relay(held[0], (seen,))
    seen = token((held[1], upper))
    lower = relay(across[1], (seen,))
    last = [swap(upper, "example", n, 1), lax.ppermute(lower, "example", ring)]
    slots += [held, last]
    return slots, [tuple(slots[2 * k + 2]) for k in range(3)] + [()], early, [slots[3][1], upper], begun


def prepare_kernel(tile, chunks, w_ref, x_ref, labels_ref, counts_ref, active_ref, *refs):
    kept = refs[:chunks]
    low_ref, target_ref, norm_ref, block_ref, label_ref, sems = refs[chunks:]
    first = [
        pltpu.make_async_copy(x_ref, block_ref, sems.at[0]),
        pltpu.make_async_copy(labels_ref, label_ref, sems.at[1]),
    ]
    copies = []
    for k in range(w_ref.shape[0] // tile):
        at = slice(k * tile, (k + 1) * tile)
        for c, keep in enumerate(kept):
            own = slice(c * keep.shape[1], (c + 1) * keep.shape[1])
            copy = pltpu.make_async_copy(
                w_ref.at[at, own], keep.at[at, :], sems.at[2 + len(copies)]
            )
            copies.append((copy, keep, at, own))
    for copy in first + [c[0] for c in copies]:
        copy.start()
    for copy in first:
        copy.wait()
    rows = x_ref.shape[0]
    slot = lax.broadcasted_iota(jnp.int32, (1, rows), 1)
    target = jnp.where(slot < counts_ref[0], label_ref[...] % active_ref[0], -1)
    target_ref[...] = target.astype(F32)
    squares = (block_ref[...] * block_ref[...]).astype(F32)
    norm = jnp.sum(squares, axis=1, keepdims=True)
    norm_ref[...] = jnp.broadcast_to(norm, (rows, LANES)).T[0:1, :]
    for copy, keep, at, own in copies:
        copy.wait()
        low_ref[at, own] = keep[at, :].astype(BF16)


def prepare(weights, features, labels, counts, active, columns):
    rows = features.shape[0]
    feature_count, classes = weights.shape
    tile, chunks = 256, classes // columns
    line = jax.ShapeDtypeStruct((1, rows), F32)
    *kept, low, target, norm = pl.pallas_call(
        functools.partial(prepare_kernel, tile, chunks),
        out_shape=(pltpu.VMEM((feature_count, columns), F32),) * chunks
        + (pltpu.VMEM((feature_count, classes), BF16), line, line),
        in_specs=[HBM, HBM, HBM, SMEM, SMEM],
        out_specs=(VMEM,) * (chunks + 3),
        scratch_shapes=[
            pltpu.VMEM(features.shape, BF16),
            pltpu.VMEM((1, rows), jnp.int32),
            pltpu.SemaphoreType.DMA((2 + chunks * (feature_count // tile),)),
        ],
        compiler_params=params(),
        cost_estimate=cost(1, 1),
        name="prepare",
    )(
        weights,
        pltpu.with_memory_space_constraint(features, pltpu.HBM),
        pltpu.with_memory_space_constraint(labels.reshape(1, rows), pltpu.HBM),
        counts,
        active,
    )
    return kept, low, target, norm


def arriving_kernel(count, pieces, start, *refs):
    parts, w_ref = refs[:count], refs[count]
    plain_ref, outs = refs[-pieces - 1], refs[-pieces:]
    done = start
    for part in parts:
        plain_ref[done : done + part.shape[0], :] = part[...]
        done += part.shape[0]
    columns = 256
    for first in range(0, w_ref.shape[1], columns):
        own = slice(first, first + columns)
        found = jnp.dot(plain_ref[start:done, :], w_ref[:, own], preferred_element_type=F32)
        for k, out in enumerate(outs):
            out[:, own] = found[k * out.shape[0] : (k + 1) * out.shape[0], :]


def arriving_logits(parts, w_low, plain, start, all_rows, piece, tokens):
    rows = sum(p.shape[0] for p in parts)
    pieces, count = rows // piece, len(parts)
    plain, *logits = pl.pallas_call(
        functools.partial(arriving_kernel, count, pieces, start),
        out_shape=(pltpu.VMEM((all_rows, w_low.shape[0]), BF16),)
        + (jax.ShapeDtypeStruct((piece, w_low.shape[1]), F32),) * pieces,
        in_specs=[VMEM] * (count + 1 + len(plain)) + [ANY] * len(tokens),
        out_specs=(VMEM,) * (pieces + 1),
        input_output_aliases={count + 1: 0} if plain else {},
        compiler_params=params(),
        cost_estimate=cost(1, 1),
        name="arriving_logits",
    )(*parts, w_low, *plain, *tokens)
    return plain, logits


def turn_kernel(start, rows, plain_ref, *refs):
    turned_ref, squares_ref = refs[-2:]
    at = slice(start, start + rows)
    block = plain_ref[at, :].T
    turned_ref[:, at] = block
    squares_ref[:, at] = block * block


def turn(plain, start, rows, buffers):
    buffer = pltpu.VMEM(plain.shape[::-1], BF16)
    return pl.pallas_call(
        functools.partial(turn_kernel, start, rows),
        out_shape=(buffer, buffer),
        in_specs=[VMEM] * (1 + len(buffers)),
        out_specs=(VMEM, VMEM),
        input_output_aliases={1: 0, 2: 1} if buffers else {},
        compiler_params=params(),
        cost_estimate=cost(1, 1),
        name="turn",
    )(plain, *buffers)


def lane_pack(columns, rows):
    lane = lax.broadcasted_iota(jnp.int32, (rows, LANES), 1)
    packed = jnp.zeros((rows, LANES), F32)
    for k, column in enumerate(columns):
        packed = jnp.where(lane == k, column, packed)
    return packed


def put_stats(packed, place, shape):
    lines = packed.T
    line = jnp.concatenate([lines[k : k + 1, :] for k in range(3)], axis=1)
    here = lax.broadcasted_iota(jnp.int32, shape, 0) == place
    return jnp.where(here, line, 0.0)


def first_stats_kernel(slot, pieces, earlier, last, tokens, *refs):
    own, other = refs[:pieces], refs[pieces : 2 * pieces]
    active_ref, refs = refs[2 * pieces], refs[2 * pieces + 1 :]
    lines = refs[: 3 * last]
    older = refs[3 * last : 3 * last + earlier]
    outs = refs[3 * last + earlier + tokens :]
    e_ref, stats_ref, pack_ref = outs[0], outs[1], outs[-1]
    rows, classes = e_ref.shape
    active, place = active_ref[0], lax.axis_index("example")
    class_start = place * classes
    index = class_start + lax.broadcasted_iota(jnp.int32, (1, classes), 1)
    live = index < active
    for k in range(rows // STEP):
        at = slice(k * STEP, (k + 1) * STEP)
        piece, first = k * STEP // own[0].shape[0], k * STEP % own[0].shape[0]
        here = slice(first, first + STEP)
        logits = jnp.where(live, own[piece][here, :] + other[piece][here, :], NEGATIVE)
        peak = jnp.max(logits, axis=1, keepdims=True)
        e = jnp.exp(logits - peak)
        e_ref[at, :] = e
        total = jnp.sum(e, axis=1, keepdims=True)
        square = jnp.sum(e * e, axis=1, keepdims=True)
        pack_ref[at, :] = lane_pack((peak, total, square), STEP)
    shape = stats_ref.shape
    n = shape[0]
    stats = older[0][...] if earlier else jnp.zeros(shape, F32)
    for k in range(rows // LANES):
        stats += put_stats(pack_ref[k * LANES : (k + 1) * LANES, :], block_of(place, slot + k, n), shape)
    stats_ref[...] = stats
    if last:
        copies_ref = outs[2]
        target, norm = lines[0][...], lines[1][...] + lines[2][...]
        wide = [jnp.broadcast_to(line, (shape[0], LANES)) for line in (target, norm)]
        full = jnp.concatenate([stats] + wide, axis=1)
        copies_ref[...] = jnp.broadcast_to(full[None], copies_ref.shape)


def first_stats(own, other, active, slot, n, earlier, side, tokens):
    pieces, classes = len(own), own[0].shape[1]
    rows = pieces * own[0].shape[0]
    last = len(side) > 0
    shapes = [jax.ShapeDtypeStruct((rows, classes), F32), jax.ShapeDtypeStruct((n, 3 * LANES), F32)]
    if last:
        shapes.append(jax.ShapeDtypeStruct((n, n, 5 * LANES), F32))
    extra = list(side) + list(earlier)
    return pl.pallas_call(
        functools.partial(
            first_stats_kernel, slot, pieces, len(earlier), last, len(tokens)
        ),
        out_shape=tuple(shapes),
        in_specs=[VMEM] * (2 * pieces) + [SMEM] + [VMEM] * len(extra) + [ANY] * len(tokens),
        out_specs=(VMEM,) * len(shapes),
        scratch_shapes=[pltpu.VMEM((rows, LANES), F32)],
        compiler_params=params(),
        cost_estimate=cost(1, 1),
        name="first_stats",
    )(*own, *other, active, *extra, *tokens)


def combine(own_ref, all_ref):
    n = all_ref.shape[0]
    part = lambda d, k: all_ref[d, :, k * LANES : (k + 1) * LANES]
    peaks = [part(d, 0) for d in range(n)]
    peak = functools.reduce(jnp.maximum, peaks)
    scales = [jnp.exp(p - peak) for p in peaks]
    total = sum(part(d, 1) * scales[d] for d in range(n))
    own_scale = jnp.exp(own_ref[:, 0:LANES] - peak)
    return part, peak, scales, total, own_scale


def to_slots(value, line_ref, place):
    n = value.shape[0]
    line_ref[...] = value
    return jnp.concatenate([line_ref[pl.ds(block_of(place, j, n), 1), :] for j in range(n)], axis=0)


def to_columns(lines):
    stacked = jnp.concatenate(lines, axis=0)
    rest = jnp.zeros((LANES - stacked.shape[0], LANES), F32)
    return jnp.concatenate([stacked, rest], axis=0).T


def first_weights_kernel(entries, parts, own_ref, all_ref, *refs):
    e_refs = refs[:parts]
    residual_ref, fisher_ref, damping_ref, target_ref, column_ref, line_ref = refs[parts:]
    n = all_ref.shape[0]
    classes = residual_ref.shape[1]
    place = lax.axis_index("example")
    class_start = place * classes
    part, peak, scales, total, own_scale = combine(own_ref, all_ref)
    square = sum(part(d, 2) * (scales[d] * scales[d]) for d in range(n))
    inverse = 1.0 / total
    spread = 1.0 - square * inverse * inverse
    target = jnp.concatenate([all_ref[d, 0:1, 3 * LANES : 4 * LANES] for d in range(n)], axis=0)
    norm = jnp.concatenate([all_ref[d, 0:1, 4 * LANES : 5 * LANES] for d in range(n)], axis=0)
    valid = (target >= 0.0).astype(F32)
    share = valid / jnp.sum(valid)
    fisher_sum = jnp.sum(norm * share * spread)
    damping_ref[...] = jnp.full(
        damping_ref.shape, DAMPING_SHARE * fisher_sum / entries + EPSILON, F32
    )
    factor = to_slots(own_scale * inverse, line_ref, place)
    share = to_slots(share, line_ref, place)
    target = to_slots(target, line_ref, place)
    target_ref[...] = target
    column_ref[...] = to_columns([factor, share, target])
    index = class_start + lax.broadcasted_iota(jnp.int32, (1, classes), 1)
    done = 0
    for e_ref in e_refs:
        for k in range(e_ref.shape[0] // LANES):
            j = done + k

            def step(i, _, j=j, k=k, e_ref=e_ref):
                start = i * STEP
                at = pl.ds(j * LANES + start, STEP)
                column = column_ref[pl.ds(start, STEP), :]
                e = e_ref[pl.ds(k * LANES + start, STEP), :]
                probability = e * column[:, j : j + 1]
                hit = index == column[:, 2 * n + j : 2 * n + j + 1].astype(jnp.int32)
                part = column[:, n + j : n + j + 1]
                residual_ref[at, :] = (part * (probability - hit.astype(F32))).astype(BF16)
                fisher_ref[at, :] = (part * probability * (1.0 - probability)).astype(BF16)
                return 0

            for i in range(LANES // STEP):
                step(i, 0)
        done += e_ref.shape[0] // LANES


def first_weights(own, every, e_parts, entries):
    n = own.shape[0]
    classes = e_parts[0].shape[1]
    weight = pltpu.VMEM((n * LANES, classes), BF16)
    return pl.pallas_call(
        functools.partial(first_weights_kernel, float(entries), len(e_parts)),
        out_shape=(
            weight,
            weight,
            jax.ShapeDtypeStruct((8, LANES), F32),
            jax.ShapeDtypeStruct((n, LANES), F32),
        ),
        in_specs=[VMEM] * (2 + len(e_parts)),
        out_specs=(VMEM,) * 4,
        scratch_shapes=[pltpu.VMEM((LANES, LANES), F32), pltpu.VMEM((n, LANES), F32)],
        compiler_params=params(),
        cost_estimate=cost(0, 8 * n * LANES * classes),
        name="first_weights",
    )(own, every, *e_parts)


def update_kernel(start, tile, turned_ref, squares_ref, w_ref, residual_ref, fisher_ref,
                  damping_ref, moved_ref, inverse_ref, low_ref):
    features, columns = moved_ref.shape
    damping = damping_ref[0:1, 0:1]
    own = slice(start, start + columns)
    for k in range(features // tile):
        at = slice(k * tile, (k + 1) * tile)
        fisher = jnp.dot(squares_ref[at, :], fisher_ref[:, own], preferred_element_type=F32)
        gradient = jnp.dot(turned_ref[at, :], residual_ref[:, own], preferred_element_type=F32)
        inverse = 1.0 / (fisher + damping)
        change = gradient * inverse
        inverse_ref[at, :] = inverse
        low_ref[at, :] = (w_ref[at, :] - LEARNING_RATE * change).astype(BF16)
        moved_ref[at, :] = -change


def update(turned, squares, weights, residual, fisher_weight, damping, start):
    features, rows = turned.shape
    columns = weights.shape[1]
    return pl.pallas_call(
        functools.partial(update_kernel, start, 512),
        out_shape=(
            pltpu.VMEM((features, columns), F32),
            pltpu.VMEM((features, columns), F32),
            pltpu.VMEM((features, columns), BF16),
        ),
        in_specs=[VMEM] * 6,
        out_specs=(VMEM, VMEM, VMEM),
        input_output_aliases={2: 0},
        compiler_params=params(),
        cost_estimate=cost(4 * rows * features * columns),
        name="update",
    )(turned, squares, weights, residual, fisher_weight, damping)


def next_logits_kernel(start, tile, plain_ref, low_ref, out_ref):
    for first in range(0, out_ref.shape[0], tile):
        out_ref[first : first + tile, :] = jnp.dot(
            plain_ref[start + first : start + first + tile, :],
            low_ref[...],
            preferred_element_type=F32,
        )


def next_logits(plain, low, start, rows):
    features, columns = low.shape
    return pl.pallas_call(
        functools.partial(next_logits_kernel, start, min(512, rows)),
        out_shape=jax.ShapeDtypeStruct((rows, columns), F32),
        in_specs=[VMEM, VMEM],
        out_specs=VMEM,
        compiler_params=params(),
        cost_estimate=cost(2 * rows * features * columns),
        name="next_logits",
    )(plain, low)


def last_stats_kernel(slot, last, pieces, offsets, earlier, *refs):
    own, other = refs[:pieces], refs[pieces : 2 * pieces]
    target_ref, active_ref = refs[2 * pieces : 2 * pieces + 2]
    older = refs[2 * pieces + 2 : 2 * pieces + 2 + earlier]
    outs = refs[2 * pieces + 2 + earlier :]
    e_ref, stats_ref, pack_ref, column_ref = outs[0], outs[1], outs[-2], outs[-1]
    rows, classes = e_ref.shape
    active, place = active_ref[0], lax.axis_index("example")
    class_start = place * classes
    n = stats_ref.shape[0]
    column_ref[...] = to_columns([target_ref[...]])
    index = class_start + lax.broadcasted_iota(jnp.int32, (1, classes), 1)
    live = index < active
    for k in range(rows // LANES):
        def step(i, _, k=k):
            start = i * STEP

            def rows_of(base):
                return pl.ds(base + k * LANES + start, STEP)

            logits = jnp.concatenate(
                [a[rows_of(o), :] + b[rows_of(o), :] for a, b, o in zip(own, other, offsets)],
                axis=1,
            )
            column = column_ref[pl.ds(start, STEP), slot + k : slot + k + 1]
            hit = index == column.astype(jnp.int32)
            label = jnp.sum(jnp.where(hit, logits, 0.0), axis=1, keepdims=True)
            logits = jnp.where(live, logits, NEGATIVE)
            peak = jnp.max(logits, axis=1, keepdims=True)
            e = jnp.exp(logits - peak)
            e_ref[rows_of(0), :] = e
            total = jnp.sum(e, axis=1, keepdims=True)
            pack_ref[rows_of(0), :] = lane_pack((peak, total, label), STEP)
            return 0

        for i in range(LANES // STEP):
            step(i, 0)
    shape = stats_ref.shape
    n = shape[0]
    stats = older[0][...] if earlier else jnp.zeros(shape, F32)
    for k in range(rows // LANES):
        stats += put_stats(pack_ref[k * LANES : (k + 1) * LANES, :], block_of(place, slot + k, n), shape)
    stats_ref[...] = stats
    if last:
        outs[2][...] = jnp.broadcast_to(stats[None], outs[2].shape)


def last_stats(own, other, offsets, target, active, slot, rows, n, earlier):
    classes = sum(c.shape[1] for c in own)
    last = slot + rows // LANES == n
    shapes = [
        jax.ShapeDtypeStruct((rows, classes), F32),
        jax.ShapeDtypeStruct((n, 3 * LANES), F32),
    ]
    if last:
        shapes.append(jax.ShapeDtypeStruct((n, n, 3 * LANES), F32))
    return pl.pallas_call(
        functools.partial(
            last_stats_kernel, slot, last, len(own), tuple(offsets), len(earlier)
        ),
        out_shape=tuple(shapes),
        in_specs=[VMEM] * (2 * len(own) + 1) + [SMEM] + [VMEM] * len(earlier),
        out_specs=(VMEM,) * len(shapes),
        scratch_shapes=[pltpu.VMEM((rows, LANES), F32), pltpu.VMEM((LANES, LANES), F32)],
        compiler_params=params(),
        cost_estimate=cost(0, 24 * rows * classes),
        name="last_stats",
    )(*own, *other, target, active, *earlier)


def finish_kernel(chunks, e_parts, tile, own_ref, all_ref, target_ref, turned_ref, *refs):
    e_refs = refs[:e_parts]
    refs = refs[e_parts:]
    moved_refs, inverse_refs = refs[:chunks], refs[chunks : 2 * chunks]
    out_ref, loss_ref, residual_ref, column_ref, line_ref, held_ref, sems = refs[2 * chunks :]
    n = all_ref.shape[0]
    classes = residual_ref.shape[1]
    place = lax.axis_index("example")
    class_start = place * classes
    part, peak, scales, total, own_scale = combine(own_ref, all_ref)
    label = sum(part(d, 2) for d in range(n))
    target = target_ref[...]
    valid = (target >= 0.0).astype(F32)
    share = valid / jnp.sum(valid)
    losses = to_slots(peak + jnp.log(total) - label, line_ref, place)
    loss_ref[...] = (valid * losses)[0:1, :]
    factor = to_slots(own_scale / total, line_ref, place)
    column_ref[...] = to_columns([factor, share, target])
    index = class_start + lax.broadcasted_iota(jnp.int32, (1, classes), 1)
    done = 0
    for e_ref in e_refs:
        for k in range(e_ref.shape[0] // LANES):
            j = done + k

            def step(i, _, j=j, k=k, e_ref=e_ref):
                start = i * STEP
                at = pl.ds(j * LANES + start, STEP)
                column = column_ref[pl.ds(start, STEP), :]
                e = e_ref[pl.ds(k * LANES + start, STEP), :]
                probability = e * column[:, j : j + 1]
                hit = index == column[:, 2 * n + j : 2 * n + j + 1].astype(jnp.int32)
                part = column[:, n + j : n + j + 1]
                residual_ref[at, :] = (part * (probability - hit.astype(F32))).astype(BF16)
                return 0

            for i in range(LANES // STEP):
                step(i, 0)
        done += e_ref.shape[0] // LANES

    copies = []
    for k in range(out_ref.shape[0] // tile):
        at = slice(k * tile, (k + 1) * tile)
        done = 0
        for moved_ref, inverse_ref in zip(moved_refs, inverse_refs):
            own = slice(done, done + moved_ref.shape[1])
            gradient = jnp.dot(
                turned_ref[at, :], residual_ref[:, own], preferred_element_type=F32
            )
            held_ref[k, :, own] = moved_ref[at, :] - gradient * inverse_ref[at, :]
            done += moved_ref.shape[1]
            copies.append(
                pltpu.make_async_copy(
                    held_ref.at[k, :, own], out_ref.at[at, own], sems.at[len(copies)]
                )
            )
            copies[-1].start()
    for copy in copies:
        copy.wait()


def finish(own, every, target, e_parts, turned, moved, inverse):
    n = own.shape[0]
    features, all_rows = turned.shape
    classes = e_parts[0].shape[1]
    tile = 512
    return pl.pallas_call(
        functools.partial(finish_kernel, len(moved), len(e_parts), tile),
        out_shape=(
            jax.ShapeDtypeStruct((features, classes), F32),
            jax.ShapeDtypeStruct((1, LANES), F32),
        ),
        in_specs=[VMEM] * (4 + len(e_parts) + 2 * len(moved)),
        out_specs=(ANY, VMEM),
        scratch_shapes=[
            pltpu.VMEM((all_rows, classes), BF16),
            pltpu.VMEM((LANES, LANES), F32),
            pltpu.VMEM((n, LANES), F32),
            pltpu.VMEM((features // tile, tile, classes), F32),
            pltpu.SemaphoreType.DMA((features // tile * len(moved),)),
        ],
        compiler_params=params(16),
        cost_estimate=cost(2 * all_rows * features * classes),
        name="finish",
    )(own, every, target, turned, *e_parts, *moved, *inverse)


def exchange(copies):
    return lax.all_to_all(copies, "example", 0, 0)


def body(n, n_cls, features, weights, labels, counts, active):
    rows = features.shape[0]
    all_rows = rows * n
    feature_count, classes = weights.shape
    entries = feature_count * n_cls * classes * n
    weights = pltpu.with_memory_space_constraint(weights, pltpu.HBM)
    columns = min(512, classes)
    kept, w_low, target, norm = prepare(weights, features, labels, counts, active, columns)
    def first_logits(parts, low, tokens):
        return list(arriving_logits(parts, low, (), 0, all_rows, STEP, tokens))

    slots, waits, w_low, gates, begun = gather_blocks(features, n, w_low, first_logits)
    side = (target, norm, swap(norm, "cls", n_cls, 1))

    groups = [[k, k + 1] for k in range(0, n - 2, 2)] + [[n - 2], [n - 1]]
    count = len(groups)
    behind = max(count - 3, 0)
    plain, buffers, logits, e_parts, stats = (), (), [], [], []

    def statistics(g, tokens):
        last = g == count - 1
        other = [swap(piece, "cls", n_cls, 1) for piece in logits[g]]
        e, found, *copies = first_stats(
            logits[g], other, active, groups[g][0], n, tuple(stats[-1:]),
            side if last else (), tokens,
        )
        e_parts.append(e)
        stats.append(found)
        return copies

    for g in range(count):
        if g == count - 1 and behind:
            logits[behind:], slots[-1] = lax.optimization_barrier((logits[behind:], slots[-1]))
        parts = [part for slot in groups[g] for part in slots[slot]]
        tokens = tuple(stats[-1:]) + tuple(buffers[:1]) + tuple(waits[g] if g < n // 2 else ())
        if g == 2:
            tokens += side[2:]
        start = groups[g][0] * rows
        piece = (64,256,256,128,128)[g] if count == 5 else LANES
        if g == 0 and begun is not None:
            block, found = begun
        else:
            block, found = arriving_logits(parts, w_low, plain, start, all_rows, piece, tokens)
        plain = (block,)
        logits.append(found)
        if g < n // 2 - 1:
            buffers = turn(block, start, 2 * rows, buffers)
        if g < behind:
            logits[g], _ = lax.optimization_barrier((logits[g], gates[g]))
        if g < behind - 1:
            statistics(g, ())
    plain = plain[0]
    turned, squares = turn(plain, (n - 2) * rows, 2 * rows, buffers)
    for g in range(max(behind - 1, 0), count):
        copies = statistics(g, (logits[-1][0], turned))
    own_stats = stats[-1]
    every = exchange(copies[0])
    residual, fisher_weight, damping, target = first_weights(own_stats, every, e_parts, entries)

    moved, inverse, own, other = [], [], [], []
    for start in range(0, classes, columns):
        a, b, low = update(
            turned, squares, kept[start // columns], residual, fisher_weight, damping, start
        )
        moved.append(a)
        inverse.append(b)
        if start + columns < classes:
            own.append(next_logits(plain, low, 0, all_rows))
            other.append(swap(own[-1], "cls", n_cls, 1))
    half = n // 2
    late = [next_logits(plain, low, first * rows, half * rows) for first in (0, half)]
    late_other = [swap(c, "cls", n_cls, 1) for c in late]
    e_parts, earlier = [], ()
    for first, c, d in zip((0, half), late, late_other):
        offsets = [first * rows] * len(own) + [0]
        e, own_stats, *copies = last_stats(
            own + [c], other + [d], offsets, target, active, first, half * rows, n, earlier
        )
        e_parts.append(e)
        earlier = (own_stats,)
    every = exchange(copies[0])
    out, losses = finish(own_stats, every, target, e_parts, turned, moved, inverse)
    return out, losses.reshape(rows)


def solution(mesh):
    return jax.shard_map(
        functools.partial(body, mesh.shape["example"], mesh.shape["cls"]),
        mesh=mesh,
        in_specs=(
            P(("groups", "example"), "cls"),
            P(("groups", "cls"), "example"),
            P(("groups", "example")),
            P(("groups", "example")),
            P("groups"),
        ),
        out_specs=(P(("groups", "cls"), "example"), P(("groups", "example"))),
        check_vma=False,
    )
```

```python
import functools

import jax
import jax.numpy as jnp
from jax import lax
from jax.experimental import pallas as pl
from jax.experimental.pallas import tpu as pltpu
from jax.sharding import PartitionSpec as P

ITERS = 2
NEGATIVE = -1e30
LEARNING_RATE = 2e-05
DAMPING_SHARE = 0.1
EPSILON = 1e-06

F32 = jnp.float32
BF16 = jnp.bfloat16
VMEM = pl.BlockSpec(memory_space=pltpu.VMEM)
SMEM = pl.BlockSpec(memory_space=pltpu.SMEM)
HBM = pl.BlockSpec(memory_space=pltpu.HBM)
ANY = pl.BlockSpec(memory_space=pl.ANY)
STEP = 64
LANES = 128


def params(mib=10):
    return pltpu.CompilerParams(vmem_limit_bytes=mib << 20)


def cost(flops=0, nbytes=0):
    return pl.CostEstimate(flops=int(flops), bytes_accessed=int(nbytes), transcendentals=0)


def swap(x, axis, n, offset):
    return lax.ppermute(x, axis, [(i, i ^ offset) for i in range(n)])


def gray(v):
    return v ^ (v >> 1)


def block_of(place, slot, n):
    if n != 8:
        return lax.rem(place + n - slot, n)
    z, y = place // 2, place % 2
    return gray((gray(z) + 4 - slot // 2) & 3) * 2 + (y ^ (slot % 2))


def token_kernel(*refs):
    refs[-1][...] = jnp.zeros_like(refs[-1])


def token(values):
    return pl.pallas_call(
        token_kernel,
        out_shape=jax.ShapeDtypeStruct((8, LANES), F32),
        in_specs=[ANY] * len(values),
        out_specs=VMEM,
        compiler_params=params(),
        cost_estimate=cost(1, 1),
        name="token",
    )(*values)


def relay_kernel(*refs):
    refs[-1][...] = refs[0][...]


def relay(block, tokens):
    return pl.pallas_call(
        relay_kernel,
        out_shape=pltpu.VMEM(block.shape, block.dtype),
        in_specs=[VMEM] + [ANY] * len(tokens),
        out_specs=VMEM,
        compiler_params=params(),
        cost_estimate=cost(1, 1),
        name="relay",
    )(block, *tokens)


def gather_blocks(x, n, early, first_logits):
    if n != 8:
        ring = [(i, (i + 1) % n) for i in range(n)]
        slots = [x]
        for _ in range(n - 1):
            slots.append(lax.ppermute(slots[-1], "example", ring))
        return [[slot] for slot in slots], [()] * (n // 2), early, [slot for slot in slots[3::2]], None
    hops = ((0, 1), (1, 3), (3, 2), (2, 0))
    ring = [(a * 2 + y, b * 2 + y) for a, b in hops for y in range(2)]
    tie = lax.optimization_barrier
    rows = x.shape[0] // 2
    held, ready = [x[:rows], x[rows:]], [x[:rows], x[rows:]]
    slots = []
    for step in range(3):
        across, later = [], []
        for k in range(2):
            if step == 2 and k == 1:
                begun = first_logits(slots[0] + slots[1], early, tuple(slots[2]))
                held[k], *begun[1] = tie((held[k], *begun[1]))
            later.append(lax.ppermute(held[k], "example", ring))
            across.append(swap(ready[k], "example", n, 1))
        slots += [held, list(across)]
        if step == 0:
            later = [tie((up, early))[0] for up in later]
        if step < 2:
            ready = [tie((up, over))[0] for up, over in zip(later, across)]
        held = later
    seen = token((held[0],))
    seen = token((across[0], seen))
    upper = relay(held[0], (seen,))
    seen = token((held[1], upper))
    lower = relay(across[1], (seen,))
    last = [swap(upper, "example", n, 1), lax.ppermute(lower, "example", ring)]
    slots += [held, last]
    return slots, [tuple(slots[2 * k + 2]) for k in range(3)] + [()], early, [slots[3][1], upper], begun


def prepare_kernel(tile, chunks, w_ref, x_ref, labels_ref, counts_ref, active_ref, *refs):
    kept = refs[:chunks]
    low_ref, target_ref, norm_ref, block_ref, label_ref, sems = refs[chunks:]
    first = [
        pltpu.make_async_copy(x_ref, block_ref, sems.at[0]),
        pltpu.make_async_copy(labels_ref, label_ref, sems.at[1]),
    ]
    copies = []
    for k in range(w_ref.shape[0] // tile):
        at = slice(k * tile, (k + 1) * tile)
        for c, keep in enumerate(kept):
            own = slice(c * keep.shape[1], (c + 1) * keep.shape[1])
            copy = pltpu.make_async_copy(
                w_ref.at[at, own], keep.at[at, :], sems.at[2 + len(copies)]
            )
            copies.append((copy, keep, at, own))
    for copy in first + [c[0] for c in copies]:
        copy.start()
    for copy in first:
        copy.wait()
    rows = x_ref.shape[0]
    slot = lax.broadcasted_iota(jnp.int32, (1, rows), 1)
    target = jnp.where(slot < counts_ref[0], label_ref[...] % active_ref[0], -1)
    target_ref[...] = target.astype(F32)
    squares = (block_ref[...] * block_ref[...]).astype(F32)
    norm = jnp.sum(squares, axis=1, keepdims=True)
    norm_ref[...] = jnp.broadcast_to(norm, (rows, LANES)).T[0:1, :]
    for copy, keep, at, own in copies:
        copy.wait()
        low_ref[at, own] = keep[at, :].astype(BF16)


def prepare(weights, features, labels, counts, active, columns):
    rows = features.shape[0]
    feature_count, classes = weights.shape
    tile, chunks = 256, classes // columns
    line = jax.ShapeDtypeStruct((1, rows), F32)
    *kept, low, target, norm = pl.pallas_call(
        functools.partial(prepare_kernel, tile, chunks),
        out_shape=(pltpu.VMEM((feature_count, columns), F32),) * chunks
        + (pltpu.VMEM((feature_count, classes), BF16), line, line),
        in_specs=[HBM, HBM, HBM, SMEM, SMEM],
        out_specs=(VMEM,) * (chunks + 3),
        scratch_shapes=[
            pltpu.VMEM(features.shape, BF16),
            pltpu.VMEM((1, rows), jnp.int32),
            pltpu.SemaphoreType.DMA((2 + chunks * (feature_count // tile),)),
        ],
        compiler_params=params(),
        cost_estimate=cost(1, 1),
        name="prepare",
    )(
        weights,
        pltpu.with_memory_space_constraint(features, pltpu.HBM),
        pltpu.with_memory_space_constraint(labels.reshape(1, rows), pltpu.HBM),
        counts,
        active,
    )
    return kept, low, target, norm


def arriving_kernel(count, pieces, start, *refs):
    parts, w_ref = refs[:count], refs[count]
    plain_ref, outs = refs[-pieces - 1], refs[-pieces:]
    done = start
    for part in parts:
        plain_ref[done : done + part.shape[0], :] = part[...]
        done += part.shape[0]
    columns = 256
    for first in range(0, w_ref.shape[1], columns):
        own = slice(first, first + columns)
        found = jnp.dot(plain_ref[start:done, :], w_ref[:, own], preferred_element_type=F32)
        for k, out in enumerate(outs):
            out[:, own] = found[k * out.shape[0] : (k + 1) * out.shape[0], :]


def arriving_logits(parts, w_low, plain, start, all_rows, piece, tokens):
    rows = sum(p.shape[0] for p in parts)
    pieces, count = rows // piece, len(parts)
    plain, *logits = pl.pallas_call(
        functools.partial(arriving_kernel, count, pieces, start),
        out_shape=(pltpu.VMEM((all_rows, w_low.shape[0]), BF16),)
        + (jax.ShapeDtypeStruct((piece, w_low.shape[1]), F32),) * pieces,
        in_specs=[VMEM] * (count + 1 + len(plain)) + [ANY] * len(tokens),
        out_specs=(VMEM,) * (pieces + 1),
        input_output_aliases={count + 1: 0} if plain else {},
        compiler_params=params(),
        cost_estimate=cost(1, 1),
        name="arriving_logits",
    )(*parts, w_low, *plain, *tokens)
    return plain, logits


def turn_kernel(start, rows, plain_ref, *refs):
    turned_ref, squares_ref = refs[-2:]
    at = slice(start, start + rows)
    block = plain_ref[at, :].T
    turned_ref[:, at] = block
    squares_ref[:, at] = block * block


def turn(plain, start, rows, buffers):
    buffer = pltpu.VMEM(plain.shape[::-1], BF16)
    return pl.pallas_call(
        functools.partial(turn_kernel, start, rows),
        out_shape=(buffer, buffer),
        in_specs=[VMEM] * (1 + len(buffers)),
        out_specs=(VMEM, VMEM),
        input_output_aliases={1: 0, 2: 1} if buffers else {},
        compiler_params=params(),
        cost_estimate=cost(1, 1),
        name="turn",
    )(plain, *buffers)


def lane_pack(columns, rows):
    lane = lax.broadcasted_iota(jnp.int32, (rows, LANES), 1)
    packed = jnp.zeros((rows, LANES), F32)
    for k, column in enumerate(columns):
        packed = jnp.where(lane == k, column, packed)
    return packed


def put_stats(packed, place, shape):
    lines = packed.T
    line = jnp.concatenate([lines[k : k + 1, :] for k in range(3)], axis=1)
    here = lax.broadcasted_iota(jnp.int32, shape, 0) == place
    return jnp.where(here, line, 0.0)


def first_stats_kernel(slot, pieces, earlier, last, tokens, *refs):
    own, other = refs[:pieces], refs[pieces : 2 * pieces]
    active_ref, refs = refs[2 * pieces], refs[2 * pieces + 1 :]
    lines = refs[: 3 * last]
    older = refs[3 * last : 3 * last + earlier]
    outs = refs[3 * last + earlier + tokens :]
    e_ref, stats_ref, pack_ref = outs[0], outs[1], outs[-1]
    rows, classes = e_ref.shape
    active, place = active_ref[0], lax.axis_index("example")
    class_start = place * classes
    index = class_start + lax.broadcasted_iota(jnp.int32, (1, classes), 1)
    live = index < active
    for k in range(rows // STEP):
        at = slice(k * STEP, (k + 1) * STEP)
        piece, first = k * STEP // own[0].shape[0], k * STEP % own[0].shape[0]
        here = slice(first, first + STEP)
        logits = jnp.where(live, own[piece][here, :] + other[piece][here, :], NEGATIVE)
        peak = jnp.max(logits, axis=1, keepdims=True)
        e = jnp.exp(logits - peak)
        e_ref[at, :] = e
        total = jnp.sum(e, axis=1, keepdims=True)
        square = jnp.sum(e * e, axis=1, keepdims=True)
        pack_ref[at, :] = lane_pack((peak, total, square), STEP)
    shape = stats_ref.shape
    n = shape[0]
    stats = older[0][...] if earlier else jnp.zeros(shape, F32)
    for k in range(rows // LANES):
        stats += put_stats(pack_ref[k * LANES : (k + 1) * LANES, :], block_of(place, slot + k, n), shape)
    stats_ref[...] = stats
    if last:
        copies_ref = outs[2]
        target, norm = lines[0][...], lines[1][...] + lines[2][...]
        wide = [jnp.broadcast_to(line, (shape[0], LANES)) for line in (target, norm)]
        full = jnp.concatenate([stats] + wide, axis=1)
        copies_ref[...] = jnp.broadcast_to(full[None], copies_ref.shape)


def first_stats(own, other, active, slot, n, earlier, side, tokens):
    pieces, classes = len(own), own[0].shape[1]
    rows = pieces * own[0].shape[0]
    last = len(side) > 0
    shapes = [jax.ShapeDtypeStruct((rows, classes), F32), jax.ShapeDtypeStruct((n, 3 * LANES), F32)]
    if last:
        shapes.append(jax.ShapeDtypeStruct((n, n, 5 * LANES), F32))
    extra = list(side) + list(earlier)
    return pl.pallas_call(
        functools.partial(
            first_stats_kernel, slot, pieces, len(earlier), last, len(tokens)
        ),
        out_shape=tuple(shapes),
        in_specs=[VMEM] * (2 * pieces) + [SMEM] + [VMEM] * len(extra) + [ANY] * len(tokens),
        out_specs=(VMEM,) * len(shapes),
        scratch_shapes=[pltpu.VMEM((rows, LANES), F32)],
        compiler_params=params(),
        cost_estimate=cost(1, 1),
        name="first_stats",
    )(*own, *other, active, *extra, *tokens)


def combine(own_ref, all_ref):
    n = all_ref.shape[0]
    part = lambda d, k: all_ref[d, :, k * LANES : (k + 1) * LANES]
    peaks = [part(d, 0) for d in range(n)]
    peak = functools.reduce(jnp.maximum, peaks)
    scales = [jnp.exp(p - peak) for p in peaks]
    total = sum(part(d, 1) * scales[d] for d in range(n))
    own_scale = jnp.exp(own_ref[:, 0:LANES] - peak)
    return part, peak, scales, total, own_scale


def to_slots(value, line_ref, place):
    n = value.shape[0]
    line_ref[...] = value
    return jnp.concatenate([line_ref[pl.ds(block_of(place, j, n), 1), :] for j in range(n)], axis=0)


def to_columns(lines):
    stacked = jnp.concatenate(lines, axis=0)
    rest = jnp.zeros((LANES - stacked.shape[0], LANES), F32)
    return jnp.concatenate([stacked, rest], axis=0).T


def first_weights_kernel(entries, parts, own_ref, all_ref, *refs):
    e_refs = refs[:parts]
    residual_ref, fisher_ref, damping_ref, target_ref, column_ref, line_ref = refs[parts:]
    n = all_ref.shape[0]
    classes = residual_ref.shape[1]
    place = lax.axis_index("example")
    class_start = place * classes
    part, peak, scales, total, own_scale = combine(own_ref, all_ref)
    square = sum(part(d, 2) * (scales[d] * scales[d]) for d in range(n))
    inverse = 1.0 / total
    spread = 1.0 - square * inverse * inverse
    target = jnp.concatenate([all_ref[d, 0:1, 3 * LANES : 4 * LANES] for d in range(n)], axis=0)
    norm = jnp.concatenate([all_ref[d, 0:1, 4 * LANES : 5 * LANES] for d in range(n)], axis=0)
    valid = (target >= 0.0).astype(F32)
    share = valid / jnp.sum(valid)
    fisher_sum = jnp.sum(norm * share * spread)
    damping_ref[...] = jnp.full(
        damping_ref.shape, DAMPING_SHARE * fisher_sum / entries + EPSILON, F32
    )
    factor = to_slots(own_scale * inverse, line_ref, place)
    share = to_slots(share, line_ref, place)
    target = to_slots(target, line_ref, place)
    target_ref[...] = target
    column_ref[...] = to_columns([factor, share, target])
    index = class_start + lax.broadcasted_iota(jnp.int32, (1, classes), 1)
    done = 0
    for e_ref in e_refs:
        for k in range(e_ref.shape[0] // LANES):
            j = done + k

            def step(i, _, j=j, k=k, e_ref=e_ref):
                start = i * STEP
                at = pl.ds(j * LANES + start, STEP)
                column = column_ref[pl.ds(start, STEP), :]
                e = e_ref[pl.ds(k * LANES + start, STEP), :]
                probability = e * column[:, j : j + 1]
                hit = index == column[:, 2 * n + j : 2 * n + j + 1].astype(jnp.int32)
                part = column[:, n + j : n + j + 1]
                residual_ref[at, :] = (part * (probability - hit.astype(F32))).astype(BF16)
                fisher_ref[at, :] = (part * probability * (1.0 - probability)).astype(BF16)
                return 0

            for i in range(LANES // STEP):
                step(i, 0)
        done += e_ref.shape[0] // LANES


def first_weights(own, every, e_parts, entries):
    n = own.shape[0]
    classes = e_parts[0].shape[1]
    weight = pltpu.VMEM((n * LANES, classes), BF16)
    return pl.pallas_call(
        functools.partial(first_weights_kernel, float(entries), len(e_parts)),
        out_shape=(
            weight,
            weight,
            jax.ShapeDtypeStruct((8, LANES), F32),
            jax.ShapeDtypeStruct((n, LANES), F32),
        ),
        in_specs=[VMEM] * (2 + len(e_parts)),
        out_specs=(VMEM,) * 4,
        scratch_shapes=[pltpu.VMEM((LANES, LANES), F32), pltpu.VMEM((n, LANES), F32)],
        compiler_params=params(),
        cost_estimate=cost(0, 8 * n * LANES * classes),
        name="first_weights",
    )(own, every, *e_parts)


def update_kernel(start, tile, turned_ref, squares_ref, w_ref, residual_ref, fisher_ref,
                  damping_ref, moved_ref, inverse_ref, low_ref):
    features, columns = moved_ref.shape
    damping = damping_ref[0:1, 0:1]
    own = slice(start, start + columns)
    for k in range(features // tile):
        at = slice(k * tile, (k + 1) * tile)
        fisher = jnp.dot(squares_ref[at, :], fisher_ref[:, own], preferred_element_type=F32)
        gradient = jnp.dot(turned_ref[at, :], residual_ref[:, own], preferred_element_type=F32)
        inverse = 1.0 / (fisher + damping)
        change = gradient * inverse
        inverse_ref[at, :] = inverse
        low_ref[at, :] = (w_ref[at, :] - LEARNING_RATE * change).astype(BF16)
        moved_ref[at, :] = -change


def update(turned, squares, weights, residual, fisher_weight, damping, start):
    features, rows = turned.shape
    columns = weights.shape[1]
    return pl.pallas_call(
        functools.partial(update_kernel, start, 512),
        out_shape=(
            pltpu.VMEM((features, columns), F32),
            pltpu.VMEM((features, columns), F32),
            pltpu.VMEM((features, columns), BF16),
        ),
        in_specs=[VMEM] * 6,
        out_specs=(VMEM, VMEM, VMEM),
        input_output_aliases={2: 0},
        compiler_params=params(),
        cost_estimate=cost(4 * rows * features * columns),
        name="update",
    )(turned, squares, weights, residual, fisher_weight, damping)


def next_logits_kernel(start, tile, plain_ref, low_ref, *refs):
    out_ref = refs[-1]
    for first in range(0, out_ref.shape[0], tile):
        out_ref[first : first + tile, :] = jnp.dot(
            plain_ref[start + first : start + first + tile, :],
            low_ref[...],
            preferred_element_type=F32,
        )


def next_logits(plain, low, start, rows, tokens=()):
    features, columns = low.shape
    return pl.pallas_call(
        functools.partial(next_logits_kernel, start, min(512, rows)),
        out_shape=jax.ShapeDtypeStruct((rows, columns), F32),
        in_specs=[VMEM, VMEM] + [ANY] * len(tokens),
        out_specs=VMEM,
        compiler_params=params(),
        cost_estimate=cost(2 * rows * features * columns),
        name="next_logits",
    )(plain, low, *tokens)


def last_stats_kernel(slot, last, pieces, offsets, earlier, *refs):
    own, other = refs[:pieces], refs[pieces : 2 * pieces]
    target_ref, active_ref = refs[2 * pieces : 2 * pieces + 2]
    older = refs[2 * pieces + 2 : 2 * pieces + 2 + earlier]
    outs = refs[2 * pieces + 2 + earlier :]
    e_ref, stats_ref, pack_ref, column_ref = outs[0], outs[1], outs[-2], outs[-1]
    rows, classes = e_ref.shape
    active, place = active_ref[0], lax.axis_index("example")
    class_start = place * classes
    n = stats_ref.shape[0]
    column_ref[...] = to_columns([target_ref[...]])
    index = class_start + lax.broadcasted_iota(jnp.int32, (1, classes), 1)
    live = index < active
    for k in range(rows // LANES):
        def step(i, _, k=k):
            start = i * STEP

            def rows_of(base):
                return pl.ds(base + k * LANES + start, STEP)

            logits = jnp.concatenate(
                [a[rows_of(o), :] + b[rows_of(o), :] for a, b, o in zip(own, other, offsets)],
                axis=1,
            )
            column = column_ref[pl.ds(start, STEP), slot + k : slot + k + 1]
            hit = index == column.astype(jnp.int32)
            label = jnp.sum(jnp.where(hit, logits, 0.0), axis=1, keepdims=True)
            logits = jnp.where(live, logits, NEGATIVE)
            peak = jnp.max(logits, axis=1, keepdims=True)
            e = jnp.exp(logits - peak)
            e_ref[rows_of(0), :] = e
            total = jnp.sum(e, axis=1, keepdims=True)
            pack_ref[rows_of(0), :] = lane_pack((peak, total, label), STEP)
            return 0

        for i in range(LANES // STEP):
            step(i, 0)
    shape = stats_ref.shape
    n = shape[0]
    stats = older[0][...] if earlier else jnp.zeros(shape, F32)
    for k in range(rows // LANES):
        stats += put_stats(pack_ref[k * LANES : (k + 1) * LANES, :], block_of(place, slot + k, n), shape)
    stats_ref[...] = stats
    if last:
        outs[2][...] = jnp.broadcast_to(stats[None], outs[2].shape)


def last_stats(own, other, offsets, target, active, slot, rows, n, earlier):
    classes = sum(c.shape[1] for c in own)
    last = slot + rows // LANES == n
    shapes = [
        jax.ShapeDtypeStruct((rows, classes), F32),
        jax.ShapeDtypeStruct((n, 3 * LANES), F32),
    ]
    if last:
        shapes.append(jax.ShapeDtypeStruct((n, n, 3 * LANES), F32))
    return pl.pallas_call(
        functools.partial(
            last_stats_kernel, slot, last, len(own), tuple(offsets), len(earlier)
        ),
        out_shape=tuple(shapes),
        in_specs=[VMEM] * (2 * len(own) + 1) + [SMEM] + [VMEM] * len(earlier),
        out_specs=(VMEM,) * len(shapes),
        scratch_shapes=[pltpu.VMEM((rows, LANES), F32), pltpu.VMEM((LANES, LANES), F32)],
        compiler_params=params(),
        cost_estimate=cost(0, 24 * rows * classes),
        name="last_stats",
    )(*own, *other, target, active, *earlier)


def finish_kernel(chunks, e_parts, tile, own_ref, all_ref, target_ref, turned_ref, *refs):
    e_refs = refs[:e_parts]
    refs = refs[e_parts:]
    moved_refs, inverse_refs = refs[:chunks], refs[chunks : 2 * chunks]
    out_ref, loss_ref, residual_ref, column_ref, line_ref, held_ref, sems = refs[2 * chunks :]
    n = all_ref.shape[0]
    classes = residual_ref.shape[1]
    place = lax.axis_index("example")
    class_start = place * classes
    part, peak, scales, total, own_scale = combine(own_ref, all_ref)
    label = sum(part(d, 2) for d in range(n))
    target = target_ref[...]
    valid = (target >= 0.0).astype(F32)
    share = valid / jnp.sum(valid)
    losses = to_slots(peak + jnp.log(total) - label, line_ref, place)
    loss_ref[...] = (valid * losses)[0:1, :]
    factor = to_slots(own_scale / total, line_ref, place)
    column_ref[...] = to_columns([factor, share, target])
    index = class_start + lax.broadcasted_iota(jnp.int32, (1, classes), 1)
    done = 0
    for e_ref in e_refs:
        for k in range(e_ref.shape[0] // LANES):
            j = done + k

            def step(i, _, j=j, k=k, e_ref=e_ref):
                start = i * STEP
                at = pl.ds(j * LANES + start, STEP)
                column = column_ref[pl.ds(start, STEP), :]
                e = e_ref[pl.ds(k * LANES + start, STEP), :]
                probability = e * column[:, j : j + 1]
                hit = index == column[:, 2 * n + j : 2 * n + j + 1].astype(jnp.int32)
                part = column[:, n + j : n + j + 1]
                residual_ref[at, :] = (part * (probability - hit.astype(F32))).astype(BF16)
                return 0

            for i in range(LANES // STEP):
                step(i, 0)
        done += e_ref.shape[0] // LANES

    copies = []
    for k in range(out_ref.shape[0] // tile):
        at = slice(k * tile, (k + 1) * tile)
        done = 0
        for moved_ref, inverse_ref in zip(moved_refs, inverse_refs):
            own = slice(done, done + moved_ref.shape[1])
            gradient = jnp.dot(
                turned_ref[at, :], residual_ref[:, own], preferred_element_type=F32
            )
            held_ref[k, :, own] = moved_ref[at, :] - gradient * inverse_ref[at, :]
            done += moved_ref.shape[1]
            copies.append(
                pltpu.make_async_copy(
                    held_ref.at[k, :, own], out_ref.at[at, own], sems.at[len(copies)]
                )
            )
            copies[-1].start()
    for copy in copies:
        copy.wait()


def finish(own, every, target, e_parts, turned, moved, inverse):
    n = own.shape[0]
    features, all_rows = turned.shape
    classes = e_parts[0].shape[1]
    tile = 512
    return pl.pallas_call(
        functools.partial(finish_kernel, len(moved), len(e_parts), tile),
        out_shape=(
            jax.ShapeDtypeStruct((features, classes), F32),
            jax.ShapeDtypeStruct((1, LANES), F32),
        ),
        in_specs=[VMEM] * (4 + len(e_parts) + 2 * len(moved)),
        out_specs=(ANY, VMEM),
        scratch_shapes=[
            pltpu.VMEM((all_rows, classes), BF16),
            pltpu.VMEM((LANES, LANES), F32),
            pltpu.VMEM((n, LANES), F32),
            pltpu.VMEM((features // tile, tile, classes), F32),
            pltpu.SemaphoreType.DMA((features // tile * len(moved),)),
        ],
        compiler_params=params(16),
        cost_estimate=cost(2 * all_rows * features * classes),
        name="finish",
    )(own, every, target, turned, *e_parts, *moved, *inverse)


def exchange(copies):
    return lax.all_to_all(copies, "example", 0, 0)


def body(n, n_cls, features, weights, labels, counts, active):
    rows = features.shape[0]
    all_rows = rows * n
    feature_count, classes = weights.shape
    entries = feature_count * n_cls * classes * n
    weights = pltpu.with_memory_space_constraint(weights, pltpu.HBM)
    columns = min(512, classes)
    kept, w_low, target, norm = prepare(weights, features, labels, counts, active, columns)
    def first_logits(parts, low, tokens):
        return list(arriving_logits(parts, low, (), 0, all_rows, STEP, tokens))

    slots, waits, w_low, gates, begun = gather_blocks(features, n, w_low, first_logits)
    side = (target, norm, swap(norm, "cls", n_cls, 1))

    groups = [[k, k + 1] for k in range(0, n - 2, 2)] + [[n - 2], [n - 1]]
    count = len(groups)
    behind = max(count - 3, 0)
    plain, buffers, logits, e_parts, stats = (), (), [], [], []

    def statistics(g, tokens):
        last = g == count - 1
        other = [swap(piece, "cls", n_cls, 1) for piece in logits[g]]
        e, found, *copies = first_stats(
            logits[g], other, active, groups[g][0], n, tuple(stats[-1:]),
            side if last else (), tokens,
        )
        e_parts.append(e)
        stats.append(found)
        return copies

    for g in range(count):
        if g == count - 1 and behind:
            logits[behind:], slots[-1] = lax.optimization_barrier((logits[behind:], slots[-1]))
        parts = [part for slot in groups[g] for part in slots[slot]]
        tokens = tuple(stats[-1:]) + tuple(buffers[:1]) + tuple(waits[g] if g < n // 2 else ())
        if g == 2:
            tokens += side[2:]
        start = groups[g][0] * rows
        piece = (64,256,256,128,128)[g] if count == 5 else LANES
        if g == 0 and begun is not None:
            block, found = begun
        else:
            block, found = arriving_logits(parts, w_low, plain, start, all_rows, piece, tokens)
        plain = (block,)
        logits.append(found)
        if g < n // 2 - 1:
            buffers = turn(block, start, 2 * rows, buffers)
        if g < behind:
            logits[g], _ = lax.optimization_barrier((logits[g], gates[g]))
        if g < behind - 1:
            statistics(g, ())
    plain = plain[0]
    turned, squares = turn(plain, (n - 2) * rows, 2 * rows, buffers)
    for g in range(max(behind - 1, 0), count):
        copies = statistics(g, (logits[-1][0], turned))
    own_stats = stats[-1]
    every = exchange(copies[0])
    residual, fisher_weight, damping, target = first_weights(own_stats, every, e_parts, entries)

    moved, inverse, own, other = [], [], [], []
    for start in range(0, classes, columns):
        a, b, low = update(
            turned, squares, kept[start // columns], residual, fisher_weight, damping, start
        )
        moved.append(a)
        inverse.append(b)
        if start + columns < classes:
            own.append(next_logits(plain, low, 0, all_rows))
            other.append(swap(own[-1], "cls", n_cls, 1))
    quarter = n // 4
    starts = range(0, n, quarter)
    late = []
    for first in starts:
        late.append(next_logits(plain, low, first * rows, quarter * rows, late[-1:]))
    late_other = [swap(c, "cls", n_cls, 1) for c in late]
    e_parts, earlier = [], ()
    for first, c, d in zip(starts, late, late_other):
        offsets = [first * rows] * len(own) + [0]
        e, own_stats, *copies = last_stats(
            own + [c], other + [d], offsets, target, active, first, quarter * rows, n, earlier
        )
        e_parts.append(e)
        earlier = (own_stats,)
    every = exchange(copies[0])
    out, losses = finish(own_stats, every, target, e_parts, turned, moved, inverse)
    return out, losses.reshape(rows)


def solution(mesh):
    return jax.shard_map(
        functools.partial(body, mesh.shape["example"], mesh.shape["cls"]),
        mesh=mesh,
        in_specs=(
            P(("groups", "example"), "cls"),
            P(("groups", "cls"), "example"),
            P(("groups", "example")),
            P(("groups", "example")),
            P("groups"),
        ),
        out_specs=(P(("groups", "cls"), "example"), P(("groups", "example"))),
        check_vma=False,
    )
```
